32 devices in a mesh: dom: 8 (over z, x), rep: 4 (over y, core).
Axes of the slice: x: 2, y: 2, z: 4, core: 2. Of those that a mesh axis runs over, the one named last changes fastest.
Arguments:
- feats: bfloat16 [32768, 256], P(('dom', 'rep')), may hold values from -6 to 6
- w_self: bfloat16 [256, 256], replicated, may hold values from -0.375 to 0.375
- w_neigh: bfloat16 [256, 256], replicated, may hold values from -0.375 to 0.375
- bias: float32 [256], replicated, may hold values from -3 to 3
- out_cot: bfloat16 [32768, 256], P(('dom', 'rep')), may hold values from -6 to 6
- degree: int32 [32768], P(('dom', 'rep')), may hold values from 1 to 20
- edge_src: int32 [32768, 10], P(('dom', 'rep')), may hold values from 0 to 1119, as said below
- hub_rows: int32 [64], P(('dom', 'rep')), may hold values from 0 to 1023, as said below
- send_rows: int32 [256, 4], P(('dom', 'rep')), may hold values from -1 to 1023, as said below
Outputs:
- outputs: bfloat16 [32768, 256], P(('dom', 'rep'))
- grad_feats: bfloat16 [32768, 256], P(('dom', 'rep'))
- unit_w_self: float32 [256, 256], replicated
- unit_w_neigh: float32 [256, 256], replicated
- unit_bias: float32 [256], replicated
The draws below stay inside these ranges and needn't reach their ends.
Inputs may be any that keep to these rules, and one draw needn't show every extreme that they name: `hub_rows`: the 2 entries of one block are distinct rows of that block. `send_rows`: row q * 8 + e lists rows of block q for partition e: live entries first, then -1; every list has a live entry, every block has a full list, and one partition receives full lists from all blocks. `edge_src`: A slot of the halo part of a block's table always names a live entry of the list it comes from.
All inputs are finite; a program needn't handle non-finite values.
Results may differ from the reference program's by a relative error of at most 0.0056.
Values may be sent and summed in bfloat16 or wider, within the bound.
No kernel may reach another device: no remote copies, remote signals or barrier semaphores. Data moves between devices by JAX's collectives and lax.ppermute only.
A program may use at most 128 MiB of HBM per device.

```python
import jax
import jax.numpy as jnp
from jax import lax

F = 256
FANOUT = 10
ROWS = 1024
HUB_DEV = 2
CAP = 4
NODES = 32768
HUBS = 64
N_DOM = 8
N_REP = 4


def halo_plan(key):
    base_key = jax.random.fold_in(key, 7)
    key_counts, key_target, key_busy, key_rows = jax.random.split(base_key, 4)
    block_total = N_DOM * N_REP
    list_counts = jax.random.randint(key_counts, (block_total, N_DOM), 1, CAP + 1)
    target = jax.random.randint(key_target, (block_total, 1), 0, N_DOM)
    busiest = jax.random.randint(key_busy, (1, 1), 0, N_DOM)
    columns = jnp.arange(N_DOM, dtype=jnp.int32)[None, :]
    list_counts = jnp.where((columns == target) | (columns == busiest), CAP, list_counts)
    chosen = jax.random.randint(key_rows, (block_total, N_DOM, CAP), 0, ROWS)
    places = jnp.arange(CAP, dtype=jnp.int32)[None, None, :]
    listed = jnp.where(places < list_counts[:, :, None], chosen, -1)
    return (list_counts, listed)


def draw_send_rows(key, part):
    list_counts, listed = halo_plan(key)
    return listed.reshape(N_DOM * N_REP * N_DOM, CAP).astype(jnp.int32)


def draw_hub_rows(key, part):
    block_keys = jax.random.split(jax.random.fold_in(key, 3), N_DOM * N_REP)
    picked = jax.vmap(lambda one_key: jax.random.permutation(one_key, ROWS)[:HUB_DEV])(block_keys)
    return picked.reshape(-1).astype(jnp.int32)


def draw_edge_src(key, part):
    list_counts, listed = halo_plan(key)
    block_total = N_DOM * N_REP
    incoming = list_counts.reshape(N_DOM, N_REP, N_DOM).transpose(2, 1, 0).reshape(block_total, N_DOM)
    key_kind, key_local, key_first, key_second, key_source, key_place = jax.random.split(jax.random.fold_in(key, 11), 6)
    shape_all = (block_total, ROWS * FANOUT)
    category = jax.random.randint(key_kind, shape_all, 0, 10)
    local_pick = jax.random.randint(key_local, shape_all, 0, ROWS)
    hub_pick = jnp.minimum(jax.random.randint(key_first, shape_all, 0, HUBS), jax.random.randint(key_second, shape_all, 0, HUBS))
    source = jax.random.randint(key_source, shape_all, 0, N_DOM)
    available = jnp.take_along_axis(incoming, source, axis=1)
    position = jax.random.randint(key_place, shape_all, 0, available)
    halo_pick = ROWS + HUBS + source * CAP + position
    slot_ids = jnp.where(category < 6, local_pick, jnp.where(category < 7, ROWS + hub_pick, halo_pick))
    return slot_ids.reshape(block_total * ROWS, FANOUT).astype(jnp.int32)


def place_ends(entries, key, low, largest):
    longest = entries.shape.index(max(entries.shape))
    spots = []
    for shift in (0, 1):
        where = [jax.random.randint(jax.random.fold_in(key, axis), (), 0, length) for axis, length in enumerate(entries.shape)]
        where[longest] = (where[longest] + shift) % entries.shape[longest]
        spots.append(tuple(where))
    return entries.at[spots[0]].set(low).at[spots[1]].set(largest)


def block_scale(key, extent, shards, smallest, largest):
    level = 1.0
    for dim, parts in shards:
        steps = jax.random.uniform(jax.random.fold_in(jax.random.fold_in(key, 6), dim), (parts,), jnp.float32, smallest / len(shards), largest / len(shards))
        level = level * jnp.repeat(jnp.exp(steps), extent[dim] // parts).reshape((-1,) + (1,) * (len(extent) - 1 - dim))
    return level


def bell_draw(stream_key, extent, spread, limit, pieces=(), kind=jnp.bfloat16):
    result = spread * jax.random.normal(stream_key, extent, jnp.float32)
    if pieces:
        result = result * block_scale(stream_key, extent, pieces, -0.22, 0.18)
    return jnp.clip(result, -limit, limit).astype(kind)


def setup_inputs(seed: int = 0) -> dict:
    streams_of = jax.random.split(jax.random.key(seed), 10)
    feats = bell_draw(streams_of[0], (NODES, F), 1.0, 6.0, ((0, 32),))
    w_self = bell_draw(streams_of[1], (F, F), F ** -0.5, 0.375)
    w_neigh = bell_draw(streams_of[2], (F, F), F ** -0.5, 0.375)
    bias = bell_draw(streams_of[3], (F,), 0.5, 3.0, (), jnp.float32)
    out_cot = bell_draw(streams_of[4], (NODES, F), 1.0, 6.0, ((0, 32),))
    degree = place_ends(jax.random.randint(streams_of[5], (NODES,), 1, 2 * FANOUT + 1), jax.random.fold_in(streams_of[5], 1), 1, 2 * FANOUT).astype(jnp.int32)
    edge_src = draw_edge_src(jax.random.fold_in(streams_of[9], 71), 0)
    hub_rows = draw_hub_rows(jax.random.fold_in(streams_of[9], 71), 0)
    send_rows = draw_send_rows(jax.random.fold_in(streams_of[9], 71), 0)
    return {"feats": feats, "w_self": w_self, "w_neigh": w_neigh, "bias": bias, "out_cot": out_cot, "degree": degree, "edge_src": edge_src, "hub_rows": hub_rows, "send_rows": send_rows}


NORM_EPS = 1e-05
UNIT_EPS = 1e-06

def output_head(preact):
    act = jax.nn.elu(preact)
    return act * lax.rsqrt(lax.optimization_barrier(jnp.mean(act * act, axis=-1, keepdims=True)) + NORM_EPS)

def unit_scale(grad):
    return grad * lax.rsqrt(jnp.mean(grad * grad) + UNIT_EPS)

def slot_globals(hub_rows, send_rows):
    block_total = N_DOM * N_REP
    own_nodes = jnp.arange(block_total, dtype=jnp.int32)[:, None] * ROWS + jnp.arange(ROWS, dtype=jnp.int32)[None, :]
    hub_global = jnp.arange(HUBS, dtype=jnp.int32) // HUB_DEV * ROWS + hub_rows
    hub_part = jnp.broadcast_to(hub_global[None, :], (block_total, HUBS))
    listed = send_rows.reshape(N_DOM, N_REP, N_DOM, CAP).transpose(2, 1, 0, 3)
    sender = jnp.arange(N_DOM, dtype=jnp.int32)[None, None, :, None] * N_REP + jnp.arange(N_REP, dtype=jnp.int32)[None, :, None, None]
    halo_part = jnp.where(listed >= 0, sender * ROWS + listed, -1).reshape(block_total, N_DOM * CAP)
    return jnp.concatenate([own_nodes, hub_part, halo_part.astype(jnp.int32)], axis=1)

def reference(feats, w_self, w_neigh, bias, out_cot, degree, edge_src, hub_rows, send_rows):
    block_total = N_DOM * N_REP
    slot_nodes = slot_globals(hub_rows, send_rows)
    picked = jnp.take_along_axis(slot_nodes, edge_src.reshape(block_total, ROWS * FANOUT), axis=1)
    picked = picked.reshape(block_total * ROWS, FANOUT)
    valid_count = jnp.minimum(degree, FANOUT)
    live_mask = (jnp.arange(FANOUT, dtype=jnp.int32)[None, :] < valid_count[:, None]) & (picked >= 0)
    slot_safe = jnp.maximum(picked, 0)
    summed = jnp.zeros((block_total * ROWS, F), jnp.float32)
    for sample in range(FANOUT):
        gathered = feats[slot_safe[:, sample]].astype(jnp.float32)
        summed = summed + jnp.where(live_mask[:, sample:sample + 1], gathered, jnp.float32(0.0))
    divisor = valid_count.astype(jnp.float32)[:, None]
    neighbor_mean = (summed / divisor).astype(jnp.bfloat16)
    preact = jnp.dot(feats, w_self, preferred_element_type=jnp.float32) + jnp.dot(neighbor_mean, w_neigh, preferred_element_type=jnp.float32) + bias
    outputs, backward = jax.vjp(output_head, preact)
    grad_pre, = backward(out_cot.astype(jnp.float32))
    grad_low = grad_pre.astype(jnp.bfloat16)
    grad_w_self = jnp.dot(feats.T, grad_low, preferred_element_type=jnp.float32)
    grad_w_neigh = jnp.dot(neighbor_mean.T, grad_low, preferred_element_type=jnp.float32)
    grad_bias = lax.optimization_barrier(jnp.sum(grad_pre, axis=0))
    feat_grad = jnp.dot(grad_low, w_self.T, preferred_element_type=jnp.float32)
    edge_grad = jnp.dot(grad_low, w_neigh.T, preferred_element_type=jnp.float32) / divisor
    for sample in range(FANOUT):
        feat_grad = feat_grad.at[slot_safe[:, sample]].add(jnp.where(live_mask[:, sample:sample + 1], edge_grad, jnp.float32(0.0)))
    return (outputs.astype(jnp.bfloat16), feat_grad.astype(jnp.bfloat16), unit_scale(grad_w_self), unit_scale(grad_w_neigh), unit_scale(grad_bias))
```

```python
import functools

import jax
import jax.numpy as jnp
from jax import lax
from jax.experimental import pallas as pl
from jax.experimental.pallas import tpu as pltpu
from jax.sharding import PartitionSpec as P

NORM_EPS = 1e-05
UNIT_EPS = 1e-06
AXES = ("dom", "rep")
VMEM_LIMIT = 48 * 1024 * 1024
F32 = jnp.float32
BF16 = jnp.bfloat16
BIAS_ROWS = 2


def div_floor(value, size):
    if size & (size - 1) == 0:
        return lax.shift_right_arithmetic(value, jnp.int32(size.bit_length() - 1))
    return value // size


def remainder(value, size):
    if size & (size - 1) == 0:
        return value & jnp.int32(size - 1)
    return value - (value // size) * size


def matmul(lhs, rhs, lhs_dim=1, rhs_dim=0):
    return lax.dot_general(
        lhs, rhs, (((lhs_dim,), (rhs_dim,)), ((), ())), preferred_element_type=F32
    )


def one_hot(rows, places, first=0):
    numbers = lax.broadcasted_iota(jnp.int32, (rows, places.shape[1]), 0) + first
    return jnp.where(numbers == places, F32(1.0), F32(0.0)).astype(BF16)


def pick_kernel(sizes, hub_ref, send_ref, feats_ref, rows_ref, places_ref):
    doms, reps, cap, hub_own, tall = sizes
    slots = doms * reps * tall
    lane = lax.broadcasted_iota(jnp.int32, (1, slots), 1)
    row = remainder(lane, tall)
    block = div_floor(lane, tall)
    key = div_floor(block, reps) * tall + row
    group = remainder(block, reps)

    def list_entries(dom, places):
        for entry in range(cap):
            places = jnp.where(key == dom * tall + entry, send_ref[entry, dom], places)
        return places

    places = jnp.full((1, slots), -1, jnp.int32)
    if doms <= 16:
        for dom in range(doms):
            places = list_entries(dom, places)
    else:
        places = lax.fori_loop(0, doms, list_entries, places)
    places = jnp.where((row < cap) & (group != lax.axis_index("rep")), -1, places)
    for entry in range(hub_own):
        places = jnp.where(row == cap + entry, hub_ref[entry], places)
    places_ref[...] = places
    step = min(slots, 256)

    def pick(start):
        chosen = one_hot(feats_ref.shape[0], places_ref[:, pl.ds(start, step)])
        rows_ref[pl.ds(start, step), :] = matmul(chosen, feats_ref[...], 0, 0).astype(BF16)

    if slots == step:
        pick(0)
    else:
        pl.loop(0, slots, step=step)(lambda start: pick(pl.multiple_of(start, step)))


def layer_kernel(
    sizes,
    feats_ref,
    remote_ref,
    w_self_ref,
    w_neigh_ref,
    bias_ref,
    cot_ref,
    degree_ref,
    edge_ref,
    outputs_ref,
    feat_grad_ref,
    message_ref,
    slot_ref,
    share_ref,
    count_ref,
    table_ref,
    mean_ref,
    low_ref,
    edge_grad_ref,
    bias_sum_ref,
):
    doms, reps, cap, hub_own, tall, slab = sizes
    rows, width = feats_ref.shape
    fanout = edge_ref.shape[0]
    blocks = doms * reps
    hubs = blocks * hub_own
    slots = rows + blocks * tall
    tile = 256

    source = edge_ref[...]
    hub = source - rows
    halo = hub - hubs
    hub_slot = rows + cap + div_floor(hub, hub_own) * tall + remainder(hub, hub_own)
    halo_slot = (
        rows
        + (div_floor(halo, cap) * reps + lax.axis_index("rep")) * tall
        + remainder(halo, cap)
    )
    slot = jnp.where(source < rows, source, jnp.where(hub < hubs, hub_slot, halo_slot))
    valid = jnp.minimum(degree_ref[...], fanout)
    number = lax.broadcasted_iota(jnp.int32, (fanout, rows), 0)
    slot_ref[...] = jnp.where(number < valid, slot, -1)
    share_ref[...] = 1.0 / valid.astype(F32)

    table_ref[:, :rows] = feats_ref[...].T
    table_ref[:, rows:] = remote_ref[...].T
    bias_sum_ref[...] = jnp.zeros_like(bias_sum_ref)

    def node_tile(step):
        nodes = pl.ds(pl.multiple_of(step * tile, tile), tile)
        wanted = [
            jnp.broadcast_to(slot_ref[k : k + 1, nodes], (tile, tile)).astype(jnp.int16)
            for k in range(fanout)
        ]
        base = lax.broadcasted_iota(jnp.int32, (tile, tile), 0).astype(jnp.int16)
        total = jnp.zeros((width, tile), F32)
        for first in range(0, slots, tile):
            numbers = base + jnp.int16(first)
            count = jnp.zeros((tile, tile), BF16)
            for k in range(fanout):
                count = count + jnp.where(numbers == wanted[k], BF16(1.0), BF16(0.0))
            count_ref[first : first + tile, nodes] = count
            total = total + matmul(table_ref[:, first : first + tile], count)
        share = share_ref[:, nodes]
        mean = (total * share).astype(BF16)
        mean_ref[:, nodes] = mean
        share_column = jnp.broadcast_to(share, (128, tile)).T
        share_column = jnp.concatenate([share_column] * (width // 128), axis=1)

        preact = (
            matmul(feats_ref[nodes, :], w_self_ref[...])
            + matmul(mean, w_neigh_ref[...], 0, 0)
            + bias_ref[...]
        )
        cot = cot_ref[nodes, :].astype(F32)
        grown = jnp.exp(jnp.minimum(preact, 0.0))
        act = jnp.where(preact > 0.0, preact, grown - 1.0)
        scale = lax.rsqrt(jnp.sum(act * act, axis=1, keepdims=True) * (1.0 / width) + NORM_EPS)
        outputs_ref[nodes, :] = (act * scale).astype(BF16)
        along = jnp.sum(act * cot, axis=1, keepdims=True)
        pull = along * (scale * scale * scale) * (1.0 / width)
        grad_pre = (cot * scale - act * pull) * jnp.where(preact > 0.0, F32(1.0), grown)
        bias_sum_ref[...] += jnp.sum(grad_pre, axis=0, keepdims=True)
        grad_low = grad_pre.astype(BF16)
        low_ref[nodes, :] = grad_low
        edge_grad = matmul(grad_low, w_neigh_ref[...], 1, 1) * share_column
        edge_grad_ref[nodes, :] = edge_grad.astype(BF16)

    pl.loop(0, rows // tile)(node_tile)

    low = low_ref[...]
    w_grad = jnp.concatenate(
        [matmul(table_ref[:, :rows], low), matmul(mean_ref[...], low)], axis=0
    )
    edge_grad = edge_grad_ref[...]
    for first in range(0, rows, tile):
        feat_grad_ref[first : first + tile, :] = matmul(
            count_ref[first : first + tile, :], edge_grad
        ) + matmul(low_ref[first : first + tile, :], w_self_ref[...], 1, 1)
    remote = matmul(count_ref[rows:, :], edge_grad).reshape(blocks, tall, width)
    bias_sum = jnp.broadcast_to(bias_sum_ref[...], (tall, width))
    bias_high = bias_sum.astype(BF16).astype(F32)
    place = lax.broadcasted_iota(jnp.int32, (tall, width), 0)
    bias_rows = jnp.where(place == tall - 1, bias_sum - bias_high, bias_high)
    remote = jnp.where((place < tall - BIAS_ROWS)[None], remote, bias_rows[None])
    owners = w_grad.shape[0] // slab
    w_grad = w_grad.reshape(owners, slab, width)
    if owners < blocks:
        w_grad = jnp.concatenate([w_grad, jnp.zeros((blocks - owners, slab, width), F32)], axis=0)
    message_ref[...] = jnp.concatenate([w_grad, remote], axis=1).astype(BF16)


def slab_kernel(slab, message_ref, slab_ref, unit_bias_ref):
    message = message_ref[...].astype(F32)
    own = jnp.sum(message[:, :slab, :], axis=0)
    slab_ref[...] = jnp.broadcast_to(own[None], slab_ref.shape).astype(BF16)
    bias = jnp.sum(jnp.sum(message[:, slab:, :], axis=0)[-BIAS_ROWS:, :], axis=0, keepdims=True)
    unit_bias_ref[...] = bias * lax.rsqrt(jnp.mean(bias * bias, axis=1, keepdims=True) + UNIT_EPS)


def scatter_kernel(slab, message_ref, places_ref, feat_grad_ref, out_ref):
    blocks, tall, width = message_ref.shape
    tall -= slab
    returned = message_ref[...].astype(F32)[:, slab:, :]
    returned = returned.reshape(blocks * tall, width).astype(BF16)
    chosen = one_hot(out_ref.shape[0], places_ref[...])
    out_ref[...] = (feat_grad_ref[...] + matmul(chosen, returned)).astype(BF16)


def unit_kernel(grads_ref, unit_self_ref, unit_neigh_ref):
    size = unit_self_ref.shape[0]
    for first, unit_ref in ((0, unit_self_ref), (size, unit_neigh_ref)):
        grad = grads_ref[first : first + size, :].astype(F32)
        square = jnp.sum(jnp.sum(grad * grad, axis=0, keepdims=True), axis=1, keepdims=True)
        unit_ref[...] = grad * lax.rsqrt(square * (1.0 / grad.size) + UNIT_EPS)


def call(kernel, out_shape, in_specs=None, scratch=(), cost=(0, 0)):
    return pl.pallas_call(
        kernel,
        out_shape=out_shape,
        **({} if in_specs is None else {"in_specs": in_specs}),
        scratch_shapes=list(scratch),
        compiler_params=pltpu.CompilerParams(vmem_limit_bytes=VMEM_LIMIT),
        cost_estimate=pl.CostEstimate(flops=cost[0], bytes_accessed=cost[1], transcendentals=0),
    )


def on_device(
    doms, reps, feats, w_self, w_neigh, bias, out_cot, degree, edge_src, hub_rows, send_rows
):
    rows, width = feats.shape
    fanout = edge_src.shape[1]
    cap, hub_own = send_rows.shape[1], hub_rows.shape[0]
    blocks = doms * reps
    tall = -(-(cap + hub_own + BIAS_ROWS) // 8) * 8
    slots = rows + blocks * tall
    slab = max(8, 2 * width // blocks)
    shape = jax.ShapeDtypeStruct
    smem = pl.BlockSpec(memory_space=pltpu.SMEM)
    vmem = pl.BlockSpec(memory_space=pltpu.VMEM)

    outgoing, places = call(
        functools.partial(pick_kernel, (doms, reps, cap, hub_own, tall)),
        (shape((blocks * tall, width), BF16), shape((1, blocks * tall), jnp.int32)),
        [smem, smem, vmem],
        cost=(2 * rows * blocks * tall * width, 2 * rows * width),
    )(hub_rows, send_rows.T, feats)
    remote = lax.all_to_all(outgoing, AXES, split_axis=0, concat_axis=0, tiled=True)

    outputs, feat_grad, message = call(
        functools.partial(layer_kernel, (doms, reps, cap, hub_own, tall, slab)),
        (
            shape((rows, width), BF16),
            shape((rows, width), F32),
            shape((blocks, slab + tall, width), BF16),
        ),
        scratch=(
            pltpu.VMEM((fanout, rows), jnp.int32),
            pltpu.VMEM((1, rows), F32),
            pltpu.VMEM((slots, rows), BF16),
            pltpu.VMEM((width, slots), BF16),
            pltpu.VMEM((width, rows), BF16),
            pltpu.VMEM((rows, width), BF16),
            pltpu.VMEM((rows, width), BF16),
            pltpu.VMEM((1, width), F32),
        ),
        cost=(4 * rows * slots * width + 12 * rows * width * width, 8 * rows * width),
    )(
        feats,
        remote,
        w_self,
        w_neigh,
        bias.reshape(1, width),
        out_cot,
        degree.reshape(1, rows),
        edge_src.T,
    )
    message = lax.all_to_all(message, AXES, split_axis=0, concat_axis=0, tiled=True)

    slabs, unit_bias = call(
        functools.partial(slab_kernel, slab),
        (shape((blocks, slab, width), BF16), shape((1, width), F32)),
    )(message)
    slabs = lax.all_to_all(slabs, AXES, split_axis=0, concat_axis=0, tiled=True)
    grad_feats = call(functools.partial(scatter_kernel, slab), shape((rows, width), BF16))(
        message, places, feat_grad
    )
    unit_self, unit_neigh = call(
        unit_kernel, (shape((width, width), F32), shape((width, width), F32))
    )(slabs.reshape(blocks * slab, width)[: 2 * width])
    return outputs, grad_feats, unit_self, unit_neigh, unit_bias.reshape(width)


def solution(mesh):
    rows, whole = P(AXES, None), P()
    return jax.shard_map(
        functools.partial(on_device, mesh.shape["dom"], mesh.shape["rep"]),
        mesh=mesh,
        in_specs=(rows, whole, whole, whole, rows, P(AXES), rows, P(AXES), rows),
        out_specs=(rows, rows, whole, whole, whole),
        check_vma=False,
    )
```

```python
import functools

import jax
import jax.numpy as jnp
from jax import lax
from jax.experimental import pallas as pl
from jax.experimental.pallas import tpu as pltpu
from jax.sharding import PartitionSpec as P

NORM_EPS = 1e-05
UNIT_EPS = 1e-06
AXES = ("dom", "rep")
VMEM_LIMIT = 48 * 1024 * 1024
F32 = jnp.float32
BF16 = jnp.bfloat16
TILE = 256
STRIP = 16
BIAS_ROWS = 2


def div_floor(value, size):
    if size & (size - 1) == 0:
        return lax.shift_right_arithmetic(value, jnp.int32(size.bit_length() - 1))
    return value // size


def remainder(value, size):
    if size & (size - 1) == 0:
        return value & jnp.int32(size - 1)
    return value - (value // size) * size


def matmul(lhs, rhs, lhs_dim=1, rhs_dim=0):
    return lax.dot_general(
        lhs, rhs, (((lhs_dim,), (rhs_dim,)), ((), ())), preferred_element_type=F32
    )


def iota(shape, dim):
    return lax.broadcasted_iota(jnp.int32, shape, dim)


def one_hot(rows, places):
    return jnp.where(iota((rows, places.shape[1]), 0) == places, F32(1.0), F32(0.0)).astype(BF16)


def hub_places(doms, tall, cap, hub_own):
    lane = iota((1, doms * tall), 1)
    entry = remainder(lane, tall) - cap
    return jnp.where(
        (entry >= 0) & (entry < hub_own), div_floor(lane, tall) * hub_own + entry, -1
    )


def pick_kernel(
    sizes, hub_hbm, send_hbm, feats_hbm, rows_ref, places_ref, hub_ref, send_ref, feats_ref, sems
):
    doms, cap, hub_own, tall = sizes
    copies = [
        pltpu.make_async_copy(source, target, sems.at[number])
        for number, (source, target) in enumerate(
            ((hub_hbm, hub_ref), (send_hbm, send_ref), (feats_hbm, feats_ref))
        )
    ]
    for copy in copies:
        copy.start()
    slots = doms * tall
    lane = iota((1, slots), 1)
    row = remainder(lane, tall)

    def list_entries(dom, places):
        for entry in range(cap):
            places = jnp.where(lane == dom * tall + entry, send_ref[entry, dom], places)
        return places

    copies[0].wait()
    copies[1].wait()
    places = jnp.full((1, slots), -1, jnp.int32)
    if doms <= 16:
        for dom in range(doms):
            places = list_entries(dom, places)
    else:
        places = lax.fori_loop(0, doms, list_entries, places)
    for entry in range(hub_own):
        places = jnp.where(row == cap + entry, hub_ref[entry], places)
    places_ref[...] = places
    chosen = one_hot(feats_ref.shape[0], places)
    copies[2].wait()
    rows_ref[...] = matmul(chosen, feats_ref[...], 0, 0).astype(BF16)


def hub_kernel(sizes, rows_ref, hubs_ref):
    doms, cap, hub_own, tall = sizes
    chosen = one_hot(doms * hub_own, hub_places(doms, tall, cap, hub_own))
    hubs_ref[...] = matmul(chosen, rows_ref[...]).astype(BF16)


def count_edges(slot_ref, count_ref, nodes, first, count_rows):
    fanout, tile = slot_ref.shape[0], TILE
    wanted = [
        jnp.broadcast_to(slot_ref[k : k + 1, nodes], (STRIP, tile)).astype(jnp.int16)
        for k in range(fanout)
    ]
    base = iota((STRIP, tile), 0).astype(jnp.int16)
    for start in range(0, count_rows, STRIP):
        numbers = base + jnp.int16(first + start)
        count = jnp.zeros((STRIP, tile), BF16)
        for k in range(fanout):
            count = count + jnp.where(numbers == wanted[k], BF16(1.0), BF16(0.0))
        count_ref[start : start + STRIP, nodes] = count


def own_kernel(
    sizes,
    feats_ref,
    w_self_ref,
    bias_ref,
    degree_ref,
    edge_ref,
    slot_ref,
    share_ref,
    turned_ref,
    count_ref,
    total_ref,
    preact_ref,
):
    doms, reps, cap, hub_own, tall = sizes
    rows = feats_ref.shape[0]
    fanout = edge_ref.shape[0]
    hubs = doms * reps * hub_own

    source = edge_ref[...]
    hub = source - rows
    halo = hub - hubs
    owner = div_floor(hub, hub_own)
    back = remainder(lax.axis_index("rep") - remainder(owner, reps) + reps, reps)
    hub_slot = (
        rows
        + doms * tall
        + (back * doms + div_floor(owner, reps)) * hub_own
        + remainder(hub, hub_own)
    )
    halo_slot = rows + div_floor(halo, cap) * tall + remainder(halo, cap)
    slot = jnp.where(source < rows, source, jnp.where(hub < hubs, hub_slot, halo_slot))
    valid = jnp.minimum(degree_ref[...], fanout)
    slot_ref[...] = jnp.where(iota((fanout, rows), 0) < valid, slot, -1)
    share_ref[...] = 1.0 / valid.astype(F32)
    turned_ref[...] = feats_ref[...].T

    @pl.loop(0, rows // TILE)
    def node_tile(step):
        nodes = pl.ds(pl.multiple_of(step * TILE, TILE), TILE)
        count_edges(slot_ref, count_ref, nodes, 0, rows)
        total_ref[:, nodes] = matmul(turned_ref[...], count_ref[:, nodes])
        preact_ref[nodes, :] = matmul(feats_ref[nodes, :], w_self_ref[...]) + bias_ref[...]


def joint_kernel(sizes, *refs):
    doms, reps, cap, hub_own, tall = sizes
    received_ref, *hub_refs = refs[: 1 + reps]
    (
        turned_ref,
        total_ref,
        self_ref,
        slot_ref,
        share_ref,
        w_neigh_hbm,
        cot_hbm,
        outputs_ref,
        message_ref,
        halo_ref,
        low_ref,
        edge_grad_ref,
        w_neigh_ref,
        cot_ref,
        table_ref,
        count_ref,
        mean_ref,
        bias_sum_ref,
        sems,
    ) = refs[1 + reps :]
    rows, width = outputs_ref.shape
    table_rows = table_ref.shape[0]
    hub_rows = doms * hub_own
    copies = [
        pltpu.make_async_copy(w_neigh_hbm, w_neigh_ref, sems.at[0]),
        pltpu.make_async_copy(cot_hbm, cot_ref, sems.at[1]),
    ]
    for copy in copies:
        copy.start()
    table_ref[: doms * tall, :] = received_ref[...]
    for back, hub_ref in enumerate(hub_refs):
        first = doms * tall + back * hub_rows
        table_ref[first : first + hub_rows, :] = hub_ref[...]
    table = table_ref[...].T
    bias_sum_ref[...] = jnp.zeros_like(bias_sum_ref)
    for copy in copies:
        copy.wait()

    @pl.loop(0, rows // TILE)
    def node_tile(step):
        nodes = pl.ds(pl.multiple_of(step * TILE, TILE), TILE)
        count_edges(slot_ref, count_ref, nodes, rows, table_rows)
        share = share_ref[:, nodes]
        mean = (total_ref[:, nodes] + matmul(table, count_ref[:, nodes])) * share
        mean = mean.astype(BF16)
        mean_ref[:, nodes] = mean
        share_column = jnp.broadcast_to(share, (128, TILE)).T
        share_column = jnp.concatenate([share_column] * (width // 128), axis=1)

        preact = self_ref[nodes, :] + matmul(mean, w_neigh_ref[...], 0, 0)
        cot = cot_ref[nodes, :].astype(F32)
        grown = jnp.exp(jnp.minimum(preact, 0.0))
        act = jnp.where(preact > 0.0, preact, grown - 1.0)
        scale = lax.rsqrt(jnp.sum(act * act, axis=1, keepdims=True) * (1.0 / width) + NORM_EPS)
        outputs_ref[nodes, :] = (act * scale).astype(BF16)
        along = jnp.sum(act * cot, axis=1, keepdims=True)
        pull = along * (scale * scale * scale) * (1.0 / width)
        grad_pre = (cot * scale - act * pull) * jnp.where(preact > 0.0, F32(1.0), grown)
        bias_sum_ref[...] += jnp.sum(grad_pre, axis=0, keepdims=True)
        grad_low = grad_pre.astype(BF16)
        low_ref[nodes, :] = grad_low
        edge_grad = matmul(grad_low, w_neigh_ref[...], 1, 1) * share_column
        edge_grad_ref[nodes, :] = edge_grad.astype(BF16)

    remote = matmul(count_ref[...], edge_grad_ref[...])
    halo_ref[...] = remote[: doms * tall, :]
    low = low_ref[...]
    w_grad = jnp.concatenate([matmul(turned_ref[...], low), matmul(mean_ref[...], low)], axis=0)
    bias_sum = jnp.broadcast_to(bias_sum_ref[...], (8, width))
    bias_high = bias_sum.astype(BF16).astype(F32)
    bias_rows = jnp.where(iota((8, width), 0) == 0, bias_high, bias_sum - bias_high)
    share_rows = w_grad.shape[0] // reps
    mine = lax.axis_index("rep")
    for back in range(reps):
        group = remainder(mine - back + reps, reps)
        first = doms * tall + back * hub_rows
        message_ref[group, share_rows:, :] = jnp.concatenate(
            [remote[first : first + hub_rows, :], bias_rows], axis=0
        ).astype(BF16)
    for group in range(reps):
        message_ref[group, :share_rows, :] = w_grad[
            group * share_rows : (group + 1) * share_rows, :
        ].astype(BF16)


def rep_sum_kernel(sizes, slab, received_ref, halo_ref, message_ref):
    doms, cap, hub_own, tall = sizes
    width = halo_ref.shape[1]
    hub_rows = doms * hub_own
    total = jnp.sum(received_ref[...].astype(F32), axis=0)
    share_rows = total.shape[0] - hub_rows - 8
    owners = share_rows // slab
    w_grad = total[:share_rows, :].reshape(owners, slab, width)
    if owners < doms:
        w_grad = jnp.concatenate([w_grad, jnp.zeros((doms - owners, slab, width), F32)], axis=0)
    hub = total[share_rows : share_rows + hub_rows, :].astype(BF16)
    chosen = one_hot(hub_rows, hub_places(doms, tall, cap, hub_own))
    rest = (halo_ref[...] + matmul(chosen, hub, 0, 0)).reshape(doms, tall, width)
    bias = total[share_rows + hub_rows :, :]
    bias = jnp.broadcast_to(bias[0:1, :] + bias[1:2, :], (tall, width))
    bias_high = bias.astype(BF16).astype(F32)
    place = iota((tall, width), 0)
    bias_rows = jnp.where(place == tall - 1, bias - bias_high, bias_high)
    rest = jnp.where((place < tall - BIAS_ROWS)[None], rest, bias_rows[None])
    message_ref[...] = jnp.concatenate([w_grad, rest], axis=1).astype(BF16)


def dom_sum_kernel(slab, message_ref, slab_ref, unit_bias_ref):
    total = jnp.sum(message_ref[...].astype(F32), axis=0)
    slab_ref[...] = jnp.broadcast_to(total[None, :slab, :], slab_ref.shape).astype(BF16)
    bias = jnp.sum(total[-BIAS_ROWS:, :], axis=0, keepdims=True)
    unit_bias_ref[...] = bias * lax.rsqrt(jnp.mean(bias * bias, axis=1, keepdims=True) + UNIT_EPS)


def feat_grad_kernel(
    slab, message_ref, places_ref, count_ref, edge_grad_ref, low_ref, w_self_ref, out_ref
):
    doms, tall, width = message_ref.shape
    tall -= slab
    returned = message_ref[...].astype(F32)[:, slab:, :]
    returned = returned.reshape(doms * tall, width).astype(BF16)
    chosen = one_hot(out_ref.shape[0], places_ref[...])
    for first in range(0, out_ref.shape[0], TILE):
        last = first + TILE
        out_ref[first:last, :] = (
            matmul(count_ref[first:last, :], edge_grad_ref[...])
            + matmul(low_ref[first:last, :], w_self_ref[...], 1, 1)
            + matmul(chosen[first:last, :], returned)
        ).astype(BF16)


def unit_kernel(*refs):
    *part_refs, unit_self_ref, unit_neigh_ref, grads_ref = refs
    reps, share_rows = len(part_refs), part_refs[0].shape[0]
    mine = lax.axis_index("rep")
    for back, part_ref in enumerate(part_refs):
        group = remainder(mine - back + reps, reps)
        place = pl.ds(pl.multiple_of(group * share_rows, share_rows), share_rows)
        grads_ref[place, :] = part_ref[...].astype(F32)
    size = unit_self_ref.shape[0]
    for first, unit_ref in ((0, unit_self_ref), (size, unit_neigh_ref)):
        grad = grads_ref[first : first + size, :]
        square = jnp.sum(jnp.sum(grad * grad, axis=0, keepdims=True), axis=1, keepdims=True)
        unit_ref[...] = grad * lax.rsqrt(square * (1.0 / grad.size) + UNIT_EPS)


def call(kernel, out_shape, in_specs=None, scratch=(), cost=(0, 0)):
    return pl.pallas_call(
        kernel,
        out_shape=out_shape,
        **({} if in_specs is None else {"in_specs": in_specs}),
        scratch_shapes=list(scratch),
        compiler_params=pltpu.CompilerParams(vmem_limit_bytes=VMEM_LIMIT),
        cost_estimate=pl.CostEstimate(flops=cost[0], bytes_accessed=cost[1], transcendentals=0),
    )


def swap(array, axis):
    return lax.all_to_all(array, axis, split_axis=0, concat_axis=0, tiled=True)


def from_groups(array, reps):
    parts = [array]
    for back in range(1, reps):
        pairs = [(group, (group + back) % reps) for group in range(reps)]
        parts.append(lax.ppermute(array, "rep", pairs))
    return parts


def on_device(
    doms, reps, feats, w_self, w_neigh, bias, out_cot, degree, edge_src, hub_rows, send_rows
):
    rows, width = feats.shape
    fanout = edge_src.shape[1]
    cap, hub_own = send_rows.shape[1], hub_rows.shape[0]
    tall = -(-(cap + hub_own + BIAS_ROWS) // 8) * 8
    slots = doms * tall
    remote = slots + doms * reps * hub_own
    share_rows = 2 * width // reps
    slab = max(8, share_rows // doms)
    sizes = (doms, reps, cap, hub_own, tall)
    dom_sizes = (doms, cap, hub_own, tall)
    shape = jax.ShapeDtypeStruct
    hbm = pl.BlockSpec(memory_space=pltpu.HBM)
    vmem = pl.BlockSpec(memory_space=pltpu.VMEM)

    outgoing, places = call(
        functools.partial(pick_kernel, dom_sizes),
        (shape((slots, width), BF16), shape((1, slots), jnp.int32)),
        [hbm, hbm, hbm],
        (
            pltpu.SMEM((hub_own,), jnp.int32),
            pltpu.SMEM((cap, doms), jnp.int32),
            pltpu.VMEM((rows, width), BF16),
            pltpu.SemaphoreType.DMA((3,)),
        ),
        cost=(2 * rows * slots * width, 2 * rows * width),
    )(hub_rows, send_rows.T, feats)
    received = swap(outgoing, "dom")
    slot, share, turned, count, own_total, self_part = call(
        functools.partial(own_kernel, sizes),
        (
            shape((fanout, rows), jnp.int32),
            shape((1, rows), F32),
            shape((width, rows), BF16),
            shape((rows, rows), BF16),
            shape((width, rows), F32),
            shape((rows, width), F32),
        ),
        cost=(8 * rows * rows * width, 12 * rows * width + 2 * rows * rows),
    )(feats, w_self, bias.reshape(1, width), degree.reshape(1, rows), edge_src.T)
    hubs = call(
        functools.partial(hub_kernel, dom_sizes), shape((doms * hub_own, width), BF16)
    )(received)
    hubs = from_groups(hubs, reps)

    outputs, message, halo, low, edge_grad = call(
        functools.partial(joint_kernel, sizes),
        (
            shape((rows, width), BF16),
            shape((reps, share_rows + doms * hub_own + 8, width), BF16),
            shape((slots, width), F32),
            shape((rows, width), BF16),
            shape((rows, width), BF16),
        ),
        [vmem] * (6 + reps) + [hbm] * 2,
        (
            pltpu.VMEM((width, width), BF16),
            pltpu.VMEM((rows, width), BF16),
            pltpu.VMEM((remote, width), BF16),
            pltpu.VMEM((remote, rows), BF16),
            pltpu.VMEM((width, rows), BF16),
            pltpu.VMEM((1, width), F32),
            pltpu.SemaphoreType.DMA((2,)),
        ),
        cost=(4 * rows * remote * width + 8 * rows * width * width, 16 * rows * width),
    )(received, *hubs, turned, own_total, self_part, slot, share, w_neigh, out_cot)

    message = call(
        functools.partial(rep_sum_kernel, dom_sizes, slab),
        shape((doms, slab + tall, width), BF16),
    )(swap(message, "rep"), halo)
    message = swap(message, "dom")
    slabs, unit_bias = call(
        functools.partial(dom_sum_kernel, slab),
        (shape((doms, slab, width), BF16), shape((1, width), F32)),
    )(message)
    slabs = swap(slabs, "dom").reshape(doms * slab, width)[:share_rows]
    grad_feats = call(
        functools.partial(feat_grad_kernel, slab),
        shape((rows, width), BF16),
        cost=(2 * rows * rows * width + 2 * rows * width * width, 6 * rows * width),
    )(message, places, count, edge_grad, low, w_self)
    unit_self, unit_neigh = call(
        unit_kernel,
        (shape((width, width), F32), shape((width, width), F32)),
        scratch=(pltpu.VMEM((2 * width, width), F32),),
    )(*from_groups(slabs, reps))
    return outputs, grad_feats, unit_self, unit_neigh, unit_bias.reshape(width)


def solution(mesh):
    rows, whole = P(AXES, None), P()
    return jax.shard_map(
        functools.partial(on_device, mesh.shape["dom"], mesh.shape["rep"]),
        mesh=mesh,
        in_specs=(rows, whole, whole, whole, rows, P(AXES), rows, P(AXES), rows),
        out_specs=(rows, rows, whole, whole, whole),
        check_vma=False,
    )
```

```python
import functools

import jax
import jax.numpy as jnp
from jax import lax
from jax.experimental import pallas as pl
from jax.experimental.pallas import tpu as pltpu
from jax.sharding import PartitionSpec as P

NORM_EPS = 1e-05
UNIT_EPS = 1e-06
AXES = ("dom", "rep")
VMEM_LIMIT = 48 * 1024 * 1024
F32 = jnp.float32
BF16 = jnp.bfloat16
TILE = 256
STRIP = 16
BIAS_ROWS = 2


def div_floor(value, size):
    if size & (size - 1) == 0:
        return lax.shift_right_arithmetic(value, jnp.int32(size.bit_length() - 1))
    return value // size


def remainder(value, size):
    if size & (size - 1) == 0:
        return value & jnp.int32(size - 1)
    return value - (value // size) * size


def matmul(lhs, rhs, lhs_dim=1, rhs_dim=0):
    return lax.dot_general(
        lhs, rhs, (((lhs_dim,), (rhs_dim,)), ((), ())), preferred_element_type=F32
    )


def iota(shape, dim):
    return lax.broadcasted_iota(jnp.int32, shape, dim)


def one_hot(rows, places):
    return jnp.where(iota((rows, places.shape[1]), 0) == places, F32(1.0), F32(0.0)).astype(BF16)


def hub_places(doms, tall, cap, hub_own):
    lane = iota((1, doms * tall), 1)
    entry = remainder(lane, tall) - cap
    return jnp.where(
        (entry >= 0) & (entry < hub_own), div_floor(lane, tall) * hub_own + entry, -1
    )


def apart(doms):
    return doms <= 16 and doms & (doms - 1) == 0


def twist(doms):
    return lax.axis_index("dom") if apart(doms) else jnp.int32(0)


def put(refs, number, value):
    if len(refs) == 1:
        refs[0][number] = value
    else:
        refs[number][...] = value


def messages(refs):
    if len(refs) == 1:
        return refs[0][...].astype(F32).reshape(-1, refs[0].shape[2])
    return jnp.concatenate([ref[...].astype(F32) for ref in refs], axis=0)


def fetch(pairs, sems):
    copies = [
        pltpu.make_async_copy(source, target, sems.at[number])
        for number, (source, target) in enumerate(pairs)
    ]
    for copy in copies:
        copy.start()
    return copies


def pick_kernel(sizes, hub_hbm, send_hbm, feats_hbm, *refs):
    doms, cap, hub_own, tall = sizes
    *row_refs, places_ref, hub_ref, send_ref, feats_ref, sems = refs
    copies = fetch(((hub_hbm, hub_ref), (send_hbm, send_ref), (feats_hbm, feats_ref)), sems)
    slots = doms * tall
    lane = iota((1, slots), 1)
    row = remainder(lane, tall)
    turn = twist(doms)

    def list_entries(number, places):
        dom = number ^ turn
        for entry in range(cap):
            places = jnp.where(lane == number * tall + entry, send_ref[entry, dom], places)
        return places

    copies[0].wait()
    copies[1].wait()
    places = jnp.full((1, slots), -1, jnp.int32)
    if doms <= 16:
        for number in range(doms):
            places = list_entries(number, places)
    else:
        places = lax.fori_loop(0, doms, list_entries, places)
    for entry in range(hub_own):
        places = jnp.where(row == cap + entry, hub_ref[entry], places)
    places_ref[...] = places
    chosen = one_hot(feats_ref.shape[0], places)
    copies[2].wait()
    rows = matmul(chosen, feats_ref[...], 0, 0)
    for number in range(doms):
        put(row_refs, number, rows[number * tall : (number + 1) * tall, :].astype(BF16))


def hub_kernel(sizes, *refs):
    doms, cap, hub_own, tall = sizes
    *row_refs, hubs_ref = refs
    chosen = one_hot(doms * hub_own, hub_places(doms, tall, cap, hub_own))
    hubs_ref[...] = matmul(chosen, messages(row_refs).astype(BF16)).astype(BF16)


def count_edges(slot_ref, count_ref, nodes, first, count_rows):
    fanout, tile = slot_ref.shape[0], TILE
    wanted = [
        jnp.broadcast_to(slot_ref[k : k + 1, nodes], (STRIP, tile)).astype(jnp.int16)
        for k in range(fanout)
    ]
    base = iota((STRIP, tile), 0).astype(jnp.int16)
    for start in range(0, count_rows, STRIP):
        numbers = base + jnp.int16(first + start)
        count = jnp.zeros((STRIP, tile), BF16)
        for k in range(fanout):
            count = count + jnp.where(numbers == wanted[k], BF16(1.0), BF16(0.0))
        count_ref[start : start + STRIP, nodes] = count


def own_kernel(sizes, *refs):
    doms, reps, cap, hub_own, tall = sizes
    inputs, (slot_ref, share_ref, turned_ref, count_ref, total_ref, preact_ref) = refs[:5], refs[5:11]
    degree_ref, edge_ref, feats_ref, w_self_ref, bias_ref, sems = refs[11:]
    copies = fetch(zip(inputs, (degree_ref, edge_ref, feats_ref, w_self_ref, bias_ref)), sems)
    rows = feats_ref.shape[0]
    fanout = edge_ref.shape[0]
    hubs = doms * reps * hub_own
    copies[0].wait()
    copies[1].wait()

    source = edge_ref[...]
    hub = source - rows
    halo = hub - hubs
    owner = div_floor(hub, hub_own)
    turn = twist(doms)
    partner = remainder(owner, reps) ^ lax.axis_index("rep")
    hub_slot = (
        rows
        + doms * tall
        + (partner * doms + (div_floor(owner, reps) ^ turn)) * hub_own
        + remainder(hub, hub_own)
    )
    halo_slot = rows + (div_floor(halo, cap) ^ turn) * tall + remainder(halo, cap)
    slot = jnp.where(source < rows, source, jnp.where(hub < hubs, hub_slot, halo_slot))
    valid = jnp.minimum(degree_ref[...], fanout)
    slot_ref[...] = jnp.where(iota((fanout, rows), 0) < valid, slot, -1)
    share_ref[...] = 1.0 / valid.astype(F32)
    for copy in copies[2:]:
        copy.wait()
    turned_ref[...] = feats_ref[...].T

    @pl.loop(0, rows // TILE)
    def node_tile(step):
        nodes = pl.ds(pl.multiple_of(step * TILE, TILE), TILE)
        count_edges(slot_ref, count_ref, nodes, 0, rows)
        total_ref[:, nodes] = matmul(turned_ref[...], count_ref[:, nodes])
        preact_ref[nodes, :] = matmul(feats_ref[nodes, :], w_self_ref[...]) + bias_ref[...]


def joint_kernel(sizes, row_count, *refs):
    doms, reps, cap, hub_own, tall = sizes
    row_refs, refs = refs[:row_count], refs[row_count:]
    hub_refs, refs = refs[:reps], refs[reps:]
    (turned_ref, total_ref, self_ref, slot_ref, share_ref, w_neigh_hbm, cot_hbm), refs = (
        refs[:7],
        refs[7:],
    )
    message_refs, refs = refs[:reps], refs[reps:]
    (
        outputs_ref,
        halo_ref,
        low_ref,
        edge_grad_ref,
        w_neigh_ref,
        cot_ref,
        count_ref,
        mean_ref,
        bias_sum_ref,
        w_grad_ref,
        sems,
    ) = refs
    rows, width = outputs_ref.shape
    hub_rows = doms * hub_own
    copies = fetch(((w_neigh_hbm, w_neigh_ref), (cot_hbm, cot_ref)), sems)
    table = jnp.concatenate([messages(row_refs)] + [ref[...].astype(F32) for ref in hub_refs], axis=0)
    table_rows = table.shape[0]
    table = table.T.astype(BF16)
    bias_sum_ref[...] = jnp.zeros_like(bias_sum_ref)
    for copy in copies:
        copy.wait()

    @pl.loop(0, rows // TILE)
    def node_tile(step):
        nodes = pl.ds(pl.multiple_of(step * TILE, TILE), TILE)
        count_edges(slot_ref, count_ref, nodes, rows, table_rows)
        share = share_ref[:, nodes]
        mean = (total_ref[:, nodes] + matmul(table, count_ref[:, nodes])) * share
        mean = mean.astype(BF16)
        mean_ref[:, nodes] = mean
        share_column = jnp.broadcast_to(share, (128, TILE)).T
        share_column = jnp.concatenate([share_column] * (width // 128), axis=1)

        preact = self_ref[nodes, :] + matmul(mean, w_neigh_ref[...], 0, 0)
        cot = cot_ref[nodes, :].astype(F32)
        grown = jnp.exp(jnp.minimum(preact, 0.0))
        act = jnp.where(preact > 0.0, preact, grown - 1.0)
        scale = lax.rsqrt(jnp.sum(act * act, axis=1, keepdims=True) * (1.0 / width) + NORM_EPS)
        outputs_ref[nodes, :] = (act * scale).astype(BF16)
        along = jnp.sum(act * cot, axis=1, keepdims=True)
        pull = along * (scale * scale * scale) * (1.0 / width)
        grad_pre = (cot * scale - act * pull) * jnp.where(preact > 0.0, F32(1.0), grown)
        bias_sum_ref[...] += jnp.sum(grad_pre, axis=0, keepdims=True)
        grad_low = grad_pre.astype(BF16)
        low_ref[nodes, :] = grad_low
        edge_grad = matmul(grad_low, w_neigh_ref[...], 1, 1) * share_column
        edge_grad_ref[nodes, :] = edge_grad.astype(BF16)

    remote = matmul(count_ref[...], edge_grad_ref[...])
    halo_ref[...] = remote[: doms * tall, :]
    low = low_ref[...]
    w_grad_ref[:width, :] = matmul(turned_ref[...], low)
    w_grad_ref[width:, :] = matmul(mean_ref[...], low)
    bias_sum = jnp.broadcast_to(bias_sum_ref[...], (8, width))
    bias_high = bias_sum.astype(BF16).astype(F32)
    bias_rows = jnp.where(iota((8, width), 0) == 0, bias_high, bias_sum - bias_high)
    share_rows = 2 * width // reps
    mine = lax.axis_index("rep")
    for number, message_ref in enumerate(message_refs):
        place = pl.multiple_of((mine ^ number) * share_rows, share_rows)
        first = doms * tall + number * hub_rows
        message_ref[...] = jnp.concatenate(
            [w_grad_ref[pl.ds(place, share_rows), :], remote[first : first + hub_rows, :], bias_rows],
            axis=0,
        ).astype(BF16)


def rep_sum_kernel(sizes, slab, group_count, *refs):
    doms, cap, hub_own, tall = sizes
    received_refs, halo_ref, refs = refs[:group_count], refs[group_count], refs[group_count + 1 :]
    *message_refs, total_ref = refs
    width = halo_ref.shape[1]
    hub_rows = doms * hub_own
    total = received_refs[0][...].astype(F32)
    for received_ref in received_refs[1:]:
        total = total + received_ref[...].astype(F32)
    share_rows = total.shape[0] - hub_rows - 8
    owners = share_rows // slab
    total_ref[...] = total[:share_rows, :]
    hub = total[share_rows : share_rows + hub_rows, :].astype(BF16)
    chosen = one_hot(hub_rows, hub_places(doms, tall, cap, hub_own))
    rest = halo_ref[...] + matmul(chosen, hub, 0, 0)
    bias = total[share_rows + hub_rows :, :]
    bias = jnp.broadcast_to(bias[0:1, :] + bias[1:2, :], (tall, width))
    bias_high = bias.astype(BF16).astype(F32)
    place = iota((tall, width), 0)
    bias_rows = jnp.where(place == tall - 1, bias - bias_high, bias_high)
    turn = twist(doms)
    for number in range(doms):
        tail = rest[number * tall : (number + 1) * tall, :]
        tail = jnp.where(place < tall - BIAS_ROWS, tail, bias_rows)
        if number < owners or apart(doms):
            first = pl.multiple_of((number ^ turn) * slab, slab)
            w_grad = total_ref[pl.ds(first, slab), :]
        else:
            w_grad = jnp.zeros((slab, width), F32)
        put(message_refs, number, jnp.concatenate([w_grad, tail], axis=0).astype(BF16))


def dom_sum_kernel(slab, *refs):
    *message_refs, slab_ref, unit_bias_ref = refs
    if len(message_refs) == 1:
        total = jnp.sum(message_refs[0][...].astype(F32), axis=0)
        slab_ref[...] = jnp.broadcast_to(total[None, :slab, :], slab_ref.shape).astype(BF16)
    else:
        total = message_refs[0][...].astype(F32)
        for message_ref in message_refs[1:]:
            total = total + message_ref[...].astype(F32)
        slab_ref[...] = total[:slab, :].astype(BF16)
    bias = jnp.sum(total[-BIAS_ROWS:, :], axis=0, keepdims=True)
    unit_bias_ref[...] = bias * lax.rsqrt(jnp.mean(bias * bias, axis=1, keepdims=True) + UNIT_EPS)


def feat_grad_kernel(slab, *refs):
    *message_refs, places_ref, count_ref, edge_grad_ref, low_ref, w_self_ref, out_ref = refs
    if len(message_refs) == 1:
        returned = message_refs[0][...].astype(F32)[:, slab:, :].reshape(-1, out_ref.shape[1])
    else:
        returned = [ref[...].astype(F32)[slab:, :] for ref in message_refs]
        returned = jnp.concatenate(returned, axis=0)
    returned = returned.astype(BF16)
    chosen = one_hot(out_ref.shape[0], places_ref[...])
    for first in range(0, out_ref.shape[0], TILE):
        last = first + TILE
        out_ref[first:last, :] = (
            matmul(count_ref[first:last, :], edge_grad_ref[...])
            + matmul(low_ref[first:last, :], w_self_ref[...], 1, 1)
            + matmul(chosen[first:last, :], returned)
        ).astype(BF16)


def join_kernel(*refs):
    *slab_refs, out_ref = refs
    slab = slab_refs[0].shape[0]
    for number, slab_ref in enumerate(slab_refs):
        first = pl.multiple_of((number ^ lax.axis_index("dom")) * slab, slab)
        out_ref[pl.ds(first, slab), :] = slab_ref[...]


def unit_kernel(*refs):
    *part_refs, unit_self_ref, unit_neigh_ref, grads_ref = refs
    share_rows = part_refs[0].shape[0]
    mine = lax.axis_index("rep")
    for number, part_ref in enumerate(part_refs):
        place = pl.ds(pl.multiple_of((mine ^ number) * share_rows, share_rows), share_rows)
        grads_ref[place, :] = part_ref[...].astype(F32)
    size = unit_self_ref.shape[0]
    for first, unit_ref in ((0, unit_self_ref), (size, unit_neigh_ref)):
        grad = grads_ref[first : first + size, :]
        square = jnp.sum(jnp.sum(grad * grad, axis=0, keepdims=True), axis=1, keepdims=True)
        unit_ref[...] = grad * lax.rsqrt(square * (1.0 / grad.size) + UNIT_EPS)


def call(kernel, out_shape, in_specs=None, scratch=(), cost=(0, 0)):
    return pl.pallas_call(
        kernel,
        out_shape=out_shape,
        **({} if in_specs is None else {"in_specs": in_specs}),
        scratch_shapes=list(scratch),
        compiler_params=pltpu.CompilerParams(vmem_limit_bytes=VMEM_LIMIT),
        cost_estimate=pl.CostEstimate(flops=cost[0], bytes_accessed=cost[1], transcendentals=0),
    )


def in_hbm(*arrays):
    return [pltpu.with_memory_space_constraint(array, pltpu.HBM) for array in arrays]


def trade(parts, axis):
    pairs = range(len(parts))
    return [parts[0]] + [
        lax.ppermute(parts[number], axis, [(index, index ^ number) for index in pairs])
        for number in pairs[1:]
    ]


def trade_doms(parts):
    if len(parts) > 1:
        return trade(parts, "dom")
    return [lax.all_to_all(parts[0], "dom", split_axis=0, concat_axis=0, tiled=True)]


def on_device(
    doms, reps, feats, w_self, w_neigh, bias, out_cot, degree, edge_src, hub_rows, send_rows
):
    rows, width = feats.shape
    fanout = edge_src.shape[1]
    cap, hub_own = send_rows.shape[1], hub_rows.shape[0]
    tall = -(-(cap + hub_own + BIAS_ROWS) // 8) * 8
    slots = doms * tall
    remote = slots + doms * reps * hub_own
    share_rows = 2 * width // reps
    slab = max(8, share_rows // doms)
    sizes = (doms, reps, cap, hub_own, tall)
    dom_sizes = (doms, cap, hub_own, tall)
    shape = jax.ShapeDtypeStruct
    hbm = pl.BlockSpec(memory_space=pltpu.HBM)
    vmem = pl.BlockSpec(memory_space=pltpu.VMEM)

    def dom_messages(height):
        if apart(doms):
            return (shape((height, width), BF16),) * doms
        return (shape((doms, height, width), BF16),)

    *outgoing, places = call(
        functools.partial(pick_kernel, dom_sizes),
        (*dom_messages(tall), shape((1, slots), jnp.int32)),
        [hbm] * 3,
        (
            pltpu.SMEM((hub_own,), jnp.int32),
            pltpu.SMEM((cap, doms), jnp.int32),
            pltpu.VMEM((rows, width), BF16),
            pltpu.SemaphoreType.DMA((3,)),
        ),
        cost=(2 * rows * slots * width, 2 * rows * width),
    )(*in_hbm(hub_rows, send_rows.T, feats))
    received = trade_doms(outgoing)
    slot, share, turned, count, own_total, self_part = call(
        functools.partial(own_kernel, sizes),
        (
            shape((fanout, rows), jnp.int32),
            shape((1, rows), F32),
            shape((width, rows), BF16),
            shape((rows, rows), BF16),
            shape((width, rows), F32),
            shape((rows, width), F32),
        ),
        [hbm] * 5,
        (
            pltpu.VMEM((1, rows), jnp.int32),
            pltpu.VMEM((fanout, rows), jnp.int32),
            pltpu.VMEM((rows, width), BF16),
            pltpu.VMEM((width, width), BF16),
            pltpu.VMEM((1, width), F32),
            pltpu.SemaphoreType.DMA((5,)),
        ),
        cost=(8 * rows * rows * width, 12 * rows * width + 2 * rows * rows),
    )(*in_hbm(degree.reshape(1, rows), edge_src.T, feats, w_self, bias.reshape(1, width)))
    hubs = call(
        functools.partial(hub_kernel, dom_sizes), shape((doms * hub_own, width), BF16)
    )(*received)
    hubs = trade([hubs] * reps, "rep")

    *message, outputs, halo, low, edge_grad = call(
        functools.partial(joint_kernel, sizes, len(received)),
        (
            *((shape((share_rows + doms * hub_own + 8, width), BF16),) * reps),
            shape((rows, width), BF16),
            shape((slots, width), F32),
            shape((rows, width), BF16),
            shape((rows, width), BF16),
        ),
        [vmem] * (len(received) + reps + 5) + [hbm] * 2,
        (
            pltpu.VMEM((width, width), BF16),
            pltpu.VMEM((rows, width), BF16),
            pltpu.VMEM((remote, rows), BF16),
            pltpu.VMEM((width, rows), BF16),
            pltpu.VMEM((1, width), F32),
            pltpu.VMEM((2 * width, width), F32),
            pltpu.SemaphoreType.DMA((2,)),
        ),
        cost=(4 * rows * remote * width + 8 * rows * width * width, 16 * rows * width),
    )(*received, *hubs, turned, own_total, self_part, slot, share, *in_hbm(w_neigh, out_cot))

    message = call(
        functools.partial(rep_sum_kernel, dom_sizes, slab, reps),
        dom_messages(slab + tall),
        scratch=(pltpu.VMEM((share_rows, width), F32),),
    )(*trade(message, "rep"), halo)
    message = trade_doms(message)
    slabs, unit_bias = call(
        functools.partial(dom_sum_kernel, slab),
        (
            shape((slab, width) if apart(doms) else (doms, slab, width), BF16),
            shape((1, width), F32),
        ),
    )(*message)
    if apart(doms):
        slabs = call(join_kernel, shape((doms * slab, width), BF16))(*trade([slabs] * doms, "dom"))
    else:
        slabs = trade_doms([slabs])[0].reshape(doms * slab, width)
    grad_feats = call(
        functools.partial(feat_grad_kernel, slab),
        shape((rows, width), BF16),
        cost=(2 * rows * rows * width + 2 * rows * width * width, 6 * rows * width),
    )(*message, places, count, edge_grad, low, w_self)
    unit_self, unit_neigh = call(
        unit_kernel,
        (shape((width, width), F32), shape((width, width), F32)),
        scratch=(pltpu.VMEM((2 * width, width), F32),),
    )(*trade([slabs[:share_rows]] * reps, "rep"))
    return outputs, grad_feats, unit_self, unit_neigh, unit_bias.reshape(width)


def solution(mesh):
    rows, whole = P(AXES, None), P()
    return jax.shard_map(
        functools.partial(on_device, mesh.shape["dom"], mesh.shape["rep"]),
        mesh=mesh,
        in_specs=(rows, whole, whole, whole, rows, P(AXES), rows, P(AXES), rows),
        out_specs=(rows, rows, whole, whole, whole),
        check_vma=False,
    )
```

```python
import functools

import jax
import jax.numpy as jnp
from jax import lax
from jax.experimental import pallas as pl
from jax.experimental.pallas import tpu as pltpu
from jax.sharding import PartitionSpec as P

NORM_EPS = 1e-05
UNIT_EPS = 1e-06
SPLIT_AXES = ("dom", "pair", "side")
PEERS = ("dom", "pair")
SIDES = 2
VMEM_LIMIT = 48 * 1024 * 1024
F32 = jnp.float32
BF16 = jnp.bfloat16
TILE = 256
STRIP = 16
BIAS_ROWS = 2


def div_floor(value, size):
    if size & (size - 1) == 0:
        return lax.shift_right_arithmetic(value, jnp.int32(size.bit_length() - 1))
    return value // size


def remainder(value, size):
    if size & (size - 1) == 0:
        return value & jnp.int32(size - 1)
    return value - (value // size) * size


def matmul(lhs, rhs, lhs_dim=1, rhs_dim=0):
    return lax.dot_general(
        lhs, rhs, (((lhs_dim,), (rhs_dim,)), ((), ())), preferred_element_type=F32
    )


def iota(shape, dim):
    return lax.broadcasted_iota(jnp.int32, shape, dim)


def one_hot(rows, places):
    return jnp.where(iota((rows, places.shape[1]), 0) == places, F32(1.0), F32(0.0)).astype(BF16)


def fetch(pairs, sems):
    copies = [
        pltpu.make_async_copy(source, target, sems.at[number])
        for number, (source, target) in enumerate(pairs)
    ]
    for copy in copies:
        copy.start()
    return copies


def pick_kernel(sizes, hub_hbm, send_hbm, feats_hbm, *refs):
    doms, reps, cap, hub_own, tall = sizes
    rows_ref, places_ref, peer_places_ref, hub_ref, send_ref, feats_ref, sems = refs
    copies = fetch(((hub_hbm, hub_ref), (send_hbm, send_ref), (feats_hbm, feats_ref)), sems)
    copies[0].wait()
    copies[1].wait()
    pair = lax.axis_index("pair")
    for groups, wanted, out_ref in (
        (reps, pair * SIDES + lax.axis_index("side"), places_ref),
        (reps // SIDES, pair, peer_places_ref),
    ):
        lane = iota(out_ref.shape, 1)
        row = remainder(lane, tall)
        block = div_floor(lane, tall)
        key = div_floor(block, groups) * tall + row

        def list_entries(dom, places):
            for entry in range(cap):
                places = jnp.where(key == dom * tall + entry, send_ref[entry, dom], places)
            return places

        places = jnp.full(lane.shape, -1, jnp.int32)
        if doms <= 16:
            for dom in range(doms):
                places = list_entries(dom, places)
        else:
            places = lax.fori_loop(0, doms, list_entries, places)
        places = jnp.where((row < cap) & (remainder(block, groups) != wanted), -1, places)
        for entry in range(hub_own):
            places = jnp.where(row == cap + entry, hub_ref[entry], places)
        out_ref[...] = places
    slots = places_ref.shape[1]
    step = min(slots, TILE)
    copies[2].wait()

    def pick(start):
        chosen = one_hot(feats_ref.shape[0], places_ref[:, pl.ds(start, step)])
        rows_ref[pl.ds(start, step), :] = matmul(chosen, feats_ref[...], 0, 0).astype(BF16)

    if slots == step:
        pick(0)
    else:
        pl.loop(0, slots, step=step)(lambda start: pick(pl.multiple_of(start, step)))


def count_edges(slot_ref, count_ref, nodes):
    fanout, tile = slot_ref.shape[0], TILE
    slots = count_ref.shape[0]
    wanted = [
        jnp.broadcast_to(slot_ref[k : k + 1, nodes], (STRIP, tile)).astype(jnp.int16)
        for k in range(fanout)
    ]
    base = iota((STRIP, tile), 0)

    def strips(first, last, start):
        for strip in range(first, last, STRIP):
            numbers = (base + (start + strip)).astype(jnp.int16)
            count = jnp.zeros((STRIP, tile), BF16)
            for k in range(fanout):
                count = count + jnp.where(numbers == wanted[k], BF16(1.0), BF16(0.0))
            if isinstance(start, int):
                count_ref[start + strip : start + strip + STRIP, nodes] = count
            else:
                count_ref[pl.ds(pl.multiple_of(start + strip, STRIP), STRIP), nodes] = count

    if slots <= 2048:
        strips(0, slots, 0)
    else:
        pl.loop(0, slots, step=TILE)(lambda start: strips(0, TILE, start))


def own_kernel(sizes, *refs):
    doms, reps, cap, hub_own, tall = sizes
    inputs, (share_ref, turned_ref, count_ref, total_ref, preact_ref) = refs[:5], refs[5:10]
    degree_ref, edge_ref, feats_ref, w_self_ref, bias_ref, slot_ref, sems = refs[10:]
    copies = fetch(zip(inputs, (degree_ref, edge_ref, feats_ref, w_self_ref, bias_ref)), sems)
    rows = feats_ref.shape[0]
    fanout = edge_ref.shape[0]
    hubs = doms * reps * hub_own
    copies[0].wait()
    copies[1].wait()

    source = edge_ref[...]
    hub = source - rows
    halo = hub - hubs
    group = lax.axis_index("pair") * SIDES + lax.axis_index("side")
    hub_slot = rows + cap + div_floor(hub, hub_own) * tall + remainder(hub, hub_own)
    halo_slot = rows + (div_floor(halo, cap) * reps + group) * tall + remainder(halo, cap)
    slot = jnp.where(source < rows, source, jnp.where(hub < hubs, hub_slot, halo_slot))
    valid = jnp.minimum(degree_ref[...], fanout)
    slot_ref[...] = jnp.where(iota((fanout, rows), 0) < valid, slot, -1)
    share_ref[...] = 1.0 / valid.astype(F32)
    for copy in copies[2:]:
        copy.wait()
    turned_ref[...] = feats_ref[...].T

    @pl.loop(0, rows // TILE)
    def node_tile(step):
        nodes = pl.ds(pl.multiple_of(step * TILE, TILE), TILE)
        count_edges(slot_ref, count_ref, nodes)
        total_ref[:, nodes] = matmul(turned_ref[...], count_ref[:rows, nodes])
        preact_ref[nodes, :] = matmul(feats_ref[nodes, :], w_self_ref[...]) + bias_ref[...]


def joint_kernel(sizes, *refs):
    doms, reps, cap, hub_own, tall = sizes
    (
        remote_ref,
        turned_ref,
        total_ref,
        self_ref,
        count_ref,
        share_ref,
        w_neigh_hbm,
        cot_hbm,
        outputs_ref,
        own_ref,
        rest_ref,
        message_ref,
        low_ref,
        edge_grad_ref,
        w_neigh_ref,
        cot_ref,
        mean_ref,
        w_grad_ref,
        sems,
    ) = refs
    rows, width = outputs_ref.shape
    copies = fetch(((w_neigh_hbm, w_neigh_ref), (cot_hbm, cot_ref)), sems)
    table = remote_ref[...].T
    for copy in copies:
        copy.wait()
    bias_sum = jnp.zeros((1, width), F32)
    for first in range(0, rows, TILE):
        nodes = slice(first, first + TILE)
        share = share_ref[:, nodes]
        mean = (total_ref[:, nodes] + matmul(table, count_ref[rows:, nodes])) * share
        mean = mean.astype(BF16)
        mean_ref[:, nodes] = mean
        share_column = jnp.broadcast_to(share, (128, TILE)).T
        share_column = jnp.concatenate([share_column] * (width // 128), axis=1)

        preact = self_ref[nodes, :] + matmul(mean, w_neigh_ref[...], 0, 0)
        cot = cot_ref[nodes, :].astype(F32)
        grown = jnp.exp(jnp.minimum(preact, 0.0))
        act = jnp.where(preact > 0.0, preact, grown - 1.0)
        scale = lax.rsqrt(jnp.sum(act * act, axis=1, keepdims=True) * (1.0 / width) + NORM_EPS)
        outputs_ref[nodes, :] = (act * scale).astype(BF16)
        along = jnp.sum(act * cot, axis=1, keepdims=True)
        pull = along * (scale * scale * scale) * (1.0 / width)
        grad_pre = (cot * scale - act * pull) * jnp.where(preact > 0.0, F32(1.0), grown)
        bias_sum = bias_sum + jnp.sum(grad_pre, axis=0, keepdims=True)
        grad_low = grad_pre.astype(BF16)
        low_ref[nodes, :] = grad_low
        edge_grad = matmul(grad_low, w_neigh_ref[...], 1, 1) * share_column
        edge_grad_ref[nodes, :] = edge_grad.astype(BF16)

    low = low_ref[...]
    w_grad_ref[0] = matmul(turned_ref[...], low)
    w_grad_ref[1] = matmul(mean_ref[...], low)
    remote = matmul(count_ref[rows:, :], edge_grad_ref[...])
    bias_sum = jnp.broadcast_to(bias_sum, (tall, width))
    bias_high = bias_sum.astype(BF16).astype(F32)
    place = iota((tall, width), 0)
    bias_rows = jnp.where(place == tall - 1, bias_sum - bias_high, bias_high)
    remote = remote.reshape(doms * reps // SIDES, SIDES, tall, width)
    rest_ref[...] = jnp.where((place < tall - BIAS_ROWS)[None, None], remote, bias_rows[None, None])
    mine = lax.axis_index("side")
    own_ref[...] = w_grad_ref[mine]
    message_ref[:width, :] = w_grad_ref[1 - mine].astype(BF16)
    message_ref[width:, :] = rest_ref[:, 1 - mine].reshape(-1, width).astype(BF16)


def side_sum_kernel(slab, own_ref, rest_ref, received_ref, message_ref):
    peers, _, tall, width = rest_ref.shape
    w_grad = own_ref[...] + received_ref[:width, :].astype(F32)
    owners = width // slab
    w_grad = w_grad.reshape(owners, slab, width)
    if owners < peers:
        w_grad = jnp.concatenate([w_grad, jnp.zeros((peers - owners, slab, width), F32)], axis=0)
    rest = received_ref[width:, :].astype(F32).reshape(peers, tall, width)
    rest = rest + rest_ref[:, lax.axis_index("side")]
    bias = jnp.sum(rest[0, tall - BIAS_ROWS :, :], axis=0, keepdims=True)
    bias = jnp.broadcast_to(bias, (tall, width))
    bias_high = bias.astype(BF16).astype(F32)
    place = iota((tall, width), 0)
    bias_rows = jnp.where(place == tall - 1, bias - bias_high, bias_high)
    rest = jnp.where((place < tall - BIAS_ROWS)[None], rest, bias_rows[None])
    message_ref[...] = jnp.concatenate([w_grad, rest], axis=1).astype(BF16)


def peer_sum_kernel(slab, message_ref, slab_ref, unit_bias_ref):
    total = jnp.sum(message_ref[...].astype(F32), axis=0)
    slab_ref[...] = jnp.broadcast_to(total[None, :slab, :], slab_ref.shape).astype(BF16)
    bias = jnp.sum(total[-BIAS_ROWS:, :], axis=0, keepdims=True)
    unit_bias_ref[...] = bias * lax.rsqrt(jnp.mean(bias * bias, axis=1, keepdims=True) + UNIT_EPS)


def feat_grad_kernel(
    slab, message_ref, places_ref, count_ref, edge_grad_ref, low_ref, w_self_ref, out_ref
):
    returned = message_ref[...].astype(F32)[:, slab:, :]
    returned = returned.reshape(-1, out_ref.shape[1]).astype(BF16)
    chosen = one_hot(out_ref.shape[0], places_ref[...])
    for first in range(0, out_ref.shape[0], TILE):
        last = first + TILE
        out_ref[first:last, :] = (
            matmul(count_ref[first:last, :], edge_grad_ref[...])
            + matmul(low_ref[first:last, :], w_self_ref[...], 1, 1)
            + matmul(chosen[first:last, :], returned)
        ).astype(BF16)


def unit_kernel(mine_ref, other_ref, unit_self_ref, unit_neigh_ref, units_ref):
    side = lax.axis_index("side")
    for place, grad_ref in ((side, mine_ref), (1 - side, other_ref)):
        grad = grad_ref[...].astype(F32)
        square = jnp.sum(jnp.sum(grad * grad, axis=0, keepdims=True), axis=1, keepdims=True)
        units_ref[place] = grad * lax.rsqrt(square * (1.0 / grad.size) + UNIT_EPS)
    unit_self_ref[...] = units_ref[0]
    unit_neigh_ref[...] = units_ref[1]


def call(kernel, out_shape, in_specs=None, scratch=(), cost=(0, 0)):
    return pl.pallas_call(
        kernel,
        out_shape=out_shape,
        **({} if in_specs is None else {"in_specs": in_specs}),
        scratch_shapes=list(scratch),
        compiler_params=pltpu.CompilerParams(vmem_limit_bytes=VMEM_LIMIT),
        cost_estimate=pl.CostEstimate(flops=cost[0], bytes_accessed=cost[1], transcendentals=0),
    )


def in_hbm(*arrays):
    return [pltpu.with_memory_space_constraint(array, pltpu.HBM) for array in arrays]


def swap(array, axes):
    return lax.all_to_all(array, axes, split_axis=0, concat_axis=0, tiled=True)


def other_side(array):
    return lax.ppermute(array, "side", [(0, 1), (1, 0)])


def on_device(
    doms, reps, feats, w_self, w_neigh, bias, out_cot, degree, edge_src, hub_rows, send_rows
):
    rows, width = feats.shape
    fanout = edge_src.shape[1]
    cap, hub_own = send_rows.shape[1], hub_rows.shape[0]
    blocks, peers = doms * reps, doms * reps // SIDES
    tall = -(-(cap + hub_own + BIAS_ROWS) // 8) * 8
    slots = blocks * tall
    slab = max(8, width // peers)
    sizes = (doms, reps, cap, hub_own, tall)
    shape = jax.ShapeDtypeStruct
    hbm = pl.BlockSpec(memory_space=pltpu.HBM)
    vmem = pl.BlockSpec(memory_space=pltpu.VMEM)

    outgoing, places, peer_places = call(
        functools.partial(pick_kernel, sizes),
        (
            shape((slots, width), BF16),
            shape((1, slots), jnp.int32),
            shape((1, peers * tall), jnp.int32),
        ),
        [hbm] * 3,
        (
            pltpu.SMEM((hub_own,), jnp.int32),
            pltpu.SMEM((cap, doms), jnp.int32),
            pltpu.VMEM((rows, width), BF16),
            pltpu.SemaphoreType.DMA((3,)),
        ),
        cost=(2 * rows * slots * width, 2 * rows * width),
    )(*in_hbm(hub_rows, send_rows.T, feats))
    remote = swap(outgoing, SPLIT_AXES)
    share, turned, count, own_total, self_part = call(
        functools.partial(own_kernel, sizes),
        (
            shape((1, rows), F32),
            shape((width, rows), BF16),
            shape((rows + slots, rows), BF16),
            shape((width, rows), F32),
            shape((rows, width), F32),
        ),
        [hbm] * 5,
        (
            pltpu.VMEM((1, rows), jnp.int32),
            pltpu.VMEM((fanout, rows), jnp.int32),
            pltpu.VMEM((rows, width), BF16),
            pltpu.VMEM((width, width), BF16),
            pltpu.VMEM((1, width), F32),
            pltpu.VMEM((fanout, rows), jnp.int32),
            pltpu.SemaphoreType.DMA((5,)),
        ),
        cost=(8 * rows * (rows + slots) * width, 12 * rows * width + 2 * rows * rows),
    )(*in_hbm(degree.reshape(1, rows), edge_src.T, feats, w_self, bias.reshape(1, width)))

    outputs, own_grad, rest, message, low, edge_grad = call(
        functools.partial(joint_kernel, sizes),
        (
            shape((rows, width), BF16),
            shape((width, width), F32),
            shape((peers, SIDES, tall, width), F32),
            shape((width + peers * tall, width), BF16),
            shape((rows, width), BF16),
            shape((rows, width), BF16),
        ),
        [vmem] * 6 + [hbm] * 2,
        (
            pltpu.VMEM((width, width), BF16),
            pltpu.VMEM((rows, width), BF16),
            pltpu.VMEM((width, rows), BF16),
            pltpu.VMEM((2, width, width), F32),
            pltpu.SemaphoreType.DMA((2,)),
        ),
        cost=(4 * rows * slots * width + 8 * rows * width * width, 16 * rows * width),
    )(remote, turned, own_total, self_part, count, share, *in_hbm(w_neigh, out_cot))

    message = call(
        functools.partial(side_sum_kernel, slab), shape((peers, slab + tall, width), BF16)
    )(own_grad, rest, other_side(message))
    message = swap(message, PEERS)
    slabs, unit_bias = call(
        functools.partial(peer_sum_kernel, slab),
        (shape((peers, slab, width), BF16), shape((1, width), F32)),
    )(message)
    grad = swap(slabs, PEERS).reshape(peers * slab, width)[:width]
    grad_feats = call(
        functools.partial(feat_grad_kernel, slab),
        shape((rows, width), BF16),
        cost=(2 * rows * rows * width + 2 * rows * width * width, 6 * rows * width),
    )(message, peer_places, count, edge_grad, low, w_self)
    unit_self, unit_neigh = call(
        unit_kernel,
        (shape((width, width), F32), shape((width, width), F32)),
        scratch=(pltpu.VMEM((2, width, width), F32),),
    )(grad, other_side(grad))
    return outputs, grad_feats, unit_self, unit_neigh, unit_bias.reshape(width)


def solution(mesh):
    doms, reps = mesh.shape["dom"], mesh.shape["rep"]
    split = jax.sharding.Mesh(mesh.devices.reshape(doms, reps // SIDES, SIDES), SPLIT_AXES)
    rows, whole = P(SPLIT_AXES, None), P()
    return jax.shard_map(
        functools.partial(on_device, doms, reps),
        mesh=split,
        in_specs=(rows, whole, whole, whole, rows, P(SPLIT_AXES), rows, P(SPLIT_AXES), rows),
        out_specs=(rows, rows, whole, whole, whole),
        check_vma=False,
    )
```

```python
import functools

import jax
import jax.numpy as jnp
from jax import lax
from jax.experimental import pallas as pl
from jax.experimental.pallas import tpu as pltpu
from jax.sharding import PartitionSpec as P

NORM_EPS = 1e-05
UNIT_EPS = 1e-06
SPLIT_AXES = ("dom", "pair", "side")
PEERS = ("dom", "pair")
SIDES = 2
VMEM_LIMIT = 32 * 1024 * 1024
F32 = jnp.float32
BF16 = jnp.bfloat16
TILE = 256
STRIP = 16
PIECE = 32
LANES = 128
BIAS_ROWS = 2


def div_floor(value, size):
    if size & (size - 1) == 0:
        return lax.shift_right_arithmetic(value, jnp.int32(size.bit_length() - 1))
    return value // size


def remainder(value, size):
    if size & (size - 1) == 0:
        return value & jnp.int32(size - 1)
    return value - (value // size) * size


def matmul(lhs, rhs, lhs_dim=1, rhs_dim=0):
    return lax.dot_general(
        lhs, rhs, (((lhs_dim,), (rhs_dim,)), ((), ())), preferred_element_type=F32
    )


def iota(shape, dim):
    return lax.broadcasted_iota(jnp.int32, shape, dim)


def one_hot(rows, places):
    return jnp.where(iota((rows, places.shape[1]), 0) == places, F32(1.0), F32(0.0)).astype(BF16)


def fetch(pairs, sems):
    copies = [
        pltpu.make_async_copy(source, target, sems.at[number])
        for number, (source, target) in enumerate(pairs)
    ]
    for copy in copies:
        copy.start()
    return copies


def pick_kernel(sizes, hub_hbm, send_hbm, *refs):
    doms, reps, cap, hub_own, tall = sizes
    inputs, (rows_ref, places_ref), kept, (hub_ref, send_ref, sems) = (
        refs[:5],
        refs[5:7],
        refs[7:12],
        refs[12:],
    )
    feats_ref = kept[0]
    copies = fetch(((hub_hbm, hub_ref), (send_hbm, send_ref), *zip(inputs, kept)), sems)
    lane = iota(places_ref.shape, 1)
    row = remainder(lane, tall)

    def list_entries(dom, places):
        for entry in range(cap):
            places = jnp.where(lane == dom * tall + entry, send_ref[entry, dom], places)
        return places

    copies[0].wait()
    copies[1].wait()
    places = jnp.full(lane.shape, -1, jnp.int32)
    if doms <= 16:
        for dom in range(doms):
            places = list_entries(dom, places)
    else:
        places = lax.fori_loop(0, doms, list_entries, places)
    for entry in range(hub_own):
        places = jnp.where(row == cap + entry, hub_ref[entry], places)
    places_ref[...] = places
    column = jnp.broadcast_to(places, (LANES, lane.shape[1])).T[: doms * tall, :]
    node = iota(column.shape, 1)
    chosen = [
        jnp.where(node + first == column, F32(1.0), F32(0.0)).astype(BF16)
        for first in range(0, feats_ref.shape[0], LANES)
    ]
    copies[2].wait()
    picked = matmul(jnp.concatenate(chosen, axis=1), feats_ref[...])
    place = iota((tall, picked.shape[1]), 0)
    group = lax.axis_index("pair") * SIDES + lax.axis_index("side")
    for dom in range(doms):
        block = picked[dom * tall : (dom + 1) * tall, :]
        blocks = [
            jnp.where((place >= cap) | (group == other), block, F32(0.0)) for other in range(reps)
        ]
        first = dom * reps * tall
        rows_ref[first : first + reps * tall, :] = jnp.concatenate(blocks, axis=0).astype(BF16)
    for copy in copies[3:]:
        copy.wait()


def count_edges(slot_ref, count_ref, nodes, base_slot):
    fanout, tile = slot_ref.shape[0], TILE
    slots = count_ref.shape[0]
    wanted = [
        jnp.broadcast_to(slot_ref[k : k + 1, nodes], (STRIP, tile)).astype(jnp.int16)
        for k in range(fanout)
    ]
    base = iota((STRIP, tile), 0) + base_slot

    def strips(first, last, start):
        for strip in range(first, last, STRIP):
            numbers = (base + (start + strip)).astype(jnp.int16)
            count = jnp.zeros((STRIP, tile), BF16)
            for k in range(fanout):
                count = count + jnp.where(numbers == wanted[k], BF16(1.0), BF16(0.0))
            if isinstance(start, int):
                count_ref[start + strip : start + strip + STRIP, nodes] = count
            else:
                count_ref[pl.ds(pl.multiple_of(start + strip, STRIP), STRIP), nodes] = count

    if slots <= 1024:
        strips(0, slots, 0)
    else:
        pl.loop(0, slots, step=TILE)(lambda start: strips(0, TILE, start))


def own_kernel(sizes, feats_ref, w_self_ref, bias_ref, degree_ref, edge_ref, *refs):
    doms, reps, cap, hub_own, tall = sizes
    inputs, refs = refs[:2], refs[2:]
    kept, (share_ref, turned_ref, own_count_ref, far_count_ref, total_ref, preact_ref) = (
        refs[:2],
        refs[2:8],
    )
    slot_ref, sems = refs[8:]
    copies = fetch(zip(inputs, kept), sems)
    rows = feats_ref.shape[0]
    fanout = edge_ref.shape[0]
    hubs = doms * reps * hub_own

    source = edge_ref[...]
    hub = source - rows
    halo = hub - hubs
    group = lax.axis_index("pair") * SIDES + lax.axis_index("side")
    hub_slot = rows + cap + div_floor(hub, hub_own) * tall + remainder(hub, hub_own)
    halo_slot = rows + (div_floor(halo, cap) * reps + group) * tall + remainder(halo, cap)
    slot = jnp.where(source < rows, source, jnp.where(hub < hubs, hub_slot, halo_slot))
    valid = jnp.minimum(degree_ref[...], fanout)
    slot_ref[...] = jnp.where(iota((fanout, rows), 0) < valid, slot, -1)
    share_ref[...] = 1.0 / valid.astype(F32)
    turned_ref[...] = feats_ref[...].T

    @pl.loop(0, rows // TILE)
    def node_tile(step):
        nodes = pl.ds(pl.multiple_of(step * TILE, TILE), TILE)
        count_edges(slot_ref, own_count_ref, nodes, 0)
        count_edges(slot_ref, far_count_ref, nodes, rows)
        total_ref[:, nodes] = matmul(turned_ref[...], own_count_ref[:, nodes])
        preact_ref[nodes, :] = matmul(feats_ref[nodes, :], w_self_ref[...]) + bias_ref[...]

    for copy in copies:
        copy.wait()


def joint_kernel(
    remote_ref,
    turned_ref,
    total_ref,
    self_ref,
    count_ref,
    share_ref,
    w_neigh_ref,
    cot_ref,
    outputs_ref,
    w_own_ref,
    w_message_ref,
    low_ref,
    bias_ref,
    mean_ref,
    preact_ref,
    w_grad_ref,
):
    rows, width = outputs_ref.shape
    table = remote_ref[...].T
    bias_sum = jnp.zeros((8, width), F32)
    for first in range(0, rows, TILE):
        nodes = slice(first, first + TILE)
        mean = total_ref[:, nodes] + matmul(table, count_ref[:, nodes])
        mean = (mean * share_ref[:, nodes]).astype(BF16)
        mean_ref[:, nodes] = mean
        preact_ref[nodes, :] = self_ref[nodes, :] + matmul(mean, w_neigh_ref[...], 0, 0)
        for start in range(first, first + TILE, PIECE):
            piece = slice(start, start + PIECE)
            preact = preact_ref[piece, :]
            cot = cot_ref[piece, :].astype(F32)
            grown = jnp.exp(jnp.minimum(preact, 0.0))
            act = jnp.where(preact > 0.0, preact, grown - 1.0)
            square = jnp.sum(act * act, axis=1, keepdims=True)
            along = jnp.sum(act * cot, axis=1, keepdims=True)
            scale = lax.rsqrt(square * (1.0 / width) + NORM_EPS)
            outputs_ref[piece, :] = (act * scale).astype(BF16)
            pull = along * (scale * scale * scale) * (1.0 / width)
            grad_pre = (cot * scale - act * pull) * jnp.where(preact > 0.0, F32(1.0), grown)
            bias_sum = bias_sum + jnp.sum(grad_pre.reshape(PIECE // 8, 8, width), axis=0)
            low_ref[piece, :] = grad_pre.astype(BF16)

    low = low_ref[...]
    w_grad_ref[0] = matmul(turned_ref[...], low)
    w_grad_ref[1] = matmul(mean_ref[...], low)
    bias_ref[...] = bias_sum
    mine = lax.axis_index("side")
    w_own_ref[...] = w_grad_ref[mine]
    w_message_ref[...] = w_grad_ref[1 - mine].astype(BF16)


def edge_kernel(
    sizes,
    low_ref,
    w_neigh_ref,
    w_self_ref,
    share_ref,
    own_count_ref,
    far_count_ref,
    bias_ref,
    feat_grad_ref,
    own_ref,
    message_ref,
    edge_grad_ref,
    rest_ref,
):
    doms, reps, cap, hub_own, tall = sizes
    rows, width = low_ref.shape
    for first in range(0, rows, TILE):
        nodes = slice(first, first + TILE)
        share_column = jnp.broadcast_to(share_ref[:, nodes], (LANES, TILE)).T
        share_column = jnp.concatenate([share_column] * (width // LANES), axis=1)
        edge_grad = matmul(low_ref[nodes, :], w_neigh_ref[...], 1, 1) * share_column
        edge_grad_ref[nodes, :] = edge_grad.astype(BF16)
    remote = matmul(far_count_ref[...], edge_grad_ref[...])
    bias_sum = jnp.broadcast_to(jnp.sum(bias_ref[...], axis=0, keepdims=True), (tall, width))
    bias_high = bias_sum.astype(BF16).astype(F32)
    place = iota((tall, width), 0)
    bias_rows = jnp.where(place == tall - 1, bias_sum - bias_high, bias_high)
    remote = remote.reshape(doms * reps // SIDES, SIDES, tall, width)
    rest_ref[...] = jnp.where((place < tall - BIAS_ROWS)[None, None], remote, bias_rows[None, None])
    mine = lax.axis_index("side")
    own_ref[...] = rest_ref[:, mine]
    message_ref[...] = rest_ref[:, 1 - mine].reshape(-1, width).astype(BF16)
    for first in range(0, rows, TILE):
        nodes = slice(first, first + TILE)
        feat_grad_ref[nodes, :] = matmul(own_count_ref[nodes, :], edge_grad_ref[...]) + matmul(
            low_ref[nodes, :], w_self_ref[...], 1, 1
        )


def side_sum_kernel(own_ref, received_ref, message_ref):
    peers, slab, width = message_ref.shape
    w_grad = own_ref[...] + received_ref[...].astype(F32)
    owners = width // slab
    w_grad = w_grad.reshape(owners, slab, width)
    if owners < peers:
        w_grad = jnp.concatenate([w_grad, jnp.zeros((peers - owners, slab, width), F32)], axis=0)
    message_ref[...] = w_grad.astype(BF16)


def peer_sum_kernel(slabs_ref, own_ref, received_ref, message_ref):
    peers, tall, width = own_ref.shape
    slab = slabs_ref.shape[1]
    total = jnp.sum(slabs_ref[...].astype(F32), axis=0)
    rest = own_ref[...] + received_ref[...].astype(F32).reshape(peers, tall, width)
    bias = jnp.sum(rest[0, tall - BIAS_ROWS :, :], axis=0, keepdims=True)
    bias = jnp.broadcast_to(bias, (tall, width))
    bias_high = bias.astype(BF16).astype(F32)
    place = iota((tall, width), 0)
    bias_rows = jnp.where(place == tall - 1, bias - bias_high, bias_high)
    rest = jnp.where((place < tall - BIAS_ROWS)[None], rest, bias_rows[None])
    total = jnp.broadcast_to(total[None], (peers, slab, width))
    message_ref[...] = jnp.concatenate([total, rest], axis=1).astype(BF16)


def feat_grad_kernel(sizes, slab, message_ref, places_ref, feat_grad_ref, out_ref):
    doms, reps, cap, hub_own, tall = sizes
    rows, width = out_ref.shape
    pairs = reps // SIDES
    returned = message_ref[...].astype(F32)[:, slab:, :].reshape(doms, pairs, tall, width)
    returned = [
        returned[:, pair].reshape(doms * tall, width).astype(BF16) for pair in range(pairs)
    ]
    chosen = one_hot(rows, places_ref[:, : doms * tall])
    for first in range(0, rows, TILE):
        nodes = slice(first, first + TILE)
        total = feat_grad_ref[nodes, :]
        for part in returned:
            total = total + matmul(chosen[nodes, :], part)
        out_ref[nodes, :] = total.astype(BF16)


def unit_kernel(slab, mine_ref, other_ref, unit_self_ref, unit_neigh_ref, unit_bias_ref, units_ref):
    side = lax.axis_index("side")
    size, width = unit_self_ref.shape
    for place, grad_ref in ((side, mine_ref), (1 - side, other_ref)):
        grad = grad_ref[: size // slab].astype(F32)[:, :slab, :].reshape(size, width)
        square = jnp.sum(jnp.sum(grad * grad, axis=0, keepdims=True), axis=1, keepdims=True)
        units_ref[place] = grad * lax.rsqrt(square * (1.0 / grad.size) + UNIT_EPS)
    unit_self_ref[...] = units_ref[0]
    unit_neigh_ref[...] = units_ref[1]
    bias = jnp.sum(mine_ref[...].astype(F32)[:, slab:, :], axis=0)[-BIAS_ROWS:, :]
    bias = jnp.sum(bias, axis=0, keepdims=True)
    unit_bias_ref[...] = bias * lax.rsqrt(jnp.mean(bias * bias, axis=1, keepdims=True) + UNIT_EPS)


def call(kernel, out_shape, in_specs=None, scratch=(), cost=(0, 0)):
    return pl.pallas_call(
        kernel,
        out_shape=out_shape,
        **({} if in_specs is None else {"in_specs": in_specs}),
        scratch_shapes=list(scratch),
        compiler_params=pltpu.CompilerParams(vmem_limit_bytes=VMEM_LIMIT),
        cost_estimate=pl.CostEstimate(flops=cost[0], bytes_accessed=cost[1], transcendentals=0),
    )


def in_hbm(*arrays):
    return [pltpu.with_memory_space_constraint(array, pltpu.HBM) for array in arrays]


def swap(array, axes):
    return lax.all_to_all(array, axes, split_axis=0, concat_axis=0, tiled=True)


def other_side(array):
    return lax.ppermute(array, "side", [(0, 1), (1, 0)])


def on_device(
    doms, reps, feats, w_self, w_neigh, bias, out_cot, degree, edge_src, hub_rows, send_rows
):
    rows, width = feats.shape
    fanout = edge_src.shape[1]
    cap, hub_own = send_rows.shape[1], hub_rows.shape[0]
    blocks, peers = doms * reps, doms * reps // SIDES
    tall = -(-(cap + hub_own + BIAS_ROWS) // 8) * 8
    slots = blocks * tall
    slab = max(8, width // peers)
    sizes = (doms, reps, cap, hub_own, tall)
    shape = jax.ShapeDtypeStruct
    hbm = pl.BlockSpec(memory_space=pltpu.HBM)
    vmem = pl.BlockSpec(memory_space=pltpu.VMEM)

    outgoing, places, *kept = call(
        functools.partial(pick_kernel, sizes),
        (
            shape((slots, width), BF16),
            shape((1, max(LANES, doms * tall)), jnp.int32),
            shape((rows, width), BF16),
            shape((width, width), BF16),
            shape((1, width), F32),
            shape((1, rows), jnp.int32),
            shape((fanout, rows), jnp.int32),
        ),
        [hbm] * 7,
        (
            pltpu.SMEM((hub_own,), jnp.int32),
            pltpu.SMEM((cap, doms), jnp.int32),
            pltpu.SemaphoreType.DMA((7,)),
        ),
        cost=(2 * rows * slots * width, 2 * rows * width),
    )(
        *in_hbm(
            hub_rows,
            send_rows.T,
            feats,
            w_self,
            bias.reshape(1, width),
            degree.reshape(1, rows),
            edge_src.T,
        )
    )
    remote = swap(outgoing, SPLIT_AXES)
    w_neigh_kept, cot_kept, share, turned, own_count, far_count, own_total, self_part = call(
        functools.partial(own_kernel, sizes),
        (
            shape((width, width), BF16),
            shape((rows, width), BF16),
            shape((1, rows), F32),
            shape((width, rows), BF16),
            shape((rows, rows), BF16),
            shape((slots, rows), BF16),
            shape((width, rows), F32),
            shape((rows, width), F32),
        ),
        [vmem] * 5 + [hbm] * 2,
        (pltpu.VMEM((fanout, rows), jnp.int32), pltpu.SemaphoreType.DMA((2,))),
        cost=(8 * rows * (rows + slots) * width, 12 * rows * width + 2 * rows * rows),
    )(*kept, *in_hbm(w_neigh, out_cot))

    outputs, w_own, w_message, low, bias_sum = call(
        joint_kernel,
        (
            shape((rows, width), BF16),
            shape((width, width), F32),
            shape((width, width), BF16),
            shape((rows, width), BF16),
            shape((8, width), F32),
        ),
        scratch=(
            pltpu.VMEM((width, rows), BF16),
            pltpu.VMEM((rows, width), F32),
            pltpu.VMEM((2, width, width), F32),
        ),
        cost=(2 * rows * slots * width + 6 * rows * width * width, 16 * rows * width),
    )(remote, turned, own_total, self_part, far_count, share, w_neigh_kept, cot_kept)

    message = call(side_sum_kernel, shape((peers, slab, width), BF16))(
        w_own, other_side(w_message)
    )
    slabs = swap(message, PEERS)
    feat_grad, rest, rest_message = call(
        functools.partial(edge_kernel, sizes),
        (
            shape((rows, width), F32),
            shape((peers, tall, width), F32),
            shape((peers * tall, width), BF16),
        ),
        scratch=(
            pltpu.VMEM((rows, width), BF16),
            pltpu.VMEM((peers, SIDES, tall, width), F32),
        ),
        cost=(2 * rows * (rows + slots) * width + 4 * rows * width * width, 8 * rows * width),
    )(low, w_neigh_kept, kept[1], share, own_count, far_count, bias_sum)
    message = call(peer_sum_kernel, shape((peers, slab + tall, width), BF16))(
        slabs, rest, other_side(rest_message)
    )
    message = swap(message, PEERS)
    grad_feats = call(
        functools.partial(feat_grad_kernel, sizes, slab),
        shape((rows, width), BF16),
        cost=(4 * rows * slots * width, 6 * rows * width),
    )(message, places, feat_grad)
    unit_self, unit_neigh, unit_bias = call(
        functools.partial(unit_kernel, slab),
        (shape((width, width), F32), shape((width, width), F32), shape((1, width), F32)),
        scratch=(pltpu.VMEM((2, width, width), F32),),
    )(message, other_side(message))
    return outputs, grad_feats, unit_self, unit_neigh, unit_bias.reshape(width)


def solution(mesh):
    doms, reps = mesh.shape["dom"], mesh.shape["rep"]
    split = jax.sharding.Mesh(mesh.devices.reshape(doms, reps // SIDES, SIDES), SPLIT_AXES)
    rows, whole = P(SPLIT_AXES, None), P()
    return jax.shard_map(
        functools.partial(on_device, doms, reps),
        mesh=split,
        in_specs=(rows, whole, whole, whole, rows, P(SPLIT_AXES), rows, P(SPLIT_AXES), rows),
        out_specs=(rows, rows, whole, whole, whole),
        check_vma=False,
    )
```

```python
import functools

import jax
import jax.numpy as jnp
from jax import lax
from jax.experimental import pallas as pl
from jax.experimental.pallas import tpu as pltpu
from jax.sharding import PartitionSpec as P

NORM_EPS = 1e-05
UNIT_EPS = 1e-06
SPLIT_AXES = ("dom", "pair", "side")
PEERS = ("dom", "pair")
SIDES = 2
VMEM_LIMIT = 32 * 1024 * 1024
F32 = jnp.float32
BF16 = jnp.bfloat16
TILE = 256
STRIP = 16
PIECE = 32
LANES = 128
BIAS_ROWS = 2


def div_floor(value, size):
    if size & (size - 1) == 0:
        return lax.shift_right_arithmetic(value, jnp.int32(size.bit_length() - 1))
    return value // size


def remainder(value, size):
    if size & (size - 1) == 0:
        return value & jnp.int32(size - 1)
    return value - (value // size) * size


def matmul(lhs, rhs, lhs_dim=1, rhs_dim=0):
    return lax.dot_general(
        lhs, rhs, (((lhs_dim,), (rhs_dim,)), ((), ())), preferred_element_type=F32
    )


def iota(shape, dim):
    return lax.broadcasted_iota(jnp.int32, shape, dim)


def one_hot(rows, places):
    return jnp.where(iota((rows, places.shape[1]), 0) == places, F32(1.0), F32(0.0)).astype(BF16)


def fetch(pairs, sems):
    copies = [
        pltpu.make_async_copy(source, target, sems.at[number])
        for number, (source, target) in enumerate(pairs)
    ]
    for copy in copies:
        copy.start()
    return copies


def pick_kernel(
    sizes, hub_hbm, send_hbm, feats_hbm, rows_ref, places_ref, hub_ref, send_ref, feats_ref, sems
):
    doms, reps, cap, hub_own, tall = sizes
    copies = fetch(((hub_hbm, hub_ref), (send_hbm, send_ref), (feats_hbm, feats_ref)), sems)
    lane = iota(places_ref.shape, 1)
    row = remainder(lane, tall)

    def list_entries(dom, places):
        for entry in range(cap):
            places = jnp.where(lane == dom * tall + entry, send_ref[entry, dom], places)
        return places

    copies[0].wait()
    copies[1].wait()
    places = jnp.full(lane.shape, -1, jnp.int32)
    if doms <= 16:
        for dom in range(doms):
            places = list_entries(dom, places)
    else:
        places = lax.fori_loop(0, doms, list_entries, places)
    for entry in range(hub_own):
        places = jnp.where(row == cap + entry, hub_ref[entry], places)
    places_ref[...] = places
    column = jnp.broadcast_to(places, (LANES, lane.shape[1])).T[: doms * tall, :]
    node = iota(column.shape, 1)
    chosen = [
        jnp.where(node + first == column, F32(1.0), F32(0.0)).astype(BF16)
        for first in range(0, feats_ref.shape[0], LANES)
    ]
    copies[2].wait()
    picked = matmul(jnp.concatenate(chosen, axis=1), feats_ref[...])
    place = iota((tall, picked.shape[1]), 0)
    group = lax.axis_index("pair") * SIDES + lax.axis_index("side")
    for dom in range(doms):
        block = picked[dom * tall : (dom + 1) * tall, :]
        blocks = [
            jnp.where((place >= cap) | (group == other), block, F32(0.0)) for other in range(reps)
        ]
        first = dom * reps * tall
        rows_ref[first : first + reps * tall, :] = jnp.concatenate(blocks, axis=0).astype(BF16)


def count_edges(slot_ref, count_ref, nodes, base_slot):
    fanout, tile = slot_ref.shape[0], TILE
    slots = count_ref.shape[0]
    wanted = [
        jnp.broadcast_to(slot_ref[k : k + 1, nodes], (STRIP, tile)).astype(jnp.int16)
        for k in range(fanout)
    ]
    base = iota((STRIP, tile), 0) + base_slot

    def strips(first, last, start):
        for strip in range(first, last, STRIP):
            numbers = (base + (start + strip)).astype(jnp.int16)
            count = jnp.zeros((STRIP, tile), BF16)
            for k in range(fanout):
                count = count + jnp.where(numbers == wanted[k], BF16(1.0), BF16(0.0))
            if isinstance(start, int):
                count_ref[start + strip : start + strip + STRIP, nodes] = count
            else:
                count_ref[pl.ds(pl.multiple_of(start + strip, STRIP), STRIP), nodes] = count

    if slots <= 1024:
        strips(0, slots, 0)
    else:
        pl.loop(0, slots, step=TILE)(lambda start: strips(0, TILE, start))


def own_kernel(
    sizes,
    feats_hbm,
    degree_hbm,
    edge_hbm,
    share_hbm,
    turned_hbm,
    own_count_hbm,
    far_count_hbm,
    total_hbm,
    feats_ref,
    degree_ref,
    edge_ref,
    share_ref,
    turned_ref,
    own_count_ref,
    far_count_ref,
    total_ref,
    slot_ref,
    fetch_sems,
    keep_sems,
):
    doms, reps, cap, hub_own, tall = sizes
    copies = fetch(
        ((degree_hbm, degree_ref), (edge_hbm, edge_ref), (feats_hbm, feats_ref)), fetch_sems
    )
    rows = feats_ref.shape[0]
    fanout = edge_ref.shape[0]
    hubs = doms * reps * hub_own
    copies[0].wait()
    copies[1].wait()

    source = edge_ref[...]
    hub = source - rows
    halo = hub - hubs
    group = lax.axis_index("pair") * SIDES + lax.axis_index("side")
    hub_slot = rows + cap + div_floor(hub, hub_own) * tall + remainder(hub, hub_own)
    halo_slot = rows + (div_floor(halo, cap) * reps + group) * tall + remainder(halo, cap)
    slot = jnp.where(source < rows, source, jnp.where(hub < hubs, hub_slot, halo_slot))
    valid = jnp.minimum(degree_ref[...], fanout)
    slot_ref[...] = jnp.where(iota((fanout, rows), 0) < valid, slot, -1)
    share_ref[...] = 1.0 / valid.astype(F32)
    copies[2].wait()
    turned_ref[...] = feats_ref[...].T
    kept = [
        pltpu.make_async_copy(share_ref, share_hbm, keep_sems.at[0]),
        pltpu.make_async_copy(turned_ref, turned_hbm, keep_sems.at[1]),
    ]
    for copy in kept:
        copy.start()

    def keep_tile(step, nodes):
        return [
            pltpu.make_async_copy(ref.at[:, nodes], hbm.at[:, nodes], keep_sems.at[2 + 3 * step + k])
            for k, (ref, hbm) in enumerate(
                (
                    (far_count_ref, far_count_hbm),
                    (total_ref, total_hbm),
                    (own_count_ref, own_count_hbm),
                )
            )
        ]

    @pl.loop(0, rows // TILE)
    def node_tile(step):
        nodes = pl.ds(pl.multiple_of(step * TILE, TILE), TILE)
        count_edges(slot_ref, far_count_ref, nodes, rows)
        count_edges(slot_ref, own_count_ref, nodes, 0)
        total_ref[:, nodes] = matmul(turned_ref[...], own_count_ref[:, nodes])
        for copy in keep_tile(step, nodes):
            copy.start()

    for step in range(rows // TILE):
        kept += keep_tile(step, pl.ds(step * TILE, TILE))
    for copy in kept:
        copy.wait()


def joint_kernel(
    remote_ref,
    share_hbm,
    w_neigh_hbm,
    w_self_hbm,
    bias_hbm,
    turned_hbm,
    count_hbm,
    total_hbm,
    feats_hbm,
    cot_hbm,
    w_own_ref,
    w_message_ref,
    bias_sum_ref,
    outputs_hbm,
    low_hbm,
    share_ref,
    w_neigh_ref,
    w_self_ref,
    bias_ref,
    turned_ref,
    count_ref,
    total_ref,
    feats_ref,
    cot_ref,
    outputs_ref,
    low_ref,
    mean_ref,
    preact_ref,
    w_grad_ref,
    fetch_sems,
    keep_sems,
):
    rows, width = outputs_ref.shape
    tiles = [slice(first, first + TILE) for first in range(0, rows, TILE)]
    small = fetch(
        (
            (share_hbm, share_ref),
            (w_neigh_hbm, w_neigh_ref),
            (w_self_hbm, w_self_ref),
            (bias_hbm, bias_ref),
        ),
        fetch_sems.at[pl.ds(0, 4)],
    )
    fetched = [
        fetch(
            (
                (count_hbm.at[:, nodes], count_ref.at[:, nodes]),
                (total_hbm.at[:, nodes], total_ref.at[:, nodes]),
                (feats_hbm.at[nodes, :], feats_ref.at[nodes, :]),
                (cot_hbm.at[nodes, :], cot_ref.at[nodes, :]),
            ),
            fetch_sems.at[pl.ds(4 + 4 * step, 4)],
        )
        for step, nodes in enumerate(tiles)
    ]
    turned_copy = pltpu.make_async_copy(
        turned_hbm, turned_ref, fetch_sems.at[4 + 4 * len(tiles)]
    )
    turned_copy.start()
    table = remote_ref[...].T
    for copy in small:
        copy.wait()
    bias_sum = jnp.zeros((8, width), F32)
    kept = []
    for step, nodes in enumerate(tiles):
        for copy in fetched[step]:
            copy.wait()
        mean = total_ref[:, nodes] + matmul(table, count_ref[:, nodes])
        mean = (mean * share_ref[:, nodes]).astype(BF16)
        mean_ref[:, nodes] = mean
        preact_ref[nodes, :] = (
            matmul(feats_ref[nodes, :], w_self_ref[...])
            + matmul(mean, w_neigh_ref[...], 0, 0)
            + bias_ref[...]
        )
        for start in range(nodes.start, nodes.stop, PIECE):
            piece = slice(start, start + PIECE)
            preact = preact_ref[piece, :]
            cot = cot_ref[piece, :].astype(F32)
            grown = jnp.exp(jnp.minimum(preact, 0.0))
            act = jnp.where(preact > 0.0, preact, grown - 1.0)
            square = jnp.sum(act * act, axis=1, keepdims=True)
            along = jnp.sum(act * cot, axis=1, keepdims=True)
            scale = lax.rsqrt(square * (1.0 / width) + NORM_EPS)
            outputs_ref[piece, :] = (act * scale).astype(BF16)
            pull = along * (scale * scale * scale) * (1.0 / width)
            grad_pre = (cot * scale - act * pull) * jnp.where(preact > 0.0, F32(1.0), grown)
            bias_sum = bias_sum + jnp.sum(grad_pre.reshape(PIECE // 8, 8, width), axis=0)
            low_ref[piece, :] = grad_pre.astype(BF16)
        kept += fetch(
            (
                (outputs_ref.at[nodes, :], outputs_hbm.at[nodes, :]),
                (low_ref.at[nodes, :], low_hbm.at[nodes, :]),
            ),
            keep_sems.at[pl.ds(2 * step, 2)],
        )

    turned_copy.wait()
    low = low_ref[...]
    w_grad_ref[0] = matmul(turned_ref[...], low)
    w_grad_ref[1] = matmul(mean_ref[...], low)
    bias_sum_ref[...] = bias_sum
    mine = lax.axis_index("side")
    w_own_ref[...] = w_grad_ref[mine]
    w_message_ref[...] = w_grad_ref[1 - mine].astype(BF16)
    for copy in kept:
        copy.wait()


def edge_kernel(
    sizes,
    bias_ref,
    share_hbm,
    w_neigh_hbm,
    low_hbm,
    far_count_hbm,
    w_self_hbm,
    own_count_hbm,
    own_ref,
    message_ref,
    feat_grad_hbm,
    share_ref,
    w_neigh_ref,
    low_ref,
    far_count_ref,
    w_self_ref,
    own_count_ref,
    feat_grad_ref,
    edge_grad_ref,
    rest_ref,
    fetch_sems,
    keep_sems,
):
    doms, reps, cap, hub_own, tall = sizes
    rows, width = low_ref.shape
    tiles = [slice(first, first + TILE) for first in range(0, rows, TILE)]
    copies = fetch(
        (
            (share_hbm, share_ref),
            (w_neigh_hbm, w_neigh_ref),
            (low_hbm, low_ref),
            (far_count_hbm, far_count_ref),
            (w_self_hbm, w_self_ref),
            (own_count_hbm, own_count_ref),
        ),
        fetch_sems,
    )
    for copy in copies[:3]:
        copy.wait()
    for nodes in tiles:
        share_column = jnp.broadcast_to(share_ref[:, nodes], (LANES, TILE)).T
        share_column = jnp.concatenate([share_column] * (width // LANES), axis=1)
        edge_grad = matmul(low_ref[nodes, :], w_neigh_ref[...], 1, 1) * share_column
        edge_grad_ref[nodes, :] = edge_grad.astype(BF16)
    copies[3].wait()
    remote = matmul(far_count_ref[...], edge_grad_ref[...])
    bias_sum = jnp.broadcast_to(jnp.sum(bias_ref[...], axis=0, keepdims=True), (tall, width))
    bias_high = bias_sum.astype(BF16).astype(F32)
    place = iota((tall, width), 0)
    bias_rows = jnp.where(place == tall - 1, bias_sum - bias_high, bias_high)
    remote = remote.reshape(doms * reps // SIDES, SIDES, tall, width)
    rest_ref[...] = jnp.where((place < tall - BIAS_ROWS)[None, None], remote, bias_rows[None, None])
    mine = lax.axis_index("side")
    own_ref[...] = rest_ref[:, mine]
    message_ref[...] = rest_ref[:, 1 - mine].reshape(-1, width).astype(BF16)
    copies[4].wait()
    copies[5].wait()
    kept = []
    for step, nodes in enumerate(tiles):
        feat_grad_ref[nodes, :] = matmul(own_count_ref[nodes, :], edge_grad_ref[...]) + matmul(
            low_ref[nodes, :], w_self_ref[...], 1, 1
        )
        kept += fetch(
            ((feat_grad_ref.at[nodes, :], feat_grad_hbm.at[nodes, :]),),
            keep_sems.at[pl.ds(step, 1)],
        )
    for copy in kept:
        copy.wait()


def side_sum_kernel(own_ref, received_ref, message_ref):
    peers, slab, width = message_ref.shape
    w_grad = own_ref[...] + received_ref[...].astype(F32)
    owners = width // slab
    w_grad = w_grad.reshape(owners, slab, width)
    if owners < peers:
        w_grad = jnp.concatenate([w_grad, jnp.zeros((peers - owners, slab, width), F32)], axis=0)
    message_ref[...] = w_grad.astype(BF16)


def peer_sum_kernel(slabs_ref, own_ref, received_ref, message_ref):
    peers, tall, width = own_ref.shape
    slab = slabs_ref.shape[1]
    total = jnp.sum(slabs_ref[...].astype(F32), axis=0)
    rest = own_ref[...] + received_ref[...].astype(F32).reshape(peers, tall, width)
    bias = jnp.sum(rest[0, tall - BIAS_ROWS :, :], axis=0, keepdims=True)
    bias = jnp.broadcast_to(bias, (tall, width))
    bias_high = bias.astype(BF16).astype(F32)
    place = iota((tall, width), 0)
    bias_rows = jnp.where(place == tall - 1, bias - bias_high, bias_high)
    rest = jnp.where((place < tall - BIAS_ROWS)[None], rest, bias_rows[None])
    total = jnp.broadcast_to(total[None], (peers, slab, width))
    message_ref[...] = jnp.concatenate([total, rest], axis=1).astype(BF16)


def feat_grad_kernel(sizes, slab, message_ref, places_ref, feat_grad_ref, out_ref):
    doms, reps, cap, hub_own, tall = sizes
    rows, width = out_ref.shape
    pairs = reps // SIDES
    returned = message_ref[...].astype(F32)[:, slab:, :].reshape(doms, pairs, tall, width)
    returned = [
        returned[:, pair].reshape(doms * tall, width).astype(BF16) for pair in range(pairs)
    ]
    chosen = one_hot(rows, places_ref[:, : doms * tall])
    for first in range(0, rows, TILE):
        nodes = slice(first, first + TILE)
        total = feat_grad_ref[nodes, :]
        for part in returned:
            total = total + matmul(chosen[nodes, :], part)
        out_ref[nodes, :] = total.astype(BF16)


def unit_kernel(slab, mine_ref, other_ref, unit_self_ref, unit_neigh_ref, unit_bias_ref, units_ref):
    side = lax.axis_index("side")
    size, width = unit_self_ref.shape
    for place, grad_ref in ((side, mine_ref), (1 - side, other_ref)):
        grad = grad_ref[: size // slab].astype(F32)[:, :slab, :].reshape(size, width)
        square = jnp.sum(jnp.sum(grad * grad, axis=0, keepdims=True), axis=1, keepdims=True)
        units_ref[place] = grad * lax.rsqrt(square * (1.0 / grad.size) + UNIT_EPS)
    unit_self_ref[...] = units_ref[0]
    unit_neigh_ref[...] = units_ref[1]
    bias = jnp.sum(mine_ref[...].astype(F32)[:, slab:, :], axis=0)[-BIAS_ROWS:, :]
    bias = jnp.sum(bias, axis=0, keepdims=True)
    unit_bias_ref[...] = bias * lax.rsqrt(jnp.mean(bias * bias, axis=1, keepdims=True) + UNIT_EPS)


def call(kernel, out_shape, in_specs=None, out_specs=None, scratch=(), cost=(0, 0)):
    specs = {"in_specs": in_specs, "out_specs": out_specs}
    return pl.pallas_call(
        kernel,
        out_shape=out_shape,
        **{name: spec for name, spec in specs.items() if spec is not None},
        scratch_shapes=list(scratch),
        compiler_params=pltpu.CompilerParams(vmem_limit_bytes=VMEM_LIMIT),
        cost_estimate=pl.CostEstimate(flops=cost[0], bytes_accessed=cost[1], transcendentals=0),
    )


def in_hbm(*arrays):
    return [pltpu.with_memory_space_constraint(array, pltpu.HBM) for array in arrays]


def swap(array, axes):
    return lax.all_to_all(array, axes, split_axis=0, concat_axis=0, tiled=True)


def other_side(array):
    return lax.ppermute(array, "side", [(0, 1), (1, 0)])


def on_device(
    doms, reps, feats, w_self, w_neigh, bias, out_cot, degree, edge_src, hub_rows, send_rows
):
    rows, width = feats.shape
    fanout = edge_src.shape[1]
    cap, hub_own = send_rows.shape[1], hub_rows.shape[0]
    blocks, peers = doms * reps, doms * reps // SIDES
    tall = -(-(cap + hub_own + BIAS_ROWS) // 8) * 8
    slots = blocks * tall
    slab = max(8, width // peers)
    sizes = (doms, reps, cap, hub_own, tall)
    shape = jax.ShapeDtypeStruct
    hbm = pl.BlockSpec(memory_space=pltpu.HBM)
    vmem = pl.BlockSpec(memory_space=pltpu.VMEM)

    outgoing, places = call(
        functools.partial(pick_kernel, sizes),
        (shape((slots, width), BF16), shape((1, max(LANES, doms * tall)), jnp.int32)),
        [hbm] * 3,
        scratch=(
            pltpu.SMEM((hub_own,), jnp.int32),
            pltpu.SMEM((cap, doms), jnp.int32),
            pltpu.VMEM((rows, width), BF16),
            pltpu.SemaphoreType.DMA((3,)),
        ),
        cost=(2 * rows * slots * width, 2 * rows * width),
    )(*in_hbm(hub_rows, send_rows.T, feats))
    remote = swap(outgoing, SPLIT_AXES)
    tiles = rows // TILE
    one_row = ((1, rows), F32)
    across = ((width, rows), BF16)
    nodes_low = ((rows, width), BF16)
    nodes_wide = ((rows, width), F32)
    weight = ((width, width), BF16)
    own_counts = ((rows, rows), BF16)
    far_counts = ((slots, rows), BF16)
    totals = ((width, rows), F32)
    share, turned, own_count, far_count, own_total = call(
        functools.partial(own_kernel, sizes),
        tuple(pltpu.HBM(*each) for each in (one_row, across, own_counts, far_counts, totals)),
        [hbm] * 3,
        (hbm,) * 5,
        (
            pltpu.VMEM((rows, width), BF16),
            pltpu.VMEM((1, rows), jnp.int32),
            pltpu.VMEM((fanout, rows), jnp.int32),
            *(pltpu.VMEM(*each) for each in (one_row, across, own_counts, far_counts, totals)),
            pltpu.VMEM((fanout, rows), jnp.int32),
            pltpu.SemaphoreType.DMA((3,)),
            pltpu.SemaphoreType.DMA((2 + 3 * tiles,)),
        ),
        cost=(8 * rows * (rows + slots) * width, 12 * rows * width + 2 * rows * rows),
    )(*in_hbm(feats, degree.reshape(1, rows), edge_src.T))

    row_bias = bias.reshape(1, width)
    w_own, w_message, bias_sum, outputs, low = call(
        joint_kernel,
        (
            shape((width, width), F32),
            shape((width, width), BF16),
            shape((8, width), F32),
            pltpu.HBM(*nodes_low),
            pltpu.HBM(*nodes_low),
        ),
        [vmem] + [hbm] * 9,
        (vmem,) * 3 + (hbm,) * 2,
        (
            pltpu.VMEM(*one_row),
            pltpu.VMEM(*weight),
            pltpu.VMEM(*weight),
            pltpu.VMEM((1, width), F32),
            pltpu.VMEM(*across),
            pltpu.VMEM(*far_counts),
            pltpu.VMEM(*totals),
            pltpu.VMEM(*nodes_low),
            pltpu.VMEM(*nodes_low),
            pltpu.VMEM(*nodes_low),
            pltpu.VMEM(*nodes_low),
            pltpu.VMEM(*across),
            pltpu.VMEM(*nodes_wide),
            pltpu.VMEM((2, width, width), F32),
            pltpu.SemaphoreType.DMA((5 + 4 * tiles,)),
            pltpu.SemaphoreType.DMA((2 * tiles,)),
        ),
        cost=(2 * rows * slots * width + 8 * rows * width * width, 16 * rows * width),
    )(
        remote,
        *in_hbm(
            share, w_neigh, w_self, row_bias, turned, far_count, own_total, feats, out_cot
        ),
    )

    message = call(side_sum_kernel, shape((peers, slab, width), BF16))(
        w_own, other_side(w_message)
    )
    slabs = swap(message, PEERS)
    rest, rest_message, feat_grad = call(
        functools.partial(edge_kernel, sizes),
        (
            shape((peers, tall, width), F32),
            shape((peers * tall, width), BF16),
            pltpu.HBM(*nodes_wide),
        ),
        [vmem] + [hbm] * 6,
        (vmem, vmem, hbm),
        (
            pltpu.VMEM(*one_row),
            pltpu.VMEM(*weight),
            pltpu.VMEM(*nodes_low),
            pltpu.VMEM(*far_counts),
            pltpu.VMEM(*weight),
            pltpu.VMEM(*own_counts),
            pltpu.VMEM(*nodes_wide),
            pltpu.VMEM(*nodes_low),
            pltpu.VMEM((peers, SIDES, tall, width), F32),
            pltpu.SemaphoreType.DMA((6,)),
            pltpu.SemaphoreType.DMA((tiles,)),
        ),
        cost=(2 * rows * (rows + slots) * width + 4 * rows * width * width, 8 * rows * width),
    )(bias_sum, *in_hbm(share, w_neigh, low, far_count, w_self, own_count))
    message = call(peer_sum_kernel, shape((peers, slab + tall, width), BF16))(
        slabs, rest, other_side(rest_message)
    )
    message = swap(message, PEERS)
    grad_feats = call(
        functools.partial(feat_grad_kernel, sizes, slab),
        shape((rows, width), BF16),
        cost=(4 * rows * slots * width, 6 * rows * width),
    )(message, places, feat_grad)
    unit_self, unit_neigh, unit_bias = call(
        functools.partial(unit_kernel, slab),
        (shape((width, width), F32), shape((width, width), F32), shape((1, width), F32)),
        scratch=(pltpu.VMEM((2, width, width), F32),),
    )(message, other_side(message))
    return outputs, grad_feats, unit_self, unit_neigh, unit_bias.reshape(width)


def solution(mesh):
    doms, reps = mesh.shape["dom"], mesh.shape["rep"]
    split = jax.sharding.Mesh(mesh.devices.reshape(doms, reps // SIDES, SIDES), SPLIT_AXES)
    rows, whole = P(SPLIT_AXES, None), P()
    return jax.shard_map(
        functools.partial(on_device, doms, reps),
        mesh=split,
        in_specs=(rows, whole, whole, whole, rows, P(SPLIT_AXES), rows, P(SPLIT_AXES), rows),
        out_specs=(rows, rows, whole, whole, whole),
        check_vma=False,
    )
```

```python
import functools

import jax
import jax.numpy as jnp
from jax import lax
from jax.experimental import pallas as pl
from jax.experimental.pallas import tpu as pltpu
from jax.sharding import PartitionSpec as P

NORM_EPS = 1e-05
UNIT_EPS = 1e-06
SPLIT_AXES = ("dom", "pair", "side")
PEERS = ("dom", "pair")
SIDES = 2
VMEM_LIMIT = 32 * 1024 * 1024
F32 = jnp.float32
BF16 = jnp.bfloat16
TILE = 256
STRIP = 16
PIECE = 32
LANES = 128
BIAS_ROWS = 2


def div_floor(value, size):
    if size & (size - 1) == 0:
        return lax.shift_right_arithmetic(value, jnp.int32(size.bit_length() - 1))
    return value // size


def remainder(value, size):
    if size & (size - 1) == 0:
        return value & jnp.int32(size - 1)
    return value - (value // size) * size


def matmul(lhs, rhs, lhs_dim=1, rhs_dim=0):
    return lax.dot_general(
        lhs, rhs, (((lhs_dim,), (rhs_dim,)), ((), ())), preferred_element_type=F32
    )


def iota(shape, dim):
    return lax.broadcasted_iota(jnp.int32, shape, dim)


def one_hot(rows, places):
    return jnp.where(iota((rows, places.shape[1]), 0) == places, F32(1.0), F32(0.0)).astype(BF16)


def fetch(pairs, sems):
    copies = [
        pltpu.make_async_copy(source, target, sems.at[number])
        for number, (source, target) in enumerate(pairs)
    ]
    for copy in copies:
        copy.start()
    return copies


def pick_kernel(sizes, hub_hbm, send_hbm, *refs):
    doms, reps, cap, hub_own, tall = sizes
    inputs, (rows_ref, hubs_ref, places_ref), kept, (hub_ref, send_ref, sems) = (
        refs[:5],
        refs[5:8],
        refs[8:13],
        refs[13:],
    )
    feats_ref = kept[0]
    copies = fetch(((hub_hbm, hub_ref), (send_hbm, send_ref), *zip(inputs, kept)), sems)
    slots = doms * tall
    lane = iota(places_ref.shape, 1)
    row = remainder(lane, tall)

    def list_entries(dom, places):
        for entry in range(cap):
            places = jnp.where(lane == dom * tall + entry, send_ref[entry, dom], places)
        return places

    copies[0].wait()
    copies[1].wait()
    places = jnp.full(lane.shape, -1, jnp.int32)
    if doms <= 16:
        for dom in range(doms):
            places = list_entries(dom, places)
    else:
        places = lax.fori_loop(0, doms, list_entries, places)
    for entry in range(hub_own):
        for first, inside in ((cap, lane < slots), (cap + hub_own, lane >= slots)):
            places = jnp.where((row == first + entry) & inside, hub_ref[entry], places)
    places_ref[...] = places
    column = jnp.broadcast_to(places, (LANES, lane.shape[1])).T[: slots + 2 * tall, :]
    node = iota(column.shape, 1)
    chosen = [
        jnp.where(node + first == column, F32(1.0), F32(0.0)).astype(BF16)
        for first in range(0, feats_ref.shape[0], LANES)
    ]
    copies[2].wait()
    picked = matmul(jnp.concatenate(chosen, axis=1), feats_ref[...]).astype(BF16)
    rows_ref[...] = picked[:slots, :]
    hubs_ref[...] = picked[slots:, :]
    for copy in copies[3:]:
        copy.wait()


def message_kernel(sizes, rows_ref, hubs_ref, after_ref, message_ref):
    doms, reps, cap, hub_own, tall = sizes
    del after_ref
    rows = rows_ref[...].astype(F32)
    hubs = hubs_ref[...].astype(F32)[:tall, :]
    place = iota(hubs.shape, 0)
    pair = lax.axis_index("pair")
    pairs = reps // SIDES
    for dom in range(doms):
        block = rows[dom * tall : (dom + 1) * tall, :]
        blocks = [
            jnp.where((place >= cap) | (pair == other), block, F32(0.0)) + hubs
            for other in range(pairs)
        ]
        first = dom * pairs * tall
        message_ref[first : first + pairs * tall, :] = jnp.concatenate(blocks, axis=0).astype(BF16)


def count_edges(slot_ref, count_ref, nodes, base_slot):
    fanout, tile = slot_ref.shape[0], TILE
    slots = count_ref.shape[0]
    wanted = [
        jnp.broadcast_to(slot_ref[k : k + 1, nodes], (STRIP, tile)).astype(jnp.int16)
        for k in range(fanout)
    ]
    base = iota((STRIP, tile), 0) + base_slot

    def strips(first, last, start):
        for strip in range(first, last, STRIP):
            numbers = (base + (start + strip)).astype(jnp.int16)
            count = jnp.zeros((STRIP, tile), BF16)
            for k in range(fanout):
                count = count + jnp.where(numbers == wanted[k], BF16(1.0), BF16(0.0))
            if isinstance(start, int):
                count_ref[start + strip : start + strip + STRIP, nodes] = count
            else:
                count_ref[pl.ds(pl.multiple_of(start + strip, STRIP), STRIP), nodes] = count

    if slots <= 1024:
        strips(0, slots, 0)
    else:
        pl.loop(0, slots, step=TILE)(lambda start: strips(0, TILE, start))


def own_kernel(sizes, feats_ref, w_self_ref, bias_ref, degree_ref, edge_ref, *refs):
    doms, reps, cap, hub_own, tall = sizes
    inputs, refs = refs[:2], refs[2:]
    kept, (share_ref, turned_ref, own_count_ref, far_count_ref, total_ref, preact_ref) = (
        refs[:2],
        refs[2:8],
    )
    slot_ref, sems = refs[8:]
    copies = fetch(zip(inputs, kept), sems)
    rows = feats_ref.shape[0]
    fanout = edge_ref.shape[0]
    hubs = doms * reps * hub_own

    source = edge_ref[...]
    hub = source - rows
    halo = hub - hubs
    chip = SIDES * hub_own
    entry = remainder(hub, chip) ^ (lax.axis_index("side") * hub_own)
    hub_slot = rows + cap + div_floor(hub, chip) * tall + entry
    peer = div_floor(halo, cap) * (reps // SIDES) + lax.axis_index("pair")
    halo_slot = rows + peer * tall + remainder(halo, cap)
    slot = jnp.where(source < rows, source, jnp.where(hub < hubs, hub_slot, halo_slot))
    valid = jnp.minimum(degree_ref[...], fanout)
    slot_ref[...] = jnp.where(iota((fanout, rows), 0) < valid, slot, -1)
    share_ref[...] = 1.0 / valid.astype(F32)
    turned_ref[...] = feats_ref[...].T

    @pl.loop(0, rows // TILE)
    def node_tile(step):
        nodes = pl.ds(pl.multiple_of(step * TILE, TILE), TILE)
        count_edges(slot_ref, own_count_ref, nodes, 0)
        count_edges(slot_ref, far_count_ref, nodes, rows)
        total_ref[:, nodes] = matmul(turned_ref[...], own_count_ref[:, nodes])
        preact_ref[nodes, :] = matmul(feats_ref[nodes, :], w_self_ref[...]) + bias_ref[...]

    for copy in copies:
        copy.wait()


def joint_kernel(
    remote_ref,
    turned_ref,
    total_ref,
    self_ref,
    count_ref,
    share_ref,
    w_neigh_ref,
    cot_ref,
    outputs_ref,
    w_own_ref,
    w_message_ref,
    low_ref,
    bias_ref,
    mean_ref,
    preact_ref,
    w_grad_ref,
):
    rows, width = outputs_ref.shape
    table = remote_ref[...].T
    bias_sum = jnp.zeros((8, width), F32)
    for first in range(0, rows, TILE):
        nodes = slice(first, first + TILE)
        mean = total_ref[:, nodes] + matmul(table, count_ref[:, nodes])
        mean = (mean * share_ref[:, nodes]).astype(BF16)
        mean_ref[:, nodes] = mean
        preact_ref[nodes, :] = self_ref[nodes, :] + matmul(mean, w_neigh_ref[...], 0, 0)
        for start in range(first, first + TILE, PIECE):
            piece = slice(start, start + PIECE)
            preact = preact_ref[piece, :]
            cot = cot_ref[piece, :].astype(F32)
            grown = jnp.exp(jnp.minimum(preact, 0.0))
            act = jnp.where(preact > 0.0, preact, grown - 1.0)
            square = jnp.sum(act * act, axis=1, keepdims=True)
            along = jnp.sum(act * cot, axis=1, keepdims=True)
            scale = lax.rsqrt(square * (1.0 / width) + NORM_EPS)
            outputs_ref[piece, :] = (act * scale).astype(BF16)
            pull = along * (scale * scale * scale) * (1.0 / width)
            grad_pre = (cot * scale - act * pull) * jnp.where(preact > 0.0, F32(1.0), grown)
            bias_sum = bias_sum + jnp.sum(grad_pre.reshape(PIECE // 8, 8, width), axis=0)
            low_ref[piece, :] = grad_pre.astype(BF16)

    low = low_ref[...]
    w_grad_ref[0] = matmul(turned_ref[...], low)
    w_grad_ref[1] = matmul(mean_ref[...], low)
    bias_ref[...] = bias_sum
    mine = lax.axis_index("side")
    w_own_ref[...] = w_grad_ref[mine]
    w_message_ref[...] = w_grad_ref[1 - mine].astype(BF16)


def edge_kernel(
    sizes,
    low_ref,
    w_neigh_ref,
    w_self_ref,
    share_ref,
    own_count_ref,
    far_count_ref,
    bias_ref,
    feat_grad_ref,
    own_ref,
    message_ref,
    edge_grad_ref,
):
    doms, reps, cap, hub_own, tall = sizes
    rows, width = low_ref.shape
    for first in range(0, rows, TILE):
        nodes = slice(first, first + TILE)
        share_column = jnp.broadcast_to(share_ref[:, nodes], (LANES, TILE)).T
        share_column = jnp.concatenate([share_column] * (width // LANES), axis=1)
        edge_grad = matmul(low_ref[nodes, :], w_neigh_ref[...], 1, 1) * share_column
        edge_grad_ref[nodes, :] = edge_grad.astype(BF16)
    remote = matmul(far_count_ref[...], edge_grad_ref[...])
    own_ref[...] = remote
    bias_sum = jnp.broadcast_to(jnp.sum(bias_ref[...], axis=0, keepdims=True), (tall, width))
    bias_high = bias_sum.astype(BF16).astype(F32)
    place = iota((tall, width), 0)
    bias_rows = jnp.where(place == cap, bias_high, bias_sum - bias_high)
    bias_rows = jnp.where(place < cap, F32(0.0), bias_rows)
    message = remote.reshape(-1, tall, width)
    message = jnp.where((place < cap + hub_own)[None], bias_rows[None], message)
    message_ref[...] = message.reshape(remote.shape).astype(BF16)
    for first in range(0, rows, TILE):
        nodes = slice(first, first + TILE)
        feat_grad_ref[nodes, :] = matmul(own_count_ref[nodes, :], edge_grad_ref[...]) + matmul(
            low_ref[nodes, :], w_self_ref[...], 1, 1
        )


def side_sum_kernel(own_ref, received_ref, after_ref, message_ref):
    del after_ref
    peers, slab, width = message_ref.shape
    w_grad = own_ref[...] + received_ref[...].astype(F32)
    owners = width // slab
    w_grad = w_grad.reshape(owners, slab, width)
    if owners < peers:
        w_grad = jnp.concatenate([w_grad, jnp.zeros((peers - owners, slab, width), F32)], axis=0)
    message_ref[...] = w_grad.astype(BF16)


def peer_sum_kernel(sizes, slabs_ref, own_ref, received_ref, bias_ref, message_ref):
    doms, reps, cap, hub_own, tall = sizes
    peers, slab, width = slabs_ref.shape
    total = jnp.sum(slabs_ref[...].astype(F32), axis=0)
    size = min(peers * tall, LANES)
    to, source = iota((size, size), 0), iota((size, size), 1)
    entry = remainder(to, tall) - cap
    moved = (source == to + hub_own) & (entry >= 0) & (entry < hub_own)
    moved = jnp.where(moved, F32(1.0), F32(0.0)).astype(BF16)
    rest = own_ref[...] + jnp.concatenate(
        [
            matmul(moved, received_ref[first : first + size, :])
            for first in range(0, peers * tall, size)
        ],
        axis=0,
    )
    place = iota((tall, width), 0)
    bias = received_ref[: 2 * tall, :].astype(F32)[:tall, :]
    bias = jnp.where((place >= cap) & (place < cap + BIAS_ROWS), bias, F32(0.0)) + bias_ref[...]
    bias = jnp.broadcast_to(jnp.sum(bias, axis=0, keepdims=True), (tall, width))
    bias_high = bias.astype(BF16).astype(F32)
    bias_rows = jnp.where(place == tall - 1, bias - bias_high, bias_high)
    rest = rest.reshape(peers, tall, width)
    rest = jnp.where((place < tall - BIAS_ROWS)[None], rest, bias_rows[None])
    total = jnp.broadcast_to(total[None], (peers, slab, width))
    message_ref[...] = jnp.concatenate([total, rest], axis=1).astype(BF16)


def feat_grad_kernel(sizes, slab, message_ref, places_ref, feat_grad_ref, out_ref):
    doms, reps, cap, hub_own, tall = sizes
    rows, width = out_ref.shape
    pairs = reps // SIDES
    returned = message_ref[...].astype(F32)[:, slab:, :].reshape(doms, pairs, tall, width)
    returned = [
        returned[:, pair].reshape(doms * tall, width).astype(BF16) for pair in range(pairs)
    ]
    chosen = one_hot(rows, places_ref[:, : doms * tall])
    for first in range(0, rows, TILE):
        nodes = slice(first, first + TILE)
        total = feat_grad_ref[nodes, :]
        for part in returned:
            total = total + matmul(chosen[nodes, :], part)
        out_ref[nodes, :] = total.astype(BF16)


def unit_kernel(slab, mine_ref, other_ref, unit_self_ref, unit_neigh_ref, unit_bias_ref, units_ref):
    side = lax.axis_index("side")
    size, width = unit_self_ref.shape
    for place, grad_ref in ((side, mine_ref), (1 - side, other_ref)):
        grad = grad_ref[: size // slab].astype(F32)[:, :slab, :].reshape(size, width)
        square = jnp.sum(jnp.sum(grad * grad, axis=0, keepdims=True), axis=1, keepdims=True)
        units_ref[place] = grad * lax.rsqrt(square * (1.0 / grad.size) + UNIT_EPS)
    unit_self_ref[...] = units_ref[0]
    unit_neigh_ref[...] = units_ref[1]
    bias = jnp.sum(mine_ref[...].astype(F32)[:, slab:, :], axis=0)[-BIAS_ROWS:, :]
    bias = jnp.sum(bias, axis=0, keepdims=True)
    unit_bias_ref[...] = bias * lax.rsqrt(jnp.mean(bias * bias, axis=1, keepdims=True) + UNIT_EPS)


def call(kernel, out_shape, in_specs=None, scratch=(), cost=(0, 0)):
    return pl.pallas_call(
        kernel,
        out_shape=out_shape,
        **({} if in_specs is None else {"in_specs": in_specs}),
        scratch_shapes=list(scratch),
        compiler_params=pltpu.CompilerParams(vmem_limit_bytes=VMEM_LIMIT),
        cost_estimate=pl.CostEstimate(flops=cost[0], bytes_accessed=cost[1], transcendentals=0),
    )


def in_hbm(*arrays):
    return [pltpu.with_memory_space_constraint(array, pltpu.HBM) for array in arrays]


def swap(array, axes):
    return lax.all_to_all(array, axes, split_axis=0, concat_axis=0, tiled=True)


def other_side(array):
    return lax.ppermute(array, "side", [(0, 1), (1, 0)])


def on_device(
    doms, reps, feats, w_self, w_neigh, bias, out_cot, degree, edge_src, hub_rows, send_rows
):
    rows, width = feats.shape
    fanout = edge_src.shape[1]
    cap, hub_own = send_rows.shape[1], hub_rows.shape[0]
    peers = doms * reps // SIDES
    tall = cap + SIDES * hub_own
    if tall % 8 or tall < cap + hub_own + BIAS_ROWS or hub_own & (hub_own - 1):
        raise ValueError("message height")
    slots = peers * tall
    slab = max(8, width // peers)
    sizes = (doms, reps, cap, hub_own, tall)
    shape = jax.ShapeDtypeStruct
    hbm = pl.BlockSpec(memory_space=pltpu.HBM)
    vmem = pl.BlockSpec(memory_space=pltpu.VMEM)

    picked, hubs, places, *kept = call(
        functools.partial(pick_kernel, sizes),
        (
            shape((doms * tall, width), BF16),
            shape((2 * tall, width), BF16),
            shape((1, -(-(doms + 2) * tall // LANES) * LANES), jnp.int32),
            shape((rows, width), BF16),
            shape((width, width), BF16),
            shape((1, width), F32),
            shape((1, rows), jnp.int32),
            shape((fanout, rows), jnp.int32),
        ),
        [hbm] * 7,
        (
            pltpu.SMEM((hub_own,), jnp.int32),
            pltpu.SMEM((cap, doms), jnp.int32),
            pltpu.SemaphoreType.DMA((7,)),
        ),
        cost=(2 * rows * slots * width, 2 * rows * width),
    )(
        *in_hbm(
            hub_rows,
            send_rows.T,
            feats,
            w_self,
            bias.reshape(1, width),
            degree.reshape(1, rows),
            edge_src.T,
        )
    )
    hubs = other_side(hubs)
    w_neigh_kept, cot_kept, share, turned, own_count, far_count, own_total, self_part = call(
        functools.partial(own_kernel, sizes),
        (
            shape((width, width), BF16),
            shape((rows, width), BF16),
            shape((1, rows), F32),
            shape((width, rows), BF16),
            shape((rows, rows), BF16),
            shape((slots, rows), BF16),
            shape((width, rows), F32),
            shape((rows, width), F32),
        ),
        [vmem] * 5 + [hbm] * 2,
        (pltpu.VMEM((fanout, rows), jnp.int32), pltpu.SemaphoreType.DMA((2,))),
        cost=(8 * rows * (rows + slots) * width, 12 * rows * width + 2 * rows * rows),
    )(*kept, *in_hbm(w_neigh, out_cot))

    message = call(
        functools.partial(message_kernel, sizes),
        shape((slots, width), BF16),
        [vmem, vmem, pl.BlockSpec(memory_space=pl.ANY)],
    )(picked, hubs, share)
    remote = swap(message, PEERS)

    outputs, w_own, w_message, low, bias_sum = call(
        joint_kernel,
        (
            shape((rows, width), BF16),
            shape((width, width), F32),
            shape((width, width), BF16),
            shape((rows, width), BF16),
            shape((8, width), F32),
        ),
        scratch=(
            pltpu.VMEM((width, rows), BF16),
            pltpu.VMEM((rows, width), F32),
            pltpu.VMEM((2, width, width), F32),
        ),
        cost=(2 * rows * slots * width + 6 * rows * width * width, 16 * rows * width),
    )(remote, turned, own_total, self_part, far_count, share, w_neigh_kept, cot_kept)

    w_received = other_side(w_message)
    feat_grad, rest, rest_message = call(
        functools.partial(edge_kernel, sizes),
        (
            shape((rows, width), F32),
            shape((slots, width), F32),
            shape((slots, width), BF16),
        ),
        scratch=(pltpu.VMEM((rows, width), BF16),),
        cost=(2 * rows * (rows + slots) * width + 4 * rows * width * width, 8 * rows * width),
    )(low, w_neigh_kept, kept[1], share, own_count, far_count, bias_sum)
    rest_received = other_side(rest_message)
    message = call(
        side_sum_kernel,
        shape((peers, slab, width), BF16),
        [vmem, vmem, pl.BlockSpec(memory_space=pl.ANY)],
    )(w_own, w_received, rest)
    slabs = swap(message, PEERS)
    message = call(
        functools.partial(peer_sum_kernel, sizes), shape((peers, slab + tall, width), BF16)
    )(slabs, rest, rest_received, bias_sum)
    message = swap(message, PEERS)
    grad_feats = call(
        functools.partial(feat_grad_kernel, sizes, slab),
        shape((rows, width), BF16),
        cost=(4 * rows * slots * width, 6 * rows * width),
    )(message, places, feat_grad)
    unit_self, unit_neigh, unit_bias = call(
        functools.partial(unit_kernel, slab),
        (shape((width, width), F32), shape((width, width), F32), shape((1, width), F32)),
        scratch=(pltpu.VMEM((2, width, width), F32),),
    )(message, other_side(message))
    return outputs, grad_feats, unit_self, unit_neigh, unit_bias.reshape(width)


def solution(mesh):
    doms, reps = mesh.shape["dom"], mesh.shape["rep"]
    split = jax.sharding.Mesh(mesh.devices.reshape(doms, reps // SIDES, SIDES), SPLIT_AXES)
    rows, whole = P(SPLIT_AXES, None), P()
    return jax.shard_map(
        functools.partial(on_device, doms, reps),
        mesh=split,
        in_specs=(rows, whole, whole, whole, rows, P(SPLIT_AXES), rows, P(SPLIT_AXES), rows),
        out_specs=(rows, rows, whole, whole, whole),
        check_vma=False,
    )
```

```python
import functools

import jax
import jax.numpy as jnp
from jax import lax
from jax.experimental import pallas as pl
from jax.experimental.pallas import tpu as pltpu
from jax.sharding import PartitionSpec as P

NORM_EPS = 1e-05
UNIT_EPS = 1e-06
SPLIT_AXES = ("dom", "pair", "side")
PEERS = ("dom", "pair")
SIDES = 2
VMEM_LIMIT = 32 * 1024 * 1024
F32 = jnp.float32
BF16 = jnp.bfloat16
TILE = 256
STRIP = 16
PIECE = 32
LANES = 128
BIAS_ROWS = 2


def div_floor(value, size):
    if size & (size - 1) == 0:
        return lax.shift_right_arithmetic(value, jnp.int32(size.bit_length() - 1))
    return value // size


def remainder(value, size):
    if size & (size - 1) == 0:
        return value & jnp.int32(size - 1)
    return value - (value // size) * size


def matmul(lhs, rhs, lhs_dim=1, rhs_dim=0):
    return lax.dot_general(
        lhs, rhs, (((lhs_dim,), (rhs_dim,)), ((), ())), preferred_element_type=F32
    )


def iota(shape, dim):
    return lax.broadcasted_iota(jnp.int32, shape, dim)


def one_hot(rows, places):
    return jnp.where(iota((rows, places.shape[1]), 0) == places, F32(1.0), F32(0.0)).astype(BF16)


def fetch(pairs, sems):
    copies = [
        pltpu.make_async_copy(source, target, sems.at[number])
        for number, (source, target) in enumerate(pairs)
    ]
    for copy in copies:
        copy.start()
    return copies


def pick_kernel(sizes, hub_hbm, send_hbm, *refs):
    doms, reps, cap, hub_own, tall = sizes
    inputs, (rows_ref, hubs_ref, places_ref), kept, (hub_ref, send_ref, sems) = (
        refs[:5],
        refs[5:8],
        refs[8:13],
        refs[13:],
    )
    feats_ref = kept[0]
    copies = fetch(((hub_hbm, hub_ref), (send_hbm, send_ref), *zip(inputs, kept)), sems)
    slots = doms * tall
    lane = iota(places_ref.shape, 1)
    row = remainder(lane, tall)

    def list_entries(dom, places):
        for entry in range(cap):
            places = jnp.where(lane == dom * tall + entry, send_ref[entry, dom], places)
        return places

    copies[0].wait()
    copies[1].wait()
    places = jnp.full(lane.shape, -1, jnp.int32)
    if doms <= 16:
        for dom in range(doms):
            places = list_entries(dom, places)
    else:
        places = lax.fori_loop(0, doms, list_entries, places)
    for entry in range(hub_own):
        for first, inside in ((cap, lane < slots), (cap + hub_own, lane >= slots)):
            places = jnp.where((row == first + entry) & inside, hub_ref[entry], places)
    places_ref[...] = places
    column = jnp.broadcast_to(places, (LANES, lane.shape[1])).T[: slots + 2 * tall, :]
    node = iota(column.shape, 1)
    chosen = [
        jnp.where(node + first == column, F32(1.0), F32(0.0)).astype(BF16)
        for first in range(0, feats_ref.shape[0], LANES)
    ]
    copies[2].wait()
    picked = matmul(jnp.concatenate(chosen, axis=1), feats_ref[...]).astype(BF16)
    rows_ref[...] = picked[:slots, :]
    hubs_ref[...] = picked[slots:, :]
    for copy in copies[3:]:
        copy.wait()


def message_kernel(sizes, rows_ref, hubs_ref, after_ref, message_ref):
    doms, reps, cap, hub_own, tall = sizes
    del after_ref
    rows = rows_ref[...].astype(F32)
    hubs = hubs_ref[...].astype(F32)[:tall, :]
    place = iota(hubs.shape, 0)
    pair = lax.axis_index("pair")
    pairs = reps // SIDES
    for dom in range(doms):
        block = rows[dom * tall : (dom + 1) * tall, :]
        blocks = [
            jnp.where((place >= cap) | (pair == other), block, F32(0.0)) + hubs
            for other in range(pairs)
        ]
        first = dom * pairs * tall
        message_ref[first : first + pairs * tall, :] = jnp.concatenate(blocks, axis=0).astype(BF16)


def count_edges(slot_ref, count_ref, nodes, base_slot):
    fanout, tile = slot_ref.shape[0], TILE
    slots = count_ref.shape[0]
    wanted = [
        jnp.broadcast_to(slot_ref[k : k + 1, nodes], (STRIP, tile)).astype(jnp.int16)
        for k in range(fanout)
    ]
    base = iota((STRIP, tile), 0) + base_slot

    def strips(first, last, start):
        for strip in range(first, last, STRIP):
            numbers = (base + (start + strip)).astype(jnp.int16)
            count = jnp.zeros((STRIP, tile), BF16)
            for k in range(fanout):
                count = count + jnp.where(numbers == wanted[k], BF16(1.0), BF16(0.0))
            if isinstance(start, int):
                count_ref[start + strip : start + strip + STRIP, nodes] = count
            else:
                count_ref[pl.ds(pl.multiple_of(start + strip, STRIP), STRIP), nodes] = count

    if slots <= 1024:
        strips(0, slots, 0)
    else:
        pl.loop(0, slots, step=TILE)(lambda start: strips(0, TILE, start))


def own_kernel(sizes, feats_ref, w_self_ref, bias_ref, degree_ref, edge_ref, *refs):
    doms, reps, cap, hub_own, tall = sizes
    inputs, refs = refs[:2], refs[2:]
    kept, (share_ref, turned_ref, own_count_ref, far_count_ref, total_ref, preact_ref) = (
        refs[:2],
        refs[2:8],
    )
    slot_ref, sems = refs[8:]
    copies = fetch(zip(inputs, kept), sems)
    rows = feats_ref.shape[0]
    fanout = edge_ref.shape[0]
    hubs = doms * reps * hub_own

    source = edge_ref[...]
    hub = source - rows
    halo = hub - hubs
    chip = SIDES * hub_own
    entry = remainder(hub, chip) ^ (lax.axis_index("side") * hub_own)
    hub_slot = rows + cap + div_floor(hub, chip) * tall + entry
    peer = div_floor(halo, cap) * (reps // SIDES) + lax.axis_index("pair")
    halo_slot = rows + peer * tall + remainder(halo, cap)
    slot = jnp.where(source < rows, source, jnp.where(hub < hubs, hub_slot, halo_slot))
    valid = jnp.minimum(degree_ref[...], fanout)
    slot_ref[...] = jnp.where(iota((fanout, rows), 0) < valid, slot, -1)
    share_ref[...] = 1.0 / valid.astype(F32)
    turned_ref[...] = feats_ref[...].T

    def own_sums(nodes):
        total_ref[:, nodes] = matmul(turned_ref[...], own_count_ref[:, nodes])
        preact_ref[nodes, :] = matmul(feats_ref[nodes, :], w_self_ref[...]) + bias_ref[...]

    counted = None
    for first in range(0, rows, TILE):
        nodes = slice(first, first + TILE)
        count_edges(slot_ref, own_count_ref, nodes, 0)
        if counted is not None:
            own_sums(counted)
        count_edges(slot_ref, far_count_ref, nodes, rows)
        counted = nodes
    own_sums(counted)
    for copy in copies:
        copy.wait()


def joint_kernel(
    remote_ref,
    turned_ref,
    total_ref,
    self_ref,
    count_ref,
    share_ref,
    w_neigh_ref,
    cot_ref,
    outputs_hbm,
    w_own_ref,
    w_message_ref,
    low_ref,
    bias_ref,
    outputs_ref,
    mean_ref,
    preact_ref,
    w_grad_ref,
    sems,
):
    rows, width = outputs_ref.shape
    table = remote_ref[...].T
    bias_sum = jnp.zeros((8, width), F32)
    copies = []
    for first in range(0, rows, TILE):
        nodes = slice(first, first + TILE)
        mean = total_ref[:, nodes] + matmul(table, count_ref[:, nodes])
        mean = (mean * share_ref[:, nodes]).astype(BF16)
        mean_ref[:, nodes] = mean
        preact_ref[nodes, :] = self_ref[nodes, :] + matmul(mean, w_neigh_ref[...], 0, 0)
        for start in range(first, first + TILE, PIECE):
            piece = slice(start, start + PIECE)
            preact = preact_ref[piece, :]
            cot = cot_ref[piece, :].astype(F32)
            grown = jnp.exp(jnp.minimum(preact, 0.0))
            act = jnp.where(preact > 0.0, preact, grown - 1.0)
            square = jnp.sum(act * act, axis=1, keepdims=True)
            along = jnp.sum(act * cot, axis=1, keepdims=True)
            scale = lax.rsqrt(square * (1.0 / width) + NORM_EPS)
            outputs_ref[piece, :] = (act * scale).astype(BF16)
            pull = along * (scale * scale * scale) * (1.0 / width)
            grad_pre = (cot * scale - act * pull) * jnp.where(preact > 0.0, F32(1.0), grown)
            bias_sum = bias_sum + jnp.sum(grad_pre.reshape(PIECE // 8, 8, width), axis=0)
            low_ref[piece, :] = grad_pre.astype(BF16)
        number = first // TILE
        copies += fetch(
            ((outputs_ref.at[nodes, :], outputs_hbm.at[nodes, :]),), sems.at[pl.ds(number, 1)]
        )

    low = low_ref[...]
    w_grad_ref[0] = matmul(turned_ref[...], low)
    w_grad_ref[1] = matmul(mean_ref[...], low)
    bias_ref[...] = bias_sum
    mine = lax.axis_index("side")
    w_own_ref[...] = w_grad_ref[mine]
    w_message_ref[...] = w_grad_ref[1 - mine].astype(BF16)
    for copy in copies:
        copy.wait()


def edge_kernel(
    sizes,
    low_ref,
    w_neigh_ref,
    share_ref,
    far_count_ref,
    bias_ref,
    own_ref,
    message_ref,
    edge_grad_ref,
):
    doms, reps, cap, hub_own, tall = sizes
    rows, width = low_ref.shape
    for first in range(0, rows, TILE):
        nodes = slice(first, first + TILE)
        share_column = jnp.broadcast_to(share_ref[:, nodes], (LANES, TILE)).T
        share_column = jnp.concatenate([share_column] * (width // LANES), axis=1)
        edge_grad = matmul(low_ref[nodes, :], w_neigh_ref[...], 1, 1) * share_column
        edge_grad_ref[nodes, :] = edge_grad.astype(BF16)
    remote = matmul(far_count_ref[...], edge_grad_ref[...])
    own_ref[...] = remote
    bias_sum = jnp.broadcast_to(jnp.sum(bias_ref[...], axis=0, keepdims=True), (tall, width))
    bias_high = bias_sum.astype(BF16).astype(F32)
    place = iota((tall, width), 0)
    bias_rows = jnp.where(place == cap, bias_high, bias_sum - bias_high)
    bias_rows = jnp.where(place < cap, F32(0.0), bias_rows)
    message = remote.reshape(-1, tall, width)
    message = jnp.where((place < cap + hub_own)[None], bias_rows[None], message)
    message_ref[...] = message.reshape(remote.shape).astype(BF16)


def own_grad_kernel(low_ref, w_self_ref, own_count_ref, edge_grad_ref, feat_grad_ref):
    for first in range(0, low_ref.shape[0], TILE):
        nodes = slice(first, first + TILE)
        feat_grad_ref[nodes, :] = matmul(own_count_ref[nodes, :], edge_grad_ref[...]) + matmul(
            low_ref[nodes, :], w_self_ref[...], 1, 1
        )


def side_sum_kernel(own_ref, received_ref, after_ref, after_too_ref, message_ref):
    del after_ref, after_too_ref
    peers, slab, width = message_ref.shape
    w_grad = own_ref[...] + received_ref[...].astype(F32)
    owners = width // slab
    w_grad = w_grad.reshape(owners, slab, width)
    if owners < peers:
        w_grad = jnp.concatenate([w_grad, jnp.zeros((peers - owners, slab, width), F32)], axis=0)
    message_ref[...] = w_grad.astype(BF16)


def peer_sum_kernel(sizes, slabs_ref, own_ref, received_ref, bias_ref, message_ref):
    doms, reps, cap, hub_own, tall = sizes
    peers, slab, width = slabs_ref.shape
    total = jnp.sum(slabs_ref[...].astype(F32), axis=0)
    size = min(peers * tall, LANES)
    to, source = iota((size, size), 0), iota((size, size), 1)
    entry = remainder(to, tall) - cap
    moved = (source == to + hub_own) & (entry >= 0) & (entry < hub_own)
    moved = jnp.where(moved, F32(1.0), F32(0.0)).astype(BF16)
    rest = own_ref[...] + jnp.concatenate(
        [
            matmul(moved, received_ref[first : first + size, :])
            for first in range(0, peers * tall, size)
        ],
        axis=0,
    )
    place = iota((tall, width), 0)
    bias = received_ref[: 2 * tall, :].astype(F32)[:tall, :]
    bias = jnp.where((place >= cap) & (place < cap + BIAS_ROWS), bias, F32(0.0)) + bias_ref[...]
    bias = jnp.broadcast_to(jnp.sum(bias, axis=0, keepdims=True), (tall, width))
    bias_high = bias.astype(BF16).astype(F32)
    bias_rows = jnp.where(place == tall - 1, bias - bias_high, bias_high)
    rest = rest.reshape(peers, tall, width)
    rest = jnp.where((place < tall - BIAS_ROWS)[None], rest, bias_rows[None])
    total = jnp.broadcast_to(total[None], (peers, slab, width))
    message_ref[...] = jnp.concatenate([total, rest], axis=1).astype(BF16)


def feat_grad_kernel(sizes, slab, message_ref, places_ref, feat_grad_ref, out_ref):
    doms, reps, cap, hub_own, tall = sizes
    rows, width = out_ref.shape
    pairs = reps // SIDES
    returned = message_ref[...].astype(F32)[:, slab:, :].reshape(doms, pairs, tall, width)
    returned = [
        returned[:, pair].reshape(doms * tall, width).astype(BF16) for pair in range(pairs)
    ]
    chosen = one_hot(rows, places_ref[:, : doms * tall])
    for first in range(0, rows, TILE):
        nodes = slice(first, first + TILE)
        total = feat_grad_ref[nodes, :]
        for part in returned:
            total = total + matmul(chosen[nodes, :], part)
        out_ref[nodes, :] = total.astype(BF16)


def unit_kernel(slab, mine_ref, other_ref, unit_self_ref, unit_neigh_ref, unit_bias_ref, units_ref):
    side = lax.axis_index("side")
    size, width = unit_self_ref.shape
    for place, grad_ref in ((side, mine_ref), (1 - side, other_ref)):
        grad = grad_ref[: size // slab].astype(F32)[:, :slab, :].reshape(size, width)
        square = jnp.sum(jnp.sum(grad * grad, axis=0, keepdims=True), axis=1, keepdims=True)
        units_ref[place] = grad * lax.rsqrt(square * (1.0 / grad.size) + UNIT_EPS)
    unit_self_ref[...] = units_ref[0]
    unit_neigh_ref[...] = units_ref[1]
    bias = jnp.sum(mine_ref[...].astype(F32)[:, slab:, :], axis=0)[-BIAS_ROWS:, :]
    bias = jnp.sum(bias, axis=0, keepdims=True)
    unit_bias_ref[...] = bias * lax.rsqrt(jnp.mean(bias * bias, axis=1, keepdims=True) + UNIT_EPS)


def call(kernel, out_shape, in_specs=None, scratch=(), cost=(0, 0), out_specs=None):
    specs = {"in_specs": in_specs, "out_specs": out_specs}
    return pl.pallas_call(
        kernel,
        out_shape=out_shape,
        **{name: spec for name, spec in specs.items() if spec is not None},
        scratch_shapes=list(scratch),
        compiler_params=pltpu.CompilerParams(vmem_limit_bytes=VMEM_LIMIT),
        cost_estimate=pl.CostEstimate(flops=cost[0], bytes_accessed=cost[1], transcendentals=0),
    )


def in_hbm(*arrays):
    return [pltpu.with_memory_space_constraint(array, pltpu.HBM) for array in arrays]


def swap(array, axes):
    return lax.all_to_all(array, axes, split_axis=0, concat_axis=0, tiled=True)


def other_side(array):
    return lax.ppermute(array, "side", [(0, 1), (1, 0)])


def on_device(
    doms, reps, feats, w_self, w_neigh, bias, out_cot, degree, edge_src, hub_rows, send_rows
):
    rows, width = feats.shape
    fanout = edge_src.shape[1]
    cap, hub_own = send_rows.shape[1], hub_rows.shape[0]
    peers = doms * reps // SIDES
    tall = cap + SIDES * hub_own
    if tall % 8 or tall < cap + hub_own + BIAS_ROWS or hub_own & (hub_own - 1):
        raise ValueError("message height")
    slots = peers * tall
    slab = max(8, width // peers)
    sizes = (doms, reps, cap, hub_own, tall)
    shape = jax.ShapeDtypeStruct
    hbm = pl.BlockSpec(memory_space=pltpu.HBM)
    vmem = pl.BlockSpec(memory_space=pltpu.VMEM)

    picked, hubs, places, *kept = call(
        functools.partial(pick_kernel, sizes),
        (
            shape((doms * tall, width), BF16),
            shape((2 * tall, width), BF16),
            shape((1, -(-(doms + 2) * tall // LANES) * LANES), jnp.int32),
            shape((rows, width), BF16),
            shape((width, width), BF16),
            shape((1, width), F32),
            shape((1, rows), jnp.int32),
            shape((fanout, rows), jnp.int32),
        ),
        [hbm] * 7,
        (
            pltpu.SMEM((hub_own,), jnp.int32),
            pltpu.SMEM((cap, doms), jnp.int32),
            pltpu.SemaphoreType.DMA((7,)),
        ),
        cost=(2 * rows * slots * width, 2 * rows * width),
    )(
        *in_hbm(
            hub_rows,
            send_rows.T,
            feats,
            w_self,
            bias.reshape(1, width),
            degree.reshape(1, rows),
            edge_src.T,
        )
    )
    hubs = other_side(hubs)
    w_neigh_kept, cot_kept, share, turned, own_count, far_count, own_total, self_part = call(
        functools.partial(own_kernel, sizes),
        (
            shape((width, width), BF16),
            shape((rows, width), BF16),
            shape((1, rows), F32),
            shape((width, rows), BF16),
            shape((rows, rows), BF16),
            shape((slots, rows), BF16),
            shape((width, rows), F32),
            shape((rows, width), F32),
        ),
        [vmem] * 5 + [hbm] * 2,
        (pltpu.VMEM((fanout, rows), jnp.int32), pltpu.SemaphoreType.DMA((2,))),
        cost=(8 * rows * (rows + slots) * width, 12 * rows * width + 2 * rows * rows),
    )(*kept, *in_hbm(w_neigh, out_cot))

    message = call(
        functools.partial(message_kernel, sizes),
        shape((slots, width), BF16),
        [vmem, vmem, pl.BlockSpec(memory_space=pl.ANY)],
    )(picked, hubs, share)
    remote = swap(message, PEERS)

    outputs, w_own, w_message, low, bias_sum = call(
        joint_kernel,
        (
            pltpu.HBM((rows, width), BF16),
            shape((width, width), F32),
            shape((width, width), BF16),
            shape((rows, width), BF16),
            shape((8, width), F32),
        ),
        out_specs=(hbm,) + (vmem,) * 4,
        scratch=(
            pltpu.VMEM((rows, width), BF16),
            pltpu.VMEM((width, rows), BF16),
            pltpu.VMEM((rows, width), F32),
            pltpu.VMEM((2, width, width), F32),
            pltpu.SemaphoreType.DMA((rows // TILE,)),
        ),
        cost=(2 * rows * slots * width + 6 * rows * width * width, 16 * rows * width),
    )(remote, turned, own_total, self_part, far_count, share, w_neigh_kept, cot_kept)

    w_received = other_side(w_message)
    rest, rest_message, edge_grad = call(
        functools.partial(edge_kernel, sizes),
        (
            shape((slots, width), F32),
            shape((slots, width), BF16),
            shape((rows, width), BF16),
        ),
        cost=(2 * rows * slots * width + 2 * rows * width * width, 8 * rows * width),
    )(low, w_neigh_kept, share, far_count, bias_sum)
    rest_received = other_side(rest_message)
    feat_grad = call(
        own_grad_kernel,
        shape((rows, width), F32),
        cost=(2 * rows * rows * width + 2 * rows * width * width, 8 * rows * width),
    )(low, kept[1], own_count, edge_grad)
    message = call(
        side_sum_kernel,
        shape((peers, slab, width), BF16),
        [vmem, vmem] + [pl.BlockSpec(memory_space=pl.ANY)] * 2,
    )(w_own, w_received, feat_grad, rest_received)
    slabs = swap(message, PEERS)
    message = call(
        functools.partial(peer_sum_kernel, sizes), shape((peers, slab + tall, width), BF16)
    )(slabs, rest, rest_received, bias_sum)
    message = swap(message, PEERS)
    grad_feats = call(
        functools.partial(feat_grad_kernel, sizes, slab),
        shape((rows, width), BF16),
        cost=(4 * rows * slots * width, 6 * rows * width),
    )(message, places, feat_grad)
    unit_self, unit_neigh, unit_bias = call(
        functools.partial(unit_kernel, slab),
        (shape((width, width), F32), shape((width, width), F32), shape((1, width), F32)),
        scratch=(pltpu.VMEM((2, width, width), F32),),
    )(message, other_side(message))
    return outputs, grad_feats, unit_self, unit_neigh, unit_bias.reshape(width)


def solution(mesh):
    doms, reps = mesh.shape["dom"], mesh.shape["rep"]
    split = jax.sharding.Mesh(mesh.devices.reshape(doms, reps // SIDES, SIDES), SPLIT_AXES)
    rows, whole = P(SPLIT_AXES, None), P()
    return jax.shard_map(
        functools.partial(on_device, doms, reps),
        mesh=split,
        in_specs=(rows, whole, whole, whole, rows, P(SPLIT_AXES), rows, P(SPLIT_AXES), rows),
        out_specs=(rows, rows, whole, whole, whole),
        check_vma=False,
    )
```

```python
import functools

import jax
import jax.numpy as jnp
from jax import lax
from jax.experimental import pallas as pl
from jax.experimental.pallas import tpu as pltpu
from jax.sharding import PartitionSpec as P

NORM_EPS = 1e-05
UNIT_EPS = 1e-06
SPLIT_AXES = ("dom", "pair", "side")
PEERS = ("dom", "pair")
SIDES = 2
VMEM_LIMIT = 32 * 1024 * 1024
F32 = jnp.float32
BF16 = jnp.bfloat16
TILE = 256
STRIP = 16
PIECE = 32
LANES = 128
BIAS_ROWS = 2


def div_floor(value, size):
    if size & (size - 1) == 0:
        return lax.shift_right_arithmetic(value, jnp.int32(size.bit_length() - 1))
    return value // size


def remainder(value, size):
    if size & (size - 1) == 0:
        return value & jnp.int32(size - 1)
    return value - (value // size) * size


def matmul(lhs, rhs, lhs_dim=1, rhs_dim=0):
    return lax.dot_general(
        lhs, rhs, (((lhs_dim,), (rhs_dim,)), ((), ())), preferred_element_type=F32
    )


def iota(shape, dim):
    return lax.broadcasted_iota(jnp.int32, shape, dim)


def one_hot(rows, places):
    return jnp.where(iota((rows, places.shape[1]), 0) == places, F32(1.0), F32(0.0)).astype(BF16)


def fetch(pairs, sems):
    copies = [
        pltpu.make_async_copy(source, target, sems.at[number])
        for number, (source, target) in enumerate(pairs)
    ]
    for copy in copies:
        copy.start()
    return copies


def pick_kernel(sizes, hub_hbm, send_hbm, *refs):
    doms, reps, cap, hub_own, tall = sizes
    inputs, (rows_ref, hubs_ref, places_ref), kept, (hub_ref, send_ref, sems) = (
        refs[:5],
        refs[5:8],
        refs[8:13],
        refs[13:],
    )
    feats_ref = kept[0]
    copies = fetch(((hub_hbm, hub_ref), (send_hbm, send_ref), *zip(inputs, kept)), sems)
    slots = doms * tall
    lane = iota(places_ref.shape, 1)
    row = remainder(lane, tall)

    def list_entries(dom, places):
        for entry in range(cap):
            places = jnp.where(lane == dom * tall + entry, send_ref[entry, dom], places)
        return places

    copies[0].wait()
    copies[1].wait()
    places = jnp.full(lane.shape, -1, jnp.int32)
    if doms <= 16:
        for dom in range(doms):
            places = list_entries(dom, places)
    else:
        places = lax.fori_loop(0, doms, list_entries, places)
    for entry in range(hub_own):
        for first, inside in ((cap, lane < slots), (cap + hub_own, lane >= slots)):
            places = jnp.where((row == first + entry) & inside, hub_ref[entry], places)
    places_ref[...] = places
    column = jnp.broadcast_to(places, (LANES, lane.shape[1])).T[: slots + 2 * tall, :]
    node = iota(column.shape, 1)
    chosen = [
        jnp.where(node + first == column, F32(1.0), F32(0.0)).astype(BF16)
        for first in range(0, feats_ref.shape[0], LANES)
    ]
    copies[2].wait()
    picked = matmul(jnp.concatenate(chosen, axis=1), feats_ref[...]).astype(BF16)
    rows_ref[...] = picked[:slots, :]
    hubs_ref[...] = picked[slots:, :]
    for copy in copies[3:]:
        copy.wait()


def message_kernel(sizes, rows_ref, hubs_ref, after_ref, message_ref):
    doms, reps, cap, hub_own, tall = sizes
    del after_ref
    rows = rows_ref[...].astype(F32)
    hubs = hubs_ref[...].astype(F32)[:tall, :]
    place = iota(hubs.shape, 0)
    pair = lax.axis_index("pair")
    pairs = reps // SIDES
    for dom in range(doms):
        block = rows[dom * tall : (dom + 1) * tall, :]
        blocks = [
            jnp.where((place >= cap) | (pair == other), block, F32(0.0)) + hubs
            for other in range(pairs)
        ]
        first = dom * pairs * tall
        message_ref[first : first + pairs * tall, :] = jnp.concatenate(blocks, axis=0).astype(BF16)


def count_edges(slot_ref, own_count_ref, far_count_ref, hot_ref, nodes):
    fanout, rows = slot_ref.shape[0], own_count_ref.shape[0]
    highs = (rows + far_count_ref.shape[0]) // LANES
    low, high = [], []
    for k in range(fanout):
        slot = jnp.broadcast_to(slot_ref[k : k + 1, nodes], (STRIP, TILE))
        low.append(remainder(slot, LANES).astype(jnp.int16))
        high.append(div_floor(slot, LANES).astype(jnp.int16))
    for block in range(highs):
        for k in range(fanout):
            hot_ref[block * fanout + k] = jnp.where(high[k] == block, BF16(1.0), BF16(0.0))
    for strip in range(0, LANES, STRIP):
        numbers = (iota((STRIP, TILE), 0) + strip).astype(jnp.int16)
        hot = [jnp.where(numbers == low[k], BF16(1.0), BF16(0.0)) for k in range(fanout)]
        for block in range(highs):
            count = hot[0] * hot_ref[block * fanout]
            for k in range(1, fanout):
                count = count + hot[k] * hot_ref[block * fanout + k]
            first = block * LANES + strip
            if first < rows:
                own_count_ref[first : first + STRIP, nodes] = count
            else:
                far_count_ref[first - rows : first - rows + STRIP, nodes] = count


def own_kernel(sizes, feats_ref, w_self_ref, bias_ref, degree_ref, edge_ref, *refs):
    doms, reps, cap, hub_own, tall = sizes
    inputs, refs = refs[:2], refs[2:]
    kept, (share_ref, turned_ref, own_count_ref, far_count_ref, total_ref, preact_ref) = (
        refs[:2],
        refs[2:8],
    )
    slot_ref, hot_ref, sems = refs[8:]
    copies = fetch(zip(inputs, kept), sems)
    rows = feats_ref.shape[0]
    fanout = edge_ref.shape[0]
    hubs = doms * reps * hub_own

    source = edge_ref[...]
    hub = source - rows
    halo = hub - hubs
    chip = SIDES * hub_own
    entry = remainder(hub, chip) ^ (lax.axis_index("side") * hub_own)
    hub_slot = rows + cap + div_floor(hub, chip) * tall + entry
    peer = div_floor(halo, cap) * (reps // SIDES) + lax.axis_index("pair")
    halo_slot = rows + peer * tall + remainder(halo, cap)
    slot = jnp.where(source < rows, source, jnp.where(hub < hubs, hub_slot, halo_slot))
    valid = jnp.minimum(degree_ref[...], fanout)
    slot_ref[...] = jnp.where(iota((fanout, rows), 0) < valid, slot, -1)
    share_ref[...] = 1.0 / valid.astype(F32)
    turned_ref[...] = feats_ref[...].T

    def own_sums(nodes):
        total_ref[:, nodes] = matmul(turned_ref[...], own_count_ref[:, nodes])
        preact_ref[nodes, :] = matmul(feats_ref[nodes, :], w_self_ref[...]) + bias_ref[...]

    if rows + far_count_ref.shape[0] > 2048:

        @pl.loop(0, rows, step=TILE)
        def node_tile(first):
            nodes = pl.ds(pl.multiple_of(first, TILE), TILE)
            count_edges(slot_ref, own_count_ref, far_count_ref, hot_ref.at[0], nodes)
            own_sums(nodes)

    else:
        counted = None
        for number in range(rows // TILE):
            nodes = slice(number * TILE, (number + 1) * TILE)
            count_edges(slot_ref, own_count_ref, far_count_ref, hot_ref.at[number % 2], nodes)
            if counted is not None:
                own_sums(counted)
            counted = nodes
        own_sums(counted)
    for copy in copies:
        copy.wait()


def joint_kernel(
    sizes,
    remote_ref,
    turned_ref,
    total_ref,
    self_ref,
    count_ref,
    share_ref,
    w_neigh_ref,
    cot_ref,
    outputs_hbm,
    w_own_ref,
    rest_ref,
    message_ref,
    low_ref,
    edge_grad_ref,
    bias_ref,
    outputs_ref,
    mean_ref,
    preact_ref,
    w_grad_ref,
    sems,
):
    doms, reps, cap, hub_own, tall = sizes
    rows, width = outputs_ref.shape
    tiles = [slice(first, first + TILE) for first in range(0, rows, TILE)]
    table = remote_ref[...].T

    def before_head(nodes):
        mean = total_ref[:, nodes] + matmul(table, count_ref[:, nodes])
        mean = (mean * share_ref[:, nodes]).astype(BF16)
        mean_ref[:, nodes] = mean
        preact_ref[nodes, :] = self_ref[nodes, :] + matmul(mean, w_neigh_ref[...], 0, 0)

    bias_sum = jnp.zeros((8, width), F32)
    copies = []
    before_head(tiles[0])
    for number, nodes in enumerate(tiles):
        if number + 1 < len(tiles):
            before_head(tiles[number + 1])
        for start in range(nodes.start, nodes.stop, PIECE):
            piece = slice(start, start + PIECE)
            preact = preact_ref[piece, :]
            cot = cot_ref[piece, :].astype(F32)
            grown = jnp.exp(jnp.minimum(preact, 0.0))
            act = jnp.where(preact > 0.0, preact, grown - 1.0)
            square = jnp.sum(act * act, axis=1, keepdims=True)
            along = jnp.sum(act * cot, axis=1, keepdims=True)
            scale = lax.rsqrt(square * (1.0 / width) + NORM_EPS)
            outputs_ref[piece, :] = (act * scale).astype(BF16)
            pull = along * (scale * scale * scale) * (1.0 / width)
            grad_pre = (cot * scale - act * pull) * jnp.where(preact > 0.0, F32(1.0), grown)
            bias_sum = bias_sum + jnp.sum(grad_pre.reshape(PIECE // 8, 8, width), axis=0)
            low_ref[piece, :] = grad_pre.astype(BF16)
        copies += fetch(
            ((outputs_ref.at[nodes, :], outputs_hbm.at[nodes, :]),), sems.at[pl.ds(number, 1)]
        )
        share_column = jnp.broadcast_to(share_ref[:, nodes], (LANES, TILE)).T
        share_column = jnp.concatenate([share_column] * (width // LANES), axis=1)
        edge_grad = matmul(low_ref[nodes, :], w_neigh_ref[...], 1, 1) * share_column
        edge_grad_ref[nodes, :] = edge_grad.astype(BF16)

    w_grad_ref[0] = matmul(turned_ref[...], low_ref[...])
    w_grad_ref[1] = matmul(mean_ref[...], low_ref[...])
    remote = matmul(count_ref[...], edge_grad_ref[...])
    rest_ref[...] = remote
    bias_ref[...] = bias_sum
    bias_sum = jnp.broadcast_to(jnp.sum(bias_sum, axis=0, keepdims=True), (tall, width))
    bias_high = bias_sum.astype(BF16).astype(F32)
    place = iota((tall, width), 0)
    bias_rows = jnp.where(place == cap, bias_high, bias_sum - bias_high)
    bias_rows = jnp.where(place < cap, F32(0.0), bias_rows)
    message = remote.reshape(-1, tall, width)
    message = jnp.where((place < cap + hub_own)[None], bias_rows[None], message)
    message_ref[width:, :] = message.reshape(remote.shape).astype(BF16)
    mine = lax.axis_index("side")
    w_own_ref[...] = w_grad_ref[mine]
    message_ref[:width, :] = w_grad_ref[1 - mine].astype(BF16)
    for copy in copies:
        copy.wait()


def own_grad_kernel(low_ref, w_self_ref, own_count_ref, edge_grad_ref, feat_grad_ref):
    for first in range(0, low_ref.shape[0], TILE):
        nodes = slice(first, first + TILE)
        feat_grad_ref[nodes, :] = matmul(own_count_ref[nodes, :], edge_grad_ref[...]) + matmul(
            low_ref[nodes, :], w_self_ref[...], 1, 1
        )


def side_sum_kernel(own_ref, received_ref, after_ref, message_ref):
    del after_ref
    peers, slab, width = message_ref.shape
    w_grad = own_ref[...] + received_ref[:width, :].astype(F32)
    owners = width // slab
    w_grad = w_grad.reshape(owners, slab, width)
    if owners < peers:
        w_grad = jnp.concatenate([w_grad, jnp.zeros((peers - owners, slab, width), F32)], axis=0)
    message_ref[...] = w_grad.astype(BF16)


def peer_sum_kernel(sizes, slabs_ref, own_ref, received_ref, bias_ref, message_ref):
    doms, reps, cap, hub_own, tall = sizes
    peers, slab, width = slabs_ref.shape
    total = jnp.sum(slabs_ref[...].astype(F32), axis=0)
    received_ref = received_ref.at[width:, :]
    size = min(peers * tall, LANES)
    to, source = iota((size, size), 0), iota((size, size), 1)
    entry = remainder(to, tall) - cap
    moved = (source == to + hub_own) & (entry >= 0) & (entry < hub_own)
    moved = jnp.where(moved, F32(1.0), F32(0.0)).astype(BF16)
    rest = own_ref[...] + jnp.concatenate(
        [
            matmul(moved, received_ref[first : first + size, :])
            for first in range(0, peers * tall, size)
        ],
        axis=0,
    )
    place = iota((tall, width), 0)
    bias = received_ref[: 2 * tall, :].astype(F32)[:tall, :]
    bias = jnp.where((place >= cap) & (place < cap + BIAS_ROWS), bias, F32(0.0)) + bias_ref[...]
    bias = jnp.broadcast_to(jnp.sum(bias, axis=0, keepdims=True), (tall, width))
    bias_high = bias.astype(BF16).astype(F32)
    bias_rows = jnp.where(place == tall - 1, bias - bias_high, bias_high)
    rest = rest.reshape(peers, tall, width)
    rest = jnp.where((place < tall - BIAS_ROWS)[None], rest, bias_rows[None])
    total = jnp.broadcast_to(total[None], (peers, slab, width))
    message_ref[...] = jnp.concatenate([total, rest], axis=1).astype(BF16)


def feat_grad_kernel(sizes, slab, message_ref, places_ref, feat_grad_ref, out_ref):
    doms, reps, cap, hub_own, tall = sizes
    rows, width = out_ref.shape
    pairs = reps // SIDES
    returned = message_ref[...].astype(F32)[:, slab:, :].reshape(doms, pairs, tall, width)
    returned = [
        returned[:, pair].reshape(doms * tall, width).astype(BF16) for pair in range(pairs)
    ]
    chosen = one_hot(rows, places_ref[:, : doms * tall])
    for first in range(0, rows, TILE):
        nodes = slice(first, first + TILE)
        total = feat_grad_ref[nodes, :]
        for part in returned:
            total = total + matmul(chosen[nodes, :], part)
        out_ref[nodes, :] = total.astype(BF16)


def unit_kernel(slab, mine_ref, other_ref, unit_self_ref, unit_neigh_ref, unit_bias_ref, units_ref):
    side = lax.axis_index("side")
    size, width = unit_self_ref.shape
    for place, grad_ref in ((side, mine_ref), (1 - side, other_ref)):
        grad = grad_ref[: size // slab].astype(F32)[:, :slab, :].reshape(size, width)
        square = jnp.sum(jnp.sum(grad * grad, axis=0, keepdims=True), axis=1, keepdims=True)
        units_ref[place] = grad * lax.rsqrt(square * (1.0 / grad.size) + UNIT_EPS)
    unit_self_ref[...] = units_ref[0]
    unit_neigh_ref[...] = units_ref[1]
    bias = jnp.sum(mine_ref[...].astype(F32)[:, slab:, :], axis=0)[-BIAS_ROWS:, :]
    bias = jnp.sum(bias, axis=0, keepdims=True)
    unit_bias_ref[...] = bias * lax.rsqrt(jnp.mean(bias * bias, axis=1, keepdims=True) + UNIT_EPS)


def call(kernel, out_shape, in_specs=None, scratch=(), cost=(0, 0), out_specs=None):
    specs = {"in_specs": in_specs, "out_specs": out_specs}
    return pl.pallas_call(
        kernel,
        out_shape=out_shape,
        **{name: spec for name, spec in specs.items() if spec is not None},
        scratch_shapes=list(scratch),
        compiler_params=pltpu.CompilerParams(vmem_limit_bytes=VMEM_LIMIT),
        cost_estimate=pl.CostEstimate(flops=cost[0], bytes_accessed=cost[1], transcendentals=0),
    )


def in_hbm(*arrays):
    return [pltpu.with_memory_space_constraint(array, pltpu.HBM) for array in arrays]


def swap(array, axes):
    return lax.all_to_all(array, axes, split_axis=0, concat_axis=0, tiled=True)


def other_side(array):
    return lax.ppermute(array, "side", [(0, 1), (1, 0)])


def on_device(
    doms, reps, feats, w_self, w_neigh, bias, out_cot, degree, edge_src, hub_rows, send_rows
):
    rows, width = feats.shape
    fanout = edge_src.shape[1]
    cap, hub_own = send_rows.shape[1], hub_rows.shape[0]
    peers = doms * reps // SIDES
    tall = cap + SIDES * hub_own
    if tall % 8 or tall < cap + hub_own + BIAS_ROWS or hub_own & (hub_own - 1):
        raise ValueError("message height")
    slots = peers * tall
    slab = max(8, width // peers)
    sizes = (doms, reps, cap, hub_own, tall)
    shape = jax.ShapeDtypeStruct
    hbm = pl.BlockSpec(memory_space=pltpu.HBM)
    vmem = pl.BlockSpec(memory_space=pltpu.VMEM)

    picked, hubs, places, *kept = call(
        functools.partial(pick_kernel, sizes),
        (
            shape((doms * tall, width), BF16),
            shape((2 * tall, width), BF16),
            shape((1, -(-(doms + 2) * tall // LANES) * LANES), jnp.int32),
            shape((rows, width), BF16),
            shape((width, width), BF16),
            shape((1, width), F32),
            shape((1, rows), jnp.int32),
            shape((fanout, rows), jnp.int32),
        ),
        [hbm] * 7,
        (
            pltpu.SMEM((hub_own,), jnp.int32),
            pltpu.SMEM((cap, doms), jnp.int32),
            pltpu.SemaphoreType.DMA((7,)),
        ),
        cost=(2 * rows * slots * width, 2 * rows * width),
    )(
        *in_hbm(
            hub_rows,
            send_rows.T,
            feats,
            w_self,
            bias.reshape(1, width),
            degree.reshape(1, rows),
            edge_src.T,
        )
    )
    hubs = other_side(hubs)
    w_neigh_kept, cot_kept, share, turned, own_count, far_count, own_total, self_part = call(
        functools.partial(own_kernel, sizes),
        (
            shape((width, width), BF16),
            shape((rows, width), BF16),
            shape((1, rows), F32),
            shape((width, rows), BF16),
            shape((rows, rows), BF16),
            shape((slots, rows), BF16),
            shape((width, rows), F32),
            shape((rows, width), F32),
        ),
        [vmem] * 5 + [hbm] * 2,
        (
            pltpu.VMEM((fanout, rows), jnp.int32),
            pltpu.VMEM((2, (rows + slots) // LANES * fanout, STRIP, TILE), BF16),
            pltpu.SemaphoreType.DMA((2,)),
        ),
        cost=(8 * rows * (rows + slots) * width, 12 * rows * width + 2 * rows * rows),
    )(*kept, *in_hbm(w_neigh, out_cot))

    message = call(
        functools.partial(message_kernel, sizes),
        shape((slots, width), BF16),
        [vmem, vmem, pl.BlockSpec(memory_space=pl.ANY)],
    )(picked, hubs, share)
    remote = swap(message, PEERS)

    outputs, w_own, rest, message, low, edge_grad, bias_sum = call(
        functools.partial(joint_kernel, sizes),
        (
            pltpu.HBM((rows, width), BF16),
            shape((width, width), F32),
            shape((slots, width), F32),
            shape((width + slots, width), BF16),
            shape((rows, width), BF16),
            shape((rows, width), BF16),
            shape((8, width), F32),
        ),
        out_specs=(hbm,) + (vmem,) * 6,
        scratch=(
            pltpu.VMEM((rows, width), BF16),
            pltpu.VMEM((width, rows), BF16),
            pltpu.VMEM((rows, width), F32),
            pltpu.VMEM((2, width, width), F32),
            pltpu.SemaphoreType.DMA((rows // TILE,)),
        ),
        cost=(4 * rows * slots * width + 8 * rows * width * width, 16 * rows * width),
    )(remote, turned, own_total, self_part, far_count, share, w_neigh_kept, cot_kept)

    received = other_side(message)
    feat_grad = call(
        own_grad_kernel,
        shape((rows, width), F32),
        cost=(2 * rows * rows * width + 2 * rows * width * width, 8 * rows * width),
    )(low, kept[1], own_count, edge_grad)
    message = call(
        side_sum_kernel,
        shape((peers, slab, width), BF16),
        [vmem, vmem, pl.BlockSpec(memory_space=pl.ANY)],
    )(w_own, received, feat_grad)
    slabs = swap(message, PEERS)
    message = call(
        functools.partial(peer_sum_kernel, sizes), shape((peers, slab + tall, width), BF16)
    )(slabs, rest, received, bias_sum)
    message = swap(message, PEERS)
    grad_feats = call(
        functools.partial(feat_grad_kernel, sizes, slab),
        shape((rows, width), BF16),
        cost=(4 * rows * slots * width, 6 * rows * width),
    )(message, places, feat_grad)
    unit_self, unit_neigh, unit_bias = call(
        functools.partial(unit_kernel, slab),
        (shape((width, width), F32), shape((width, width), F32), shape((1, width), F32)),
        scratch=(pltpu.VMEM((2, width, width), F32),),
    )(message, other_side(message))
    return outputs, grad_feats, unit_self, unit_neigh, unit_bias.reshape(width)


def solution(mesh):
    doms, reps = mesh.shape["dom"], mesh.shape["rep"]
    split = jax.sharding.Mesh(mesh.devices.reshape(doms, reps // SIDES, SIDES), SPLIT_AXES)
    rows, whole = P(SPLIT_AXES, None), P()
    return jax.shard_map(
        functools.partial(on_device, doms, reps),
        mesh=split,
        in_specs=(rows, whole, whole, whole, rows, P(SPLIT_AXES), rows, P(SPLIT_AXES), rows),
        out_specs=(rows, rows, whole, whole, whole),
        check_vma=False,
    )
```

```python
import functools

import jax
import jax.numpy as jnp
from jax import lax
from jax.experimental import pallas as pl
from jax.experimental.pallas import tpu as pltpu
from jax.sharding import PartitionSpec as P

NORM_EPS = 1e-05
UNIT_EPS = 1e-06
SPLIT_AXES = ("dom", "pair", "side")
PEERS = ("dom", "pair")
SIDES = 2
VMEM_LIMIT = 32 * 1024 * 1024
F32 = jnp.float32
BF16 = jnp.bfloat16
TILE = 256
STRIP = 16
PIECE = 32
LANES = 128
BIAS_ROWS = 2


def div_floor(value, size):
    if size & (size - 1) == 0:
        return lax.shift_right_arithmetic(value, jnp.int32(size.bit_length() - 1))
    return value // size


def remainder(value, size):
    if size & (size - 1) == 0:
        return value & jnp.int32(size - 1)
    return value - (value // size) * size


def matmul(lhs, rhs, lhs_dim=1, rhs_dim=0):
    return lax.dot_general(
        lhs, rhs, (((lhs_dim,), (rhs_dim,)), ((), ())), preferred_element_type=F32
    )


def iota(shape, dim):
    return lax.broadcasted_iota(jnp.int32, shape, dim)


def one_hot(rows, places):
    return jnp.where(iota((rows, places.shape[1]), 0) == places, F32(1.0), F32(0.0)).astype(BF16)


def fetch(pairs, sems):
    copies = [
        pltpu.make_async_copy(source, target, sems.at[number])
        for number, (source, target) in enumerate(pairs)
    ]
    for copy in copies:
        copy.start()
    return copies


def pick_kernel(sizes, hub_hbm, send_hbm, *refs):
    doms, reps, cap, hub_own, tall = sizes
    inputs, (rows_ref, hubs_ref, places_ref), kept, (hub_ref, send_ref, sems) = (
        refs[:5],
        refs[5:8],
        refs[8:13],
        refs[13:],
    )
    feats_ref = kept[0]
    copies = fetch(((hub_hbm, hub_ref), (send_hbm, send_ref), *zip(inputs, kept)), sems)
    slots = doms * tall
    lane = iota(places_ref.shape, 1)
    row = remainder(lane, tall)

    def list_entries(dom, places):
        for entry in range(cap):
            places = jnp.where(lane == dom * tall + entry, send_ref[entry, dom], places)
        return places

    copies[0].wait()
    copies[1].wait()
    places = jnp.full(lane.shape, -1, jnp.int32)
    if doms <= 16:
        for dom in range(doms):
            places = list_entries(dom, places)
    else:
        places = lax.fori_loop(0, doms, list_entries, places)
    for entry in range(hub_own):
        for first, inside in ((cap, lane < slots), (cap + hub_own, lane >= slots)):
            places = jnp.where((row == first + entry) & inside, hub_ref[entry], places)
    places_ref[...] = places
    column = jnp.broadcast_to(places, (LANES, lane.shape[1])).T[: slots + 2 * tall, :]
    node = iota(column.shape, 1)
    chosen = [
        jnp.where(node + first == column, F32(1.0), F32(0.0)).astype(BF16)
        for first in range(0, feats_ref.shape[0], LANES)
    ]
    copies[2].wait()
    picked = matmul(jnp.concatenate(chosen, axis=1), feats_ref[...]).astype(BF16)
    rows_ref[...] = picked[:slots, :]
    hubs_ref[...] = picked[slots:, :]
    for copy in copies[3:]:
        copy.wait()


def message_kernel(sizes, rows_ref, hubs_ref, after_ref, message_ref):
    doms, reps, cap, hub_own, tall = sizes
    del after_ref
    rows = rows_ref[...].astype(F32)
    hubs = hubs_ref[...].astype(F32)[:tall, :]
    place = iota(hubs.shape, 0)
    pair = lax.axis_index("pair")
    pairs = reps // SIDES
    for dom in range(doms):
        block = rows[dom * tall : (dom + 1) * tall, :]
        blocks = [
            jnp.where((place >= cap) | (pair == other), block, F32(0.0)) + hubs
            for other in range(pairs)
        ]
        first = dom * pairs * tall
        message_ref[first : first + pairs * tall, :] = jnp.concatenate(blocks, axis=0).astype(BF16)


def count_edges(slot_ref, own_count_ref, far_count_ref, hot_ref, nodes):
    fanout, rows = slot_ref.shape[0], own_count_ref.shape[0]
    highs = (rows + far_count_ref.shape[0]) // LANES
    low, high = [], []
    for k in range(fanout):
        slot = jnp.broadcast_to(slot_ref[k : k + 1, nodes], (STRIP, TILE))
        low.append(remainder(slot, LANES).astype(jnp.int16))
        high.append(div_floor(slot, LANES).astype(jnp.int16))
    for block in range(highs):
        for k in range(fanout):
            hot_ref[block * fanout + k] = jnp.where(high[k] == block, BF16(1.0), BF16(0.0))
    for strip in range(0, LANES, STRIP):
        numbers = (iota((STRIP, TILE), 0) + strip).astype(jnp.int16)
        hot = [jnp.where(numbers == low[k], BF16(1.0), BF16(0.0)) for k in range(fanout)]
        for block in range(highs):
            count = hot[0] * hot_ref[block * fanout]
            for k in range(1, fanout):
                count = count + hot[k] * hot_ref[block * fanout + k]
            first = block * LANES + strip
            if first < rows:
                own_count_ref[first : first + STRIP, nodes] = count
            else:
                far_count_ref[first - rows : first - rows + STRIP, nodes] = count


def own_kernel(sizes, feats_ref, w_self_ref, bias_ref, degree_ref, edge_ref, *refs):
    doms, reps, cap, hub_own, tall = sizes
    inputs, refs = refs[:2], refs[2:]
    kept, (share_ref, turned_ref, own_count_ref, far_count_ref, total_ref, preact_ref) = (
        refs[:2],
        refs[2:8],
    )
    slot_ref, hot_ref, sems = refs[8:]
    copies = fetch(zip(inputs, kept), sems)
    rows = feats_ref.shape[0]
    fanout = edge_ref.shape[0]
    hubs = doms * reps * hub_own

    source = edge_ref[...]
    hub = source - rows
    halo = hub - hubs
    chip = SIDES * hub_own
    entry = remainder(hub, chip) ^ (lax.axis_index("side") * hub_own)
    hub_slot = rows + cap + div_floor(hub, chip) * tall + entry
    peer = div_floor(halo, cap) * (reps // SIDES) + lax.axis_index("pair")
    halo_slot = rows + peer * tall + remainder(halo, cap)
    slot = jnp.where(source < rows, source, jnp.where(hub < hubs, hub_slot, halo_slot))
    valid = jnp.minimum(degree_ref[...], fanout)
    slot_ref[...] = jnp.where(iota((fanout, rows), 0) < valid, slot, -1)
    share_ref[...] = 1.0 / valid.astype(F32)
    turned_ref[...] = feats_ref[...].T

    def own_sums(nodes):
        total_ref[:, nodes] = matmul(turned_ref[...], own_count_ref[:, nodes])

    for first in range(0, rows, TILE):
        nodes = slice(first, first + TILE)
        preact_ref[nodes, :] = matmul(feats_ref[nodes, :], w_self_ref[...]) + bias_ref[...]

    if rows + far_count_ref.shape[0] > 2048:

        @pl.loop(0, rows, step=TILE)
        def node_tile(first):
            nodes = pl.ds(pl.multiple_of(first, TILE), TILE)
            count_edges(slot_ref, own_count_ref, far_count_ref, hot_ref.at[0], nodes)
            own_sums(nodes)

    else:
        counted = None
        for number in range(rows // TILE):
            nodes = slice(number * TILE, (number + 1) * TILE)
            count_edges(slot_ref, own_count_ref, far_count_ref, hot_ref.at[number % 2], nodes)
            if counted is not None:
                own_sums(counted)
            counted = nodes
        own_sums(counted)
    for copy in copies:
        copy.wait()


def joint_kernel(
    sizes,
    remote_ref,
    turned_ref,
    total_ref,
    self_ref,
    count_ref,
    share_ref,
    w_neigh_ref,
    cot_ref,
    outputs_hbm,
    w_own_ref,
    rest_ref,
    message_ref,
    low_ref,
    edge_grad_ref,
    bias_ref,
    outputs_ref,
    mean_ref,
    preact_ref,
    w_grad_ref,
    sems,
):
    doms, reps, cap, hub_own, tall = sizes
    rows, width = outputs_ref.shape
    tiles = [slice(first, first + TILE) for first in range(0, rows, TILE)]
    table = remote_ref[...].T

    def before_head(nodes):
        mean = total_ref[:, nodes] + matmul(table, count_ref[:, nodes])
        mean = (mean * share_ref[:, nodes]).astype(BF16)
        mean_ref[:, nodes] = mean
        preact_ref[nodes, :] = self_ref[nodes, :] + matmul(mean, w_neigh_ref[...], 0, 0)

    def node_sums(nodes):
        low = low_ref[nodes, :]
        return (
            matmul(turned_ref[:, nodes], low),
            matmul(mean_ref[:, nodes], low),
            matmul(count_ref[:, nodes], edge_grad_ref[nodes, :]),
        )

    bias_sum = jnp.zeros((8, width), F32)
    copies = []
    before_head(tiles[0])
    for number, nodes in enumerate(tiles):
        if number + 1 < len(tiles):
            before_head(tiles[number + 1])
        elif number:
            w_grad_ref[0], w_grad_ref[1], rest_ref[...] = node_sums(slice(0, nodes.start))
        for start in range(nodes.start, nodes.stop, PIECE):
            piece = slice(start, start + PIECE)
            preact = preact_ref[piece, :]
            cot = cot_ref[piece, :].astype(F32)
            grown = jnp.exp(jnp.minimum(preact, 0.0))
            act = jnp.where(preact > 0.0, preact, grown - 1.0)
            square = jnp.sum(act * act, axis=1, keepdims=True)
            along = jnp.sum(act * cot, axis=1, keepdims=True)
            scale = lax.rsqrt(square * (1.0 / width) + NORM_EPS)
            outputs_ref[piece, :] = (act * scale).astype(BF16)
            pull = along * (scale * scale * scale) * (1.0 / width)
            grad_pre = (cot * scale - act * pull) * jnp.where(preact > 0.0, F32(1.0), grown)
            bias_sum = bias_sum + jnp.sum(grad_pre.reshape(PIECE // 8, 8, width), axis=0)
            low_ref[piece, :] = grad_pre.astype(BF16)
        copies += fetch(
            ((outputs_ref.at[nodes, :], outputs_hbm.at[nodes, :]),), sems.at[pl.ds(number, 1)]
        )
        share_column = jnp.broadcast_to(share_ref[:, nodes], (LANES, TILE)).T
        share_column = jnp.concatenate([share_column] * (width // LANES), axis=1)
        edge_grad = matmul(low_ref[nodes, :], w_neigh_ref[...], 1, 1) * share_column
        edge_grad_ref[nodes, :] = edge_grad.astype(BF16)

    w_self_sum, w_neigh_sum, remote = node_sums(tiles[-1])
    if len(tiles) > 1:
        w_self_sum = w_self_sum + w_grad_ref[0]
        w_neigh_sum = w_neigh_sum + w_grad_ref[1]
        remote = remote + rest_ref[...]
    w_grad_ref[0] = w_self_sum
    w_grad_ref[1] = w_neigh_sum
    rest_ref[...] = remote
    bias_ref[...] = bias_sum
    bias_sum = jnp.broadcast_to(jnp.sum(bias_sum, axis=0, keepdims=True), (tall, width))
    bias_high = bias_sum.astype(BF16).astype(F32)
    place = iota((tall, width), 0)
    bias_rows = jnp.where(place == cap, bias_high, bias_sum - bias_high)
    bias_rows = jnp.where(place < cap, F32(0.0), bias_rows)
    message = remote.reshape(-1, tall, width)
    message = jnp.where((place < cap + hub_own)[None], bias_rows[None], message)
    message_ref[width:, :] = message.reshape(remote.shape).astype(BF16)
    mine = lax.axis_index("side")
    w_own_ref[...] = w_grad_ref[mine]
    message_ref[:width, :] = w_grad_ref[1 - mine].astype(BF16)
    for copy in copies:
        copy.wait()


def own_grad_kernel(low_ref, w_self_ref, own_count_ref, edge_grad_ref, feat_grad_ref):
    for first in range(0, low_ref.shape[0], TILE):
        nodes = slice(first, first + TILE)
        feat_grad_ref[nodes, :] = matmul(own_count_ref[nodes, :], edge_grad_ref[...]) + matmul(
            low_ref[nodes, :], w_self_ref[...], 1, 1
        )


def side_sum_kernel(own_ref, received_ref, after_ref, message_ref):
    del after_ref
    peers, slab, width = message_ref.shape
    w_grad = own_ref[...] + received_ref[:width, :].astype(F32)
    owners = width // slab
    w_grad = w_grad.reshape(owners, slab, width)
    if owners < peers:
        w_grad = jnp.concatenate([w_grad, jnp.zeros((peers - owners, slab, width), F32)], axis=0)
    message_ref[...] = w_grad.astype(BF16)


def peer_sum_kernel(sizes, slabs_ref, own_ref, received_ref, bias_ref, message_ref):
    doms, reps, cap, hub_own, tall = sizes
    peers, slab, width = slabs_ref.shape
    total = jnp.sum(slabs_ref[...].astype(F32), axis=0)
    received_ref = received_ref.at[width:, :]
    size = min(peers * tall, LANES)
    to, source = iota((size, size), 0), iota((size, size), 1)
    entry = remainder(to, tall) - cap
    moved = (source == to + hub_own) & (entry >= 0) & (entry < hub_own)
    moved = jnp.where(moved, F32(1.0), F32(0.0)).astype(BF16)
    rest = own_ref[...] + jnp.concatenate(
        [
            matmul(moved, received_ref[first : first + size, :])
            for first in range(0, peers * tall, size)
        ],
        axis=0,
    )
    place = iota((tall, width), 0)
    bias = received_ref[: 2 * tall, :].astype(F32)[:tall, :]
    bias = jnp.where((place >= cap) & (place < cap + BIAS_ROWS), bias, F32(0.0)) + bias_ref[...]
    bias = jnp.broadcast_to(jnp.sum(bias, axis=0, keepdims=True), (tall, width))
    bias_high = bias.astype(BF16).astype(F32)
    bias_rows = jnp.where(place == tall - 1, bias - bias_high, bias_high)
    rest = rest.reshape(peers, tall, width)
    rest = jnp.where((place < tall - BIAS_ROWS)[None], rest, bias_rows[None])
    total = jnp.broadcast_to(total[None], (peers, slab, width))
    message_ref[...] = jnp.concatenate([total, rest], axis=1).astype(BF16)


def feat_grad_kernel(sizes, slab, message_ref, places_ref, feat_grad_ref, out_ref):
    doms, reps, cap, hub_own, tall = sizes
    rows, width = out_ref.shape
    pairs = reps // SIDES
    returned = message_ref[...].astype(F32)[:, slab:, :].reshape(doms, pairs, tall, width)
    returned = [
        returned[:, pair].reshape(doms * tall, width).astype(BF16) for pair in range(pairs)
    ]
    chosen = one_hot(rows, places_ref[:, : doms * tall])
    for first in range(0, rows, TILE):
        nodes = slice(first, first + TILE)
        total = feat_grad_ref[nodes, :]
        for part in returned:
            total = total + matmul(chosen[nodes, :], part)
        out_ref[nodes, :] = total.astype(BF16)


def unit_kernel(slab, mine_ref, other_ref, self_hbm, neigh_hbm, unit_bias_ref, units_ref, sems):
    side = lax.axis_index("side")
    _, size, width = units_ref.shape
    copies = [
        pltpu.make_async_copy(units_ref.at[place], target, sems.at[place])
        for place, target in enumerate((self_hbm, neigh_hbm))
    ]
    for place, grad_ref in ((side, mine_ref), (1 - side, other_ref)):
        grad = grad_ref[: size // slab].astype(F32)[:, :slab, :].reshape(size, width)
        square = jnp.sum(jnp.sum(grad * grad, axis=0, keepdims=True), axis=1, keepdims=True)
        units_ref[place] = grad * lax.rsqrt(square * (1.0 / grad.size) + UNIT_EPS)
        for number, copy in enumerate(copies):
            pl.when(place == number)(copy.start)
    bias = jnp.sum(mine_ref[...].astype(F32)[:, slab:, :], axis=0)[-BIAS_ROWS:, :]
    bias = jnp.sum(bias, axis=0, keepdims=True)
    unit_bias_ref[...] = bias * lax.rsqrt(jnp.mean(bias * bias, axis=1, keepdims=True) + UNIT_EPS)
    for copy in copies:
        copy.wait()


def call(kernel, out_shape, in_specs=None, scratch=(), cost=(0, 0), out_specs=None):
    specs = {"in_specs": in_specs, "out_specs": out_specs}
    return pl.pallas_call(
        kernel,
        out_shape=out_shape,
        **{name: spec for name, spec in specs.items() if spec is not None},
        scratch_shapes=list(scratch),
        compiler_params=pltpu.CompilerParams(vmem_limit_bytes=VMEM_LIMIT),
        cost_estimate=pl.CostEstimate(flops=cost[0], bytes_accessed=cost[1], transcendentals=0),
    )


def in_hbm(*arrays):
    return [pltpu.with_memory_space_constraint(array, pltpu.HBM) for array in arrays]


def swap(array, axes):
    return lax.all_to_all(array, axes, split_axis=0, concat_axis=0, tiled=True)


def other_side(array):
    return lax.ppermute(array, "side", [(0, 1), (1, 0)])


def on_device(
    doms, reps, feats, w_self, w_neigh, bias, out_cot, degree, edge_src, hub_rows, send_rows
):
    rows, width = feats.shape
    fanout = edge_src.shape[1]
    cap, hub_own = send_rows.shape[1], hub_rows.shape[0]
    peers = doms * reps // SIDES
    tall = cap + SIDES * hub_own
    if tall % 8 or tall < cap + hub_own + BIAS_ROWS or hub_own & (hub_own - 1):
        raise ValueError("message height")
    slots = peers * tall
    slab = max(8, width // peers)
    sizes = (doms, reps, cap, hub_own, tall)
    shape = jax.ShapeDtypeStruct
    hbm = pl.BlockSpec(memory_space=pltpu.HBM)
    vmem = pl.BlockSpec(memory_space=pltpu.VMEM)

    picked, hubs, places, *kept = call(
        functools.partial(pick_kernel, sizes),
        (
            shape((doms * tall, width), BF16),
            shape((2 * tall, width), BF16),
            shape((1, -(-(doms + 2) * tall // LANES) * LANES), jnp.int32),
            shape((rows, width), BF16),
            shape((width, width), BF16),
            shape((1, width), F32),
            shape((1, rows), jnp.int32),
            shape((fanout, rows), jnp.int32),
        ),
        [hbm] * 7,
        (
            pltpu.SMEM((hub_own,), jnp.int32),
            pltpu.SMEM((cap, doms), jnp.int32),
            pltpu.SemaphoreType.DMA((7,)),
        ),
        cost=(2 * rows * slots * width, 2 * rows * width),
    )(
        *in_hbm(
            hub_rows,
            send_rows.T,
            feats,
            w_self,
            bias.reshape(1, width),
            degree.reshape(1, rows),
            edge_src.T,
        )
    )
    hubs = other_side(hubs)
    w_neigh_kept, cot_kept, share, turned, own_count, far_count, own_total, self_part = call(
        functools.partial(own_kernel, sizes),
        (
            shape((width, width), BF16),
            shape((rows, width), BF16),
            shape((1, rows), F32),
            shape((width, rows), BF16),
            shape((rows, rows), BF16),
            shape((slots, rows), BF16),
            shape((width, rows), F32),
            shape((rows, width), F32),
        ),
        [vmem] * 5 + [hbm] * 2,
        (
            pltpu.VMEM((fanout, rows), jnp.int32),
            pltpu.VMEM((2, (rows + slots) // LANES * fanout, STRIP, TILE), BF16),
            pltpu.SemaphoreType.DMA((2,)),
        ),
        cost=(8 * rows * (rows + slots) * width, 12 * rows * width + 2 * rows * rows),
    )(*kept, *in_hbm(w_neigh, out_cot))

    message = call(
        functools.partial(message_kernel, sizes),
        shape((slots, width), BF16),
        [vmem, vmem, pl.BlockSpec(memory_space=pl.ANY)],
    )(picked, hubs, share)
    remote = swap(message, PEERS)

    outputs, w_own, rest, message, low, edge_grad, bias_sum = call(
        functools.partial(joint_kernel, sizes),
        (
            pltpu.HBM((rows, width), BF16),
            shape((width, width), F32),
            shape((slots, width), F32),
            shape((width + slots, width), BF16),
            shape((rows, width), BF16),
            shape((rows, width), BF16),
            shape((8, width), F32),
        ),
        out_specs=(hbm,) + (vmem,) * 6,
        scratch=(
            pltpu.VMEM((rows, width), BF16),
            pltpu.VMEM((width, rows), BF16),
            pltpu.VMEM((rows, width), F32),
            pltpu.VMEM((2, width, width), F32),
            pltpu.SemaphoreType.DMA((rows // TILE,)),
        ),
        cost=(4 * rows * slots * width + 8 * rows * width * width, 16 * rows * width),
    )(remote, turned, own_total, self_part, far_count, share, w_neigh_kept, cot_kept)

    received = other_side(message)
    feat_grad = call(
        own_grad_kernel,
        shape((rows, width), F32),
        cost=(2 * rows * rows * width + 2 * rows * width * width, 8 * rows * width),
    )(low, kept[1], own_count, edge_grad)
    message = call(
        side_sum_kernel,
        shape((peers, slab, width), BF16),
        [vmem, vmem, pl.BlockSpec(memory_space=pl.ANY)],
    )(w_own, received, feat_grad)
    slabs = swap(message, PEERS)
    message = call(
        functools.partial(peer_sum_kernel, sizes), shape((peers, slab + tall, width), BF16)
    )(slabs, rest, received, bias_sum)
    message = swap(message, PEERS)
    grad_feats = call(
        functools.partial(feat_grad_kernel, sizes, slab),
        shape((rows, width), BF16),
        cost=(4 * rows * slots * width, 6 * rows * width),
    )(message, places, feat_grad)
    unit_self, unit_neigh, unit_bias = call(
        functools.partial(unit_kernel, slab),
        (pltpu.HBM((width, width), F32), pltpu.HBM((width, width), F32), shape((1, width), F32)),
        out_specs=(hbm, hbm, vmem),
        scratch=(pltpu.VMEM((2, width, width), F32), pltpu.SemaphoreType.DMA((2,))),
    )(message, other_side(message))
    return outputs, grad_feats, unit_self, unit_neigh, unit_bias.reshape(width)


def solution(mesh):
    doms, reps = mesh.shape["dom"], mesh.shape["rep"]
    split = jax.sharding.Mesh(mesh.devices.reshape(doms, reps // SIDES, SIDES), SPLIT_AXES)
    rows, whole = P(SPLIT_AXES, None), P()
    return jax.shard_map(
        functools.partial(on_device, doms, reps),
        mesh=split,
        in_specs=(rows, whole, whole, whole, rows, P(SPLIT_AXES), rows, P(SPLIT_AXES), rows),
        out_specs=(rows, rows, whole, whole, whole),
        check_vma=False,
    )
```

```python
import functools

import jax
import jax.numpy as jnp
from jax import lax
from jax.experimental import pallas as pl
from jax.experimental.pallas import tpu as pltpu
from jax.sharding import PartitionSpec as P

NORM_EPS = 1e-05
UNIT_EPS = 1e-06
SPLIT_AXES = ("dom", "pair", "side")
PEERS = ("dom", "pair")
SIDES = 2
VMEM_LIMIT = 32 * 1024 * 1024
F32 = jnp.float32
BF16 = jnp.bfloat16
TILE = 256
STRIP = 16
PIECE = 32
LANES = 128
BIAS_ROWS = 2


def div_floor(value, size):
    if size & (size - 1) == 0:
        return lax.shift_right_arithmetic(value, jnp.int32(size.bit_length() - 1))
    return value // size


def remainder(value, size):
    if size & (size - 1) == 0:
        return value & jnp.int32(size - 1)
    return value - (value // size) * size


def matmul(lhs, rhs, lhs_dim=1, rhs_dim=0):
    return lax.dot_general(
        lhs, rhs, (((lhs_dim,), (rhs_dim,)), ((), ())), preferred_element_type=F32
    )


def iota(shape, dim):
    return lax.broadcasted_iota(jnp.int32, shape, dim)


def one_hot(rows, places):
    return jnp.where(iota((rows, places.shape[1]), 0) == places, F32(1.0), F32(0.0)).astype(BF16)


def fetch(pairs, sems):
    copies = [
        pltpu.make_async_copy(source, target, sems.at[number])
        for number, (source, target) in enumerate(pairs)
    ]
    for copy in copies:
        copy.start()
    return copies


def pick_kernel(sizes, hub_hbm, send_hbm, *refs):
    doms, reps, cap, hub_own, tall = sizes
    inputs, (rows_ref, hubs_ref, places_ref), refs = refs[:5], refs[5:8], refs[8:]
    kept, (slot_ref, share_ref, own_count_ref, far_count_ref), refs = refs[:3], refs[3:7], refs[7:]
    hub_ref, send_ref, degree_ref, edge_ref, hot_ref, sems = refs
    feats_ref = kept[0]
    targets = (hub_ref, send_ref, degree_ref, edge_ref, *kept)
    copies = fetch(zip((hub_hbm, send_hbm, *inputs), targets), sems)
    slots = doms * tall
    lane = iota(places_ref.shape, 1)
    row = remainder(lane, tall)

    def list_entries(dom, places):
        for entry in range(cap):
            places = jnp.where(lane == dom * tall + entry, send_ref[entry, dom], places)
        return places

    copies[0].wait()
    copies[1].wait()
    places = jnp.full(lane.shape, -1, jnp.int32)
    if doms <= 16:
        for dom in range(doms):
            places = list_entries(dom, places)
    else:
        places = lax.fori_loop(0, doms, list_entries, places)
    for entry in range(hub_own):
        for first, inside in ((cap, lane < slots), (cap + hub_own, lane >= slots)):
            places = jnp.where((row == first + entry) & inside, hub_ref[entry], places)
    places_ref[...] = places
    column = jnp.broadcast_to(places, (LANES, lane.shape[1])).T[: slots + 2 * tall, :]
    node = iota(column.shape, 1)
    chosen = [
        jnp.where(node + first == column, F32(1.0), F32(0.0)).astype(BF16)
        for first in range(0, feats_ref.shape[0], LANES)
    ]
    copies[2].wait()
    copies[3].wait()
    find_slots(sizes, degree_ref, edge_ref, slot_ref, share_ref)
    count_edges(slot_ref, own_count_ref, far_count_ref, hot_ref, slice(0, TILE))
    copies[4].wait()
    picked = matmul(jnp.concatenate(chosen, axis=1), feats_ref[...]).astype(BF16)
    rows_ref[...] = picked[:slots, :]
    hubs_ref[...] = picked[slots:, :]
    for copy in copies[5:]:
        copy.wait()


def message_kernel(sizes, rows_ref, hubs_ref, after_ref, message_ref):
    doms, reps, cap, hub_own, tall = sizes
    del after_ref
    rows = rows_ref[...].astype(F32)
    hubs = hubs_ref[...].astype(F32)[:tall, :]
    place = iota(hubs.shape, 0)
    pair = lax.axis_index("pair")
    pairs = reps // SIDES
    for dom in range(doms):
        block = rows[dom * tall : (dom + 1) * tall, :]
        blocks = [
            jnp.where((place >= cap) | (pair == other), block, F32(0.0)) + hubs
            for other in range(pairs)
        ]
        first = dom * pairs * tall
        message_ref[first : first + pairs * tall, :] = jnp.concatenate(blocks, axis=0).astype(BF16)


def count_edges(slot_ref, own_count_ref, far_count_ref, hot_ref, nodes):
    fanout, rows = slot_ref.shape[0], own_count_ref.shape[0]
    highs = (rows + far_count_ref.shape[0]) // LANES
    low, high = [], []
    for k in range(fanout):
        slot = jnp.broadcast_to(slot_ref[k : k + 1, nodes], (STRIP, TILE))
        low.append(remainder(slot, LANES).astype(jnp.int16))
        high.append(div_floor(slot, LANES).astype(jnp.int16))
    for block in range(highs):
        for k in range(fanout):
            hot_ref[block * fanout + k] = jnp.where(high[k] == block, BF16(1.0), BF16(0.0))
    for strip in range(0, LANES, STRIP):
        numbers = (iota((STRIP, TILE), 0) + strip).astype(jnp.int16)
        hot = [jnp.where(numbers == low[k], BF16(1.0), BF16(0.0)) for k in range(fanout)]

        def count(block):
            total = hot[0] * hot_ref[block * fanout]
            for k in range(1, fanout):
                total = total + hot[k] * hot_ref[block * fanout + k]
            return total

        for block in range(rows // LANES):
            first = block * LANES + strip
            own_count_ref[first : first + STRIP, :] = count(block)
        far = far_count_ref.shape[0] // LANES
        if far <= 4:
            for block in range(far):
                first = block * LANES + strip
                far_count_ref[first : first + STRIP, :] = count(rows // LANES + block)
        else:

            @pl.loop(0, far)
            def far_block(block):
                first = pl.multiple_of(block * LANES + strip, STRIP)
                far_count_ref[pl.ds(first, STRIP), :] = count(rows // LANES + block)


def find_slots(sizes, degree_ref, edge_ref, slot_ref, share_ref):
    doms, reps, cap, hub_own, tall = sizes
    fanout, rows = edge_ref.shape
    hubs = doms * reps * hub_own
    source = edge_ref[...]
    hub = source - rows
    halo = hub - hubs
    chip = SIDES * hub_own
    entry = remainder(hub, chip) ^ (lax.axis_index("side") * hub_own)
    hub_slot = rows + cap + div_floor(hub, chip) * tall + entry
    peer = div_floor(halo, cap) * (reps // SIDES) + lax.axis_index("pair")
    halo_slot = rows + peer * tall + remainder(halo, cap)
    slot = jnp.where(source < rows, source, jnp.where(hub < hubs, hub_slot, halo_slot))
    valid = jnp.minimum(degree_ref[...], fanout)
    slot_ref[...] = jnp.where(iota((fanout, rows), 0) < valid, slot, -1)
    share_ref[...] = 1.0 / valid.astype(F32)


def own_kernel(tiles, feats_ref, w_self_ref, bias_ref, slot_ref, *refs):
    first_count_ref, inputs, kept, refs = refs[0], refs[1:3], refs[3:5], refs[5:]
    turned_ref, total_ref, preact_ref = refs[:3]
    own_refs, far_refs, (hot_ref, sems) = (
        refs[3 : 2 + tiles],
        refs[2 + tiles : 1 + 2 * tiles],
        refs[1 + 2 * tiles :],
    )
    copies = fetch(zip(inputs, kept), sems)
    turned_ref[...] = feats_ref[...].T

    def own_sums(number, count_ref):
        nodes = slice(number * TILE, (number + 1) * TILE)
        total_ref[:, nodes] = matmul(turned_ref[...], count_ref[...])
        preact_ref[nodes, :] = matmul(feats_ref[nodes, :], w_self_ref[...]) + bias_ref[...]

    counted = first_count_ref
    for number in range(1, tiles):
        nodes = slice(number * TILE, (number + 1) * TILE)
        own_ref, far_ref = own_refs[number - 1], far_refs[number - 1]
        count_edges(slot_ref, own_ref, far_ref, hot_ref.at[number % 2], nodes)
        own_sums(number - 1, counted)
        counted = own_ref
    own_sums(tiles - 1, counted)
    for copy in copies:
        copy.wait()


def joint_kernel(sizes, remote_ref, turned_ref, total_ref, self_ref, *refs):
    doms, reps, cap, hub_own, tall = sizes
    rows, width = self_ref.shape
    tiles = [slice(first, first + TILE) for first in range(0, rows, TILE)]
    count_refs, refs = refs[: len(tiles)], refs[len(tiles) :]
    (
        share_ref,
        w_neigh_ref,
        cot_ref,
        outputs_hbm,
        w_own_ref,
        rest_ref,
        message_ref,
        low_ref,
        edge_grad_ref,
        bias_ref,
        outputs_ref,
        mean_ref,
        preact_ref,
        w_grad_ref,
        sems,
    ) = refs
    table = remote_ref[...].T

    def before_head(number):
        nodes = tiles[number]
        mean = total_ref[:, nodes] + matmul(table, count_refs[number][...])
        mean = (mean * share_ref[:, nodes]).astype(BF16)
        mean_ref[:, nodes] = mean
        preact_ref[nodes, :] = self_ref[nodes, :] + matmul(mean, w_neigh_ref[...], 0, 0)

    def node_sums(numbers):
        nodes = slice(tiles[numbers[0]].start, tiles[numbers[-1]].stop)
        low = low_ref[nodes, :]
        return (
            matmul(turned_ref[:, nodes], low),
            matmul(mean_ref[:, nodes], low),
            sum(matmul(count_refs[k][...], edge_grad_ref[tiles[k], :]) for k in numbers),
        )

    bias_sum = jnp.zeros((8, width), F32)
    copies = []
    before_head(0)
    for number, nodes in enumerate(tiles):
        if number + 1 < len(tiles):
            before_head(number + 1)
        elif number:
            w_grad_ref[0], w_grad_ref[1], rest_ref[...] = node_sums(range(number))
        for start in range(nodes.start, nodes.stop, PIECE):
            piece = slice(start, start + PIECE)
            preact = preact_ref[piece, :]
            cot = cot_ref[piece, :].astype(F32)
            grown = jnp.exp(jnp.minimum(preact, 0.0))
            act = jnp.where(preact > 0.0, preact, grown - 1.0)
            square = jnp.sum(act * act, axis=1, keepdims=True)
            along = jnp.sum(act * cot, axis=1, keepdims=True)
            scale = lax.rsqrt(square * (1.0 / width) + NORM_EPS)
            outputs_ref[piece, :] = (act * scale).astype(BF16)
            pull = along * (scale * scale * scale) * (1.0 / width)
            grad_pre = (cot * scale - act * pull) * jnp.where(preact > 0.0, F32(1.0), grown)
            bias_sum = bias_sum + jnp.sum(grad_pre.reshape(PIECE // 8, 8, width), axis=0)
            low_ref[piece, :] = grad_pre.astype(BF16)
        copies += fetch(
            ((outputs_ref.at[nodes, :], outputs_hbm.at[nodes, :]),), sems.at[pl.ds(number, 1)]
        )
        share_column = jnp.broadcast_to(share_ref[:, nodes], (LANES, TILE)).T
        share_column = jnp.concatenate([share_column] * (width // LANES), axis=1)
        edge_grad = matmul(low_ref[nodes, :], w_neigh_ref[...], 1, 1) * share_column
        edge_grad_ref[nodes, :] = edge_grad.astype(BF16)

    w_self_sum, w_neigh_sum, remote = node_sums([len(tiles) - 1])
    if len(tiles) > 1:
        w_self_sum = w_self_sum + w_grad_ref[0]
        w_neigh_sum = w_neigh_sum + w_grad_ref[1]
        remote = remote + rest_ref[...]
    w_grad_ref[0] = w_self_sum
    w_grad_ref[1] = w_neigh_sum
    rest_ref[...] = remote
    bias_ref[...] = bias_sum
    bias_sum = jnp.broadcast_to(jnp.sum(bias_sum, axis=0, keepdims=True), (tall, width))
    bias_high = bias_sum.astype(BF16).astype(F32)
    place = iota((tall, width), 0)
    bias_rows = jnp.where(place == cap, bias_high, bias_sum - bias_high)
    bias_rows = jnp.where(place < cap, F32(0.0), bias_rows)
    message = remote.reshape(-1, tall, width)
    message = jnp.where((place < cap + hub_own)[None], bias_rows[None], message)
    message_ref[width:, :] = message.reshape(remote.shape).astype(BF16)
    mine = lax.axis_index("side")
    w_own_ref[...] = w_grad_ref[mine]
    message_ref[:width, :] = w_grad_ref[1 - mine].astype(BF16)
    for copy in copies:
        copy.wait()


def own_grad_kernel(low_ref, w_self_ref, edge_grad_ref, *refs):
    *count_refs, feat_grad_ref = refs
    for first in range(0, low_ref.shape[0], TILE):
        nodes = slice(first, first + TILE)
        total = matmul(low_ref[nodes, :], w_self_ref[...], 1, 1)
        for number, count_ref in enumerate(count_refs):
            edges = edge_grad_ref[number * TILE : (number + 1) * TILE, :]
            total = total + matmul(count_ref[nodes, :], edges)
        feat_grad_ref[nodes, :] = total


def side_sum_kernel(own_ref, received_ref, after_ref, message_ref):
    del after_ref
    peers, slab, width = message_ref.shape
    w_grad = own_ref[...] + received_ref[:width, :].astype(F32)
    owners = width // slab
    w_grad = w_grad.reshape(owners, slab, width)
    if owners < peers:
        w_grad = jnp.concatenate([w_grad, jnp.zeros((peers - owners, slab, width), F32)], axis=0)
    message_ref[...] = w_grad.astype(BF16)


def peer_sum_kernel(sizes, slabs_ref, own_ref, received_ref, bias_ref, message_ref):
    doms, reps, cap, hub_own, tall = sizes
    peers, slab, width = slabs_ref.shape
    total = jnp.sum(slabs_ref[...].astype(F32), axis=0)
    received_ref = received_ref.at[width:, :]
    size = min(peers * tall, LANES)
    to, source = iota((size, size), 0), iota((size, size), 1)
    entry = remainder(to, tall) - cap
    moved = (source == to + hub_own) & (entry >= 0) & (entry < hub_own)
    moved = jnp.where(moved, F32(1.0), F32(0.0)).astype(BF16)
    rest = own_ref[...] + jnp.concatenate(
        [
            matmul(moved, received_ref[first : first + size, :])
            for first in range(0, peers * tall, size)
        ],
        axis=0,
    )
    place = iota((tall, width), 0)
    bias = received_ref[: 2 * tall, :].astype(F32)[:tall, :]
    bias = jnp.where((place >= cap) & (place < cap + BIAS_ROWS), bias, F32(0.0)) + bias_ref[...]
    bias = jnp.broadcast_to(jnp.sum(bias, axis=0, keepdims=True), (tall, width))
    bias_high = bias.astype(BF16).astype(F32)
    bias_rows = jnp.where(place == tall - 1, bias - bias_high, bias_high)
    rest = rest.reshape(peers, tall, width)
    rest = jnp.where((place < tall - BIAS_ROWS)[None], rest, bias_rows[None])
    total = jnp.broadcast_to(total[None], (peers, slab, width))
    message_ref[...] = jnp.concatenate([total, rest], axis=1).astype(BF16)


def feat_grad_kernel(sizes, slab, message_ref, places_ref, feat_grad_ref, out_ref):
    doms, reps, cap, hub_own, tall = sizes
    rows, width = out_ref.shape
    pairs = reps // SIDES
    returned = message_ref[...].astype(F32)[:, slab:, :].reshape(doms, pairs, tall, width)
    returned = [
        returned[:, pair].reshape(doms * tall, width).astype(BF16) for pair in range(pairs)
    ]
    chosen = one_hot(rows, places_ref[:, : doms * tall])
    for first in range(0, rows, TILE):
        nodes = slice(first, first + TILE)
        total = feat_grad_ref[nodes, :]
        for part in returned:
            total = total + matmul(chosen[nodes, :], part)
        out_ref[nodes, :] = total.astype(BF16)


def unit_kernel(slab, mine_ref, other_ref, self_hbm, neigh_hbm, bias_hbm, units_ref, bias_ref, sems):
    side = lax.axis_index("side")
    _, size, width = units_ref.shape
    bias = jnp.sum(mine_ref[...].astype(F32)[:, slab:, :], axis=0)[-BIAS_ROWS:, :]
    bias = jnp.sum(bias, axis=0, keepdims=True)
    bias_ref[...] = bias * lax.rsqrt(jnp.mean(bias * bias, axis=1, keepdims=True) + UNIT_EPS)
    copies = [
        pltpu.make_async_copy(source, target, sems.at[number])
        for number, (source, target) in enumerate(
            ((units_ref.at[0], self_hbm), (units_ref.at[1], neigh_hbm), (bias_ref, bias_hbm))
        )
    ]
    copies[2].start()
    for place, grad_ref in ((side, mine_ref), (1 - side, other_ref)):
        grad = grad_ref[: size // slab].astype(F32)[:, :slab, :].reshape(size, width)
        square = jnp.sum(jnp.sum(grad * grad, axis=0, keepdims=True), axis=1, keepdims=True)
        units_ref[place] = grad * lax.rsqrt(square * (1.0 / grad.size) + UNIT_EPS)
        for number, copy in enumerate(copies[:2]):
            pl.when(place == number)(copy.start)
    for copy in copies:
        copy.wait()


def call(kernel, out_shape, in_specs=None, scratch=(), cost=(0, 0), out_specs=None):
    specs = {"in_specs": in_specs, "out_specs": out_specs}
    return pl.pallas_call(
        kernel,
        out_shape=out_shape,
        **{name: spec for name, spec in specs.items() if spec is not None},
        scratch_shapes=list(scratch),
        compiler_params=pltpu.CompilerParams(vmem_limit_bytes=VMEM_LIMIT),
        cost_estimate=pl.CostEstimate(flops=cost[0], bytes_accessed=cost[1], transcendentals=0),
    )


def in_hbm(*arrays):
    return [pltpu.with_memory_space_constraint(array, pltpu.HBM) for array in arrays]


def swap(array, axes):
    return lax.all_to_all(array, axes, split_axis=0, concat_axis=0, tiled=True)


def other_side(array):
    return lax.ppermute(array, "side", [(0, 1), (1, 0)])


def on_device(
    doms, reps, feats, w_self, w_neigh, bias, out_cot, degree, edge_src, hub_rows, send_rows
):
    rows, width = feats.shape
    fanout = edge_src.shape[1]
    cap, hub_own = send_rows.shape[1], hub_rows.shape[0]
    peers = doms * reps // SIDES
    tall = cap + SIDES * hub_own
    if tall % 8 or tall < cap + hub_own + BIAS_ROWS or hub_own & (hub_own - 1):
        raise ValueError("message height")
    slots = peers * tall
    slab = max(8, width // peers)
    sizes = (doms, reps, cap, hub_own, tall)
    shape = jax.ShapeDtypeStruct
    hbm = pl.BlockSpec(memory_space=pltpu.HBM)
    vmem = pl.BlockSpec(memory_space=pltpu.VMEM)

    tiles = rows // TILE
    hot = pltpu.VMEM(((rows + slots) // LANES * fanout, STRIP, TILE), BF16)
    picked, hubs, places, feats_kept, w_self_kept, bias_kept, slot, share, *first_counts = call(
        functools.partial(pick_kernel, sizes),
        (
            shape((doms * tall, width), BF16),
            shape((2 * tall, width), BF16),
            shape((1, -(-(doms + 2) * tall // LANES) * LANES), jnp.int32),
            shape((rows, width), BF16),
            shape((width, width), BF16),
            shape((1, width), F32),
            shape((fanout, rows), jnp.int32),
            shape((1, rows), F32),
            shape((rows, TILE), BF16),
            shape((slots, TILE), BF16),
        ),
        [hbm] * 7,
        (
            pltpu.SMEM((hub_own,), jnp.int32),
            pltpu.SMEM((cap, doms), jnp.int32),
            pltpu.VMEM((1, rows), jnp.int32),
            pltpu.VMEM((fanout, rows), jnp.int32),
            hot,
            pltpu.SemaphoreType.DMA((7,)),
        ),
        cost=(2 * rows * slots * width, 2 * rows * width),
    )(
        *in_hbm(
            hub_rows,
            send_rows.T,
            degree.reshape(1, rows),
            edge_src.T,
            feats,
            w_self,
            bias.reshape(1, width),
        )
    )
    hubs = other_side(hubs)
    w_neigh_kept, cot_kept, turned, own_total, self_part, *counts = call(
        functools.partial(own_kernel, tiles),
        (
            shape((width, width), BF16),
            shape((rows, width), BF16),
            shape((width, rows), BF16),
            shape((width, rows), F32),
            shape((rows, width), F32),
            *((shape((rows, TILE), BF16),) * (tiles - 1)),
            *((shape((slots, TILE), BF16),) * (tiles - 1)),
        ),
        [vmem] * 5 + [hbm] * 2,
        (
            pltpu.VMEM((2, *hot.shape), BF16),
            pltpu.SemaphoreType.DMA((2,)),
        ),
        cost=(8 * rows * (rows + slots) * width, 12 * rows * width + 2 * rows * rows),
    )(feats_kept, w_self_kept, bias_kept, slot, first_counts[0], *in_hbm(w_neigh, out_cot))
    own_counts = [first_counts[0], *counts[: tiles - 1]]
    far_counts = [first_counts[1], *counts[tiles - 1 :]]
    message = call(
        functools.partial(message_kernel, sizes),
        shape((slots, width), BF16),
        [vmem, vmem, pl.BlockSpec(memory_space=pl.ANY)],
    )(picked, hubs, own_total)
    remote = swap(message, PEERS)

    outputs, w_own, rest, message, low, edge_grad, bias_sum = call(
        functools.partial(joint_kernel, sizes),
        (
            pltpu.HBM((rows, width), BF16),
            shape((width, width), F32),
            shape((slots, width), F32),
            shape((width + slots, width), BF16),
            shape((rows, width), BF16),
            shape((rows, width), BF16),
            shape((8, width), F32),
        ),
        out_specs=(hbm,) + (vmem,) * 6,
        scratch=(
            pltpu.VMEM((rows, width), BF16),
            pltpu.VMEM((width, rows), BF16),
            pltpu.VMEM((rows, width), F32),
            pltpu.VMEM((2, width, width), F32),
            pltpu.SemaphoreType.DMA((rows // TILE,)),
        ),
        cost=(4 * rows * slots * width + 8 * rows * width * width, 16 * rows * width),
    )(remote, turned, own_total, self_part, *far_counts, share, w_neigh_kept, cot_kept)

    received = other_side(message)
    feat_grad = call(
        own_grad_kernel,
        shape((rows, width), F32),
        cost=(2 * rows * rows * width + 2 * rows * width * width, 8 * rows * width),
    )(low, w_self_kept, edge_grad, *own_counts)
    message = call(
        side_sum_kernel,
        shape((peers, slab, width), BF16),
        [vmem, vmem, pl.BlockSpec(memory_space=pl.ANY)],
    )(w_own, received, feat_grad)
    slabs = swap(message, PEERS)
    message = call(
        functools.partial(peer_sum_kernel, sizes), shape((peers, slab + tall, width), BF16)
    )(slabs, rest, received, bias_sum)
    message = swap(message, PEERS)
    grad_feats = call(
        functools.partial(feat_grad_kernel, sizes, slab),
        shape((rows, width), BF16),
        cost=(4 * rows * slots * width, 6 * rows * width),
    )(message, places, feat_grad)
    unit_self, unit_neigh, unit_bias = call(
        functools.partial(unit_kernel, slab),
        (*((pltpu.HBM((width, width), F32),) * 2), pltpu.HBM((1, width), F32)),
        out_specs=(hbm,) * 3,
        scratch=(
            pltpu.VMEM((2, width, width), F32),
            pltpu.VMEM((1, width), F32),
            pltpu.SemaphoreType.DMA((3,)),
        ),
    )(message, other_side(message))
    return outputs, grad_feats, unit_self, unit_neigh, unit_bias.reshape(width)


def solution(mesh):
    doms, reps = mesh.shape["dom"], mesh.shape["rep"]
    split = jax.sharding.Mesh(mesh.devices.reshape(doms, reps // SIDES, SIDES), SPLIT_AXES)
    rows, whole = P(SPLIT_AXES, None), P()
    return jax.shard_map(
        functools.partial(on_device, doms, reps),
        mesh=split,
        in_specs=(rows, whole, whole, whole, rows, P(SPLIT_AXES), rows, P(SPLIT_AXES), rows),
        out_specs=(rows, rows, whole, whole, whole),
        check_vma=False,
    )
```

```python
import functools

import jax
import jax.numpy as jnp
from jax import lax
from jax.experimental import pallas as pl
from jax.experimental.pallas import tpu as pltpu
from jax.sharding import PartitionSpec as P

NORM_EPS = 1e-05
UNIT_EPS = 1e-06
SPLIT_AXES = ("dom", "pair", "side")
PEERS = ("dom", "pair")
SIDES = 2
VMEM_LIMIT = 32 * 1024 * 1024
F32 = jnp.float32
BF16 = jnp.bfloat16
TILE = 256
STRIP = 16
PIECE = 32
LANES = 128
BIAS_ROWS = 2


def div_floor(value, size):
    if size & (size - 1) == 0:
        return lax.shift_right_arithmetic(value, jnp.int32(size.bit_length() - 1))
    return value // size


def remainder(value, size):
    if size & (size - 1) == 0:
        return value & jnp.int32(size - 1)
    return value - (value // size) * size


def matmul(lhs, rhs, lhs_dim=1, rhs_dim=0):
    return lax.dot_general(
        lhs, rhs, (((lhs_dim,), (rhs_dim,)), ((), ())), preferred_element_type=F32
    )


def iota(shape, dim):
    return lax.broadcasted_iota(jnp.int32, shape, dim)


def one_hot(rows, places):
    return jnp.where(iota((rows, places.shape[1]), 0) == places, F32(1.0), F32(0.0)).astype(BF16)


def fetch(pairs, sems):
    copies = [
        pltpu.make_async_copy(source, target, sems.at[number])
        for number, (source, target) in enumerate(pairs)
    ]
    for copy in copies:
        copy.start()
    return copies


def pick_kernel(sizes, hub_hbm, send_hbm, *refs):
    doms, reps, cap, hub_own, tall = sizes
    inputs, (rows_ref, hubs_ref, places_ref), refs = refs[:5], refs[5:8], refs[8:]
    kept, (slot_ref, share_ref, own_count_ref, far_count_ref), refs = refs[:3], refs[3:7], refs[7:]
    hub_ref, send_ref, degree_ref, edge_ref, hot_ref, sems = refs
    feats_ref = kept[0]
    targets = (hub_ref, send_ref, degree_ref, edge_ref, *kept)
    copies = fetch(zip((hub_hbm, send_hbm, *inputs), targets), sems)
    slots = doms * tall
    lane = iota(places_ref.shape, 1)
    row = remainder(lane, tall)

    def list_entries(dom, places):
        for entry in range(cap):
            places = jnp.where(lane == dom * tall + entry, send_ref[entry, dom], places)
        return places

    copies[0].wait()
    copies[1].wait()
    places = jnp.full(lane.shape, -1, jnp.int32)
    if doms <= 16:
        for dom in range(doms):
            places = list_entries(dom, places)
    else:
        places = lax.fori_loop(0, doms, list_entries, places)
    for entry in range(hub_own):
        for first, inside in ((cap, lane < slots), (cap + hub_own, lane >= slots)):
            places = jnp.where((row == first + entry) & inside, hub_ref[entry], places)
    places_ref[...] = places
    column = jnp.broadcast_to(places, (LANES, lane.shape[1])).T[: slots + 2 * tall, :]
    node = iota(column.shape, 1)
    chosen = [
        jnp.where(node + first == column, F32(1.0), F32(0.0)).astype(BF16)
        for first in range(0, feats_ref.shape[0], LANES)
    ]
    copies[2].wait()
    copies[3].wait()
    find_slots(sizes, degree_ref, edge_ref, slot_ref, share_ref)
    count_edges(slot_ref, own_count_ref, far_count_ref, hot_ref, slice(0, TILE))
    copies[4].wait()
    picked = matmul(jnp.concatenate(chosen, axis=1), feats_ref[...]).astype(BF16)
    rows_ref[...] = picked[:slots, :]
    hubs_ref[...] = picked[slots:, :]
    for copy in copies[5:]:
        copy.wait()


def message_kernel(sizes, rows_ref, hubs_ref, after_ref, message_ref):
    doms, reps, cap, hub_own, tall = sizes
    del after_ref
    rows = rows_ref[...].astype(F32)
    hubs = hubs_ref[...].astype(F32)[:tall, :]
    place = iota(hubs.shape, 0)
    pair = lax.axis_index("pair")
    pairs = reps // SIDES
    for dom in range(doms):
        block = rows[dom * tall : (dom + 1) * tall, :]
        blocks = [
            jnp.where((place >= cap) | (pair == other), block, F32(0.0)) + hubs
            for other in range(pairs)
        ]
        first = dom * pairs * tall
        message_ref[first : first + pairs * tall, :] = jnp.concatenate(blocks, axis=0).astype(BF16)


def count_edges(slot_ref, own_count_ref, far_count_ref, hot_ref, nodes):
    fanout, rows = slot_ref.shape[0], own_count_ref.shape[0]
    highs = (rows + far_count_ref.shape[0]) // LANES
    low, high = [], []
    for k in range(fanout):
        slot = jnp.broadcast_to(slot_ref[k : k + 1, nodes], (STRIP, TILE))
        low.append(remainder(slot, LANES).astype(jnp.int16))
        high.append(div_floor(slot, LANES).astype(jnp.int16))
    for block in range(highs):
        for k in range(fanout):
            hot_ref[block * fanout + k] = jnp.where(high[k] == block, BF16(1.0), BF16(0.0))
    for strip in range(0, LANES, STRIP):
        numbers = (iota((STRIP, TILE), 0) + strip).astype(jnp.int16)
        hot = [jnp.where(numbers == low[k], BF16(1.0), BF16(0.0)) for k in range(fanout)]

        def count(block):
            total = hot[0] * hot_ref[block * fanout]
            for k in range(1, fanout):
                total = total + hot[k] * hot_ref[block * fanout + k]
            return total

        for block in range(rows // LANES):
            first = block * LANES + strip
            own_count_ref[first : first + STRIP, :] = count(block)
        far = far_count_ref.shape[0] // LANES
        if far <= 4:
            for block in range(far):
                first = block * LANES + strip
                far_count_ref[first : first + STRIP, :] = count(rows // LANES + block)
        else:

            @pl.loop(0, far)
            def far_block(block):
                first = pl.multiple_of(block * LANES + strip, STRIP)
                far_count_ref[pl.ds(first, STRIP), :] = count(rows // LANES + block)


def find_slots(sizes, degree_ref, edge_ref, slot_ref, share_ref):
    doms, reps, cap, hub_own, tall = sizes
    fanout, rows = edge_ref.shape
    hubs = doms * reps * hub_own
    source = edge_ref[...]
    hub = source - rows
    halo = hub - hubs
    chip = SIDES * hub_own
    entry = remainder(hub, chip) ^ (lax.axis_index("side") * hub_own)
    hub_slot = rows + cap + div_floor(hub, chip) * tall + entry
    peer = div_floor(halo, cap) * (reps // SIDES) + lax.axis_index("pair")
    halo_slot = rows + peer * tall + remainder(halo, cap)
    slot = jnp.where(source < rows, source, jnp.where(hub < hubs, hub_slot, halo_slot))
    valid = jnp.minimum(degree_ref[...], fanout)
    slot_ref[...] = jnp.where(iota((fanout, rows), 0) < valid, slot, -1)
    share_ref[...] = 1.0 / valid.astype(F32)


def own_kernel(tiles, feats_ref, w_self_ref, bias_ref, slot_ref, share_ref, *refs):
    first_count_ref, inputs, kept, refs = refs[0], refs[1:3], refs[3:5], refs[5:]
    turned_ref, total_ref, preact_ref, column_ref = refs[:4]
    own_refs, far_refs, (hot_ref, sems) = (
        refs[4 : 3 + tiles],
        refs[3 + tiles : 2 + 2 * tiles],
        refs[2 + 2 * tiles :],
    )
    copies = fetch(zip(inputs, kept), sems)
    turned_ref[...] = feats_ref[...].T

    def own_sums(number, count_ref):
        nodes = slice(number * TILE, (number + 1) * TILE)
        total_ref[:, nodes] = matmul(turned_ref[...], count_ref[...])
        preact_ref[nodes, :] = matmul(feats_ref[nodes, :], w_self_ref[...]) + bias_ref[...]
        column_ref[nodes, :] = jnp.broadcast_to(share_ref[:, nodes], (LANES, TILE)).T

    counted = first_count_ref
    for number in range(1, tiles):
        nodes = slice(number * TILE, (number + 1) * TILE)
        own_ref, far_ref = own_refs[number - 1], far_refs[number - 1]
        count_edges(slot_ref, own_ref, far_ref, hot_ref.at[number % 2], nodes)
        own_sums(number - 1, counted)
        counted = own_ref
    own_sums(tiles - 1, counted)
    for copy in copies:
        copy.wait()


def joint_kernel(sizes, remote_ref, turned_ref, total_ref, self_ref, *refs):
    doms, reps, cap, hub_own, tall = sizes
    rows, width = self_ref.shape
    tiles = [slice(first, first + TILE) for first in range(0, rows, TILE)]
    count_refs, refs = refs[: len(tiles)], refs[len(tiles) :]
    (
        share_ref,
        column_ref,
        w_neigh_ref,
        cot_ref,
        outputs_hbm,
        w_own_ref,
        rest_ref,
        message_ref,
        low_ref,
        edge_grad_ref,
        bias_ref,
        outputs_ref,
        mean_ref,
        preact_ref,
        w_grad_ref,
        sems,
    ) = refs
    table = remote_ref[...].T

    steps = [slice(first, first + LANES) for first in range(0, rows, LANES)]
    per_tile = TILE // LANES

    def find_mean(step):
        nodes, inside = steps[step], steps[step % per_tile]
        mean = total_ref[:, nodes] + matmul(table, count_refs[step // per_tile][:, inside])
        mean_ref[:, nodes] = (mean * share_ref[:, nodes]).astype(BF16)

    def find_preact(step):
        nodes = steps[step]
        neigh = matmul(mean_ref[:, nodes], w_neigh_ref[...], 0, 0)
        preact_ref[nodes, :] = self_ref[nodes, :] + neigh

    def head(nodes, bias_sum):
        for start in range(nodes.start, nodes.stop, PIECE):
            piece = slice(start, start + PIECE)
            preact = preact_ref[piece, :]
            cot = cot_ref[piece, :].astype(F32)
            grown = jnp.exp(jnp.minimum(preact, 0.0))
            act = jnp.where(preact > 0.0, preact, grown - 1.0)
            square = jnp.sum(act * act, axis=1, keepdims=True)
            along = jnp.sum(act * cot, axis=1, keepdims=True)
            scale = lax.rsqrt(square * (1.0 / width) + NORM_EPS)
            outputs_ref[piece, :] = (act * scale).astype(BF16)
            pull = along * (scale * scale * scale) * (1.0 / width)
            grad_pre = (cot * scale - act * pull) * jnp.where(preact > 0.0, F32(1.0), grown)
            bias_sum = bias_sum + jnp.sum(grad_pre.reshape(PIECE // 8, 8, width), axis=0)
            low_ref[piece, :] = grad_pre.astype(BF16)
        return bias_sum

    def find_edge_grad(step):
        nodes = steps[step]
        column = jnp.concatenate([column_ref[nodes, :]] * (width // LANES), axis=1)
        edge_grad = matmul(low_ref[nodes, :], w_neigh_ref[...], 1, 1) * column
        edge_grad_ref[nodes, :] = edge_grad.astype(BF16)

    def node_sums(numbers):
        nodes = slice(tiles[numbers[0]].start, tiles[numbers[-1]].stop)
        low = low_ref[nodes, :]
        return (
            matmul(turned_ref[:, nodes], low),
            matmul(mean_ref[:, nodes], low),
            sum(matmul(count_refs[k][...], edge_grad_ref[tiles[k], :]) for k in numbers),
        )

    bias_sum = jnp.zeros((8, width), F32)
    copies = []
    last = len(steps) - 1
    find_mean(0)
    find_mean(1)
    find_preact(0)
    for step, nodes in enumerate(steps):
        if step + 2 <= last:
            find_mean(step + 2)
        if step < last:
            find_preact(step + 1)
        if step:
            find_edge_grad(step - 1)
        if step == last and len(tiles) > 1:
            w_grad_ref[0], w_grad_ref[1], rest_ref[...] = node_sums(range(len(tiles) - 1))
        bias_sum = head(nodes, bias_sum)
        if nodes.stop % TILE == 0:
            number = step // per_tile
            copies += fetch(
                ((outputs_ref.at[tiles[number], :], outputs_hbm.at[tiles[number], :]),),
                sems.at[pl.ds(number, 1)],
            )
    find_edge_grad(last)

    w_self_sum, w_neigh_sum, remote = node_sums([len(tiles) - 1])
    if len(tiles) > 1:
        w_self_sum = w_self_sum + w_grad_ref[0]
        w_neigh_sum = w_neigh_sum + w_grad_ref[1]
        remote = remote + rest_ref[...]
    w_grad_ref[0] = w_self_sum
    w_grad_ref[1] = w_neigh_sum
    rest_ref[...] = remote
    bias_ref[...] = bias_sum
    bias_sum = jnp.broadcast_to(jnp.sum(bias_sum, axis=0, keepdims=True), (tall, width))
    bias_high = bias_sum.astype(BF16).astype(F32)
    place = iota((tall, width), 0)
    bias_rows = jnp.where(place == cap, bias_high, bias_sum - bias_high)
    bias_rows = jnp.where(place < cap, F32(0.0), bias_rows)
    message = remote.reshape(-1, tall, width)
    message = jnp.where((place < cap + hub_own)[None], bias_rows[None], message)
    message_ref[width:, :] = message.reshape(remote.shape).astype(BF16)
    mine = lax.axis_index("side")
    w_own_ref[...] = w_grad_ref[mine]
    message_ref[:width, :] = w_grad_ref[1 - mine].astype(BF16)
    for copy in copies:
        copy.wait()


def own_grad_kernel(low_ref, w_self_ref, edge_grad_ref, *refs):
    *count_refs, feat_grad_ref = refs
    for first in range(0, low_ref.shape[0], TILE):
        nodes = slice(first, first + TILE)
        total = matmul(low_ref[nodes, :], w_self_ref[...], 1, 1)
        for number, count_ref in enumerate(count_refs):
            edges = edge_grad_ref[number * TILE : (number + 1) * TILE, :]
            total = total + matmul(count_ref[nodes, :], edges)
        feat_grad_ref[nodes, :] = total


def side_sum_kernel(own_ref, received_ref, after_ref, message_ref):
    del after_ref
    peers, slab, width = message_ref.shape
    w_grad = own_ref[...] + received_ref[:width, :].astype(F32)
    owners = width // slab
    w_grad = w_grad.reshape(owners, slab, width)
    if owners < peers:
        w_grad = jnp.concatenate([w_grad, jnp.zeros((peers - owners, slab, width), F32)], axis=0)
    message_ref[...] = w_grad.astype(BF16)


def peer_sum_kernel(sizes, slabs_ref, own_ref, received_ref, bias_ref, message_ref):
    doms, reps, cap, hub_own, tall = sizes
    peers, slab, width = slabs_ref.shape
    total = jnp.sum(slabs_ref[...].astype(F32), axis=0)
    received_ref = received_ref.at[width:, :]
    size = min(peers * tall, LANES)
    to, source = iota((size, size), 0), iota((size, size), 1)
    entry = remainder(to, tall) - cap
    moved = (source == to + hub_own) & (entry >= 0) & (entry < hub_own)
    moved = jnp.where(moved, F32(1.0), F32(0.0)).astype(BF16)
    rest = own_ref[...] + jnp.concatenate(
        [
            matmul(moved, received_ref[first : first + size, :])
            for first in range(0, peers * tall, size)
        ],
        axis=0,
    )
    place = iota((tall, width), 0)
    bias = received_ref[: 2 * tall, :].astype(F32)[:tall, :]
    bias = jnp.where((place >= cap) & (place < cap + BIAS_ROWS), bias, F32(0.0)) + bias_ref[...]
    bias = jnp.broadcast_to(jnp.sum(bias, axis=0, keepdims=True), (tall, width))
    bias_high = bias.astype(BF16).astype(F32)
    bias_rows = jnp.where(place == tall - 1, bias - bias_high, bias_high)
    rest = rest.reshape(peers, tall, width)
    rest = jnp.where((place < tall - BIAS_ROWS)[None], rest, bias_rows[None])
    total = jnp.broadcast_to(total[None], (peers, slab, width))
    message_ref[...] = jnp.concatenate([total, rest], axis=1).astype(BF16)


def feat_grad_kernel(sizes, slab, message_ref, places_ref, feat_grad_ref, out_ref):
    doms, reps, cap, hub_own, tall = sizes
    rows, width = out_ref.shape
    pairs = reps // SIDES
    returned = message_ref[...].astype(F32)[:, slab:, :].reshape(doms, pairs, tall, width)
    returned = [
        returned[:, pair].reshape(doms * tall, width).astype(BF16) for pair in range(pairs)
    ]
    chosen = one_hot(rows, places_ref[:, : doms * tall])
    for first in range(0, rows, TILE):
        nodes = slice(first, first + TILE)
        total = feat_grad_ref[nodes, :]
        for part in returned:
            total = total + matmul(chosen[nodes, :], part)
        out_ref[nodes, :] = total.astype(BF16)


def unit_kernel(slab, mine_ref, other_ref, self_hbm, neigh_hbm, bias_hbm, units_ref, bias_ref, sems):
    side = lax.axis_index("side")
    _, size, width = units_ref.shape
    bias = jnp.sum(mine_ref[...].astype(F32)[:, slab:, :], axis=0)[-BIAS_ROWS:, :]
    bias = jnp.sum(bias, axis=0, keepdims=True)
    bias_ref[...] = bias * lax.rsqrt(jnp.mean(bias * bias, axis=1, keepdims=True) + UNIT_EPS)
    copies = [
        pltpu.make_async_copy(source, target, sems.at[number])
        for number, (source, target) in enumerate(
            ((units_ref.at[0], self_hbm), (units_ref.at[1], neigh_hbm), (bias_ref, bias_hbm))
        )
    ]
    copies[2].start()
    for place, grad_ref in ((side, mine_ref), (1 - side, other_ref)):
        grad = grad_ref[: size // slab].astype(F32)[:, :slab, :].reshape(size, width)
        square = jnp.sum(jnp.sum(grad * grad, axis=0, keepdims=True), axis=1, keepdims=True)
        units_ref[place] = grad * lax.rsqrt(square * (1.0 / grad.size) + UNIT_EPS)
        for number, copy in enumerate(copies[:2]):
            pl.when(place == number)(copy.start)
    for copy in copies:
        copy.wait()


def call(kernel, out_shape, in_specs=None, scratch=(), cost=(0, 0), out_specs=None):
    specs = {"in_specs": in_specs, "out_specs": out_specs}
    return pl.pallas_call(
        kernel,
        out_shape=out_shape,
        **{name: spec for name, spec in specs.items() if spec is not None},
        scratch_shapes=list(scratch),
        compiler_params=pltpu.CompilerParams(vmem_limit_bytes=VMEM_LIMIT),
        cost_estimate=pl.CostEstimate(flops=cost[0], bytes_accessed=cost[1], transcendentals=0),
    )


def in_hbm(*arrays):
    return [pltpu.with_memory_space_constraint(array, pltpu.HBM) for array in arrays]


def swap(array, axes):
    return lax.all_to_all(array, axes, split_axis=0, concat_axis=0, tiled=True)


def other_side(array):
    return lax.ppermute(array, "side", [(0, 1), (1, 0)])


def on_device(
    doms, reps, feats, w_self, w_neigh, bias, out_cot, degree, edge_src, hub_rows, send_rows
):
    rows, width = feats.shape
    fanout = edge_src.shape[1]
    cap, hub_own = send_rows.shape[1], hub_rows.shape[0]
    peers = doms * reps // SIDES
    tall = cap + SIDES * hub_own
    if tall % 8 or tall < cap + hub_own + BIAS_ROWS or hub_own & (hub_own - 1):
        raise ValueError("message height")
    slots = peers * tall
    slab = max(8, width // peers)
    sizes = (doms, reps, cap, hub_own, tall)
    shape = jax.ShapeDtypeStruct
    hbm = pl.BlockSpec(memory_space=pltpu.HBM)
    vmem = pl.BlockSpec(memory_space=pltpu.VMEM)

    tiles = rows // TILE
    hot = pltpu.VMEM(((rows + slots) // LANES * fanout, STRIP, TILE), BF16)
    picked, hubs, places, feats_kept, w_self_kept, bias_kept, slot, share, *first_counts = call(
        functools.partial(pick_kernel, sizes),
        (
            shape((doms * tall, width), BF16),
            shape((2 * tall, width), BF16),
            shape((1, -(-(doms + 2) * tall // LANES) * LANES), jnp.int32),
            shape((rows, width), BF16),
            shape((width, width), BF16),
            shape((1, width), F32),
            shape((fanout, rows), jnp.int32),
            shape((1, rows), F32),
            shape((rows, TILE), BF16),
            shape((slots, TILE), BF16),
        ),
        [hbm] * 7,
        (
            pltpu.SMEM((hub_own,), jnp.int32),
            pltpu.SMEM((cap, doms), jnp.int32),
            pltpu.VMEM((1, rows), jnp.int32),
            pltpu.VMEM((fanout, rows), jnp.int32),
            hot,
            pltpu.SemaphoreType.DMA((7,)),
        ),
        cost=(2 * rows * slots * width, 2 * rows * width),
    )(
        *in_hbm(
            hub_rows,
            send_rows.T,
            degree.reshape(1, rows),
            edge_src.T,
            feats,
            w_self,
            bias.reshape(1, width),
        )
    )
    hubs = other_side(hubs)
    w_neigh_kept, cot_kept, turned, own_total, self_part, share_column, *counts = call(
        functools.partial(own_kernel, tiles),
        (
            shape((width, width), BF16),
            shape((rows, width), BF16),
            shape((width, rows), BF16),
            shape((width, rows), F32),
            shape((rows, width), F32),
            shape((rows, LANES), F32),
            *((shape((rows, TILE), BF16),) * (tiles - 1)),
            *((shape((slots, TILE), BF16),) * (tiles - 1)),
        ),
        [vmem] * 6 + [hbm] * 2,
        (
            pltpu.VMEM((2, *hot.shape), BF16),
            pltpu.SemaphoreType.DMA((2,)),
        ),
        cost=(8 * rows * (rows + slots) * width, 12 * rows * width + 2 * rows * rows),
    )(feats_kept, w_self_kept, bias_kept, slot, share, first_counts[0], *in_hbm(w_neigh, out_cot))
    own_counts = [first_counts[0], *counts[: tiles - 1]]
    far_counts = [first_counts[1], *counts[tiles - 1 :]]
    message = call(
        functools.partial(message_kernel, sizes),
        shape((slots, width), BF16),
        [vmem, vmem, pl.BlockSpec(memory_space=pl.ANY)],
    )(picked, hubs, own_total)
    remote = swap(message, PEERS)

    outputs, w_own, rest, message, low, edge_grad, bias_sum = call(
        functools.partial(joint_kernel, sizes),
        (
            pltpu.HBM((rows, width), BF16),
            shape((width, width), F32),
            shape((slots, width), F32),
            shape((width + slots, width), BF16),
            shape((rows, width), BF16),
            shape((rows, width), BF16),
            shape((8, width), F32),
        ),
        out_specs=(hbm,) + (vmem,) * 6,
        scratch=(
            pltpu.VMEM((rows, width), BF16),
            pltpu.VMEM((width, rows), BF16),
            pltpu.VMEM((rows, width), F32),
            pltpu.VMEM((2, width, width), F32),
            pltpu.SemaphoreType.DMA((rows // TILE,)),
        ),
        cost=(4 * rows * slots * width + 8 * rows * width * width, 16 * rows * width),
    )(
        remote,
        turned,
        own_total,
        self_part,
        *far_counts,
        share,
        share_column,
        w_neigh_kept,
        cot_kept,
    )

    received = other_side(message)
    feat_grad = call(
        own_grad_kernel,
        shape((rows, width), F32),
        cost=(2 * rows * rows * width + 2 * rows * width * width, 8 * rows * width),
    )(low, w_self_kept, edge_grad, *own_counts)
    message = call(
        side_sum_kernel,
        shape((peers, slab, width), BF16),
        [vmem, vmem, pl.BlockSpec(memory_space=pl.ANY)],
    )(w_own, received, feat_grad)
    slabs = swap(message, PEERS)
    message = call(
        functools.partial(peer_sum_kernel, sizes), shape((peers, slab + tall, width), BF16)
    )(slabs, rest, received, bias_sum)
    message = swap(message, PEERS)
    grad_feats = call(
        functools.partial(feat_grad_kernel, sizes, slab),
        shape((rows, width), BF16),
        cost=(4 * rows * slots * width, 6 * rows * width),
    )(message, places, feat_grad)
    unit_self, unit_neigh, unit_bias = call(
        functools.partial(unit_kernel, slab),
        (*((pltpu.HBM((width, width), F32),) * 2), pltpu.HBM((1, width), F32)),
        out_specs=(hbm,) * 3,
        scratch=(
            pltpu.VMEM((2, width, width), F32),
            pltpu.VMEM((1, width), F32),
            pltpu.SemaphoreType.DMA((3,)),
        ),
    )(message, other_side(message))
    return outputs, grad_feats, unit_self, unit_neigh, unit_bias.reshape(width)


def solution(mesh):
    doms, reps = mesh.shape["dom"], mesh.shape["rep"]
    split = jax.sharding.Mesh(mesh.devices.reshape(doms, reps // SIDES, SIDES), SPLIT_AXES)
    rows, whole = P(SPLIT_AXES, None), P()
    return jax.shard_map(
        functools.partial(on_device, doms, reps),
        mesh=split,
        in_specs=(rows, whole, whole, whole, rows, P(SPLIT_AXES), rows, P(SPLIT_AXES), rows),
        out_specs=(rows, rows, whole, whole, whole),
        check_vma=False,
    )
```

```python
import functools

import jax
import jax.numpy as jnp
from jax import lax
from jax.experimental import pallas as pl
from jax.experimental.pallas import tpu as pltpu
from jax.sharding import PartitionSpec as P

NORM_EPS = 1e-05
UNIT_EPS = 1e-06
SPLIT_AXES = ("dom", "pair", "side")
PEERS = ("dom", "pair")
SIDES = 2
VMEM_LIMIT = 32 * 1024 * 1024
F32 = jnp.float32
BF16 = jnp.bfloat16
TILE = 256
STRIP = 16
PIECE = 32
LANES = 128
BIAS_ROWS = 2


def div_floor(value, size):
    if size & (size - 1) == 0:
        return lax.shift_right_arithmetic(value, jnp.int32(size.bit_length() - 1))
    return value // size


def remainder(value, size):
    if size & (size - 1) == 0:
        return value & jnp.int32(size - 1)
    return value - (value // size) * size


def matmul(lhs, rhs, lhs_dim=1, rhs_dim=0):
    return lax.dot_general(
        lhs, rhs, (((lhs_dim,), (rhs_dim,)), ((), ())), preferred_element_type=F32
    )


def iota(shape, dim):
    return lax.broadcasted_iota(jnp.int32, shape, dim)


def one_hot(rows, places):
    return jnp.where(iota((rows, places.shape[1]), 0) == places, F32(1.0), F32(0.0)).astype(BF16)


def fetch(pairs, sems):
    copies = [
        pltpu.make_async_copy(source, target, sems.at[number])
        for number, (source, target) in enumerate(pairs)
    ]
    for copy in copies:
        copy.start()
    return copies


def pick_kernel(sizes, hub_hbm, send_hbm, *refs):
    doms, reps, cap, hub_own, tall = sizes
    inputs, (rows_ref, hubs_ref, places_ref), refs = refs[:5], refs[5:8], refs[8:]
    kept, (slot_ref, share_ref, own_count_ref, far_count_ref), refs = refs[:3], refs[3:7], refs[7:]
    hub_ref, send_ref, degree_ref, edge_ref, hot_ref, sems = refs
    feats_ref = kept[0]
    targets = (hub_ref, send_ref, degree_ref, edge_ref, *kept)
    copies = fetch(zip((hub_hbm, send_hbm, *inputs), targets), sems)
    slots = doms * tall
    lane = iota(places_ref.shape, 1)
    row = remainder(lane, tall)

    def list_entries(dom, places):
        for entry in range(cap):
            places = jnp.where(lane == dom * tall + entry, send_ref[entry, dom], places)
        return places

    copies[0].wait()
    copies[1].wait()
    places = jnp.full(lane.shape, -1, jnp.int32)
    if doms <= 16:
        for dom in range(doms):
            places = list_entries(dom, places)
    else:
        places = lax.fori_loop(0, doms, list_entries, places)
    for entry in range(hub_own):
        for first, inside in ((cap, lane < slots), (cap + hub_own, lane >= slots)):
            places = jnp.where((row == first + entry) & inside, hub_ref[entry], places)
    places_ref[...] = places
    column = jnp.broadcast_to(places, (LANES, lane.shape[1])).T[: slots + 2 * tall, :]
    node = iota(column.shape, 1)
    chosen = [
        jnp.where(node + first == column, F32(1.0), F32(0.0)).astype(BF16)
        for first in range(0, feats_ref.shape[0], LANES)
    ]
    copies[2].wait()
    copies[3].wait()
    find_slots(sizes, degree_ref, edge_ref, slot_ref, share_ref)
    count_edges(slot_ref, own_count_ref, far_count_ref, hot_ref, slice(0, TILE))
    copies[4].wait()
    picked = matmul(jnp.concatenate(chosen, axis=1), feats_ref[...]).astype(BF16)
    rows_ref[...] = picked[:slots, :]
    hubs_ref[...] = picked[slots:, :]
    for copy in copies[5:]:
        copy.wait()


def message_kernel(sizes, rows_ref, hubs_ref, after_ref, message_ref):
    doms, reps, cap, hub_own, tall = sizes
    del after_ref
    rows = rows_ref[...].astype(F32)
    hubs = hubs_ref[...].astype(F32)[:tall, :]
    place = iota(hubs.shape, 0)
    pair = lax.axis_index("pair")
    pairs = reps // SIDES
    for dom in range(doms):
        block = rows[dom * tall : (dom + 1) * tall, :]
        blocks = [
            jnp.where((place >= cap) | (pair == other), block, F32(0.0)) + hubs
            for other in range(pairs)
        ]
        first = dom * pairs * tall
        message_ref[first : first + pairs * tall, :] = jnp.concatenate(blocks, axis=0).astype(BF16)


def count_edges(slot_ref, own_count_ref, far_count_ref, hot_ref, nodes):
    fanout, rows = slot_ref.shape[0], own_count_ref.shape[0]
    highs = (rows + far_count_ref.shape[0]) // LANES
    low, high = [], []
    for k in range(fanout):
        slot = jnp.broadcast_to(slot_ref[k : k + 1, nodes], (STRIP, TILE))
        low.append(remainder(slot, LANES).astype(jnp.int16))
        high.append(div_floor(slot, LANES).astype(jnp.int16))
    for block in range(highs):
        for k in range(fanout):
            hot_ref[block * fanout + k] = jnp.where(high[k] == block, BF16(1.0), BF16(0.0))
    for strip in range(0, LANES, STRIP):
        numbers = (iota((STRIP, TILE), 0) + strip).astype(jnp.int16)
        hot = [jnp.where(numbers == low[k], BF16(1.0), BF16(0.0)) for k in range(fanout)]

        def count(block):
            total = hot[0] * hot_ref[block * fanout]
            for k in range(1, fanout):
                total = total + hot[k] * hot_ref[block * fanout + k]
            return total

        for block in range(rows // LANES):
            first = block * LANES + strip
            own_count_ref[first : first + STRIP, :] = count(block)
        far = far_count_ref.shape[0] // LANES
        if far <= 4:
            for block in range(far):
                first = block * LANES + strip
                far_count_ref[first : first + STRIP, :] = count(rows // LANES + block)
        else:

            @pl.loop(0, far)
            def far_block(block):
                first = pl.multiple_of(block * LANES + strip, STRIP)
                far_count_ref[pl.ds(first, STRIP), :] = count(rows // LANES + block)


def find_slots(sizes, degree_ref, edge_ref, slot_ref, share_ref):
    doms, reps, cap, hub_own, tall = sizes
    fanout, rows = edge_ref.shape
    hubs = doms * reps * hub_own
    source = edge_ref[...]
    hub = source - rows
    halo = hub - hubs
    chip = SIDES * hub_own
    entry = remainder(hub, chip) ^ (lax.axis_index("side") * hub_own)
    hub_slot = rows + cap + div_floor(hub, chip) * tall + entry
    peer = div_floor(halo, cap) * (reps // SIDES) + lax.axis_index("pair")
    halo_slot = rows + peer * tall + remainder(halo, cap)
    slot = jnp.where(source < rows, source, jnp.where(hub < hubs, hub_slot, halo_slot))
    valid = jnp.minimum(degree_ref[...], fanout)
    slot_ref[...] = jnp.where(iota((fanout, rows), 0) < valid, slot, -1)
    share_ref[...] = 1.0 / valid.astype(F32)


def own_kernel(tiles, feats_ref, w_self_ref, bias_ref, slot_ref, share_ref, *refs):
    first_count_ref, inputs, kept, refs = refs[0], refs[1:3], refs[3:5], refs[5:]
    turned_ref, total_ref, preact_ref, column_ref = refs[:4]
    own_refs, far_refs, (hot_ref, sems) = (
        refs[4 : 3 + tiles],
        refs[3 + tiles : 2 + 2 * tiles],
        refs[2 + 2 * tiles :],
    )
    copies = fetch(zip(inputs, kept), sems)
    turned_ref[...] = feats_ref[...].T

    def own_sums(number, count_ref):
        nodes = slice(number * TILE, (number + 1) * TILE)
        total_ref[:, nodes] = matmul(turned_ref[...], count_ref[...])
        preact_ref[nodes, :] = matmul(feats_ref[nodes, :], w_self_ref[...]) + bias_ref[...]
        column_ref[nodes, :] = jnp.broadcast_to(share_ref[:, nodes], (LANES, TILE)).T

    counted = first_count_ref
    for number in range(1, tiles):
        nodes = slice(number * TILE, (number + 1) * TILE)
        own_ref, far_ref = own_refs[number - 1], far_refs[number - 1]
        count_edges(slot_ref, own_ref, far_ref, hot_ref.at[number % 2], nodes)
        own_sums(number - 1, counted)
        counted = own_ref
    own_sums(tiles - 1, counted)
    for copy in copies:
        copy.wait()


def joint_kernel(sizes, remote_ref, turned_ref, total_ref, self_ref, *refs):
    doms, reps, cap, hub_own, tall = sizes
    rows, width = self_ref.shape
    tiles = [slice(first, first + TILE) for first in range(0, rows, TILE)]
    count_refs, refs = refs[: len(tiles)], refs[len(tiles) :]
    (
        share_ref,
        column_ref,
        w_neigh_ref,
        cot_ref,
        outputs_hbm,
        w_own_ref,
        rest_ref,
        message_ref,
        low_ref,
        edge_grad_ref,
        bias_ref,
        outputs_ref,
        mean_ref,
        preact_ref,
        w_grad_ref,
        sems,
    ) = refs
    table = remote_ref[...].T

    def before_head(number):
        nodes = tiles[number]
        mean = total_ref[:, nodes] + matmul(table, count_refs[number][...])
        mean = (mean * share_ref[:, nodes]).astype(BF16)
        mean_ref[:, nodes] = mean
        preact_ref[nodes, :] = self_ref[nodes, :] + matmul(mean, w_neigh_ref[...], 0, 0)

    def node_sums(numbers):
        nodes = slice(tiles[numbers[0]].start, tiles[numbers[-1]].stop)
        both = jnp.concatenate([turned_ref[:, nodes], mean_ref[:, nodes]], axis=0)
        return (
            matmul(both, low_ref[nodes, :]).reshape(2, width, width),
            sum(matmul(count_refs[k][...], edge_grad_ref[tiles[k], :]) for k in numbers),
        )

    bias_sum = jnp.zeros((8, width), F32)
    copies = []
    before_head(0)
    for number, nodes in enumerate(tiles):
        if number + 1 < len(tiles):
            before_head(number + 1)
        elif number:
            w_grad_ref[...], rest_ref[...] = node_sums(range(number))
        for start in range(nodes.start, nodes.stop, PIECE):
            piece = slice(start, start + PIECE)
            preact = preact_ref[piece, :]
            cot = cot_ref[piece, :].astype(F32)
            grown = jnp.exp(jnp.minimum(preact, 0.0))
            act = jnp.where(preact > 0.0, preact, grown - 1.0)
            square = jnp.sum(act * act, axis=1, keepdims=True)
            along = jnp.sum(act * cot, axis=1, keepdims=True)
            scale = lax.rsqrt(square * (1.0 / width) + NORM_EPS)
            outputs_ref[piece, :] = (act * scale).astype(BF16)
            pull = along * (scale * scale * scale) * (1.0 / width)
            grad_pre = (cot * scale - act * pull) * jnp.where(preact > 0.0, F32(1.0), grown)
            bias_sum = bias_sum + jnp.sum(grad_pre.reshape(PIECE // 8, 8, width), axis=0)
            low_ref[piece, :] = grad_pre.astype(BF16)
        copies += fetch(
            ((outputs_ref.at[nodes, :], outputs_hbm.at[nodes, :]),), sems.at[pl.ds(number, 1)]
        )
        column = jnp.concatenate([column_ref[nodes, :]] * (width // LANES), axis=1)
        edge_grad = matmul(low_ref[nodes, :], w_neigh_ref[...], 1, 1) * column
        edge_grad_ref[nodes, :] = edge_grad.astype(BF16)

    w_grad, remote = node_sums([len(tiles) - 1])
    if len(tiles) > 1:
        w_grad = w_grad + w_grad_ref[...]
        remote = remote + rest_ref[...]
    w_grad_ref[...] = w_grad
    rest_ref[...] = remote
    bias_ref[...] = bias_sum
    bias_sum = jnp.broadcast_to(jnp.sum(bias_sum, axis=0, keepdims=True), (tall, width))
    bias_high = bias_sum.astype(BF16).astype(F32)
    place = iota((tall, width), 0)
    bias_rows = jnp.where(place == cap, bias_high, bias_sum - bias_high)
    bias_rows = jnp.where(place < cap, F32(0.0), bias_rows)
    message = remote.reshape(-1, tall, width)
    message = jnp.where((place < cap + hub_own)[None], bias_rows[None], message)
    message_ref[width:, :] = message.reshape(remote.shape).astype(BF16)
    mine = lax.axis_index("side")
    w_own_ref[...] = w_grad_ref[mine]
    message_ref[:width, :] = w_grad_ref[1 - mine].astype(BF16)
    for copy in copies:
        copy.wait()


def own_grad_kernel(low_ref, w_self_ref, edge_grad_ref, *refs):
    *count_refs, feat_grad_ref = refs
    for first in range(0, low_ref.shape[0], TILE):
        nodes = slice(first, first + TILE)
        total = matmul(low_ref[nodes, :], w_self_ref[...], 1, 1)
        for number, count_ref in enumerate(count_refs):
            edges = edge_grad_ref[number * TILE : (number + 1) * TILE, :]
            total = total + matmul(count_ref[nodes, :], edges)
        feat_grad_ref[nodes, :] = total


def side_sum_kernel(own_ref, received_ref, after_ref, message_ref):
    del after_ref
    peers, slab, width = message_ref.shape
    w_grad = own_ref[...] + received_ref[:width, :].astype(F32)
    owners = width // slab
    w_grad = w_grad.reshape(owners, slab, width)
    if owners < peers:
        w_grad = jnp.concatenate([w_grad, jnp.zeros((peers - owners, slab, width), F32)], axis=0)
    message_ref[...] = w_grad.astype(BF16)


def peer_sum_kernel(sizes, slabs_ref, own_ref, received_ref, bias_ref, message_ref):
    doms, reps, cap, hub_own, tall = sizes
    peers, slab, width = slabs_ref.shape
    total = jnp.sum(slabs_ref[...].astype(F32), axis=0)
    received_ref = received_ref.at[width:, :]
    size = min(peers * tall, LANES)
    to, source = iota((size, size), 0), iota((size, size), 1)
    entry = remainder(to, tall) - cap
    moved = (source == to + hub_own) & (entry >= 0) & (entry < hub_own)
    moved = jnp.where(moved, F32(1.0), F32(0.0)).astype(BF16)
    rest = own_ref[...] + jnp.concatenate(
        [
            matmul(moved, received_ref[first : first + size, :])
            for first in range(0, peers * tall, size)
        ],
        axis=0,
    )
    place = iota((tall, width), 0)
    bias = received_ref[: 2 * tall, :].astype(F32)[:tall, :]
    bias = jnp.where((place >= cap) & (place < cap + BIAS_ROWS), bias, F32(0.0)) + bias_ref[...]
    bias = jnp.broadcast_to(jnp.sum(bias, axis=0, keepdims=True), (tall, width))
    bias_high = bias.astype(BF16).astype(F32)
    bias_rows = jnp.where(place == tall - 1, bias - bias_high, bias_high)
    rest = rest.reshape(peers, tall, width)
    rest = jnp.where((place < tall - BIAS_ROWS)[None], rest, bias_rows[None])
    total = jnp.broadcast_to(total[None], (peers, slab, width))
    message_ref[...] = jnp.concatenate([total, rest], axis=1).astype(BF16)


def feat_grad_kernel(sizes, slab, message_ref, places_ref, feat_grad_ref, out_ref):
    doms, reps, cap, hub_own, tall = sizes
    rows, width = out_ref.shape
    pairs = reps // SIDES
    returned = message_ref[...].astype(F32)[:, slab:, :].reshape(doms, pairs, tall, width)
    returned = [
        returned[:, pair].reshape(doms * tall, width).astype(BF16) for pair in range(pairs)
    ]
    chosen = one_hot(rows, places_ref[:, : doms * tall])
    for first in range(0, rows, TILE):
        nodes = slice(first, first + TILE)
        total = feat_grad_ref[nodes, :]
        for part in returned:
            total = total + matmul(chosen[nodes, :], part)
        out_ref[nodes, :] = total.astype(BF16)


def unit_kernel(slab, mine_ref, other_ref, self_hbm, neigh_hbm, bias_hbm, units_ref, bias_ref, sems):
    side = lax.axis_index("side")
    _, size, width = units_ref.shape
    bias = jnp.sum(mine_ref[...].astype(F32)[:, slab:, :], axis=0)[-BIAS_ROWS:, :]
    bias = jnp.sum(bias, axis=0, keepdims=True)
    bias_ref[...] = bias * lax.rsqrt(jnp.mean(bias * bias, axis=1, keepdims=True) + UNIT_EPS)
    copies = [
        pltpu.make_async_copy(source, target, sems.at[number])
        for number, (source, target) in enumerate(
            ((units_ref.at[0], self_hbm), (units_ref.at[1], neigh_hbm), (bias_ref, bias_hbm))
        )
    ]
    copies[2].start()
    for place, grad_ref in ((side, mine_ref), (1 - side, other_ref)):
        grad = grad_ref[: size // slab].astype(F32)[:, :slab, :].reshape(size, width)
        square = jnp.sum(jnp.sum(grad * grad, axis=0, keepdims=True), axis=1, keepdims=True)
        units_ref[place] = grad * lax.rsqrt(square * (1.0 / grad.size) + UNIT_EPS)
        for number, copy in enumerate(copies[:2]):
            pl.when(place == number)(copy.start)
    for copy in copies:
        copy.wait()


def call(kernel, out_shape, in_specs=None, scratch=(), cost=(0, 0), out_specs=None):
    specs = {"in_specs": in_specs, "out_specs": out_specs}
    return pl.pallas_call(
        kernel,
        out_shape=out_shape,
        **{name: spec for name, spec in specs.items() if spec is not None},
        scratch_shapes=list(scratch),
        compiler_params=pltpu.CompilerParams(vmem_limit_bytes=VMEM_LIMIT),
        cost_estimate=pl.CostEstimate(flops=cost[0], bytes_accessed=cost[1], transcendentals=0),
    )


def in_hbm(*arrays):
    return [pltpu.with_memory_space_constraint(array, pltpu.HBM) for array in arrays]


def swap(array, axes):
    return lax.all_to_all(array, axes, split_axis=0, concat_axis=0, tiled=True)


def other_side(array):
    return lax.ppermute(array, "side", [(0, 1), (1, 0)])


def on_device(
    doms, reps, feats, w_self, w_neigh, bias, out_cot, degree, edge_src, hub_rows, send_rows
):
    rows, width = feats.shape
    fanout = edge_src.shape[1]
    cap, hub_own = send_rows.shape[1], hub_rows.shape[0]
    peers = doms * reps // SIDES
    tall = cap + SIDES * hub_own
    if tall % 8 or tall < cap + hub_own + BIAS_ROWS or hub_own & (hub_own - 1):
        raise ValueError("message height")
    slots = peers * tall
    slab = max(8, width // peers)
    sizes = (doms, reps, cap, hub_own, tall)
    shape = jax.ShapeDtypeStruct
    hbm = pl.BlockSpec(memory_space=pltpu.HBM)
    vmem = pl.BlockSpec(memory_space=pltpu.VMEM)

    tiles = rows // TILE
    hot = pltpu.VMEM(((rows + slots) // LANES * fanout, STRIP, TILE), BF16)
    picked, hubs, places, feats_kept, w_self_kept, bias_kept, slot, share, *first_counts = call(
        functools.partial(pick_kernel, sizes),
        (
            shape((doms * tall, width), BF16),
            shape((2 * tall, width), BF16),
            shape((1, -(-(doms + 2) * tall // LANES) * LANES), jnp.int32),
            shape((rows, width), BF16),
            shape((width, width), BF16),
            shape((1, width), F32),
            shape((fanout, rows), jnp.int32),
            shape((1, rows), F32),
            shape((rows, TILE), BF16),
            shape((slots, TILE), BF16),
        ),
        [hbm] * 7,
        (
            pltpu.SMEM((hub_own,), jnp.int32),
            pltpu.SMEM((cap, doms), jnp.int32),
            pltpu.VMEM((1, rows), jnp.int32),
            pltpu.VMEM((fanout, rows), jnp.int32),
            hot,
            pltpu.SemaphoreType.DMA((7,)),
        ),
        cost=(2 * rows * slots * width, 2 * rows * width),
    )(
        *in_hbm(
            hub_rows,
            send_rows.T,
            degree.reshape(1, rows),
            edge_src.T,
            feats,
            w_self,
            bias.reshape(1, width),
        )
    )
    hubs = other_side(hubs)
    w_neigh_kept, cot_kept, turned, own_total, self_part, share_column, *counts = call(
        functools.partial(own_kernel, tiles),
        (
            shape((width, width), BF16),
            shape((rows, width), BF16),
            shape((width, rows), BF16),
            shape((width, rows), F32),
            shape((rows, width), F32),
            shape((rows, LANES), F32),
            *((shape((rows, TILE), BF16),) * (tiles - 1)),
            *((shape((slots, TILE), BF16),) * (tiles - 1)),
        ),
        [vmem] * 6 + [hbm] * 2,
        (
            pltpu.VMEM((2, *hot.shape), BF16),
            pltpu.SemaphoreType.DMA((2,)),
        ),
        cost=(8 * rows * (rows + slots) * width, 12 * rows * width + 2 * rows * rows),
    )(feats_kept, w_self_kept, bias_kept, slot, share, first_counts[0], *in_hbm(w_neigh, out_cot))
    own_counts = [first_counts[0], *counts[: tiles - 1]]
    far_counts = [first_counts[1], *counts[tiles - 1 :]]
    message = call(
        functools.partial(message_kernel, sizes),
        shape((slots, width), BF16),
        [vmem, vmem, pl.BlockSpec(memory_space=pl.ANY)],
    )(picked, hubs, own_total)
    remote = swap(message, PEERS)

    outputs, w_own, rest, message, low, edge_grad, bias_sum = call(
        functools.partial(joint_kernel, sizes),
        (
            pltpu.HBM((rows, width), BF16),
            shape((width, width), F32),
            shape((slots, width), F32),
            shape((width + slots, width), BF16),
            shape((rows, width), BF16),
            shape((rows, width), BF16),
            shape((8, width), F32),
        ),
        out_specs=(hbm,) + (vmem,) * 6,
        scratch=(
            pltpu.VMEM((rows, width), BF16),
            pltpu.VMEM((width, rows), BF16),
            pltpu.VMEM((rows, width), F32),
            pltpu.VMEM((2, width, width), F32),
            pltpu.SemaphoreType.DMA((rows // TILE,)),
        ),
        cost=(4 * rows * slots * width + 8 * rows * width * width, 16 * rows * width),
    )(
        remote,
        turned,
        own_total,
        self_part,
        *far_counts,
        share,
        share_column,
        w_neigh_kept,
        cot_kept,
    )

    received = other_side(message)
    feat_grad = call(
        own_grad_kernel,
        shape((rows, width), F32),
        cost=(2 * rows * rows * width + 2 * rows * width * width, 8 * rows * width),
    )(low, w_self_kept, edge_grad, *own_counts)
    message = call(
        side_sum_kernel,
        shape((peers, slab, width), BF16),
        [vmem, vmem, pl.BlockSpec(memory_space=pl.ANY)],
    )(w_own, received, feat_grad)
    slabs = swap(message, PEERS)
    message = call(
        functools.partial(peer_sum_kernel, sizes), shape((peers, slab + tall, width), BF16)
    )(slabs, rest, received, bias_sum)
    message = swap(message, PEERS)
    grad_feats = call(
        functools.partial(feat_grad_kernel, sizes, slab),
        shape((rows, width), BF16),
        cost=(4 * rows * slots * width, 6 * rows * width),
    )(message, places, feat_grad)
    unit_self, unit_neigh, unit_bias = call(
        functools.partial(unit_kernel, slab),
        (*((pltpu.HBM((width, width), F32),) * 2), pltpu.HBM((1, width), F32)),
        out_specs=(hbm,) * 3,
        scratch=(
            pltpu.VMEM((2, width, width), F32),
            pltpu.VMEM((1, width), F32),
            pltpu.SemaphoreType.DMA((3,)),
        ),
    )(message, other_side(message))
    return outputs, grad_feats, unit_self, unit_neigh, unit_bias.reshape(width)


def solution(mesh):
    doms, reps = mesh.shape["dom"], mesh.shape["rep"]
    split = jax.sharding.Mesh(mesh.devices.reshape(doms, reps // SIDES, SIDES), SPLIT_AXES)
    rows, whole = P(SPLIT_AXES, None), P()
    return jax.shard_map(
        functools.partial(on_device, doms, reps),
        mesh=split,
        in_specs=(rows, whole, whole, whole, rows, P(SPLIT_AXES), rows, P(SPLIT_AXES), rows),
        out_specs=(rows, rows, whole, whole, whole),
        check_vma=False,
    )
```

```python
import functools

import jax
import jax.numpy as jnp
from jax import lax
from jax.experimental import pallas as pl
from jax.experimental.pallas import tpu as pltpu
from jax.sharding import PartitionSpec as P

NORM_EPS = 1e-05
UNIT_EPS = 1e-06
SPLIT_AXES = ("far", "near", "pair", "side")
NEARS = SIDES = 2
PEERS = ("near", "pair", "far")
VMEM_LIMIT = 32 * 1024 * 1024
F32 = jnp.float32
BF16 = jnp.bfloat16
TILE = 256
STRIP = 16
PIECE = 32
LANES = 128
BIAS_ROWS = 2


def div_floor(value, size):
    if size & (size - 1) == 0:
        return lax.shift_right_arithmetic(value, jnp.int32(size.bit_length() - 1))
    return value // size


def remainder(value, size):
    if size & (size - 1) == 0:
        return value & jnp.int32(size - 1)
    return value - (value // size) * size


def matmul(lhs, rhs, lhs_dim=1, rhs_dim=0):
    return lax.dot_general(
        lhs, rhs, (((lhs_dim,), (rhs_dim,)), ((), ())), preferred_element_type=F32
    )


def peer_place(dom, pair, doms, pairs):
    near, far = remainder(dom, NEARS), div_floor(dom, NEARS)
    return (near * pairs + pair) * (doms // NEARS) + far


def iota(shape, dim):
    return lax.broadcasted_iota(jnp.int32, shape, dim)


def one_hot(rows, places):
    return jnp.where(iota((rows, places.shape[1]), 0) == places, F32(1.0), F32(0.0)).astype(BF16)


def fetch(pairs, sems):
    copies = [
        pltpu.make_async_copy(source, target, sems.at[number])
        for number, (source, target) in enumerate(pairs)
    ]
    for copy in copies:
        copy.start()
    return copies


def pick_kernel(sizes, hub_hbm, send_hbm, *refs):
    doms, reps, cap, hub_own, tall = sizes
    inputs, (rows_ref, hubs_ref, places_ref), refs = refs[:5], refs[5:8], refs[8:]
    kept, (slot_ref, share_ref, own_count_ref, far_count_ref), refs = refs[:3], refs[3:7], refs[7:]
    hub_ref, send_ref, degree_ref, edge_ref, hot_ref, sems = refs
    feats_ref = kept[0]
    targets = (hub_ref, send_ref, degree_ref, edge_ref, *kept)
    copies = fetch(zip((hub_hbm, send_hbm, *inputs), targets), sems)
    slots = doms * tall
    lane = iota(places_ref.shape, 1)
    row = remainder(lane, tall)

    def list_entries(dom, places):
        for entry in range(cap):
            places = jnp.where(lane == dom * tall + entry, send_ref[entry, dom], places)
        return places

    copies[0].wait()
    copies[1].wait()
    places = jnp.full(lane.shape, -1, jnp.int32)
    if doms <= 16:
        for dom in range(doms):
            places = list_entries(dom, places)
    else:
        places = lax.fori_loop(0, doms, list_entries, places)
    for entry in range(hub_own):
        for first, inside in ((cap, lane < slots), (cap + hub_own, lane >= slots)):
            places = jnp.where((row == first + entry) & inside, hub_ref[entry], places)
    places_ref[...] = places
    column = jnp.broadcast_to(places, (LANES, lane.shape[1])).T[: slots + 2 * tall, :]
    node = iota(column.shape, 1)
    chosen = [
        jnp.where(node + first == column, F32(1.0), F32(0.0)).astype(BF16)
        for first in range(0, feats_ref.shape[0], LANES)
    ]
    copies[2].wait()
    copies[3].wait()
    find_slots(sizes, degree_ref, edge_ref, slot_ref, share_ref)
    count_edges(slot_ref, own_count_ref, far_count_ref, hot_ref, slice(0, TILE))
    copies[4].wait()
    picked = matmul(jnp.concatenate(chosen, axis=1), feats_ref[...]).astype(BF16)
    rows_ref[...] = picked[:slots, :]
    hubs_ref[...] = picked[slots:, :]
    for copy in copies[5:]:
        copy.wait()


def message_kernel(sizes, rows_ref, hubs_ref, after_ref, message_ref):
    doms, reps, cap, hub_own, tall = sizes
    del after_ref
    rows = rows_ref[...].astype(F32)
    hubs = hubs_ref[...].astype(F32)[:tall, :]
    place = iota(hubs.shape, 0)
    pair = lax.axis_index("pair")
    pairs = reps // SIDES
    blocks = []
    for near in range(NEARS):
        for other in range(pairs):
            for dom in range(near, doms, NEARS):
                block = rows[dom * tall : (dom + 1) * tall, :]
                kept = (place >= cap) | (pair == other)
                blocks.append(jnp.where(kept, block, F32(0.0)) + hubs)
    message_ref[...] = jnp.concatenate(blocks, axis=0).astype(BF16)


def count_edges(slot_ref, own_count_ref, far_count_ref, hot_ref, nodes):
    fanout, rows = slot_ref.shape[0], own_count_ref.shape[0]
    highs = (rows + far_count_ref.shape[0]) // LANES
    low, high = [], []
    for k in range(fanout):
        slot = jnp.broadcast_to(slot_ref[k : k + 1, nodes], (STRIP, TILE))
        low.append(remainder(slot, LANES).astype(jnp.int16))
        high.append(div_floor(slot, LANES).astype(jnp.int16))
    for block in range(highs):
        for k in range(fanout):
            hot_ref[block * fanout + k] = jnp.where(high[k] == block, BF16(1.0), BF16(0.0))
    for strip in range(0, LANES, STRIP):
        numbers = (iota((STRIP, TILE), 0) + strip).astype(jnp.int16)
        hot = [jnp.where(numbers == low[k], BF16(1.0), BF16(0.0)) for k in range(fanout)]

        def count(block):
            total = hot[0] * hot_ref[block * fanout]
            for k in range(1, fanout):
                total = total + hot[k] * hot_ref[block * fanout + k]
            return total

        for block in range(rows // LANES):
            first = block * LANES + strip
            own_count_ref[first : first + STRIP, :] = count(block)
        far = far_count_ref.shape[0] // LANES
        if far <= 4:
            for block in range(far):
                first = block * LANES + strip
                far_count_ref[first : first + STRIP, :] = count(rows // LANES + block)
        else:

            @pl.loop(0, far)
            def far_block(block):
                first = pl.multiple_of(block * LANES + strip, STRIP)
                far_count_ref[pl.ds(first, STRIP), :] = count(rows // LANES + block)


def find_slots(sizes, degree_ref, edge_ref, slot_ref, share_ref):
    doms, reps, cap, hub_own, tall = sizes
    fanout, rows = edge_ref.shape
    hubs = doms * reps * hub_own
    source = edge_ref[...]
    hub = source - rows
    halo = hub - hubs
    chip = SIDES * hub_own
    entry = remainder(hub, chip) ^ (lax.axis_index("side") * hub_own)
    pairs = reps // SIDES
    owner = div_floor(hub, chip)
    peer = peer_place(div_floor(owner, pairs), remainder(owner, pairs), doms, pairs)
    hub_slot = rows + cap + peer * tall + entry
    peer = peer_place(div_floor(halo, cap), lax.axis_index("pair"), doms, pairs)
    halo_slot = rows + peer * tall + remainder(halo, cap)
    slot = jnp.where(source < rows, source, jnp.where(hub < hubs, hub_slot, halo_slot))
    valid = jnp.minimum(degree_ref[...], fanout)
    slot_ref[...] = jnp.where(iota((fanout, rows), 0) < valid, slot, -1)
    share_ref[...] = 1.0 / valid.astype(F32)


def own_kernel(tiles, feats_ref, w_self_ref, bias_ref, slot_ref, *refs):
    first_count_ref, inputs, kept, refs = refs[0], refs[1:3], refs[3:5], refs[5:]
    turned_ref, total_ref, preact_ref = refs[:3]
    own_refs, far_refs, (hot_ref, sems) = (
        refs[3 : 2 + tiles],
        refs[2 + tiles : 1 + 2 * tiles],
        refs[1 + 2 * tiles :],
    )
    copies = fetch(zip(inputs, kept), sems)
    turned_ref[...] = feats_ref[...].T

    def own_sums(number, count_ref):
        nodes = slice(number * TILE, (number + 1) * TILE)
        total_ref[:, nodes] = matmul(turned_ref[...], count_ref[...])
        preact_ref[nodes, :] = matmul(feats_ref[nodes, :], w_self_ref[...]) + bias_ref[...]

    counted = first_count_ref
    for number in range(1, tiles):
        nodes = slice(number * TILE, (number + 1) * TILE)
        own_ref, far_ref = own_refs[number - 1], far_refs[number - 1]
        count_edges(slot_ref, own_ref, far_ref, hot_ref.at[number % 2], nodes)
        own_sums(number - 1, counted)
        counted = own_ref
    own_sums(tiles - 1, counted)
    for copy in copies:
        copy.wait()


def joint_kernel(sizes, remote_ref, turned_ref, total_ref, self_ref, *refs):
    doms, reps, cap, hub_own, tall = sizes
    rows, width = self_ref.shape
    tiles = [slice(first, first + TILE) for first in range(0, rows, TILE)]
    count_refs, refs = refs[: len(tiles)], refs[len(tiles) :]
    (
        share_ref,
        w_neigh_ref,
        cot_ref,
        outputs_hbm,
        w_own_ref,
        rest_ref,
        message_ref,
        low_ref,
        edge_grad_ref,
        bias_ref,
        outputs_ref,
        mean_ref,
        preact_ref,
        w_grad_ref,
        sems,
    ) = refs
    table = remote_ref[...].T

    def before_head(number):
        nodes = tiles[number]
        mean = total_ref[:, nodes] + matmul(table, count_refs[number][...])
        mean = (mean * share_ref[:, nodes]).astype(BF16)
        mean_ref[:, nodes] = mean
        preact_ref[nodes, :] = self_ref[nodes, :] + matmul(mean, w_neigh_ref[...], 0, 0)

    def node_sums(numbers):
        nodes = slice(tiles[numbers[0]].start, tiles[numbers[-1]].stop)
        low = low_ref[nodes, :]
        return (
            matmul(turned_ref[:, nodes], low),
            matmul(mean_ref[:, nodes], low),
            sum(matmul(count_refs[k][...], edge_grad_ref[tiles[k], :]) for k in numbers),
        )

    bias_sum = jnp.zeros((8, width), F32)
    copies = []
    before_head(0)
    for number, nodes in enumerate(tiles):
        if number + 1 < len(tiles):
            before_head(number + 1)
        elif number:
            w_grad_ref[0], w_grad_ref[1], rest_ref[...] = node_sums(range(number))
        for start in range(nodes.start, nodes.stop, PIECE):
            piece = slice(start, start + PIECE)
            preact = preact_ref[piece, :]
            cot = cot_ref[piece, :].astype(F32)
            grown = jnp.exp(jnp.minimum(preact, 0.0))
            act = jnp.where(preact > 0.0, preact, grown - 1.0)
            square = jnp.sum(act * act, axis=1, keepdims=True)
            along = jnp.sum(act * cot, axis=1, keepdims=True)
            scale = lax.rsqrt(square * (1.0 / width) + NORM_EPS)
            outputs_ref[piece, :] = (act * scale).astype(BF16)
            pull = along * (scale * scale * scale) * (1.0 / width)
            grad_pre = (cot * scale - act * pull) * jnp.where(preact > 0.0, F32(1.0), grown)
            bias_sum = bias_sum + jnp.sum(grad_pre.reshape(PIECE // 8, 8, width), axis=0)
            low_ref[piece, :] = grad_pre.astype(BF16)
        copies += fetch(
            ((outputs_ref.at[nodes, :], outputs_hbm.at[nodes, :]),), sems.at[pl.ds(number, 1)]
        )
        share_column = jnp.broadcast_to(share_ref[:, nodes], (LANES, TILE)).T
        share_column = jnp.concatenate([share_column] * (width // LANES), axis=1)
        edge_grad = matmul(low_ref[nodes, :], w_neigh_ref[...], 1, 1) * share_column
        edge_grad_ref[nodes, :] = edge_grad.astype(BF16)

    w_self_sum, w_neigh_sum, remote = node_sums([len(tiles) - 1])
    if len(tiles) > 1:
        w_self_sum = w_self_sum + w_grad_ref[0]
        w_neigh_sum = w_neigh_sum + w_grad_ref[1]
        remote = remote + rest_ref[...]
    w_grad_ref[0] = w_self_sum
    w_grad_ref[1] = w_neigh_sum
    rest_ref[...] = remote
    bias_ref[...] = bias_sum
    bias_sum = jnp.broadcast_to(jnp.sum(bias_sum, axis=0, keepdims=True), (tall, width))
    bias_high = bias_sum.astype(BF16).astype(F32)
    place = iota((tall, width), 0)
    bias_rows = jnp.where(place == cap, bias_high, bias_sum - bias_high)
    bias_rows = jnp.where(place < cap, F32(0.0), bias_rows)
    message = remote.reshape(-1, tall, width)
    message = jnp.where((place < cap + hub_own)[None], bias_rows[None], message)
    message_ref[width:, :] = message.reshape(remote.shape).astype(BF16)
    mine = lax.axis_index("side")
    w_own_ref[...] = w_grad_ref[mine]
    message_ref[:width, :] = w_grad_ref[1 - mine].astype(BF16)
    for copy in copies:
        copy.wait()


def own_grad_kernel(low_ref, w_self_ref, edge_grad_ref, *refs):
    *count_refs, feat_grad_ref = refs
    for first in range(0, low_ref.shape[0], TILE):
        nodes = slice(first, first + TILE)
        total = matmul(low_ref[nodes, :], w_self_ref[...], 1, 1)
        for number, count_ref in enumerate(count_refs):
            edges = edge_grad_ref[number * TILE : (number + 1) * TILE, :]
            total = total + matmul(count_ref[nodes, :], edges)
        feat_grad_ref[nodes, :] = total


def side_sum_kernel(own_ref, received_ref, after_ref, message_ref):
    del after_ref
    peers, slab, width = message_ref.shape
    w_grad = own_ref[...] + received_ref[:width, :].astype(F32)
    owners = width // slab
    w_grad = w_grad.reshape(owners, slab, width)
    if owners < peers:
        w_grad = jnp.concatenate([w_grad, jnp.zeros((peers - owners, slab, width), F32)], axis=0)
    message_ref[...] = w_grad.astype(BF16)


def peer_sum_kernel(sizes, slabs_ref, own_ref, received_ref, bias_ref, message_ref):
    doms, reps, cap, hub_own, tall = sizes
    peers, slab, width = slabs_ref.shape
    total = jnp.sum(slabs_ref[...].astype(F32), axis=0)
    received_ref = received_ref.at[width:, :]
    size = min(peers * tall, LANES)
    to, source = iota((size, size), 0), iota((size, size), 1)
    entry = remainder(to, tall) - cap
    moved = (source == to + hub_own) & (entry >= 0) & (entry < hub_own)
    moved = jnp.where(moved, F32(1.0), F32(0.0)).astype(BF16)
    rest = own_ref[...] + jnp.concatenate(
        [
            matmul(moved, received_ref[first : first + size, :])
            for first in range(0, peers * tall, size)
        ],
        axis=0,
    )
    place = iota((tall, width), 0)
    bias = received_ref[: 2 * tall, :].astype(F32)[:tall, :]
    bias = jnp.where((place >= cap) & (place < cap + BIAS_ROWS), bias, F32(0.0)) + bias_ref[...]
    bias = jnp.broadcast_to(jnp.sum(bias, axis=0, keepdims=True), (tall, width))
    bias_high = bias.astype(BF16).astype(F32)
    bias_rows = jnp.where(place == tall - 1, bias - bias_high, bias_high)
    rest = rest.reshape(peers, tall, width)
    rest = jnp.where((place < tall - BIAS_ROWS)[None], rest, bias_rows[None])
    total = jnp.broadcast_to(total[None], (peers, slab, width))
    message_ref[...] = jnp.concatenate([total, rest], axis=1).astype(BF16)


def feat_grad_kernel(sizes, slab, message_ref, places_ref, feat_grad_ref, out_ref):
    doms, reps, cap, hub_own, tall = sizes
    rows, width = out_ref.shape
    pairs = reps // SIDES
    returned = message_ref[...].astype(F32)[:, slab:, :]
    returned = returned.reshape(NEARS, pairs, doms // NEARS, tall, width)
    returned = [
        jnp.concatenate(
            [returned[dom % NEARS, pair, dom // NEARS] for dom in range(doms)], axis=0
        ).astype(BF16)
        for pair in range(pairs)
    ]
    chosen = one_hot(rows, places_ref[:, : doms * tall])
    for first in range(0, rows, TILE):
        nodes = slice(first, first + TILE)
        total = feat_grad_ref[nodes, :]
        for part in returned:
            total = total + matmul(chosen[nodes, :], part)
        out_ref[nodes, :] = total.astype(BF16)


def unit_kernel(slab, mine_ref, other_ref, self_hbm, neigh_hbm, bias_hbm, units_ref, bias_ref, sems):
    side = lax.axis_index("side")
    _, size, width = units_ref.shape
    bias = jnp.sum(mine_ref[...].astype(F32)[:, slab:, :], axis=0)[-BIAS_ROWS:, :]
    bias = jnp.sum(bias, axis=0, keepdims=True)
    bias_ref[...] = bias * lax.rsqrt(jnp.mean(bias * bias, axis=1, keepdims=True) + UNIT_EPS)
    copies = [
        pltpu.make_async_copy(source, target, sems.at[number])
        for number, (source, target) in enumerate(
            ((units_ref.at[0], self_hbm), (units_ref.at[1], neigh_hbm), (bias_ref, bias_hbm))
        )
    ]
    copies[2].start()
    for place, grad_ref in ((side, mine_ref), (1 - side, other_ref)):
        grad = grad_ref[: size // slab].astype(F32)[:, :slab, :].reshape(size, width)
        square = jnp.sum(jnp.sum(grad * grad, axis=0, keepdims=True), axis=1, keepdims=True)
        units_ref[place] = grad * lax.rsqrt(square * (1.0 / grad.size) + UNIT_EPS)
        for number, copy in enumerate(copies[:2]):
            pl.when(place == number)(copy.start)
    for copy in copies:
        copy.wait()


def call(kernel, out_shape, in_specs=None, scratch=(), cost=(0, 0), out_specs=None):
    specs = {"in_specs": in_specs, "out_specs": out_specs}
    return pl.pallas_call(
        kernel,
        out_shape=out_shape,
        **{name: spec for name, spec in specs.items() if spec is not None},
        scratch_shapes=list(scratch),
        compiler_params=pltpu.CompilerParams(vmem_limit_bytes=VMEM_LIMIT),
        cost_estimate=pl.CostEstimate(flops=cost[0], bytes_accessed=cost[1], transcendentals=0),
    )


def in_hbm(*arrays):
    return [pltpu.with_memory_space_constraint(array, pltpu.HBM) for array in arrays]


def swap(array, axes):
    return lax.all_to_all(array, axes, split_axis=0, concat_axis=0, tiled=True)


def other_side(array):
    return lax.ppermute(array, "side", [(0, 1), (1, 0)])


def on_device(
    doms, reps, feats, w_self, w_neigh, bias, out_cot, degree, edge_src, hub_rows, send_rows
):
    rows, width = feats.shape
    fanout = edge_src.shape[1]
    cap, hub_own = send_rows.shape[1], hub_rows.shape[0]
    peers = doms * reps // SIDES
    tall = cap + SIDES * hub_own
    if tall % 8 or tall < cap + hub_own + BIAS_ROWS or hub_own & (hub_own - 1):
        raise ValueError("message height")
    slots = peers * tall
    slab = max(8, width // peers)
    sizes = (doms, reps, cap, hub_own, tall)
    shape = jax.ShapeDtypeStruct
    hbm = pl.BlockSpec(memory_space=pltpu.HBM)
    vmem = pl.BlockSpec(memory_space=pltpu.VMEM)

    tiles = rows // TILE
    hot = pltpu.VMEM(((rows + slots) // LANES * fanout, STRIP, TILE), BF16)
    picked, hubs, places, feats_kept, w_self_kept, bias_kept, slot, share, *first_counts = call(
        functools.partial(pick_kernel, sizes),
        (
            shape((doms * tall, width), BF16),
            shape((2 * tall, width), BF16),
            shape((1, -(-(doms + 2) * tall // LANES) * LANES), jnp.int32),
            shape((rows, width), BF16),
            shape((width, width), BF16),
            shape((1, width), F32),
            shape((fanout, rows), jnp.int32),
            shape((1, rows), F32),
            shape((rows, TILE), BF16),
            shape((slots, TILE), BF16),
        ),
        [hbm] * 7,
        (
            pltpu.SMEM((hub_own,), jnp.int32),
            pltpu.SMEM((cap, doms), jnp.int32),
            pltpu.VMEM((1, rows), jnp.int32),
            pltpu.VMEM((fanout, rows), jnp.int32),
            hot,
            pltpu.SemaphoreType.DMA((7,)),
        ),
        cost=(2 * rows * slots * width, 2 * rows * width),
    )(
        *in_hbm(
            hub_rows,
            send_rows.T,
            degree.reshape(1, rows),
            edge_src.T,
            feats,
            w_self,
            bias.reshape(1, width),
        )
    )
    hubs = other_side(hubs)
    w_neigh_kept, cot_kept, turned, own_total, self_part, *counts = call(
        functools.partial(own_kernel, tiles),
        (
            shape((width, width), BF16),
            shape((rows, width), BF16),
            shape((width, rows), BF16),
            shape((width, rows), F32),
            shape((rows, width), F32),
            *((shape((rows, TILE), BF16),) * (tiles - 1)),
            *((shape((slots, TILE), BF16),) * (tiles - 1)),
        ),
        [vmem] * 5 + [hbm] * 2,
        (
            pltpu.VMEM((2, *hot.shape), BF16),
            pltpu.SemaphoreType.DMA((2,)),
        ),
        cost=(8 * rows * (rows + slots) * width, 12 * rows * width + 2 * rows * rows),
    )(feats_kept, w_self_kept, bias_kept, slot, first_counts[0], *in_hbm(w_neigh, out_cot))
    own_counts = [first_counts[0], *counts[: tiles - 1]]
    far_counts = [first_counts[1], *counts[tiles - 1 :]]
    message = call(
        functools.partial(message_kernel, sizes),
        shape((slots, width), BF16),
        [vmem, vmem, pl.BlockSpec(memory_space=pl.ANY)],
    )(picked, hubs, own_total)
    remote = swap(message, PEERS)

    outputs, w_own, rest, message, low, edge_grad, bias_sum = call(
        functools.partial(joint_kernel, sizes),
        (
            pltpu.HBM((rows, width), BF16),
            shape((width, width), F32),
            shape((slots, width), F32),
            shape((width + slots, width), BF16),
            shape((rows, width), BF16),
            shape((rows, width), BF16),
            shape((8, width), F32),
        ),
        out_specs=(hbm,) + (vmem,) * 6,
        scratch=(
            pltpu.VMEM((rows, width), BF16),
            pltpu.VMEM((width, rows), BF16),
            pltpu.VMEM((rows, width), F32),
            pltpu.VMEM((2, width, width), F32),
            pltpu.SemaphoreType.DMA((rows // TILE,)),
        ),
        cost=(4 * rows * slots * width + 8 * rows * width * width, 16 * rows * width),
    )(remote, turned, own_total, self_part, *far_counts, share, w_neigh_kept, cot_kept)

    received = other_side(message)
    feat_grad = call(
        own_grad_kernel,
        shape((rows, width), F32),
        cost=(2 * rows * rows * width + 2 * rows * width * width, 8 * rows * width),
    )(low, w_self_kept, edge_grad, *own_counts)
    message = call(
        side_sum_kernel,
        shape((peers, slab, width), BF16),
        [vmem, vmem, pl.BlockSpec(memory_space=pl.ANY)],
    )(w_own, received, feat_grad)
    slabs = swap(message, PEERS)
    message = call(
        functools.partial(peer_sum_kernel, sizes), shape((peers, slab + tall, width), BF16)
    )(slabs, rest, received, bias_sum)
    message = swap(message, PEERS)
    grad_feats = call(
        functools.partial(feat_grad_kernel, sizes, slab),
        shape((rows, width), BF16),
        cost=(4 * rows * slots * width, 6 * rows * width),
    )(message, places, feat_grad)
    unit_self, unit_neigh, unit_bias = call(
        functools.partial(unit_kernel, slab),
        (*((pltpu.HBM((width, width), F32),) * 2), pltpu.HBM((1, width), F32)),
        out_specs=(hbm,) * 3,
        scratch=(
            pltpu.VMEM((2, width, width), F32),
            pltpu.VMEM((1, width), F32),
            pltpu.SemaphoreType.DMA((3,)),
        ),
    )(message, other_side(message))
    return outputs, grad_feats, unit_self, unit_neigh, unit_bias.reshape(width)


def solution(mesh):
    doms, reps = mesh.shape["dom"], mesh.shape["rep"]
    shape = (doms // NEARS, NEARS, reps // SIDES, SIDES)
    split = jax.sharding.Mesh(mesh.devices.reshape(shape), SPLIT_AXES)
    rows, whole = P(SPLIT_AXES, None), P()
    return jax.shard_map(
        functools.partial(on_device, doms, reps),
        mesh=split,
        in_specs=(rows, whole, whole, whole, rows, P(SPLIT_AXES), rows, P(SPLIT_AXES), rows),
        out_specs=(rows, rows, whole, whole, whole),
        check_vma=False,
    )
```

```python
import functools

import jax
import jax.numpy as jnp
from jax import lax
from jax.experimental import pallas as pl
from jax.experimental.pallas import tpu as pltpu
from jax.sharding import PartitionSpec as P

NORM_EPS = 1e-05
UNIT_EPS = 1e-06
SPLIT_AXES = ("dom", "pair", "side")
PEERS = ("dom", "pair")
SIDES = 2
VMEM_LIMIT = 32 * 1024 * 1024
F32 = jnp.float32
BF16 = jnp.bfloat16
TILE = 256
STRIP = 16
PIECE = 32
LANES = 128
BIAS_ROWS = 2


def div_floor(value, size):
    if size & (size - 1) == 0:
        return lax.shift_right_arithmetic(value, jnp.int32(size.bit_length() - 1))
    return value // size


def remainder(value, size):
    if size & (size - 1) == 0:
        return value & jnp.int32(size - 1)
    return value - (value // size) * size


def matmul(lhs, rhs, lhs_dim=1, rhs_dim=0):
    return lax.dot_general(
        lhs, rhs, (((lhs_dim,), (rhs_dim,)), ((), ())), preferred_element_type=F32
    )


def iota(shape, dim):
    return lax.broadcasted_iota(jnp.int32, shape, dim)


def one_hot(rows, places):
    return jnp.where(iota((rows, places.shape[1]), 0) == places, F32(1.0), F32(0.0)).astype(BF16)


def fetch(pairs, sems):
    copies = [
        pltpu.make_async_copy(source, target, sems.at[number])
        for number, (source, target) in enumerate(pairs)
    ]
    for copy in copies:
        copy.start()
    return copies


def pick_kernel(sizes, hub_hbm, send_hbm, *refs):
    doms, reps, cap, hub_own, tall = sizes
    inputs, (rows_ref, hubs_ref, places_ref), refs = refs[:5], refs[5:8], refs[8:]
    kept, (slot_ref, share_ref, own_count_ref, far_count_ref), refs = refs[:3], refs[3:7], refs[7:]
    hub_ref, send_ref, degree_ref, edge_ref, hot_ref, sems = refs
    feats_ref = kept[0]
    targets = (hub_ref, send_ref, degree_ref, edge_ref, *kept)
    copies = fetch(zip((hub_hbm, send_hbm, *inputs), targets), sems)
    slots = doms * tall
    lane = iota(places_ref.shape, 1)
    row = remainder(lane, tall)

    def list_entries(dom, places):
        for entry in range(cap):
            places = jnp.where(lane == dom * tall + entry, send_ref[entry, dom], places)
        return places

    copies[0].wait()
    copies[1].wait()
    places = jnp.full(lane.shape, -1, jnp.int32)
    if doms <= 16:
        for dom in range(doms):
            places = list_entries(dom, places)
    else:
        places = lax.fori_loop(0, doms, list_entries, places)
    for entry in range(hub_own):
        for first, inside in ((cap, lane < slots), (cap + hub_own, lane >= slots)):
            places = jnp.where((row == first + entry) & inside, hub_ref[entry], places)
    places_ref[...] = places
    column = jnp.broadcast_to(places, (LANES, lane.shape[1])).T[: slots + 2 * tall, :]
    node = iota(column.shape, 1)
    chosen = [
        jnp.where(node + first == column, F32(1.0), F32(0.0)).astype(BF16)
        for first in range(0, feats_ref.shape[0], LANES)
    ]
    copies[2].wait()
    copies[3].wait()
    find_slots(sizes, degree_ref, edge_ref, slot_ref, share_ref)
    count_edges(slot_ref, own_count_ref, far_count_ref, hot_ref, slice(0, TILE))
    copies[4].wait()
    picked = matmul(jnp.concatenate(chosen, axis=1), feats_ref[...]).astype(BF16)
    rows_ref[...] = picked[:slots, :]
    hubs_ref[...] = picked[slots:, :]
    for copy in copies[5:]:
        copy.wait()


def message_kernel(sizes, rows_ref, hubs_ref, after_ref, message_ref):
    doms, reps, cap, hub_own, tall = sizes
    del after_ref
    rows = rows_ref[...].astype(F32)
    hubs = hubs_ref[...].astype(F32)[:tall, :]
    place = iota(hubs.shape, 0)
    pair = lax.axis_index("pair")
    pairs = reps // SIDES
    for dom in range(doms):
        block = rows[dom * tall : (dom + 1) * tall, :]
        blocks = [
            jnp.where((place >= cap) | (pair == other), block, F32(0.0)) + hubs
            for other in range(pairs)
        ]
        first = dom * pairs * tall
        message_ref[first : first + pairs * tall, :] = jnp.concatenate(blocks, axis=0).astype(BF16)


def count_edges(slot_ref, own_count_ref, far_count_ref, hot_ref, nodes):
    fanout, rows = slot_ref.shape[0], own_count_ref.shape[0]
    highs = (rows + far_count_ref.shape[0]) // LANES
    low, high = [], []
    for k in range(fanout):
        slot = jnp.broadcast_to(slot_ref[k : k + 1, nodes], (STRIP, TILE))
        low.append(remainder(slot, LANES).astype(jnp.int16))
        high.append(div_floor(slot, LANES).astype(jnp.int16))
    for block in range(highs):
        for k in range(fanout):
            hot_ref[block * fanout + k] = jnp.where(high[k] == block, BF16(1.0), BF16(0.0))
    for strip in range(0, LANES, STRIP):
        numbers = (iota((STRIP, TILE), 0) + strip).astype(jnp.int16)
        hot = [jnp.where(numbers == low[k], BF16(1.0), BF16(0.0)) for k in range(fanout)]

        def count(block):
            total = hot[0] * hot_ref[block * fanout]
            for k in range(1, fanout):
                total = total + hot[k] * hot_ref[block * fanout + k]
            return total

        for block in range(rows // LANES):
            first = block * LANES + strip
            own_count_ref[first : first + STRIP, :] = count(block)
        far = far_count_ref.shape[0] // LANES
        if far <= 4:
            for block in range(far):
                first = block * LANES + strip
                far_count_ref[first : first + STRIP, :] = count(rows // LANES + block)
        else:

            @pl.loop(0, far)
            def far_block(block):
                first = pl.multiple_of(block * LANES + strip, STRIP)
                far_count_ref[pl.ds(first, STRIP), :] = count(rows // LANES + block)


def find_slots(sizes, degree_ref, edge_ref, slot_ref, share_ref):
    doms, reps, cap, hub_own, tall = sizes
    fanout, rows = edge_ref.shape
    hubs = doms * reps * hub_own
    source = edge_ref[...]
    hub = source - rows
    halo = hub - hubs
    chip = SIDES * hub_own
    entry = remainder(hub, chip) ^ (lax.axis_index("side") * hub_own)
    hub_slot = rows + cap + div_floor(hub, chip) * tall + entry
    peer = div_floor(halo, cap) * (reps // SIDES) + lax.axis_index("pair")
    halo_slot = rows + peer * tall + remainder(halo, cap)
    slot = jnp.where(source < rows, source, jnp.where(hub < hubs, hub_slot, halo_slot))
    valid = jnp.minimum(degree_ref[...], fanout)
    slot_ref[...] = jnp.where(iota((fanout, rows), 0) < valid, slot, -1)
    share_ref[...] = 1.0 / valid.astype(F32)


def own_kernel(tiles, feats_ref, w_self_ref, bias_ref, slot_ref, *refs):
    first_count_ref, inputs, kept, refs = refs[0], refs[1:3], refs[3:5], refs[5:]
    turned_ref, total_ref, preact_ref = refs[:3]
    own_refs, far_refs, (hot_ref, sems) = (
        refs[3 : 2 + tiles],
        refs[2 + tiles : 1 + 2 * tiles],
        refs[1 + 2 * tiles :],
    )
    copies = fetch(zip(inputs, kept), sems)
    turned_ref[...] = feats_ref[...].T

    def own_sums(number, count_ref):
        nodes = slice(number * TILE, (number + 1) * TILE)
        total_ref[:, nodes] = matmul(turned_ref[...], count_ref[...])
        preact_ref[nodes, :] = matmul(feats_ref[nodes, :], w_self_ref[...]) + bias_ref[...]

    counted = first_count_ref
    for number in range(1, tiles):
        nodes = slice(number * TILE, (number + 1) * TILE)
        own_ref, far_ref = own_refs[number - 1], far_refs[number - 1]
        count_edges(slot_ref, own_ref, far_ref, hot_ref.at[number % 2], nodes)
        own_sums(number - 1, counted)
        counted = own_ref
    own_sums(tiles - 1, counted)
    for copy in copies:
        copy.wait()


def joint_kernel(sizes, remote_ref, turned_ref, total_ref, self_ref, *refs):
    doms, reps, cap, hub_own, tall = sizes
    rows, width = self_ref.shape
    tiles = [slice(first, first + TILE) for first in range(0, rows, TILE)]
    count_refs, refs = refs[: len(tiles)], refs[len(tiles) :]
    (
        share_ref,
        w_neigh_ref,
        cot_ref,
        outputs_hbm,
        w_own_ref,
        rest_ref,
        message_ref,
        low_ref,
        edge_grad_ref,
        bias_ref,
        outputs_ref,
        mean_ref,
        preact_ref,
        w_grad_ref,
        sems,
    ) = refs
    table = remote_ref[...].T

    def before_head(number):
        nodes = tiles[number]
        mean = total_ref[:, nodes] + matmul(table, count_refs[number][...])
        mean = (mean * share_ref[:, nodes]).astype(BF16)
        mean_ref[:, nodes] = mean
        preact_ref[nodes, :] = self_ref[nodes, :] + matmul(mean, w_neigh_ref[...], 0, 0)

    def node_sums(numbers):
        nodes = slice(tiles[numbers[0]].start, tiles[numbers[-1]].stop)
        low = low_ref[nodes, :]
        return (
            matmul(turned_ref[:, nodes], low),
            matmul(mean_ref[:, nodes], low),
            sum(matmul(count_refs[k][...], edge_grad_ref[tiles[k], :]) for k in numbers),
        )

    def start_head(piece):
        preact = preact_ref[piece, :]
        grown = jnp.exp(jnp.minimum(preact, 0.0))
        act = jnp.where(preact > 0.0, preact, grown - 1.0)
        slope = jnp.where(preact > 0.0, F32(1.0), grown)
        square = jnp.sum(act * act, axis=1, keepdims=True)
        along = jnp.sum(act * cot_ref[piece, :].astype(F32), axis=1, keepdims=True)
        return act, slope, square, along

    def finish_head(piece, act, slope, square, along):
        scale = lax.rsqrt(square * (1.0 / width) + NORM_EPS)
        outputs_ref[piece, :] = (act * scale).astype(BF16)
        pull = along * (scale * scale * scale) * (1.0 / width)
        grad_pre = (cot_ref[piece, :].astype(F32) * scale - act * pull) * slope
        low_ref[piece, :] = grad_pre.astype(BF16)
        return jnp.sum(grad_pre.reshape(PIECE // 8, 8, width), axis=0)

    pieces = [slice(start, start + PIECE) for start in range(0, rows, PIECE)]
    bias_sum = jnp.zeros((8, width), F32)
    copies = []
    before_head(0)
    started = start_head(pieces[0])
    for order, piece in enumerate(pieces):
        number = piece.start // TILE
        if piece.start % TILE == 0:
            if number + 1 < len(tiles):
                before_head(number + 1)
            elif number:
                w_grad_ref[0], w_grad_ref[1], rest_ref[...] = node_sums(range(number))
        ahead = start_head(pieces[order + 1]) if order + 1 < len(pieces) else None
        bias_sum = bias_sum + finish_head(piece, *started)
        started = ahead
        if piece.stop % TILE == 0:
            nodes = tiles[number]
            copies += fetch(
                ((outputs_ref.at[nodes, :], outputs_hbm.at[nodes, :]),), sems.at[pl.ds(number, 1)]
            )
            share_column = jnp.broadcast_to(share_ref[:, nodes], (LANES, TILE)).T
            share_column = jnp.concatenate([share_column] * (width // LANES), axis=1)
            edge_grad = matmul(low_ref[nodes, :], w_neigh_ref[...], 1, 1) * share_column
            edge_grad_ref[nodes, :] = edge_grad.astype(BF16)

    w_self_sum, w_neigh_sum, remote = node_sums([len(tiles) - 1])
    if len(tiles) > 1:
        w_self_sum = w_self_sum + w_grad_ref[0]
        w_neigh_sum = w_neigh_sum + w_grad_ref[1]
        remote = remote + rest_ref[...]
    w_grad_ref[0] = w_self_sum
    w_grad_ref[1] = w_neigh_sum
    rest_ref[...] = remote
    bias_ref[...] = bias_sum
    bias_sum = jnp.broadcast_to(jnp.sum(bias_sum, axis=0, keepdims=True), (tall, width))
    bias_high = bias_sum.astype(BF16).astype(F32)
    place = iota((tall, width), 0)
    bias_rows = jnp.where(place == cap, bias_high, bias_sum - bias_high)
    bias_rows = jnp.where(place < cap, F32(0.0), bias_rows)
    message = remote.reshape(-1, tall, width)
    message = jnp.where((place < cap + hub_own)[None], bias_rows[None], message)
    message_ref[width:, :] = message.reshape(remote.shape).astype(BF16)
    mine = lax.axis_index("side")
    w_own_ref[...] = w_grad_ref[mine]
    message_ref[:width, :] = w_grad_ref[1 - mine].astype(BF16)
    for copy in copies:
        copy.wait()


def own_grad_kernel(low_ref, w_self_ref, edge_grad_ref, *refs):
    *count_refs, feat_grad_ref = refs
    for first in range(0, low_ref.shape[0], TILE):
        nodes = slice(first, first + TILE)
        total = matmul(low_ref[nodes, :], w_self_ref[...], 1, 1)
        for number, count_ref in enumerate(count_refs):
            edges = edge_grad_ref[number * TILE : (number + 1) * TILE, :]
            total = total + matmul(count_ref[nodes, :], edges)
        feat_grad_ref[nodes, :] = total


def side_sum_kernel(own_ref, received_ref, after_ref, message_ref):
    del after_ref
    peers, slab, width = message_ref.shape
    w_grad = own_ref[...] + received_ref[:width, :].astype(F32)
    owners = width // slab
    w_grad = w_grad.reshape(owners, slab, width)
    if owners < peers:
        w_grad = jnp.concatenate([w_grad, jnp.zeros((peers - owners, slab, width), F32)], axis=0)
    message_ref[...] = w_grad.astype(BF16)


def peer_sum_kernel(sizes, slabs_ref, own_ref, received_ref, bias_ref, message_ref):
    doms, reps, cap, hub_own, tall = sizes
    peers, slab, width = slabs_ref.shape
    total = jnp.sum(slabs_ref[...].astype(F32), axis=0)
    received_ref = received_ref.at[width:, :]
    size = min(peers * tall, LANES)
    to, source = iota((size, size), 0), iota((size, size), 1)
    entry = remainder(to, tall) - cap
    moved = (source == to + hub_own) & (entry >= 0) & (entry < hub_own)
    moved = jnp.where(moved, F32(1.0), F32(0.0)).astype(BF16)
    rest = own_ref[...] + jnp.concatenate(
        [
            matmul(moved, received_ref[first : first + size, :])
            for first in range(0, peers * tall, size)
        ],
        axis=0,
    )
    place = iota((tall, width), 0)
    bias = received_ref[: 2 * tall, :].astype(F32)[:tall, :]
    bias = jnp.where((place >= cap) & (place < cap + BIAS_ROWS), bias, F32(0.0)) + bias_ref[...]
    bias = jnp.broadcast_to(jnp.sum(bias, axis=0, keepdims=True), (tall, width))
    bias_high = bias.astype(BF16).astype(F32)
    bias_rows = jnp.where(place == tall - 1, bias - bias_high, bias_high)
    rest = rest.reshape(peers, tall, width)
    rest = jnp.where((place < tall - BIAS_ROWS)[None], rest, bias_rows[None])
    total = jnp.broadcast_to(total[None], (peers, slab, width))
    message_ref[...] = jnp.concatenate([total, rest], axis=1).astype(BF16)


def feat_grad_kernel(sizes, slab, message_ref, places_ref, feat_grad_ref, out_ref):
    doms, reps, cap, hub_own, tall = sizes
    rows, width = out_ref.shape
    pairs = reps // SIDES
    returned = message_ref[...].astype(F32)[:, slab:, :].reshape(doms, pairs, tall, width)
    returned = [
        returned[:, pair].reshape(doms * tall, width).astype(BF16) for pair in range(pairs)
    ]
    chosen = one_hot(rows, places_ref[:, : doms * tall])
    for first in range(0, rows, TILE):
        nodes = slice(first, first + TILE)
        total = feat_grad_ref[nodes, :]
        for part in returned:
            total = total + matmul(chosen[nodes, :], part)
        out_ref[nodes, :] = total.astype(BF16)


def unit_kernel(slab, mine_ref, other_ref, self_hbm, neigh_hbm, bias_hbm, units_ref, bias_ref, sems):
    side = lax.axis_index("side")
    _, size, width = units_ref.shape
    bias = jnp.sum(mine_ref[...].astype(F32)[:, slab:, :], axis=0)[-BIAS_ROWS:, :]
    bias = jnp.sum(bias, axis=0, keepdims=True)
    bias_ref[...] = bias * lax.rsqrt(jnp.mean(bias * bias, axis=1, keepdims=True) + UNIT_EPS)
    copies = [
        pltpu.make_async_copy(source, target, sems.at[number])
        for number, (source, target) in enumerate(
            ((units_ref.at[0], self_hbm), (units_ref.at[1], neigh_hbm), (bias_ref, bias_hbm))
        )
    ]
    copies[2].start()
    for place, grad_ref in ((side, mine_ref), (1 - side, other_ref)):
        grad = grad_ref[: size // slab].astype(F32)[:, :slab, :].reshape(size, width)
        square = jnp.sum(jnp.sum(grad * grad, axis=0, keepdims=True), axis=1, keepdims=True)
        units_ref[place] = grad * lax.rsqrt(square * (1.0 / grad.size) + UNIT_EPS)
        for number, copy in enumerate(copies[:2]):
            pl.when(place == number)(copy.start)
    for copy in copies:
        copy.wait()


def call(kernel, out_shape, in_specs=None, scratch=(), cost=(0, 0), out_specs=None):
    specs = {"in_specs": in_specs, "out_specs": out_specs}
    return pl.pallas_call(
        kernel,
        out_shape=out_shape,
        **{name: spec for name, spec in specs.items() if spec is not None},
        scratch_shapes=list(scratch),
        compiler_params=pltpu.CompilerParams(vmem_limit_bytes=VMEM_LIMIT),
        cost_estimate=pl.CostEstimate(flops=cost[0], bytes_accessed=cost[1], transcendentals=0),
    )


def in_hbm(*arrays):
    return [pltpu.with_memory_space_constraint(array, pltpu.HBM) for array in arrays]


def swap(array, axes):
    return lax.all_to_all(array, axes, split_axis=0, concat_axis=0, tiled=True)


def other_side(array):
    return lax.ppermute(array, "side", [(0, 1), (1, 0)])


def on_device(
    doms, reps, feats, w_self, w_neigh, bias, out_cot, degree, edge_src, hub_rows, send_rows
):
    rows, width = feats.shape
    fanout = edge_src.shape[1]
    cap, hub_own = send_rows.shape[1], hub_rows.shape[0]
    peers = doms * reps // SIDES
    tall = cap + SIDES * hub_own
    if tall % 8 or tall < cap + hub_own + BIAS_ROWS or hub_own & (hub_own - 1):
        raise ValueError("message height")
    slots = peers * tall
    slab = max(8, width // peers)
    sizes = (doms, reps, cap, hub_own, tall)
    shape = jax.ShapeDtypeStruct
    hbm = pl.BlockSpec(memory_space=pltpu.HBM)
    vmem = pl.BlockSpec(memory_space=pltpu.VMEM)

    tiles = rows // TILE
    hot = pltpu.VMEM(((rows + slots) // LANES * fanout, STRIP, TILE), BF16)
    picked, hubs, places, feats_kept, w_self_kept, bias_kept, slot, share, *first_counts = call(
        functools.partial(pick_kernel, sizes),
        (
            shape((doms * tall, width), BF16),
            shape((2 * tall, width), BF16),
            shape((1, -(-(doms + 2) * tall // LANES) * LANES), jnp.int32),
            shape((rows, width), BF16),
            shape((width, width), BF16),
            shape((1, width), F32),
            shape((fanout, rows), jnp.int32),
            shape((1, rows), F32),
            shape((rows, TILE), BF16),
            shape((slots, TILE), BF16),
        ),
        [hbm] * 7,
        (
            pltpu.SMEM((hub_own,), jnp.int32),
            pltpu.SMEM((cap, doms), jnp.int32),
            pltpu.VMEM((1, rows), jnp.int32),
            pltpu.VMEM((fanout, rows), jnp.int32),
            hot,
            pltpu.SemaphoreType.DMA((7,)),
        ),
        cost=(2 * rows * slots * width, 2 * rows * width),
    )(
        *in_hbm(
            hub_rows,
            send_rows.T,
            degree.reshape(1, rows),
            edge_src.T,
            feats,
            w_self,
            bias.reshape(1, width),
        )
    )
    hubs = other_side(hubs)
    w_neigh_kept, cot_kept, turned, own_total, self_part, *counts = call(
        functools.partial(own_kernel, tiles),
        (
            shape((width, width), BF16),
            shape((rows, width), BF16),
            shape((width, rows), BF16),
            shape((width, rows), F32),
            shape((rows, width), F32),
            *((shape((rows, TILE), BF16),) * (tiles - 1)),
            *((shape((slots, TILE), BF16),) * (tiles - 1)),
        ),
        [vmem] * 5 + [hbm] * 2,
        (
            pltpu.VMEM((2, *hot.shape), BF16),
            pltpu.SemaphoreType.DMA((2,)),
        ),
        cost=(8 * rows * (rows + slots) * width, 12 * rows * width + 2 * rows * rows),
    )(feats_kept, w_self_kept, bias_kept, slot, first_counts[0], *in_hbm(w_neigh, out_cot))
    own_counts = [first_counts[0], *counts[: tiles - 1]]
    far_counts = [first_counts[1], *counts[tiles - 1 :]]
    message = call(
        functools.partial(message_kernel, sizes),
        shape((slots, width), BF16),
        [vmem, vmem, pl.BlockSpec(memory_space=pl.ANY)],
    )(picked, hubs, own_total)
    remote = swap(message, PEERS)

    outputs, w_own, rest, message, low, edge_grad, bias_sum = call(
        functools.partial(joint_kernel, sizes),
        (
            pltpu.HBM((rows, width), BF16),
            shape((width, width), F32),
            shape((slots, width), F32),
            shape((width + slots, width), BF16),
            shape((rows, width), BF16),
            shape((rows, width), BF16),
            shape((8, width), F32),
        ),
        out_specs=(hbm,) + (vmem,) * 6,
        scratch=(
            pltpu.VMEM((rows, width), BF16),
            pltpu.VMEM((width, rows), BF16),
            pltpu.VMEM((rows, width), F32),
            pltpu.VMEM((2, width, width), F32),
            pltpu.SemaphoreType.DMA((rows // TILE,)),
        ),
        cost=(4 * rows * slots * width + 8 * rows * width * width, 16 * rows * width),
    )(remote, turned, own_total, self_part, *far_counts, share, w_neigh_kept, cot_kept)

    received = other_side(message)
    feat_grad = call(
        own_grad_kernel,
        shape((rows, width), F32),
        cost=(2 * rows * rows * width + 2 * rows * width * width, 8 * rows * width),
    )(low, w_self_kept, edge_grad, *own_counts)
    message = call(
        side_sum_kernel,
        shape((peers, slab, width), BF16),
        [vmem, vmem, pl.BlockSpec(memory_space=pl.ANY)],
    )(w_own, received, feat_grad)
    slabs = swap(message, PEERS)
    message = call(
        functools.partial(peer_sum_kernel, sizes), shape((peers, slab + tall, width), BF16)
    )(slabs, rest, received, bias_sum)
    message = swap(message, PEERS)
    grad_feats = call(
        functools.partial(feat_grad_kernel, sizes, slab),
        shape((rows, width), BF16),
        cost=(4 * rows * slots * width, 6 * rows * width),
    )(message, places, feat_grad)
    unit_self, unit_neigh, unit_bias = call(
        functools.partial(unit_kernel, slab),
        (*((pltpu.HBM((width, width), F32),) * 2), pltpu.HBM((1, width), F32)),
        out_specs=(hbm,) * 3,
        scratch=(
            pltpu.VMEM((2, width, width), F32),
            pltpu.VMEM((1, width), F32),
            pltpu.SemaphoreType.DMA((3,)),
        ),
    )(message, other_side(message))
    return outputs, grad_feats, unit_self, unit_neigh, unit_bias.reshape(width)


def solution(mesh):
    doms, reps = mesh.shape["dom"], mesh.shape["rep"]
    split = jax.sharding.Mesh(mesh.devices.reshape(doms, reps // SIDES, SIDES), SPLIT_AXES)
    rows, whole = P(SPLIT_AXES, None), P()
    return jax.shard_map(
        functools.partial(on_device, doms, reps),
        mesh=split,
        in_specs=(rows, whole, whole, whole, rows, P(SPLIT_AXES), rows, P(SPLIT_AXES), rows),
        out_specs=(rows, rows, whole, whole, whole),
        check_vma=False,
    )
```

```python
import functools

import jax
import jax.numpy as jnp
from jax import lax
from jax.experimental import pallas as pl
from jax.experimental.pallas import tpu as pltpu
from jax.sharding import PartitionSpec as P

NORM_EPS = 1e-05
UNIT_EPS = 1e-06
SPLIT_AXES = ("dom", "pair", "side")
PEERS = ("dom", "pair")
SIDES = 2
VMEM_LIMIT = 32 * 1024 * 1024
F32 = jnp.float32
BF16 = jnp.bfloat16
TILE = 256
STRIP = 16
PIECE = 32
LANES = 128
BIAS_ROWS = 2


def div_floor(value, size):
    if size & (size - 1) == 0:
        return lax.shift_right_arithmetic(value, jnp.int32(size.bit_length() - 1))
    return value // size


def remainder(value, size):
    if size & (size - 1) == 0:
        return value & jnp.int32(size - 1)
    return value - (value // size) * size


def matmul(lhs, rhs, lhs_dim=1, rhs_dim=0):
    return lax.dot_general(
        lhs, rhs, (((lhs_dim,), (rhs_dim,)), ((), ())), preferred_element_type=F32
    )


def iota(shape, dim):
    return lax.broadcasted_iota(jnp.int32, shape, dim)


def one_hot(rows, places):
    return jnp.where(iota((rows, places.shape[1]), 0) == places, F32(1.0), F32(0.0)).astype(BF16)


def fetch(pairs, sems):
    copies = [
        pltpu.make_async_copy(source, target, sems.at[number])
        for number, (source, target) in enumerate(pairs)
    ]
    for copy in copies:
        copy.start()
    return copies


def pick_kernel(sizes, hub_hbm, send_hbm, *refs):
    doms, reps, cap, hub_own, tall = sizes
    inputs, (rows_ref, hubs_ref, places_ref), refs = refs[:5], refs[5:8], refs[8:]
    kept, (slot_ref, share_ref, own_count_ref, far_count_ref), refs = refs[:3], refs[3:7], refs[7:]
    hub_ref, send_ref, degree_ref, edge_ref, hot_ref, sems = refs
    feats_ref = kept[0]
    targets = (hub_ref, send_ref, degree_ref, edge_ref, *kept)
    copies = fetch(zip((hub_hbm, send_hbm, *inputs), targets), sems)
    slots = doms * tall
    lane = iota(places_ref.shape, 1)
    row = remainder(lane, tall)

    def list_entries(dom, places):
        for entry in range(cap):
            places = jnp.where(lane == dom * tall + entry, send_ref[entry, dom], places)
        return places

    copies[0].wait()
    copies[1].wait()
    places = jnp.full(lane.shape, -1, jnp.int32)
    if doms <= 16:
        for dom in range(doms):
            places = list_entries(dom, places)
    else:
        places = lax.fori_loop(0, doms, list_entries, places)
    for entry in range(hub_own):
        for first, inside in ((cap, lane < slots), (cap + hub_own, lane >= slots)):
            places = jnp.where((row == first + entry) & inside, hub_ref[entry], places)
    places_ref[...] = places
    column = jnp.broadcast_to(places, (LANES, lane.shape[1])).T[: slots + 2 * tall, :]
    node = iota(column.shape, 1)
    chosen = [
        jnp.where(node + first == column, F32(1.0), F32(0.0)).astype(BF16)
        for first in range(0, feats_ref.shape[0], LANES)
    ]
    copies[2].wait()
    copies[3].wait()
    find_slots(sizes, degree_ref, edge_ref, slot_ref, share_ref)
    count_edges(slot_ref, own_count_ref, far_count_ref, hot_ref, slice(0, TILE))
    copies[4].wait()
    picked = matmul(jnp.concatenate(chosen, axis=1), feats_ref[...]).astype(BF16)
    rows_ref[...] = picked[:slots, :]
    hubs_ref[...] = picked[slots:, :]
    for copy in copies[5:]:
        copy.wait()


def message_kernel(sizes, rows_ref, hubs_ref, after_ref, message_ref):
    doms, reps, cap, hub_own, tall = sizes
    del after_ref
    rows = rows_ref[...].astype(F32)
    hubs = hubs_ref[...].astype(F32)[:tall, :]
    place = iota(hubs.shape, 0)
    pair = lax.axis_index("pair")
    pairs = reps // SIDES
    for dom in range(doms):
        block = rows[dom * tall : (dom + 1) * tall, :]
        blocks = [
            jnp.where((place >= cap) | (pair == other), block, F32(0.0)) + hubs
            for other in range(pairs)
        ]
        first = dom * pairs * tall
        message_ref[first : first + pairs * tall, :] = jnp.concatenate(blocks, axis=0).astype(BF16)


def count_edges(slot_ref, own_count_ref, far_count_ref, hot_ref, nodes):
    fanout, rows = slot_ref.shape[0], own_count_ref.shape[0]
    highs = (rows + far_count_ref.shape[0]) // LANES
    low, high = [], []
    for k in range(fanout):
        slot = jnp.broadcast_to(slot_ref[k : k + 1, nodes], (STRIP, TILE))
        low.append(remainder(slot, LANES).astype(jnp.int16))
        high.append(div_floor(slot, LANES).astype(jnp.int16))
    for block in range(highs):
        for k in range(fanout):
            hot_ref[block * fanout + k] = jnp.where(high[k] == block, BF16(1.0), BF16(0.0))
    for strip in range(0, LANES, STRIP):
        numbers = (iota((STRIP, TILE), 0) + strip).astype(jnp.int16)
        hot = [jnp.where(numbers == low[k], BF16(1.0), BF16(0.0)) for k in range(fanout)]

        def count(block):
            terms = [hot[k] * hot_ref[block * fanout + k] for k in range(fanout)]
            while len(terms) > 1:
                pairs = [left + right for left, right in zip(terms[::2], terms[1::2])]
                terms = pairs + terms[2 * len(pairs) :]
            return terms[0]

        for block in range(rows // LANES):
            first = block * LANES + strip
            own_count_ref[first : first + STRIP, :] = count(block)
        far = far_count_ref.shape[0] // LANES
        if far <= 4:
            for block in range(far):
                first = block * LANES + strip
                far_count_ref[first : first + STRIP, :] = count(rows // LANES + block)
        else:

            @pl.loop(0, far)
            def far_block(block):
                first = pl.multiple_of(block * LANES + strip, STRIP)
                far_count_ref[pl.ds(first, STRIP), :] = count(rows // LANES + block)


def find_slots(sizes, degree_ref, edge_ref, slot_ref, share_ref):
    doms, reps, cap, hub_own, tall = sizes
    fanout, rows = edge_ref.shape
    hubs = doms * reps * hub_own
    source = edge_ref[...]
    hub = source - rows
    halo = hub - hubs
    chip = SIDES * hub_own
    entry = remainder(hub, chip) ^ (lax.axis_index("side") * hub_own)
    hub_slot = rows + cap + div_floor(hub, chip) * tall + entry
    peer = div_floor(halo, cap) * (reps // SIDES) + lax.axis_index("pair")
    halo_slot = rows + peer * tall + remainder(halo, cap)
    slot = jnp.where(source < rows, source, jnp.where(hub < hubs, hub_slot, halo_slot))
    valid = jnp.minimum(degree_ref[...], fanout)
    slot_ref[...] = jnp.where(iota((fanout, rows), 0) < valid, slot, -1)
    share_ref[...] = 1.0 / valid.astype(F32)


def own_kernel(tiles, feats_ref, w_self_ref, bias_ref, slot_ref, *refs):
    first_count_ref, inputs, kept, refs = refs[0], refs[1:3], refs[3:5], refs[5:]
    turned_ref, total_ref, preact_ref = refs[:3]
    own_refs, far_refs, (hot_ref, sems) = (
        refs[3 : 2 + tiles],
        refs[2 + tiles : 1 + 2 * tiles],
        refs[1 + 2 * tiles :],
    )
    copies = fetch(zip(inputs, kept), sems)
    turned_ref[...] = feats_ref[...].T

    def own_sums(number, count_ref):
        nodes = slice(number * TILE, (number + 1) * TILE)
        total_ref[:, nodes] = matmul(turned_ref[...], count_ref[...])
        preact_ref[nodes, :] = matmul(feats_ref[nodes, :], w_self_ref[...]) + bias_ref[...]

    counted = first_count_ref
    for number in range(1, tiles):
        nodes = slice(number * TILE, (number + 1) * TILE)
        own_ref, far_ref = own_refs[number - 1], far_refs[number - 1]
        count_edges(slot_ref, own_ref, far_ref, hot_ref.at[number % 2], nodes)
        own_sums(number - 1, counted)
        counted = own_ref
    own_sums(tiles - 1, counted)
    for copy in copies:
        copy.wait()


def joint_kernel(sizes, remote_ref, turned_ref, total_ref, self_ref, *refs):
    doms, reps, cap, hub_own, tall = sizes
    rows, width = self_ref.shape
    tiles = [slice(first, first + TILE) for first in range(0, rows, TILE)]
    count_refs, refs = refs[: len(tiles)], refs[len(tiles) :]
    (
        share_ref,
        w_neigh_ref,
        cot_ref,
        outputs_hbm,
        w_own_ref,
        rest_ref,
        message_ref,
        low_ref,
        edge_grad_ref,
        bias_ref,
        outputs_ref,
        mean_ref,
        preact_ref,
        w_grad_ref,
        sems,
    ) = refs
    table = remote_ref[...].T

    def before_head(number):
        nodes = tiles[number]
        mean = total_ref[:, nodes] + matmul(table, count_refs[number][...])
        mean = (mean * share_ref[:, nodes]).astype(BF16)
        mean_ref[:, nodes] = mean
        preact_ref[nodes, :] = self_ref[nodes, :] + matmul(mean, w_neigh_ref[...], 0, 0)

    def node_sums(numbers):
        nodes = slice(tiles[numbers[0]].start, tiles[numbers[-1]].stop)
        low = low_ref[nodes, :]
        return (
            matmul(turned_ref[:, nodes], low),
            matmul(mean_ref[:, nodes], low),
            sum(matmul(count_refs[k][...], edge_grad_ref[tiles[k], :]) for k in numbers),
        )

    bias_sum = jnp.zeros((8, width), F32)
    copies = []
    before_head(0)
    for number, nodes in enumerate(tiles):
        if number + 1 < len(tiles):
            before_head(number + 1)
        elif number:
            w_grad_ref[0], w_grad_ref[1], rest_ref[...] = node_sums(range(number))
        for start in range(nodes.start, nodes.stop, PIECE):
            piece = slice(start, start + PIECE)
            preact = preact_ref[piece, :]
            cot = cot_ref[piece, :].astype(F32)
            grown = jnp.exp(jnp.minimum(preact, 0.0))
            act = jnp.maximum(preact, 0.0) + (grown - 1.0)
            square = jnp.sum(act * act, axis=1, keepdims=True)
            along = jnp.sum(act * cot, axis=1, keepdims=True)
            scale = lax.rsqrt(square * (1.0 / width) + NORM_EPS)
            outputs_ref[piece, :] = (act * scale).astype(BF16)
            pull = along * (scale * scale * scale) * (1.0 / width)
            grad_pre = (cot * scale - act * pull) * grown
            bias_sum = bias_sum + jnp.sum(grad_pre.reshape(PIECE // 8, 8, width), axis=0)
            low_ref[piece, :] = grad_pre.astype(BF16)
        copies += fetch(
            ((outputs_ref.at[nodes, :], outputs_hbm.at[nodes, :]),), sems.at[pl.ds(number, 1)]
        )
        share_column = jnp.broadcast_to(share_ref[:, nodes], (LANES, TILE)).T
        share_column = jnp.concatenate([share_column] * (width // LANES), axis=1)
        edge_grad = matmul(low_ref[nodes, :], w_neigh_ref[...], 1, 1) * share_column
        edge_grad_ref[nodes, :] = edge_grad.astype(BF16)

    w_self_sum, w_neigh_sum, remote = node_sums([len(tiles) - 1])
    if len(tiles) > 1:
        w_self_sum = w_self_sum + w_grad_ref[0]
        w_neigh_sum = w_neigh_sum + w_grad_ref[1]
        remote = remote + rest_ref[...]
    w_grad_ref[0] = w_self_sum
    w_grad_ref[1] = w_neigh_sum
    rest_ref[...] = remote
    bias_ref[...] = bias_sum
    bias_sum = jnp.broadcast_to(jnp.sum(bias_sum, axis=0, keepdims=True), (tall, width))
    bias_high = bias_sum.astype(BF16).astype(F32)
    place = iota((tall, width), 0)
    bias_rows = jnp.where(place == cap, bias_high, bias_sum - bias_high)
    bias_rows = jnp.where(place < cap, F32(0.0), bias_rows)
    message = remote.reshape(-1, tall, width)
    message = jnp.where((place < cap + hub_own)[None], bias_rows[None], message)
    message_ref[width:, :] = message.reshape(remote.shape).astype(BF16)
    mine = lax.axis_index("side")
    w_own_ref[...] = w_grad_ref[mine]
    message_ref[:width, :] = w_grad_ref[1 - mine].astype(BF16)
    for copy in copies:
        copy.wait()


def own_grad_kernel(low_ref, w_self_ref, edge_grad_ref, *refs):
    *count_refs, feat_grad_ref = refs
    for first in range(0, low_ref.shape[0], TILE):
        nodes = slice(first, first + TILE)
        total = matmul(low_ref[nodes, :], w_self_ref[...], 1, 1)
        for number, count_ref in enumerate(count_refs):
            edges = edge_grad_ref[number * TILE : (number + 1) * TILE, :]
            total = total + matmul(count_ref[nodes, :], edges)
        feat_grad_ref[nodes, :] = total


def side_sum_kernel(own_ref, received_ref, after_ref, message_ref):
    del after_ref
    peers, slab, width = message_ref.shape
    w_grad = own_ref[...] + received_ref[:width, :].astype(F32)
    owners = width // slab
    w_grad = w_grad.reshape(owners, slab, width)
    if owners < peers:
        w_grad = jnp.concatenate([w_grad, jnp.zeros((peers - owners, slab, width), F32)], axis=0)
    message_ref[...] = w_grad.astype(BF16)


def peer_sum_kernel(sizes, slabs_ref, own_ref, received_ref, bias_ref, message_ref):
    doms, reps, cap, hub_own, tall = sizes
    peers, slab, width = slabs_ref.shape
    total = jnp.sum(slabs_ref[...].astype(F32), axis=0)
    received_ref = received_ref.at[width:, :]
    size = min(peers * tall, LANES)
    to, source = iota((size, size), 0), iota((size, size), 1)
    entry = remainder(to, tall) - cap
    moved = (source == to + hub_own) & (entry >= 0) & (entry < hub_own)
    moved = jnp.where(moved, F32(1.0), F32(0.0)).astype(BF16)
    rest = own_ref[...] + jnp.concatenate(
        [
            matmul(moved, received_ref[first : first + size, :])
            for first in range(0, peers * tall, size)
        ],
        axis=0,
    )
    place = iota((tall, width), 0)
    bias = received_ref[: 2 * tall, :].astype(F32)[:tall, :]
    bias = jnp.where((place >= cap) & (place < cap + BIAS_ROWS), bias, F32(0.0)) + bias_ref[...]
    bias = jnp.broadcast_to(jnp.sum(bias, axis=0, keepdims=True), (tall, width))
    bias_high = bias.astype(BF16).astype(F32)
    bias_rows = jnp.where(place == tall - 1, bias - bias_high, bias_high)
    rest = rest.reshape(peers, tall, width)
    rest = jnp.where((place < tall - BIAS_ROWS)[None], rest, bias_rows[None])
    total = jnp.broadcast_to(total[None], (peers, slab, width))
    message_ref[...] = jnp.concatenate([total, rest], axis=1).astype(BF16)


def feat_grad_kernel(sizes, slab, message_ref, places_ref, feat_grad_ref, out_ref):
    doms, reps, cap, hub_own, tall = sizes
    rows, width = out_ref.shape
    pairs = reps // SIDES
    returned = message_ref[...].astype(F32)[:, slab:, :].reshape(doms, pairs, tall, width)
    returned = [
        returned[:, pair].reshape(doms * tall, width).astype(BF16) for pair in range(pairs)
    ]
    chosen = one_hot(rows, places_ref[:, : doms * tall])
    for first in range(0, rows, TILE):
        nodes = slice(first, first + TILE)
        total = feat_grad_ref[nodes, :]
        for part in returned:
            total = total + matmul(chosen[nodes, :], part)
        out_ref[nodes, :] = total.astype(BF16)


def unit_kernel(slab, mine_ref, other_ref, self_hbm, neigh_hbm, bias_hbm, units_ref, bias_ref, sems):
    side = lax.axis_index("side")
    _, size, width = units_ref.shape
    bias = jnp.sum(mine_ref[...].astype(F32)[:, slab:, :], axis=0)[-BIAS_ROWS:, :]
    bias = jnp.sum(bias, axis=0, keepdims=True)
    bias_ref[...] = bias * lax.rsqrt(jnp.mean(bias * bias, axis=1, keepdims=True) + UNIT_EPS)
    copies = [
        pltpu.make_async_copy(source, target, sems.at[number])
        for number, (source, target) in enumerate(
            ((units_ref.at[0], self_hbm), (units_ref.at[1], neigh_hbm), (bias_ref, bias_hbm))
        )
    ]
    copies[2].start()
    for place, grad_ref in ((side, mine_ref), (1 - side, other_ref)):
        grad = grad_ref[: size // slab].astype(F32)[:, :slab, :].reshape(size, width)
        square = jnp.sum(jnp.sum(grad * grad, axis=0, keepdims=True), axis=1, keepdims=True)
        units_ref[place] = grad * lax.rsqrt(square * (1.0 / grad.size) + UNIT_EPS)
        for number, copy in enumerate(copies[:2]):
            pl.when(place == number)(copy.start)
    for copy in copies:
        copy.wait()


def call(kernel, out_shape, in_specs=None, scratch=(), cost=(0, 0), out_specs=None):
    specs = {"in_specs": in_specs, "out_specs": out_specs}
    return pl.pallas_call(
        kernel,
        out_shape=out_shape,
        **{name: spec for name, spec in specs.items() if spec is not None},
        scratch_shapes=list(scratch),
        compiler_params=pltpu.CompilerParams(vmem_limit_bytes=VMEM_LIMIT),
        cost_estimate=pl.CostEstimate(flops=cost[0], bytes_accessed=cost[1], transcendentals=0),
    )


def in_hbm(*arrays):
    return [pltpu.with_memory_space_constraint(array, pltpu.HBM) for array in arrays]


def swap(array, axes):
    return lax.all_to_all(array, axes, split_axis=0, concat_axis=0, tiled=True)


def other_side(array):
    return lax.ppermute(array, "side", [(0, 1), (1, 0)])


def on_device(
    doms, reps, feats, w_self, w_neigh, bias, out_cot, degree, edge_src, hub_rows, send_rows
):
    rows, width = feats.shape
    fanout = edge_src.shape[1]
    cap, hub_own = send_rows.shape[1], hub_rows.shape[0]
    peers = doms * reps // SIDES
    tall = cap + SIDES * hub_own
    if tall % 8 or tall < cap + hub_own + BIAS_ROWS or hub_own & (hub_own - 1):
        raise ValueError("message height")
    slots = peers * tall
    slab = max(8, width // peers)
    sizes = (doms, reps, cap, hub_own, tall)
    shape = jax.ShapeDtypeStruct
    hbm = pl.BlockSpec(memory_space=pltpu.HBM)
    vmem = pl.BlockSpec(memory_space=pltpu.VMEM)

    tiles = rows // TILE
    hot = pltpu.VMEM(((rows + slots) // LANES * fanout, STRIP, TILE), BF16)
    picked, hubs, places, feats_kept, w_self_kept, bias_kept, slot, share, *first_counts = call(
        functools.partial(pick_kernel, sizes),
        (
            shape((doms * tall, width), BF16),
            shape((2 * tall, width), BF16),
            shape((1, -(-(doms + 2) * tall // LANES) * LANES), jnp.int32),
            shape((rows, width), BF16),
            shape((width, width), BF16),
            shape((1, width), F32),
            shape((fanout, rows), jnp.int32),
            shape((1, rows), F32),
            shape((rows, TILE), BF16),
            shape((slots, TILE), BF16),
        ),
        [hbm] * 7,
        (
            pltpu.SMEM((hub_own,), jnp.int32),
            pltpu.SMEM((cap, doms), jnp.int32),
            pltpu.VMEM((1, rows), jnp.int32),
            pltpu.VMEM((fanout, rows), jnp.int32),
            hot,
            pltpu.SemaphoreType.DMA((7,)),
        ),
        cost=(2 * rows * slots * width, 2 * rows * width),
    )(
        *in_hbm(
            hub_rows,
            send_rows.T,
            degree.reshape(1, rows),
            edge_src.T,
            feats,
            w_self,
            bias.reshape(1, width),
        )
    )
    hubs = other_side(hubs)
    w_neigh_kept, cot_kept, turned, own_total, self_part, *counts = call(
        functools.partial(own_kernel, tiles),
        (
            shape((width, width), BF16),
            shape((rows, width), BF16),
            shape((width, rows), BF16),
            shape((width, rows), F32),
            shape((rows, width), F32),
            *((shape((rows, TILE), BF16),) * (tiles - 1)),
            *((shape((slots, TILE), BF16),) * (tiles - 1)),
        ),
        [vmem] * 5 + [hbm] * 2,
        (
            pltpu.VMEM((2, *hot.shape), BF16),
            pltpu.SemaphoreType.DMA((2,)),
        ),
        cost=(8 * rows * (rows + slots) * width, 12 * rows * width + 2 * rows * rows),
    )(feats_kept, w_self_kept, bias_kept, slot, first_counts[0], *in_hbm(w_neigh, out_cot))
    own_counts = [first_counts[0], *counts[: tiles - 1]]
    far_counts = [first_counts[1], *counts[tiles - 1 :]]
    message = call(
        functools.partial(message_kernel, sizes),
        shape((slots, width), BF16),
        [vmem, vmem, pl.BlockSpec(memory_space=pl.ANY)],
    )(picked, hubs, own_total)
    remote = swap(message, PEERS)

    outputs, w_own, rest, message, low, edge_grad, bias_sum = call(
        functools.partial(joint_kernel, sizes),
        (
            pltpu.HBM((rows, width), BF16),
            shape((width, width), F32),
            shape((slots, width), F32),
            shape((width + slots, width), BF16),
            shape((rows, width), BF16),
            shape((rows, width), BF16),
            shape((8, width), F32),
        ),
        out_specs=(hbm,) + (vmem,) * 6,
        scratch=(
            pltpu.VMEM((rows, width), BF16),
            pltpu.VMEM((width, rows), BF16),
            pltpu.VMEM((rows, width), F32),
            pltpu.VMEM((2, width, width), F32),
            pltpu.SemaphoreType.DMA((rows // TILE,)),
        ),
        cost=(4 * rows * slots * width + 8 * rows * width * width, 16 * rows * width),
    )(remote, turned, own_total, self_part, *far_counts, share, w_neigh_kept, cot_kept)

    received = other_side(message)
    feat_grad = call(
        own_grad_kernel,
        shape((rows, width), F32),
        cost=(2 * rows * rows * width + 2 * rows * width * width, 8 * rows * width),
    )(low, w_self_kept, edge_grad, *own_counts)
    message = call(
        side_sum_kernel,
        shape((peers, slab, width), BF16),
        [vmem, vmem, pl.BlockSpec(memory_space=pl.ANY)],
    )(w_own, received, feat_grad)
    slabs = swap(message, PEERS)
    message = call(
        functools.partial(peer_sum_kernel, sizes), shape((peers, slab + tall, width), BF16)
    )(slabs, rest, received, bias_sum)
    message = swap(message, PEERS)
    grad_feats = call(
        functools.partial(feat_grad_kernel, sizes, slab),
        shape((rows, width), BF16),
        cost=(4 * rows * slots * width, 6 * rows * width),
    )(message, places, feat_grad)
    unit_self, unit_neigh, unit_bias = call(
        functools.partial(unit_kernel, slab),
        (*((pltpu.HBM((width, width), F32),) * 2), pltpu.HBM((1, width), F32)),
        out_specs=(hbm,) * 3,
        scratch=(
            pltpu.VMEM((2, width, width), F32),
            pltpu.VMEM((1, width), F32),
            pltpu.SemaphoreType.DMA((3,)),
        ),
    )(message, other_side(message))
    return outputs, grad_feats, unit_self, unit_neigh, unit_bias.reshape(width)


def solution(mesh):
    doms, reps = mesh.shape["dom"], mesh.shape["rep"]
    split = jax.sharding.Mesh(mesh.devices.reshape(doms, reps // SIDES, SIDES), SPLIT_AXES)
    rows, whole = P(SPLIT_AXES, None), P()
    return jax.shard_map(
        functools.partial(on_device, doms, reps),
        mesh=split,
        in_specs=(rows, whole, whole, whole, rows, P(SPLIT_AXES), rows, P(SPLIT_AXES), rows),
        out_specs=(rows, rows, whole, whole, whole),
        check_vma=False,
    )
```

```python
import functools

import jax
import jax.numpy as jnp
from jax import lax
from jax.experimental import pallas as pl
from jax.experimental.pallas import tpu as pltpu
from jax.sharding import PartitionSpec as P

NORM_EPS = 1e-05
UNIT_EPS = 1e-06
SPLIT_AXES = ("dom", "pair", "side")
PEERS = ("dom", "pair")
SIDES = 2
VMEM_LIMIT = 32 * 1024 * 1024
F32 = jnp.float32
BF16 = jnp.bfloat16
TILE = 256
STRIP = 16
PIECE = 32
LANES = 128
BIAS_ROWS = 2


def div_floor(value, size):
    if size & (size - 1) == 0:
        return lax.shift_right_arithmetic(value, jnp.int32(size.bit_length() - 1))
    return value // size


def remainder(value, size):
    if size & (size - 1) == 0:
        return value & jnp.int32(size - 1)
    return value - (value // size) * size


def matmul(lhs, rhs, lhs_dim=1, rhs_dim=0):
    return lax.dot_general(
        lhs, rhs, (((lhs_dim,), (rhs_dim,)), ((), ())), preferred_element_type=F32
    )


def iota(shape, dim):
    return lax.broadcasted_iota(jnp.int32, shape, dim)


def one_hot(rows, places):
    return jnp.where(iota((rows, places.shape[1]), 0) == places, F32(1.0), F32(0.0)).astype(BF16)


def fetch(pairs, sems):
    copies = [
        pltpu.make_async_copy(source, target, sems.at[number])
        for number, (source, target) in enumerate(pairs)
    ]
    for copy in copies:
        copy.start()
    return copies


def pick_kernel(sizes, hub_hbm, send_hbm, *refs):
    doms, reps, cap, hub_own, tall = sizes
    inputs, (rows_ref, hubs_ref, places_ref), refs = refs[:5], refs[5:8], refs[8:]
    kept, (slot_ref, share_ref, own_count_ref, far_count_ref), refs = refs[:3], refs[3:7], refs[7:]
    hub_ref, send_ref, degree_ref, edge_ref, hot_ref, sems = refs
    feats_ref = kept[0]
    targets = (hub_ref, send_ref, degree_ref, edge_ref, *kept)
    copies = fetch(zip((hub_hbm, send_hbm, *inputs), targets), sems)
    slots = doms * tall
    lane = iota(places_ref.shape, 1)
    row = remainder(lane, tall)

    def list_entries(dom, places):
        for entry in range(cap):
            places = jnp.where(lane == dom * tall + entry, send_ref[entry, dom], places)
        return places

    copies[0].wait()
    copies[1].wait()
    places = jnp.full(lane.shape, -1, jnp.int32)
    if doms <= 16:
        for dom in range(doms):
            places = list_entries(dom, places)
    else:
        places = lax.fori_loop(0, doms, list_entries, places)
    for entry in range(hub_own):
        for first, inside in ((cap, lane < slots), (cap + hub_own, lane >= slots)):
            places = jnp.where((row == first + entry) & inside, hub_ref[entry], places)
    places_ref[...] = places
    column = jnp.broadcast_to(places, (LANES, lane.shape[1])).T[: slots + 2 * tall, :]
    node = iota(column.shape, 1)
    chosen = [
        jnp.where(node + first == column, F32(1.0), F32(0.0)).astype(BF16)
        for first in range(0, feats_ref.shape[0], LANES)
    ]
    copies[2].wait()
    copies[3].wait()
    find_slots(sizes, degree_ref, edge_ref, slot_ref, share_ref)
    count_edges(slot_ref, own_count_ref, far_count_ref, hot_ref, slice(0, TILE))
    copies[4].wait()
    picked = matmul(jnp.concatenate(chosen, axis=1), feats_ref[...]).astype(BF16)
    rows_ref[...] = picked[:slots, :]
    hubs_ref[...] = picked[slots:, :]
    for copy in copies[5:]:
        copy.wait()


def message_kernel(sizes, rows_ref, hubs_ref, after_ref, message_ref):
    doms, reps, cap, hub_own, tall = sizes
    del after_ref
    rows = rows_ref[...].astype(F32)
    hubs = hubs_ref[...].astype(F32)[:tall, :]
    place = iota(hubs.shape, 0)
    pair = lax.axis_index("pair")
    pairs = reps // SIDES
    for dom in range(doms):
        block = rows[dom * tall : (dom + 1) * tall, :]
        blocks = [
            jnp.where((place >= cap) | (pair == other), block, F32(0.0)) + hubs
            for other in range(pairs)
        ]
        first = dom * pairs * tall
        message_ref[first : first + pairs * tall, :] = jnp.concatenate(blocks, axis=0).astype(BF16)


def count_edges(slot_ref, own_count_ref, far_count_ref, hot_ref, nodes):
    fanout, rows = slot_ref.shape[0], own_count_ref.shape[0]
    highs = (rows + far_count_ref.shape[0]) // LANES
    low, high = [], []
    for k in range(fanout):
        slot = jnp.broadcast_to(slot_ref[k : k + 1, nodes], (STRIP, TILE))
        low.append(remainder(slot, LANES).astype(jnp.int16))
        high.append(div_floor(slot, LANES).astype(jnp.int16))
    for block in range(highs):
        for k in range(fanout):
            hot_ref[block * fanout + k] = jnp.where(high[k] == block, BF16(1.0), BF16(0.0))
    for strip in range(0, LANES, 2 * STRIP):
        hot = []
        for start in (strip, strip + STRIP):
            numbers = (iota((STRIP, TILE), 0) + start).astype(jnp.int16)
            hot.append([jnp.where(numbers == low[k], BF16(1.0), BF16(0.0)) for k in range(fanout)])

        def count(block):
            part = hot_ref[block * fanout]
            totals = [hot[0][0] * part, hot[1][0] * part]
            for k in range(1, fanout):
                part = hot_ref[block * fanout + k]
                totals = [total + each[k] * part for total, each in zip(totals, hot)]
            return jnp.concatenate(totals, axis=0)

        for block in range(rows // LANES):
            first = block * LANES + strip
            own_count_ref[first : first + 2 * STRIP, :] = count(block)
        far = far_count_ref.shape[0] // LANES
        if far <= 4:
            for block in range(far):
                first = block * LANES + strip
                far_count_ref[first : first + 2 * STRIP, :] = count(rows // LANES + block)
        else:

            @pl.loop(0, far)
            def far_block(block):
                first = pl.multiple_of(block * LANES + strip, 2 * STRIP)
                far_count_ref[pl.ds(first, 2 * STRIP), :] = count(rows // LANES + block)


def find_slots(sizes, degree_ref, edge_ref, slot_ref, share_ref):
    doms, reps, cap, hub_own, tall = sizes
    fanout, rows = edge_ref.shape
    hubs = doms * reps * hub_own
    source = edge_ref[...]
    hub = source - rows
    halo = hub - hubs
    chip = SIDES * hub_own
    entry = remainder(hub, chip) ^ (lax.axis_index("side") * hub_own)
    hub_slot = rows + cap + div_floor(hub, chip) * tall + entry
    peer = div_floor(halo, cap) * (reps // SIDES) + lax.axis_index("pair")
    halo_slot = rows + peer * tall + remainder(halo, cap)
    slot = jnp.where(source < rows, source, jnp.where(hub < hubs, hub_slot, halo_slot))
    valid = jnp.minimum(degree_ref[...], fanout)
    slot_ref[...] = jnp.where(iota((fanout, rows), 0) < valid, slot, -1)
    share_ref[...] = 1.0 / valid.astype(F32)


def own_kernel(tiles, feats_ref, w_self_ref, bias_ref, slot_ref, *refs):
    first_count_ref, inputs, kept, refs = refs[0], refs[1:3], refs[3:5], refs[5:]
    turned_ref, total_ref, preact_ref = refs[:3]
    own_refs, far_refs, (hot_ref, sems) = (
        refs[3 : 2 + tiles],
        refs[2 + tiles : 1 + 2 * tiles],
        refs[1 + 2 * tiles :],
    )
    copies = fetch(zip(inputs, kept), sems)
    turned_ref[...] = feats_ref[...].T

    def own_sums(number, count_ref):
        nodes = slice(number * TILE, (number + 1) * TILE)
        total_ref[:, nodes] = matmul(turned_ref[...], count_ref[...])
        preact_ref[nodes, :] = matmul(feats_ref[nodes, :], w_self_ref[...]) + bias_ref[...]

    counted = first_count_ref
    for number in range(1, tiles):
        nodes = slice(number * TILE, (number + 1) * TILE)
        own_ref, far_ref = own_refs[number - 1], far_refs[number - 1]
        count_edges(slot_ref, own_ref, far_ref, hot_ref.at[number % 2], nodes)
        own_sums(number - 1, counted)
        counted = own_ref
    own_sums(tiles - 1, counted)
    for copy in copies:
        copy.wait()


def joint_kernel(sizes, remote_ref, turned_ref, total_ref, self_ref, *refs):
    doms, reps, cap, hub_own, tall = sizes
    rows, width = self_ref.shape
    tiles = [slice(first, first + TILE) for first in range(0, rows, TILE)]
    count_refs, refs = refs[: len(tiles)], refs[len(tiles) :]
    (
        share_ref,
        w_neigh_ref,
        cot_ref,
        outputs_hbm,
        w_own_ref,
        rest_ref,
        message_ref,
        low_ref,
        edge_grad_ref,
        bias_ref,
        outputs_ref,
        mean_ref,
        preact_ref,
        w_grad_ref,
        sems,
    ) = refs
    table = remote_ref[...].T

    def before_head(number):
        nodes = tiles[number]
        mean = total_ref[:, nodes] + matmul(table, count_refs[number][...])
        mean = (mean * share_ref[:, nodes]).astype(BF16)
        mean_ref[:, nodes] = mean
        preact_ref[nodes, :] = self_ref[nodes, :] + matmul(mean, w_neigh_ref[...], 0, 0)

    def node_sums(numbers):
        nodes = slice(tiles[numbers[0]].start, tiles[numbers[-1]].stop)
        low = low_ref[nodes, :]
        return (
            matmul(turned_ref[:, nodes], low),
            matmul(mean_ref[:, nodes], low),
            sum(matmul(count_refs[k][...], edge_grad_ref[tiles[k], :]) for k in numbers),
        )

    bias_sum = jnp.zeros((8, width), F32)
    copies = []
    before_head(0)
    for number, nodes in enumerate(tiles):
        if number + 1 < len(tiles):
            before_head(number + 1)
        elif number:
            w_grad_ref[0], w_grad_ref[1], rest_ref[...] = node_sums(range(number))
        for start in range(nodes.start, nodes.stop, PIECE):
            piece = slice(start, start + PIECE)
            preact = preact_ref[piece, :]
            cot = cot_ref[piece, :].astype(F32)
            grown = jnp.exp(jnp.minimum(preact, 0.0))
            act = jnp.where(preact > 0.0, preact, grown - 1.0)
            square = jnp.sum(act * act, axis=1, keepdims=True)
            along = jnp.sum(act * cot, axis=1, keepdims=True)
            scale = lax.rsqrt(square * (1.0 / width) + NORM_EPS)
            outputs_ref[piece, :] = (act * scale).astype(BF16)
            pull = along * (scale * scale * scale) * (1.0 / width)
            grad_pre = (cot * scale - act * pull) * jnp.where(preact > 0.0, F32(1.0), grown)
            bias_sum = bias_sum + jnp.sum(grad_pre.reshape(PIECE // 8, 8, width), axis=0)
            low_ref[piece, :] = grad_pre.astype(BF16)
        copies += fetch(
            ((outputs_ref.at[nodes, :], outputs_hbm.at[nodes, :]),), sems.at[pl.ds(number, 1)]
        )
        share_column = jnp.broadcast_to(share_ref[:, nodes], (LANES, TILE)).T
        share_column = jnp.concatenate([share_column] * (width // LANES), axis=1)
        edge_grad = matmul(low_ref[nodes, :], w_neigh_ref[...], 1, 1) * share_column
        edge_grad_ref[nodes, :] = edge_grad.astype(BF16)

    w_self_sum, w_neigh_sum, remote = node_sums([len(tiles) - 1])
    if len(tiles) > 1:
        w_self_sum = w_self_sum + w_grad_ref[0]
        w_neigh_sum = w_neigh_sum + w_grad_ref[1]
        remote = remote + rest_ref[...]
    w_grad_ref[0] = w_self_sum
    w_grad_ref[1] = w_neigh_sum
    rest_ref[...] = remote
    bias_ref[...] = bias_sum
    bias_sum = jnp.broadcast_to(jnp.sum(bias_sum, axis=0, keepdims=True), (tall, width))
    bias_high = bias_sum.astype(BF16).astype(F32)
    place = iota((tall, width), 0)
    bias_rows = jnp.where(place == cap, bias_high, bias_sum - bias_high)
    bias_rows = jnp.where(place < cap, F32(0.0), bias_rows)
    message = remote.reshape(-1, tall, width)
    message = jnp.where((place < cap + hub_own)[None], bias_rows[None], message)
    message_ref[width:, :] = message.reshape(remote.shape).astype(BF16)
    mine = lax.axis_index("side")
    w_own_ref[...] = w_grad_ref[mine]
    message_ref[:width, :] = w_grad_ref[1 - mine].astype(BF16)
    for copy in copies:
        copy.wait()


def own_grad_kernel(low_ref, w_self_ref, edge_grad_ref, *refs):
    *count_refs, feat_grad_ref = refs
    for first in range(0, low_ref.shape[0], TILE):
        nodes = slice(first, first + TILE)
        total = matmul(low_ref[nodes, :], w_self_ref[...], 1, 1)
        for number, count_ref in enumerate(count_refs):
            edges = edge_grad_ref[number * TILE : (number + 1) * TILE, :]
            total = total + matmul(count_ref[nodes, :], edges)
        feat_grad_ref[nodes, :] = total


def side_sum_kernel(own_ref, received_ref, after_ref, message_ref):
    del after_ref
    peers, slab, width = message_ref.shape
    w_grad = own_ref[...] + received_ref[:width, :].astype(F32)
    owners = width // slab
    w_grad = w_grad.reshape(owners, slab, width)
    if owners < peers:
        w_grad = jnp.concatenate([w_grad, jnp.zeros((peers - owners, slab, width), F32)], axis=0)
    message_ref[...] = w_grad.astype(BF16)


def peer_sum_kernel(sizes, slabs_ref, own_ref, received_ref, bias_ref, message_ref):
    doms, reps, cap, hub_own, tall = sizes
    peers, slab, width = slabs_ref.shape
    total = jnp.sum(slabs_ref[...].astype(F32), axis=0)
    received_ref = received_ref.at[width:, :]
    size = min(peers * tall, LANES)
    to, source = iota((size, size), 0), iota((size, size), 1)
    entry = remainder(to, tall) - cap
    moved = (source == to + hub_own) & (entry >= 0) & (entry < hub_own)
    moved = jnp.where(moved, F32(1.0), F32(0.0)).astype(BF16)
    rest = own_ref[...] + jnp.concatenate(
        [
            matmul(moved, received_ref[first : first + size, :])
            for first in range(0, peers * tall, size)
        ],
        axis=0,
    )
    place = iota((tall, width), 0)
    bias = received_ref[: 2 * tall, :].astype(F32)[:tall, :]
    bias = jnp.where((place >= cap) & (place < cap + BIAS_ROWS), bias, F32(0.0)) + bias_ref[...]
    bias = jnp.broadcast_to(jnp.sum(bias, axis=0, keepdims=True), (tall, width))
    bias_high = bias.astype(BF16).astype(F32)
    bias_rows = jnp.where(place == tall - 1, bias - bias_high, bias_high)
    rest = rest.reshape(peers, tall, width)
    rest = jnp.where((place < tall - BIAS_ROWS)[None], rest, bias_rows[None])
    total = jnp.broadcast_to(total[None], (peers, slab, width))
    message_ref[...] = jnp.concatenate([total, rest], axis=1).astype(BF16)


def feat_grad_kernel(sizes, slab, message_ref, places_ref, feat_grad_ref, out_ref):
    doms, reps, cap, hub_own, tall = sizes
    rows, width = out_ref.shape
    pairs = reps // SIDES
    returned = message_ref[...].astype(F32)[:, slab:, :].reshape(doms, pairs, tall, width)
    returned = [
        returned[:, pair].reshape(doms * tall, width).astype(BF16) for pair in range(pairs)
    ]
    chosen = one_hot(rows, places_ref[:, : doms * tall])
    for first in range(0, rows, TILE):
        nodes = slice(first, first + TILE)
        total = feat_grad_ref[nodes, :]
        for part in returned:
            total = total + matmul(chosen[nodes, :], part)
        out_ref[nodes, :] = total.astype(BF16)


def unit_kernel(slab, mine_ref, other_ref, self_hbm, neigh_hbm, bias_hbm, units_ref, bias_ref, sems):
    side = lax.axis_index("side")
    _, size, width = units_ref.shape
    bias = jnp.sum(mine_ref[...].astype(F32)[:, slab:, :], axis=0)[-BIAS_ROWS:, :]
    bias = jnp.sum(bias, axis=0, keepdims=True)
    bias_ref[...] = bias * lax.rsqrt(jnp.mean(bias * bias, axis=1, keepdims=True) + UNIT_EPS)
    copies = [
        pltpu.make_async_copy(source, target, sems.at[number])
        for number, (source, target) in enumerate(
            ((units_ref.at[0], self_hbm), (units_ref.at[1], neigh_hbm), (bias_ref, bias_hbm))
        )
    ]
    copies[2].start()
    for place, grad_ref in ((side, mine_ref), (1 - side, other_ref)):
        grad = grad_ref[: size // slab].astype(F32)[:, :slab, :].reshape(size, width)
        square = jnp.sum(jnp.sum(grad * grad, axis=0, keepdims=True), axis=1, keepdims=True)
        units_ref[place] = grad * lax.rsqrt(square * (1.0 / grad.size) + UNIT_EPS)
        for number, copy in enumerate(copies[:2]):
            pl.when(place == number)(copy.start)
    for copy in copies:
        copy.wait()


def call(kernel, out_shape, in_specs=None, scratch=(), cost=(0, 0), out_specs=None):
    specs = {"in_specs": in_specs, "out_specs": out_specs}
    return pl.pallas_call(
        kernel,
        out_shape=out_shape,
        **{name: spec for name, spec in specs.items() if spec is not None},
        scratch_shapes=list(scratch),
        compiler_params=pltpu.CompilerParams(vmem_limit_bytes=VMEM_LIMIT),
        cost_estimate=pl.CostEstimate(flops=cost[0], bytes_accessed=cost[1], transcendentals=0),
    )


def in_hbm(*arrays):
    return [pltpu.with_memory_space_constraint(array, pltpu.HBM) for array in arrays]


def swap(array, axes):
    return lax.all_to_all(array, axes, split_axis=0, concat_axis=0, tiled=True)


def other_side(array):
    return lax.ppermute(array, "side", [(0, 1), (1, 0)])


def on_device(
    doms, reps, feats, w_self, w_neigh, bias, out_cot, degree, edge_src, hub_rows, send_rows
):
    rows, width = feats.shape
    fanout = edge_src.shape[1]
    cap, hub_own = send_rows.shape[1], hub_rows.shape[0]
    peers = doms * reps // SIDES
    tall = cap + SIDES * hub_own
    if tall % 8 or tall < cap + hub_own + BIAS_ROWS or hub_own & (hub_own - 1):
        raise ValueError("message height")
    slots = peers * tall
    slab = max(8, width // peers)
    sizes = (doms, reps, cap, hub_own, tall)
    shape = jax.ShapeDtypeStruct
    hbm = pl.BlockSpec(memory_space=pltpu.HBM)
    vmem = pl.BlockSpec(memory_space=pltpu.VMEM)

    tiles = rows // TILE
    hot = pltpu.VMEM(((rows + slots) // LANES * fanout, STRIP, TILE), BF16)
    picked, hubs, places, feats_kept, w_self_kept, bias_kept, slot, share, *first_counts = call(
        functools.partial(pick_kernel, sizes),
        (
            shape((doms * tall, width), BF16),
            shape((2 * tall, width), BF16),
            shape((1, -(-(doms + 2) * tall // LANES) * LANES), jnp.int32),
            shape((rows, width), BF16),
            shape((width, width), BF16),
            shape((1, width), F32),
            shape((fanout, rows), jnp.int32),
            shape((1, rows), F32),
            shape((rows, TILE), BF16),
            shape((slots, TILE), BF16),
        ),
        [hbm] * 7,
        (
            pltpu.SMEM((hub_own,), jnp.int32),
            pltpu.SMEM((cap, doms), jnp.int32),
            pltpu.VMEM((1, rows), jnp.int32),
            pltpu.VMEM((fanout, rows), jnp.int32),
            hot,
            pltpu.SemaphoreType.DMA((7,)),
        ),
        cost=(2 * rows * slots * width, 2 * rows * width),
    )(
        *in_hbm(
            hub_rows,
            send_rows.T,
            degree.reshape(1, rows),
            edge_src.T,
            feats,
            w_self,
            bias.reshape(1, width),
        )
    )
    hubs = other_side(hubs)
    w_neigh_kept, cot_kept, turned, own_total, self_part, *counts = call(
        functools.partial(own_kernel, tiles),
        (
            shape((width, width), BF16),
            shape((rows, width), BF16),
            shape((width, rows), BF16),
            shape((width, rows), F32),
            shape((rows, width), F32),
            *((shape((rows, TILE), BF16),) * (tiles - 1)),
            *((shape((slots, TILE), BF16),) * (tiles - 1)),
        ),
        [vmem] * 5 + [hbm] * 2,
        (
            pltpu.VMEM((2, *hot.shape), BF16),
            pltpu.SemaphoreType.DMA((2,)),
        ),
        cost=(8 * rows * (rows + slots) * width, 12 * rows * width + 2 * rows * rows),
    )(feats_kept, w_self_kept, bias_kept, slot, first_counts[0], *in_hbm(w_neigh, out_cot))
    own_counts = [first_counts[0], *counts[: tiles - 1]]
    far_counts = [first_counts[1], *counts[tiles - 1 :]]
    message = call(
        functools.partial(message_kernel, sizes),
        shape((slots, width), BF16),
        [vmem, vmem, pl.BlockSpec(memory_space=pl.ANY)],
    )(picked, hubs, own_total)
    remote = swap(message, PEERS)

    outputs, w_own, rest, message, low, edge_grad, bias_sum = call(
        functools.partial(joint_kernel, sizes),
        (
            pltpu.HBM((rows, width), BF16),
            shape((width, width), F32),
            shape((slots, width), F32),
            shape((width + slots, width), BF16),
            shape((rows, width), BF16),
            shape((rows, width), BF16),
            shape((8, width), F32),
        ),
        out_specs=(hbm,) + (vmem,) * 6,
        scratch=(
            pltpu.VMEM((rows, width), BF16),
            pltpu.VMEM((width, rows), BF16),
            pltpu.VMEM((rows, width), F32),
            pltpu.VMEM((2, width, width), F32),
            pltpu.SemaphoreType.DMA((rows // TILE,)),
        ),
        cost=(4 * rows * slots * width + 8 * rows * width * width, 16 * rows * width),
    )(remote, turned, own_total, self_part, *far_counts, share, w_neigh_kept, cot_kept)

    received = other_side(message)
    feat_grad = call(
        own_grad_kernel,
        shape((rows, width), F32),
        cost=(2 * rows * rows * width + 2 * rows * width * width, 8 * rows * width),
    )(low, w_self_kept, edge_grad, *own_counts)
    message = call(
        side_sum_kernel,
        shape((peers, slab, width), BF16),
        [vmem, vmem, pl.BlockSpec(memory_space=pl.ANY)],
    )(w_own, received, feat_grad)
    slabs = swap(message, PEERS)
    message = call(
        functools.partial(peer_sum_kernel, sizes), shape((peers, slab + tall, width), BF16)
    )(slabs, rest, received, bias_sum)
    message = swap(message, PEERS)
    grad_feats = call(
        functools.partial(feat_grad_kernel, sizes, slab),
        shape((rows, width), BF16),
        cost=(4 * rows * slots * width, 6 * rows * width),
    )(message, places, feat_grad)
    unit_self, unit_neigh, unit_bias = call(
        functools.partial(unit_kernel, slab),
        (*((pltpu.HBM((width, width), F32),) * 2), pltpu.HBM((1, width), F32)),
        out_specs=(hbm,) * 3,
        scratch=(
            pltpu.VMEM((2, width, width), F32),
            pltpu.VMEM((1, width), F32),
            pltpu.SemaphoreType.DMA((3,)),
        ),
    )(message, other_side(message))
    return outputs, grad_feats, unit_self, unit_neigh, unit_bias.reshape(width)


def solution(mesh):
    doms, reps = mesh.shape["dom"], mesh.shape["rep"]
    split = jax.sharding.Mesh(mesh.devices.reshape(doms, reps // SIDES, SIDES), SPLIT_AXES)
    rows, whole = P(SPLIT_AXES, None), P()
    return jax.shard_map(
        functools.partial(on_device, doms, reps),
        mesh=split,
        in_specs=(rows, whole, whole, whole, rows, P(SPLIT_AXES), rows, P(SPLIT_AXES), rows),
        out_specs=(rows, rows, whole, whole, whole),
        check_vma=False,
    )
```

```python
import functools

import jax
import jax.numpy as jnp
from jax import lax
from jax.experimental import pallas as pl
from jax.experimental.pallas import tpu as pltpu
from jax.sharding import PartitionSpec as P

NORM_EPS = 1e-05
UNIT_EPS = 1e-06
SPLIT_AXES = ("dom", "pair", "side")
PEERS = ("dom", "pair")
SIDES = 2
VMEM_LIMIT = 32 * 1024 * 1024
F32 = jnp.float32
BF16 = jnp.bfloat16
TILE = 256
STRIP = 16
PIECE = 32
LANES = 128
BIAS_ROWS = 2


def div_floor(value, size):
    if size & (size - 1) == 0:
        return lax.shift_right_arithmetic(value, jnp.int32(size.bit_length() - 1))
    return value // size


def remainder(value, size):
    if size & (size - 1) == 0:
        return value & jnp.int32(size - 1)
    return value - (value // size) * size


def matmul(lhs, rhs, lhs_dim=1, rhs_dim=0):
    return lax.dot_general(
        lhs, rhs, (((lhs_dim,), (rhs_dim,)), ((), ())), preferred_element_type=F32
    )


def iota(shape, dim):
    return lax.broadcasted_iota(jnp.int32, shape, dim)


def one_hot(rows, places):
    return jnp.where(iota((rows, places.shape[1]), 0) == places, F32(1.0), F32(0.0)).astype(BF16)


def fetch(pairs, sems):
    copies = [
        pltpu.make_async_copy(source, target, sems.at[number])
        for number, (source, target) in enumerate(pairs)
    ]
    for copy in copies:
        copy.start()
    return copies


def pick_kernel(sizes, hub_hbm, send_hbm, *refs):
    doms, reps, cap, hub_own, tall = sizes
    inputs, (rows_ref, hubs_ref, places_ref), refs = refs[:5], refs[5:8], refs[8:]
    kept, (slot_ref, share_ref, own_count_ref, far_count_ref), refs = refs[:3], refs[3:7], refs[7:]
    hub_ref, send_ref, degree_ref, edge_ref, hot_ref, sems = refs
    feats_ref = kept[0]
    targets = (hub_ref, send_ref, degree_ref, edge_ref, *kept)
    copies = fetch(zip((hub_hbm, send_hbm, *inputs), targets), sems)
    slots = doms * tall
    lane = iota(places_ref.shape, 1)
    row = remainder(lane, tall)

    def list_entries(dom, places):
        for entry in range(cap):
            places = jnp.where(lane == dom * tall + entry, send_ref[entry, dom], places)
        return places

    copies[0].wait()
    copies[1].wait()
    places = jnp.full(lane.shape, -1, jnp.int32)
    if doms <= 16:
        for dom in range(doms):
            places = list_entries(dom, places)
    else:
        places = lax.fori_loop(0, doms, list_entries, places)
    for entry in range(hub_own):
        for first, inside in ((cap, lane < slots), (cap + hub_own, lane >= slots)):
            places = jnp.where((row == first + entry) & inside, hub_ref[entry], places)
    places_ref[...] = places
    column = jnp.broadcast_to(places, (LANES, lane.shape[1])).T[: slots + 2 * tall, :]
    node = iota(column.shape, 1)
    chosen = [
        jnp.where(node + first == column, F32(1.0), F32(0.0)).astype(BF16)
        for first in range(0, feats_ref.shape[0], LANES)
    ]
    copies[2].wait()
    copies[3].wait()
    find_slots(sizes, degree_ref, edge_ref, slot_ref, share_ref)
    count_edges(slot_ref, own_count_ref, far_count_ref, hot_ref, slice(0, TILE))
    copies[4].wait()
    picked = matmul(jnp.concatenate(chosen, axis=1), feats_ref[...]).astype(BF16)
    rows_ref[...] = picked[:slots, :]
    hubs_ref[...] = picked[slots:, :]
    for copy in copies[5:]:
        copy.wait()


def message_kernel(sizes, rows_ref, hubs_ref, after_ref, message_ref):
    doms, reps, cap, hub_own, tall = sizes
    del after_ref
    rows = rows_ref[...].astype(F32)
    hubs = hubs_ref[...].astype(F32)[:tall, :]
    place = iota(hubs.shape, 0)
    pair = lax.axis_index("pair")
    pairs = reps // SIDES
    for dom in range(doms):
        block = rows[dom * tall : (dom + 1) * tall, :]
        blocks = [
            jnp.where((place >= cap) | (pair == other), block, F32(0.0)) + hubs
            for other in range(pairs)
        ]
        first = dom * pairs * tall
        message_ref[first : first + pairs * tall, :] = jnp.concatenate(blocks, axis=0).astype(BF16)


def count_edges(slot_ref, own_count_ref, far_count_ref, hot_ref, nodes):
    fanout, rows = slot_ref.shape[0], own_count_ref.shape[0]
    highs = (rows + far_count_ref.shape[0]) // LANES
    low, high = [], []
    for k in range(fanout):
        slot = jnp.broadcast_to(slot_ref[k : k + 1, nodes], (STRIP, TILE))
        low.append(remainder(slot, LANES).astype(jnp.int16))
        high.append(div_floor(slot, LANES).astype(jnp.int16))
    for block in range(highs):
        for k in range(fanout):
            hot_ref[block * fanout + k] = jnp.where(high[k] == block, BF16(1.0), BF16(0.0))
    for strip in range(0, LANES, 2 * STRIP):
        hot = []
        for start in (strip, strip + STRIP):
            numbers = (iota((STRIP, TILE), 0) + start).astype(jnp.int16)
            hot.append([jnp.where(numbers == low[k], BF16(1.0), BF16(0.0)) for k in range(fanout)])

        def count(block):
            part = hot_ref[block * fanout]
            totals = [hot[0][0] * part, hot[1][0] * part]
            for k in range(1, fanout):
                part = hot_ref[block * fanout + k]
                totals = [total + each[k] * part for total, each in zip(totals, hot)]
            return jnp.concatenate(totals, axis=0)

        for block in range(rows // LANES):
            first = block * LANES + strip
            own_count_ref[first : first + 2 * STRIP, :] = count(block)
        far = far_count_ref.shape[0] // LANES
        if far <= 4:
            for block in range(far):
                first = block * LANES + strip
                far_count_ref[first : first + 2 * STRIP, :] = count(rows // LANES + block)
        else:

            @pl.loop(0, far)
            def far_block(block):
                first = pl.multiple_of(block * LANES + strip, 2 * STRIP)
                far_count_ref[pl.ds(first, 2 * STRIP), :] = count(rows // LANES + block)


def find_slots(sizes, degree_ref, edge_ref, slot_ref, share_ref):
    doms, reps, cap, hub_own, tall = sizes
    fanout, rows = edge_ref.shape
    hubs = doms * reps * hub_own
    source = edge_ref[...]
    hub = source - rows
    halo = hub - hubs
    chip = SIDES * hub_own
    entry = remainder(hub, chip) ^ (lax.axis_index("side") * hub_own)
    hub_slot = rows + cap + div_floor(hub, chip) * tall + entry
    peer = div_floor(halo, cap) * (reps // SIDES) + lax.axis_index("pair")
    halo_slot = rows + peer * tall + remainder(halo, cap)
    slot = jnp.where(source < rows, source, jnp.where(hub < hubs, hub_slot, halo_slot))
    valid = jnp.minimum(degree_ref[...], fanout)
    slot_ref[...] = jnp.where(iota((fanout, rows), 0) < valid, slot, -1)
    share_ref[...] = 1.0 / valid.astype(F32)


def own_kernel(tiles, feats_ref, w_self_ref, bias_ref, slot_ref, *refs):
    first_count_ref, inputs, kept, refs = refs[0], refs[1:3], refs[3:5], refs[5:]
    turned_ref, total_ref, preact_ref = refs[:3]
    own_refs, far_refs, (hot_ref, sems) = (
        refs[3 : 2 + tiles],
        refs[2 + tiles : 1 + 2 * tiles],
        refs[1 + 2 * tiles :],
    )
    copies = fetch(zip(inputs, kept), sems)
    turned_ref[...] = feats_ref[...].T

    def own_sums(number, count_ref):
        nodes = slice(number * TILE, (number + 1) * TILE)
        total_ref[:, nodes] = matmul(turned_ref[...], count_ref[...])
        preact_ref[nodes, :] = matmul(feats_ref[nodes, :], w_self_ref[...]) + bias_ref[...]

    counted = first_count_ref
    for number in range(1, tiles):
        nodes = slice(number * TILE, (number + 1) * TILE)
        own_ref, far_ref = own_refs[number - 1], far_refs[number - 1]
        count_edges(slot_ref, own_ref, far_ref, hot_ref.at[number % 2], nodes)
        own_sums(number - 1, counted)
        counted = own_ref
    own_sums(tiles - 1, counted)
    for copy in copies:
        copy.wait()


def joint_kernel(sizes, remote_ref, turned_ref, total_ref, self_ref, *refs):
    doms, reps, cap, hub_own, tall = sizes
    rows, width = self_ref.shape
    tiles = [slice(first, first + TILE) for first in range(0, rows, TILE)]
    count_refs, refs = refs[: len(tiles)], refs[len(tiles) :]
    (
        share_ref,
        w_neigh_ref,
        cot_ref,
        outputs_hbm,
        w_own_ref,
        rest_ref,
        message_ref,
        low_ref,
        edge_grad_ref,
        bias_ref,
        outputs_ref,
        mean_ref,
        preact_ref,
        w_grad_ref,
        sems,
    ) = refs
    table = remote_ref[...].T

    def before_head(number):
        nodes = tiles[number]
        mean = total_ref[:, nodes] + matmul(table, count_refs[number][...])
        mean = (mean * share_ref[:, nodes]).astype(BF16)
        mean_ref[:, nodes] = mean
        preact_ref[nodes, :] = self_ref[nodes, :] + matmul(mean, w_neigh_ref[...], 0, 0)

    def node_sums(numbers):
        nodes = slice(tiles[numbers[0]].start, tiles[numbers[-1]].stop)
        low = low_ref[nodes, :]
        counts = jnp.concatenate([count_refs[k][...] for k in numbers], axis=1)
        return (
            matmul(turned_ref[:, nodes], low),
            matmul(mean_ref[:, nodes], low),
            matmul(counts, edge_grad_ref[nodes, :]),
        )

    bias_sum = jnp.zeros((8, width), F32)
    copies = []
    before_head(0)
    for number, nodes in enumerate(tiles):
        if number + 1 < len(tiles):
            before_head(number + 1)
        elif number:
            w_grad_ref[0], w_grad_ref[1], rest_ref[...] = node_sums(range(number))
        for start in range(nodes.start, nodes.stop, PIECE):
            piece = slice(start, start + PIECE)
            preact = preact_ref[piece, :]
            cot = cot_ref[piece, :].astype(F32)
            grown = jnp.exp(jnp.minimum(preact, 0.0))
            act = jnp.where(preact > 0.0, preact, grown - 1.0)
            square = jnp.sum(act * act, axis=1, keepdims=True)
            along = jnp.sum(act * cot, axis=1, keepdims=True)
            scale = lax.rsqrt(square * (1.0 / width) + NORM_EPS)
            outputs_ref[piece, :] = (act * scale).astype(BF16)
            pull = along * (scale * scale * scale) * (1.0 / width)
            grad_pre = (cot * scale - act * pull) * jnp.where(preact > 0.0, F32(1.0), grown)
            bias_sum = bias_sum + jnp.sum(grad_pre.reshape(PIECE // 8, 8, width), axis=0)
            low_ref[piece, :] = grad_pre.astype(BF16)
        copies += fetch(
            ((outputs_ref.at[nodes, :], outputs_hbm.at[nodes, :]),), sems.at[pl.ds(number, 1)]
        )
        share_column = jnp.broadcast_to(share_ref[:, nodes], (LANES, TILE)).T
        share_column = jnp.concatenate([share_column] * (width // LANES), axis=1)
        edge_grad = matmul(low_ref[nodes, :], w_neigh_ref[...], 1, 1) * share_column
        edge_grad_ref[nodes, :] = edge_grad.astype(BF16)

    w_self_sum, w_neigh_sum, remote = node_sums([len(tiles) - 1])
    if len(tiles) > 1:
        w_self_sum = w_self_sum + w_grad_ref[0]
        w_neigh_sum = w_neigh_sum + w_grad_ref[1]
        remote = remote + rest_ref[...]
    w_grad_ref[0] = w_self_sum
    w_grad_ref[1] = w_neigh_sum
    rest_ref[...] = remote
    bias_ref[...] = bias_sum
    bias_sum = jnp.broadcast_to(jnp.sum(bias_sum, axis=0, keepdims=True), (tall, width))
    bias_high = bias_sum.astype(BF16).astype(F32)
    place = iota((tall, width), 0)
    bias_rows = jnp.where(place == cap, bias_high, bias_sum - bias_high)
    bias_rows = jnp.where(place < cap, F32(0.0), bias_rows)
    message = remote.reshape(-1, tall, width)
    message = jnp.where((place < cap + hub_own)[None], bias_rows[None], message)
    message_ref[width:, :] = message.reshape(remote.shape).astype(BF16)
    mine = lax.axis_index("side")
    w_own_ref[...] = w_grad_ref[mine]
    message_ref[:width, :] = w_grad_ref[1 - mine].astype(BF16)
    for copy in copies:
        copy.wait()


def own_grad_kernel(low_ref, w_self_ref, edge_grad_ref, *refs):
    *count_refs, feat_grad_ref = refs
    for first in range(0, low_ref.shape[0], TILE):
        nodes = slice(first, first + TILE)
        counts = jnp.concatenate([count_ref[nodes, :] for count_ref in count_refs], axis=1)
        feat_grad_ref[nodes, :] = matmul(counts, edge_grad_ref[...]) + matmul(
            low_ref[nodes, :], w_self_ref[...], 1, 1
        )


def side_sum_kernel(own_ref, received_ref, after_ref, message_ref):
    del after_ref
    peers, slab, width = message_ref.shape
    w_grad = own_ref[...] + received_ref[:width, :].astype(F32)
    owners = width // slab
    w_grad = w_grad.reshape(owners, slab, width)
    if owners < peers:
        w_grad = jnp.concatenate([w_grad, jnp.zeros((peers - owners, slab, width), F32)], axis=0)
    message_ref[...] = w_grad.astype(BF16)


def peer_sum_kernel(sizes, slabs_ref, own_ref, received_ref, bias_ref, message_ref):
    doms, reps, cap, hub_own, tall = sizes
    peers, slab, width = slabs_ref.shape
    total = jnp.sum(slabs_ref[...].astype(F32), axis=0)
    received_ref = received_ref.at[width:, :]
    size = min(peers * tall, LANES)
    to, source = iota((size, size), 0), iota((size, size), 1)
    entry = remainder(to, tall) - cap
    moved = (source == to + hub_own) & (entry >= 0) & (entry < hub_own)
    moved = jnp.where(moved, F32(1.0), F32(0.0)).astype(BF16)
    rest = own_ref[...] + jnp.concatenate(
        [
            matmul(moved, received_ref[first : first + size, :])
            for first in range(0, peers * tall, size)
        ],
        axis=0,
    )
    place = iota((tall, width), 0)
    bias = received_ref[: 2 * tall, :].astype(F32)[:tall, :]
    bias = jnp.where((place >= cap) & (place < cap + BIAS_ROWS), bias, F32(0.0)) + bias_ref[...]
    bias = jnp.broadcast_to(jnp.sum(bias, axis=0, keepdims=True), (tall, width))
    bias_high = bias.astype(BF16).astype(F32)
    bias_rows = jnp.where(place == tall - 1, bias - bias_high, bias_high)
    rest = rest.reshape(peers, tall, width)
    rest = jnp.where((place < tall - BIAS_ROWS)[None], rest, bias_rows[None])
    total = jnp.broadcast_to(total[None], (peers, slab, width))
    message_ref[...] = jnp.concatenate([total, rest], axis=1).astype(BF16)


def feat_grad_kernel(sizes, slab, message_ref, places_ref, feat_grad_ref, out_ref):
    doms, reps, cap, hub_own, tall = sizes
    rows, width = out_ref.shape
    pairs = reps // SIDES
    returned = message_ref[...].astype(F32)[:, slab:, :].reshape(doms, pairs, tall, width)
    returned = [
        returned[:, pair].reshape(doms * tall, width).astype(BF16) for pair in range(pairs)
    ]
    chosen = one_hot(rows, places_ref[:, : doms * tall])
    for first in range(0, rows, TILE):
        nodes = slice(first, first + TILE)
        total = feat_grad_ref[nodes, :]
        for part in returned:
            total = total + matmul(chosen[nodes, :], part)
        out_ref[nodes, :] = total.astype(BF16)


def unit_kernel(slab, mine_ref, other_ref, self_hbm, neigh_hbm, bias_hbm, units_ref, bias_ref, sems):
    side = lax.axis_index("side")
    _, size, width = units_ref.shape
    bias = jnp.sum(mine_ref[...].astype(F32)[:, slab:, :], axis=0)[-BIAS_ROWS:, :]
    bias = jnp.sum(bias, axis=0, keepdims=True)
    bias_ref[...] = bias * lax.rsqrt(jnp.mean(bias * bias, axis=1, keepdims=True) + UNIT_EPS)
    copies = [
        pltpu.make_async_copy(source, target, sems.at[number])
        for number, (source, target) in enumerate(
            ((units_ref.at[0], self_hbm), (units_ref.at[1], neigh_hbm), (bias_ref, bias_hbm))
        )
    ]
    copies[2].start()
    for place, grad_ref in ((side, mine_ref), (1 - side, other_ref)):
        grad = grad_ref[: size // slab].astype(F32)[:, :slab, :].reshape(size, width)
        square = jnp.sum(jnp.sum(grad * grad, axis=0, keepdims=True), axis=1, keepdims=True)
        units_ref[place] = grad * lax.rsqrt(square * (1.0 / grad.size) + UNIT_EPS)
        for number, copy in enumerate(copies[:2]):
            pl.when(place == number)(copy.start)
    for copy in copies:
        copy.wait()


def call(kernel, out_shape, in_specs=None, scratch=(), cost=(0, 0), out_specs=None):
    specs = {"in_specs": in_specs, "out_specs": out_specs}
    return pl.pallas_call(
        kernel,
        out_shape=out_shape,
        **{name: spec for name, spec in specs.items() if spec is not None},
        scratch_shapes=list(scratch),
        compiler_params=pltpu.CompilerParams(vmem_limit_bytes=VMEM_LIMIT),
        cost_estimate=pl.CostEstimate(flops=cost[0], bytes_accessed=cost[1], transcendentals=0),
    )


def in_hbm(*arrays):
    return [pltpu.with_memory_space_constraint(array, pltpu.HBM) for array in arrays]


def swap(array, axes):
    return lax.all_to_all(array, axes, split_axis=0, concat_axis=0, tiled=True)


def other_side(array):
    return lax.ppermute(array, "side", [(0, 1), (1, 0)])


def on_device(
    doms, reps, feats, w_self, w_neigh, bias, out_cot, degree, edge_src, hub_rows, send_rows
):
    rows, width = feats.shape
    fanout = edge_src.shape[1]
    cap, hub_own = send_rows.shape[1], hub_rows.shape[0]
    peers = doms * reps // SIDES
    tall = cap + SIDES * hub_own
    if tall % 8 or tall < cap + hub_own + BIAS_ROWS or hub_own & (hub_own - 1):
        raise ValueError("message height")
    slots = peers * tall
    slab = max(8, width // peers)
    sizes = (doms, reps, cap, hub_own, tall)
    shape = jax.ShapeDtypeStruct
    hbm = pl.BlockSpec(memory_space=pltpu.HBM)
    vmem = pl.BlockSpec(memory_space=pltpu.VMEM)

    tiles = rows // TILE
    hot = pltpu.VMEM(((rows + slots) // LANES * fanout, STRIP, TILE), BF16)
    picked, hubs, places, feats_kept, w_self_kept, bias_kept, slot, share, *first_counts = call(
        functools.partial(pick_kernel, sizes),
        (
            shape((doms * tall, width), BF16),
            shape((2 * tall, width), BF16),
            shape((1, -(-(doms + 2) * tall // LANES) * LANES), jnp.int32),
            shape((rows, width), BF16),
            shape((width, width), BF16),
            shape((1, width), F32),
            shape((fanout, rows), jnp.int32),
            shape((1, rows), F32),
            shape((rows, TILE), BF16),
            shape((slots, TILE), BF16),
        ),
        [hbm] * 7,
        (
            pltpu.SMEM((hub_own,), jnp.int32),
            pltpu.SMEM((cap, doms), jnp.int32),
            pltpu.VMEM((1, rows), jnp.int32),
            pltpu.VMEM((fanout, rows), jnp.int32),
            hot,
            pltpu.SemaphoreType.DMA((7,)),
        ),
        cost=(2 * rows * slots * width, 2 * rows * width),
    )(
        *in_hbm(
            hub_rows,
            send_rows.T,
            degree.reshape(1, rows),
            edge_src.T,
            feats,
            w_self,
            bias.reshape(1, width),
        )
    )
    hubs = other_side(hubs)
    w_neigh_kept, cot_kept, turned, own_total, self_part, *counts = call(
        functools.partial(own_kernel, tiles),
        (
            shape((width, width), BF16),
            shape((rows, width), BF16),
            shape((width, rows), BF16),
            shape((width, rows), F32),
            shape((rows, width), F32),
            *((shape((rows, TILE), BF16),) * (tiles - 1)),
            *((shape((slots, TILE), BF16),) * (tiles - 1)),
        ),
        [vmem] * 5 + [hbm] * 2,
        (
            pltpu.VMEM((2, *hot.shape), BF16),
            pltpu.SemaphoreType.DMA((2,)),
        ),
        cost=(8 * rows * (rows + slots) * width, 12 * rows * width + 2 * rows * rows),
    )(feats_kept, w_self_kept, bias_kept, slot, first_counts[0], *in_hbm(w_neigh, out_cot))
    own_counts = [first_counts[0], *counts[: tiles - 1]]
    far_counts = [first_counts[1], *counts[tiles - 1 :]]
    message = call(
        functools.partial(message_kernel, sizes),
        shape((slots, width), BF16),
        [vmem, vmem, pl.BlockSpec(memory_space=pl.ANY)],
    )(picked, hubs, own_total)
    remote = swap(message, PEERS)

    outputs, w_own, rest, message, low, edge_grad, bias_sum = call(
        functools.partial(joint_kernel, sizes),
        (
            pltpu.HBM((rows, width), BF16),
            shape((width, width), F32),
            shape((slots, width), F32),
            shape((width + slots, width), BF16),
            shape((rows, width), BF16),
            shape((rows, width), BF16),
            shape((8, width), F32),
        ),
        out_specs=(hbm,) + (vmem,) * 6,
        scratch=(
            pltpu.VMEM((rows, width), BF16),
            pltpu.VMEM((width, rows), BF16),
            pltpu.VMEM((rows, width), F32),
            pltpu.VMEM((2, width, width), F32),
            pltpu.SemaphoreType.DMA((rows // TILE,)),
        ),
        cost=(4 * rows * slots * width + 8 * rows * width * width, 16 * rows * width),
    )(remote, turned, own_total, self_part, *far_counts, share, w_neigh_kept, cot_kept)

    received = other_side(message)
    feat_grad = call(
        own_grad_kernel,
        shape((rows, width), F32),
        cost=(2 * rows * rows * width + 2 * rows * width * width, 8 * rows * width),
    )(low, w_self_kept, edge_grad, *own_counts)
    message = call(
        side_sum_kernel,
        shape((peers, slab, width), BF16),
        [vmem, vmem, pl.BlockSpec(memory_space=pl.ANY)],
    )(w_own, received, feat_grad)
    slabs = swap(message, PEERS)
    message = call(
        functools.partial(peer_sum_kernel, sizes), shape((peers, slab + tall, width), BF16)
    )(slabs, rest, received, bias_sum)
    message = swap(message, PEERS)
    grad_feats = call(
        functools.partial(feat_grad_kernel, sizes, slab),
        shape((rows, width), BF16),
        cost=(4 * rows * slots * width, 6 * rows * width),
    )(message, places, feat_grad)
    unit_self, unit_neigh, unit_bias = call(
        functools.partial(unit_kernel, slab),
        (*((pltpu.HBM((width, width), F32),) * 2), pltpu.HBM((1, width), F32)),
        out_specs=(hbm,) * 3,
        scratch=(
            pltpu.VMEM((2, width, width), F32),
            pltpu.VMEM((1, width), F32),
            pltpu.SemaphoreType.DMA((3,)),
        ),
    )(message, other_side(message))
    return outputs, grad_feats, unit_self, unit_neigh, unit_bias.reshape(width)


def solution(mesh):
    doms, reps = mesh.shape["dom"], mesh.shape["rep"]
    split = jax.sharding.Mesh(mesh.devices.reshape(doms, reps // SIDES, SIDES), SPLIT_AXES)
    rows, whole = P(SPLIT_AXES, None), P()
    return jax.shard_map(
        functools.partial(on_device, doms, reps),
        mesh=split,
        in_specs=(rows, whole, whole, whole, rows, P(SPLIT_AXES), rows, P(SPLIT_AXES), rows),
        out_specs=(rows, rows, whole, whole, whole),
        check_vma=False,
    )
```

```python
import functools

import jax
import jax.numpy as jnp
from jax import lax
from jax.experimental import pallas as pl
from jax.experimental.pallas import tpu as pltpu
from jax.sharding import PartitionSpec as P

NORM_EPS = 1e-05
UNIT_EPS = 1e-06
SPLIT_AXES = ("dom", "pair", "side")
PEERS = ("dom", "pair")
SIDES = 2
VMEM_LIMIT = 32 * 1024 * 1024
F32 = jnp.float32
BF16 = jnp.bfloat16
TILE = 256
STRIP = 16
PIECE = 32
LANES = 128
BIAS_ROWS = 2


def div_floor(value, size):
    if size & (size - 1) == 0:
        return lax.shift_right_arithmetic(value, jnp.int32(size.bit_length() - 1))
    return value // size


def remainder(value, size):
    if size & (size - 1) == 0:
        return value & jnp.int32(size - 1)
    return value - (value // size) * size


def matmul(lhs, rhs, lhs_dim=1, rhs_dim=0):
    return lax.dot_general(
        lhs, rhs, (((lhs_dim,), (rhs_dim,)), ((), ())), preferred_element_type=F32
    )


def iota(shape, dim):
    return lax.broadcasted_iota(jnp.int32, shape, dim)


def one_hot(rows, places):
    return jnp.where(iota((rows, places.shape[1]), 0) == places, F32(1.0), F32(0.0)).astype(BF16)


def fetch(pairs, sems):
    copies = [
        pltpu.make_async_copy(source, target, sems.at[number])
        for number, (source, target) in enumerate(pairs)
    ]
    for copy in copies:
        copy.start()
    return copies


def pick_kernel(sizes, hub_hbm, send_hbm, *refs):
    doms, reps, cap, hub_own, tall = sizes
    inputs, (rows_ref, hubs_ref, places_ref), refs = refs[:5], refs[5:8], refs[8:]
    kept, (slot_ref, share_ref, own_count_ref, far_count_ref), refs = refs[:3], refs[3:7], refs[7:]
    hub_ref, send_ref, degree_ref, edge_ref, hot_ref, sems = refs
    feats_ref = kept[0]
    targets = (hub_ref, send_ref, degree_ref, edge_ref, *kept)
    copies = fetch(zip((hub_hbm, send_hbm, *inputs), targets), sems)
    slots = doms * tall
    lane = iota(places_ref.shape, 1)
    row = remainder(lane, tall)

    def list_entries(dom, places):
        for entry in range(cap):
            places = jnp.where(lane == dom * tall + entry, send_ref[entry, dom], places)
        return places

    copies[0].wait()
    copies[1].wait()
    places = jnp.full(lane.shape, -1, jnp.int32)
    if doms <= 16:
        for dom in range(doms):
            places = list_entries(dom, places)
    else:
        places = lax.fori_loop(0, doms, list_entries, places)
    for entry in range(hub_own):
        for first, inside in ((cap, lane < slots), (cap + hub_own, lane >= slots)):
            places = jnp.where((row == first + entry) & inside, hub_ref[entry], places)
    places_ref[...] = places
    column = jnp.broadcast_to(places, (LANES, lane.shape[1])).T[: slots + 2 * tall, :]
    node = iota(column.shape, 1)
    chosen = [
        jnp.where(node + first == column, F32(1.0), F32(0.0)).astype(BF16)
        for first in range(0, feats_ref.shape[0], LANES)
    ]
    copies[2].wait()
    copies[3].wait()
    find_slots(sizes, degree_ref, edge_ref, slot_ref, share_ref)
    count_edges(slot_ref, own_count_ref, far_count_ref, hot_ref, slice(0, TILE))
    copies[4].wait()
    picked = matmul(jnp.concatenate(chosen, axis=1), feats_ref[...]).astype(BF16)
    rows_ref[...] = picked[:slots, :]
    hubs_ref[...] = picked[slots:, :]
    for copy in copies[5:]:
        copy.wait()


def message_kernel(sizes, rows_ref, hubs_ref, after_ref, message_ref):
    doms, reps, cap, hub_own, tall = sizes
    del after_ref
    rows = rows_ref[...].astype(F32)
    hubs = hubs_ref[...].astype(F32)[:tall, :]
    place = iota(hubs.shape, 0)
    pair = lax.axis_index("pair")
    pairs = reps // SIDES
    for dom in range(doms):
        block = rows[dom * tall : (dom + 1) * tall, :]
        blocks = [
            jnp.where((place >= cap) | (pair == other), block, F32(0.0)) + hubs
            for other in range(pairs)
        ]
        first = dom * pairs * tall
        message_ref[first : first + pairs * tall, :] = jnp.concatenate(blocks, axis=0).astype(BF16)


def count_edges(slot_ref, own_count_ref, far_count_ref, hot_ref, nodes):
    fanout, rows = slot_ref.shape[0], own_count_ref.shape[0]
    highs = (rows + far_count_ref.shape[0]) // LANES
    low, high = [], []
    for k in range(fanout):
        slot = jnp.broadcast_to(slot_ref[k : k + 1, nodes], (STRIP, TILE))
        low.append(remainder(slot, LANES).astype(jnp.int16))
        high.append(div_floor(slot, LANES).astype(jnp.int16))
    for block in range(highs):
        for k in range(fanout):
            hot_ref[block * fanout + k] = jnp.where(high[k] == block, BF16(1.0), BF16(0.0))
    for strip in range(0, LANES, 2 * STRIP):
        hot = []
        for start in (strip, strip + STRIP):
            numbers = (iota((STRIP, TILE), 0) + start).astype(jnp.int16)
            hot.append([jnp.where(numbers == low[k], BF16(1.0), BF16(0.0)) for k in range(fanout)])

        def count(block):
            part = hot_ref[block * fanout]
            totals = [hot[0][0] * part, hot[1][0] * part]
            for k in range(1, fanout):
                part = hot_ref[block * fanout + k]
                totals = [total + each[k] * part for total, each in zip(totals, hot)]
            return jnp.concatenate(totals, axis=0)

        for block in range(rows // LANES):
            first = block * LANES + strip
            own_count_ref[first : first + 2 * STRIP, :] = count(block)
        far = far_count_ref.shape[0] // LANES
        if far <= 4:
            for block in range(far):
                first = block * LANES + strip
                far_count_ref[first : first + 2 * STRIP, :] = count(rows // LANES + block)
        else:

            @pl.loop(0, far)
            def far_block(block):
                first = pl.multiple_of(block * LANES + strip, 2 * STRIP)
                far_count_ref[pl.ds(first, 2 * STRIP), :] = count(rows // LANES + block)


def find_slots(sizes, degree_ref, edge_ref, slot_ref, share_ref):
    doms, reps, cap, hub_own, tall = sizes
    fanout, rows = edge_ref.shape
    hubs = doms * reps * hub_own
    source = edge_ref[...]
    hub = source - rows
    halo = hub - hubs
    chip = SIDES * hub_own
    entry = remainder(hub, chip) ^ (lax.axis_index("side") * hub_own)
    hub_slot = rows + cap + div_floor(hub, chip) * tall + entry
    peer = div_floor(halo, cap) * (reps // SIDES) + lax.axis_index("pair")
    halo_slot = rows + peer * tall + remainder(halo, cap)
    slot = jnp.where(source < rows, source, jnp.where(hub < hubs, hub_slot, halo_slot))
    valid = jnp.minimum(degree_ref[...], fanout)
    slot_ref[...] = jnp.where(iota((fanout, rows), 0) < valid, slot, -1)
    share_ref[...] = 1.0 / valid.astype(F32)


def own_kernel(tiles, feats_ref, w_self_ref, bias_ref, slot_ref, *refs):
    first_count_ref, inputs, kept, refs = refs[0], refs[1:3], refs[3:5], refs[5:]
    turned_ref, total_ref, preact_ref = refs[:3]
    own_refs, far_refs, (hot_ref, sems) = (
        refs[3 : 2 + tiles],
        refs[2 + tiles : 1 + 2 * tiles],
        refs[1 + 2 * tiles :],
    )
    copies = fetch(zip(inputs, kept), sems)
    turned_ref[...] = feats_ref[...].T

    def own_sums(number, count_ref):
        nodes = slice(number * TILE, (number + 1) * TILE)
        total_ref[:, nodes] = matmul(turned_ref[...], count_ref[...])
        preact_ref[nodes, :] = matmul(feats_ref[nodes, :], w_self_ref[...]) + bias_ref[...]

    counted = first_count_ref
    for number in range(1, tiles):
        nodes = slice(number * TILE, (number + 1) * TILE)
        own_ref, far_ref = own_refs[number - 1], far_refs[number - 1]
        count_edges(slot_ref, own_ref, far_ref, hot_ref.at[number % 2], nodes)
        own_sums(number - 1, counted)
        counted = own_ref
    own_sums(tiles - 1, counted)
    for copy in copies:
        copy.wait()


def joint_kernel(sizes, remote_ref, turned_ref, total_ref, self_ref, *refs):
    doms, reps, cap, hub_own, tall = sizes
    rows, width = self_ref.shape
    tiles = [slice(first, first + TILE) for first in range(0, rows, TILE)]
    count_refs, refs = refs[: len(tiles)], refs[len(tiles) :]
    (
        share_ref,
        w_neigh_ref,
        cot_ref,
        outputs_hbm,
        w_own_ref,
        rest_ref,
        message_ref,
        low_ref,
        edge_grad_ref,
        bias_ref,
        outputs_ref,
        mean_ref,
        preact_ref,
        w_grad_ref,
        sems,
    ) = refs
    table = remote_ref[...].T

    def before_head(number):
        nodes = tiles[number]
        mean = total_ref[:, nodes] + matmul(table, count_refs[number][...])
        mean = (mean * share_ref[:, nodes]).astype(BF16)
        mean_ref[:, nodes] = mean
        preact_ref[nodes, :] = self_ref[nodes, :] + matmul(mean, w_neigh_ref[...], 0, 0)

    def node_sums(numbers):
        nodes = slice(tiles[numbers[0]].start, tiles[numbers[-1]].stop)
        low = low_ref[nodes, :]
        return (
            matmul(turned_ref[:, nodes], low),
            matmul(mean_ref[:, nodes], low),
            sum(matmul(count_refs[k][...], edge_grad_ref[tiles[k], :]) for k in numbers),
        )

    bias_sum = jnp.zeros((8, width), F32)
    copies = []
    before_head(0)
    for number, nodes in enumerate(tiles):
        if number + 1 < len(tiles):
            before_head(number + 1)
        elif number:
            w_grad_ref[0], w_grad_ref[1], rest_ref[...] = node_sums(range(number))
        for start in range(nodes.start, nodes.stop, PIECE):
            piece = slice(start, start + PIECE)
            preact = preact_ref[piece, :]
            cot = cot_ref[piece, :].astype(F32)
            grown = jnp.exp(jnp.minimum(preact, 0.0))
            act = jnp.where(preact > 0.0, preact, grown - 1.0)
            square = jnp.sum(act * act, axis=1, keepdims=True)
            along = jnp.sum(act * cot, axis=1, keepdims=True)
            scale = lax.rsqrt(square * (1.0 / width) + NORM_EPS)
            outputs_ref[piece, :] = (act * scale).astype(BF16)
            pull = along * (scale * scale * scale) * (1.0 / width)
            grad_pre = (cot * scale - act * pull) * jnp.where(preact > 0.0, F32(1.0), grown)
            bias_sum = bias_sum + jnp.sum(grad_pre.reshape(PIECE // 8, 8, width), axis=0)
            low_ref[piece, :] = grad_pre.astype(BF16)
        copies += fetch(
            ((outputs_ref.at[nodes, :], outputs_hbm.at[nodes, :]),), sems.at[pl.ds(number, 1)]
        )
        share_column = jnp.broadcast_to(share_ref[:, nodes], (LANES, TILE)).T
        share_column = jnp.concatenate([share_column] * (width // LANES), axis=1)
        edge_grad = matmul(low_ref[nodes, :], w_neigh_ref[...], 1, 1) * share_column
        edge_grad_ref[nodes, :] = edge_grad.astype(BF16)

    w_self_sum, w_neigh_sum, remote = node_sums([len(tiles) - 1])
    if len(tiles) > 1:
        w_self_sum = w_self_sum + w_grad_ref[0]
        w_neigh_sum = w_neigh_sum + w_grad_ref[1]
        remote = remote + rest_ref[...]
    w_grad_ref[0] = w_self_sum
    w_grad_ref[1] = w_neigh_sum
    rest_ref[...] = remote
    bias_ref[...] = bias_sum
    bias_sum = jnp.broadcast_to(jnp.sum(bias_sum, axis=0, keepdims=True), (tall, width))
    bias_high = bias_sum.astype(BF16).astype(F32)
    place = iota((tall, width), 0)
    bias_rows = jnp.where(place == 0, bias_high, bias_sum - bias_high)
    hubs = remote.shape[0] // tall * hub_own
    row = iota((hubs, remote.shape[0]), 0)
    source = div_floor(row, hub_own) * tall + cap + hub_own + remainder(row, hub_own)
    wanted = iota(source.shape, 1) == source
    wanted = jnp.where(wanted, F32(1.0), F32(0.0)).astype(BF16)
    packed = [matmul(wanted, remote.astype(BF16)), bias_rows, jnp.zeros_like(bias_rows)]
    message_ref[width:, :] = jnp.concatenate(packed, axis=0).astype(BF16)
    mine = lax.axis_index("side")
    w_own_ref[...] = w_grad_ref[mine]
    message_ref[:width, :] = w_grad_ref[1 - mine].astype(BF16)
    for copy in copies:
        copy.wait()


def own_grad_kernel(low_ref, w_self_ref, edge_grad_ref, *refs):
    *count_refs, feat_grad_ref = refs
    for first in range(0, low_ref.shape[0], TILE):
        nodes = slice(first, first + TILE)
        total = matmul(low_ref[nodes, :], w_self_ref[...], 1, 1)
        for number, count_ref in enumerate(count_refs):
            edges = edge_grad_ref[number * TILE : (number + 1) * TILE, :]
            total = total + matmul(count_ref[nodes, :], edges)
        feat_grad_ref[nodes, :] = total


def side_sum_kernel(own_ref, received_ref, after_ref, message_ref):
    del after_ref
    peers, slab, width = message_ref.shape
    w_grad = own_ref[...] + received_ref[:width, :].astype(F32)
    owners = width // slab
    w_grad = w_grad.reshape(owners, slab, width)
    if owners < peers:
        w_grad = jnp.concatenate([w_grad, jnp.zeros((peers - owners, slab, width), F32)], axis=0)
    message_ref[...] = w_grad.astype(BF16)


def peer_sum_kernel(sizes, slabs_ref, own_ref, received_ref, bias_ref, message_ref):
    doms, reps, cap, hub_own, tall = sizes
    peers, slab, width = slabs_ref.shape
    total = jnp.sum(slabs_ref[...].astype(F32), axis=0)
    received_ref = received_ref.at[width:, :]
    hubs = peers * hub_own
    to, source = iota((peers * tall, hubs), 0), iota((peers * tall, hubs), 1)
    entry = remainder(to, tall) - cap
    moved = (source == div_floor(to, tall) * hub_own + entry) & (entry >= 0) & (entry < hub_own)
    moved = jnp.where(moved, F32(1.0), F32(0.0)).astype(BF16)
    rest = own_ref[...] + matmul(moved, received_ref[:hubs, :])
    place = iota((tall, width), 0)
    bias = received_ref[hubs:, :].astype(F32)[:tall, :]
    bias = jnp.where(place < BIAS_ROWS, bias, F32(0.0)) + bias_ref[...]
    bias = jnp.broadcast_to(jnp.sum(bias, axis=0, keepdims=True), (tall, width))
    bias_high = bias.astype(BF16).astype(F32)
    bias_rows = jnp.where(place == tall - 1, bias - bias_high, bias_high)
    rest = rest.reshape(peers, tall, width)
    rest = jnp.where((place < tall - BIAS_ROWS)[None], rest, bias_rows[None])
    total = jnp.broadcast_to(total[None], (peers, slab, width))
    message_ref[...] = jnp.concatenate([total, rest], axis=1).astype(BF16)


def feat_grad_kernel(sizes, slab, message_ref, places_ref, feat_grad_ref, out_ref):
    doms, reps, cap, hub_own, tall = sizes
    rows, width = out_ref.shape
    pairs = reps // SIDES
    returned = message_ref[...].astype(F32)[:, slab:, :].reshape(doms, pairs, tall, width)
    returned = [
        returned[:, pair].reshape(doms * tall, width).astype(BF16) for pair in range(pairs)
    ]
    chosen = one_hot(rows, places_ref[:, : doms * tall])
    for first in range(0, rows, TILE):
        nodes = slice(first, first + TILE)
        total = feat_grad_ref[nodes, :]
        for part in returned:
            total = total + matmul(chosen[nodes, :], part)
        out_ref[nodes, :] = total.astype(BF16)


def unit_kernel(slab, mine_ref, other_ref, self_hbm, neigh_hbm, bias_hbm, units_ref, bias_ref, sems):
    side = lax.axis_index("side")
    _, size, width = units_ref.shape
    bias = jnp.sum(mine_ref[...].astype(F32)[:, slab:, :], axis=0)[-BIAS_ROWS:, :]
    bias = jnp.sum(bias, axis=0, keepdims=True)
    bias_ref[...] = bias * lax.rsqrt(jnp.mean(bias * bias, axis=1, keepdims=True) + UNIT_EPS)
    copies = [
        pltpu.make_async_copy(source, target, sems.at[number])
        for number, (source, target) in enumerate(
            ((units_ref.at[0], self_hbm), (units_ref.at[1], neigh_hbm), (bias_ref, bias_hbm))
        )
    ]
    copies[2].start()
    for place, grad_ref in ((side, mine_ref), (1 - side, other_ref)):
        grad = grad_ref[: size // slab].astype(F32)[:, :slab, :].reshape(size, width)
        square = jnp.sum(jnp.sum(grad * grad, axis=0, keepdims=True), axis=1, keepdims=True)
        units_ref[place] = grad * lax.rsqrt(square * (1.0 / grad.size) + UNIT_EPS)
        for number, copy in enumerate(copies[:2]):
            pl.when(place == number)(copy.start)
    for copy in copies:
        copy.wait()


def call(kernel, out_shape, in_specs=None, scratch=(), cost=(0, 0), out_specs=None):
    specs = {"in_specs": in_specs, "out_specs": out_specs}
    return pl.pallas_call(
        kernel,
        out_shape=out_shape,
        **{name: spec for name, spec in specs.items() if spec is not None},
        scratch_shapes=list(scratch),
        compiler_params=pltpu.CompilerParams(vmem_limit_bytes=VMEM_LIMIT),
        cost_estimate=pl.CostEstimate(flops=cost[0], bytes_accessed=cost[1], transcendentals=0),
    )


def in_hbm(*arrays):
    return [pltpu.with_memory_space_constraint(array, pltpu.HBM) for array in arrays]


def swap(array, axes):
    return lax.all_to_all(array, axes, split_axis=0, concat_axis=0, tiled=True)


def other_side(array):
    return lax.ppermute(array, "side", [(0, 1), (1, 0)])


def on_device(
    doms, reps, feats, w_self, w_neigh, bias, out_cot, degree, edge_src, hub_rows, send_rows
):
    rows, width = feats.shape
    fanout = edge_src.shape[1]
    cap, hub_own = send_rows.shape[1], hub_rows.shape[0]
    peers = doms * reps // SIDES
    tall = cap + SIDES * hub_own
    if tall % 8 or tall < cap + hub_own + BIAS_ROWS or hub_own & (hub_own - 1):
        raise ValueError("message height")
    slots = peers * tall
    slab = max(8, width // peers)
    sizes = (doms, reps, cap, hub_own, tall)
    shape = jax.ShapeDtypeStruct
    hbm = pl.BlockSpec(memory_space=pltpu.HBM)
    vmem = pl.BlockSpec(memory_space=pltpu.VMEM)

    tiles = rows // TILE
    hot = pltpu.VMEM(((rows + slots) // LANES * fanout, STRIP, TILE), BF16)
    picked, hubs, places, feats_kept, w_self_kept, bias_kept, slot, share, *first_counts = call(
        functools.partial(pick_kernel, sizes),
        (
            shape((doms * tall, width), BF16),
            shape((2 * tall, width), BF16),
            shape((1, -(-(doms + 2) * tall // LANES) * LANES), jnp.int32),
            shape((rows, width), BF16),
            shape((width, width), BF16),
            shape((1, width), F32),
            shape((fanout, rows), jnp.int32),
            shape((1, rows), F32),
            shape((rows, TILE), BF16),
            shape((slots, TILE), BF16),
        ),
        [hbm] * 7,
        (
            pltpu.SMEM((hub_own,), jnp.int32),
            pltpu.SMEM((cap, doms), jnp.int32),
            pltpu.VMEM((1, rows), jnp.int32),
            pltpu.VMEM((fanout, rows), jnp.int32),
            hot,
            pltpu.SemaphoreType.DMA((7,)),
        ),
        cost=(2 * rows * slots * width, 2 * rows * width),
    )(
        *in_hbm(
            hub_rows,
            send_rows.T,
            degree.reshape(1, rows),
            edge_src.T,
            feats,
            w_self,
            bias.reshape(1, width),
        )
    )
    hubs = other_side(hubs)
    w_neigh_kept, cot_kept, turned, own_total, self_part, *counts = call(
        functools.partial(own_kernel, tiles),
        (
            shape((width, width), BF16),
            shape((rows, width), BF16),
            shape((width, rows), BF16),
            shape((width, rows), F32),
            shape((rows, width), F32),
            *((shape((rows, TILE), BF16),) * (tiles - 1)),
            *((shape((slots, TILE), BF16),) * (tiles - 1)),
        ),
        [vmem] * 5 + [hbm] * 2,
        (
            pltpu.VMEM((2, *hot.shape), BF16),
            pltpu.SemaphoreType.DMA((2,)),
        ),
        cost=(8 * rows * (rows + slots) * width, 12 * rows * width + 2 * rows * rows),
    )(feats_kept, w_self_kept, bias_kept, slot, first_counts[0], *in_hbm(w_neigh, out_cot))
    own_counts = [first_counts[0], *counts[: tiles - 1]]
    far_counts = [first_counts[1], *counts[tiles - 1 :]]
    message = call(
        functools.partial(message_kernel, sizes),
        shape((slots, width), BF16),
        [vmem, vmem, pl.BlockSpec(memory_space=pl.ANY)],
    )(picked, hubs, own_total)
    remote = swap(message, PEERS)

    outputs, w_own, rest, message, low, edge_grad, bias_sum = call(
        functools.partial(joint_kernel, sizes),
        (
            pltpu.HBM((rows, width), BF16),
            shape((width, width), F32),
            shape((slots, width), F32),
            shape((width + peers * hub_own + 2 * tall, width), BF16),
            shape((rows, width), BF16),
            shape((rows, width), BF16),
            shape((8, width), F32),
        ),
        out_specs=(hbm,) + (vmem,) * 6,
        scratch=(
            pltpu.VMEM((rows, width), BF16),
            pltpu.VMEM((width, rows), BF16),
            pltpu.VMEM((rows, width), F32),
            pltpu.VMEM((2, width, width), F32),
            pltpu.SemaphoreType.DMA((rows // TILE,)),
        ),
        cost=(4 * rows * slots * width + 8 * rows * width * width, 16 * rows * width),
    )(remote, turned, own_total, self_part, *far_counts, share, w_neigh_kept, cot_kept)

    received = other_side(message)
    feat_grad = call(
        own_grad_kernel,
        shape((rows, width), F32),
        cost=(2 * rows * rows * width + 2 * rows * width * width, 8 * rows * width),
    )(low, w_self_kept, edge_grad, *own_counts)
    message = call(
        side_sum_kernel,
        shape((peers, slab, width), BF16),
        [vmem, vmem, pl.BlockSpec(memory_space=pl.ANY)],
    )(w_own, received, feat_grad)
    slabs = swap(message, PEERS)
    message = call(
        functools.partial(peer_sum_kernel, sizes), shape((peers, slab + tall, width), BF16)
    )(slabs, rest, received, bias_sum)
    message = swap(message, PEERS)
    grad_feats = call(
        functools.partial(feat_grad_kernel, sizes, slab),
        shape((rows, width), BF16),
        cost=(4 * rows * slots * width, 6 * rows * width),
    )(message, places, feat_grad)
    unit_self, unit_neigh, unit_bias = call(
        functools.partial(unit_kernel, slab),
        (*((pltpu.HBM((width, width), F32),) * 2), pltpu.HBM((1, width), F32)),
        out_specs=(hbm,) * 3,
        scratch=(
            pltpu.VMEM((2, width, width), F32),
            pltpu.VMEM((1, width), F32),
            pltpu.SemaphoreType.DMA((3,)),
        ),
    )(message, other_side(message))
    return outputs, grad_feats, unit_self, unit_neigh, unit_bias.reshape(width)


def solution(mesh):
    doms, reps = mesh.shape["dom"], mesh.shape["rep"]
    split = jax.sharding.Mesh(mesh.devices.reshape(doms, reps // SIDES, SIDES), SPLIT_AXES)
    rows, whole = P(SPLIT_AXES, None), P()
    return jax.shard_map(
        functools.partial(on_device, doms, reps),
        mesh=split,
        in_specs=(rows, whole, whole, whole, rows, P(SPLIT_AXES), rows, P(SPLIT_AXES), rows),
        out_specs=(rows, rows, whole, whole, whole),
        check_vma=False,
    )
```
